32 devices in a mesh: groups: 2 (over y), gx: 4 (over x, core), gy: 4 (over z).
Axes of the slice: x: 2, y: 2, z: 4, core: 2. Of those that a mesh axis runs over, the one named last changes fastest.
Arguments:
- field: bfloat16 [64, 16, 16, 512], P(None, ('groups', 'gx'), 'gy'), parts along dimension 1, may hold values from -100 to 100
- cotangent: bfloat16 [64, 16, 16, 512], P(None, ('groups', 'gx'), 'gy'), parts along dimension 1, may hold values from -6 to 6
- qk_weight: float32 [3, 2, 64, 64], replicated, may hold values from -0.75 to 0.75
- w_value: bfloat16 [64, 64], replicated, may hold values from -0.75 to 0.75
- w_out: bfloat16 [64, 64], replicated, may hold values from -0.75 to 0.75
Outputs:
- layer_output: bfloat16 [64, 16, 16, 512], P(None, ('groups', 'gx'), 'gy'), parts along dimension 1
- field_grad: bfloat16 [64, 16, 16, 512], P(None, ('groups', 'gx'), 'gy'), parts along dimension 1
The draws below stay inside these ranges and needn't reach their ends.
There are 2 independent parts, one for each index of `groups`. The reference program is written for one: setup_inputs(seed, part) draws one part's arguments, and reference() takes and returns one part's arrays. A program takes and returns all parts, laid end to end along the dimension named above; an argument that names none is the same for every part. Nothing has to cross between parts.
All inputs are finite; a program needn't handle non-finite values.
Results may differ from the reference program's by a relative error of at most 0.0075.
Values may be sent and summed in bfloat16 or wider, within the bound.
No kernel may reach another device: no remote copies, remote signals or barrier semaphores. Data moves between devices by JAX's collectives and lax.ppermute only.
A program may use at most 64 MiB of HBM per device.

```python
import math
import jax
import jax.numpy as jnp
from jax import lax

WIDTH = 64
HEADS = 8
HEAD_DIM = 8
GRID_Z = 512
GRID_X = 8
GRID_Y = 16


def draw_field(key, part):
    key = jax.random.fold_in(key, 7)
    keys_list = jax.random.split(key, 4)
    shape_full = (WIDTH, GRID_X, GRID_Y, GRID_Z)
    channel_scale = jnp.exp(jax.random.uniform(keys_list[0], (WIDTH, 1, 1, 1), jnp.float32, math.log(0.3), math.log(3.0)))
    place_x = jnp.arange(GRID_X, dtype=jnp.float32) / (GRID_X - 1) - 0.5
    place_y = jnp.arange(GRID_Y, dtype=jnp.float32) / (GRID_Y - 1) - 0.5
    ramp_x = jnp.exp(math.log(3.0) * place_x + jax.random.uniform(keys_list[1], (GRID_X,), jnp.float32, -0.22, 0.22))
    ramp_y = jnp.exp(math.log(3.0) * place_y + jax.random.uniform(keys_list[2], (GRID_Y,), jnp.float32, -0.22, 0.22))
    roughness = jax.random.normal(keys_list[3], shape_full, jnp.float32)
    roughness = jnp.clip(roughness, -6.0, 6.0)
    scaled = roughness * channel_scale * ramp_x[None, :, None, None] * ramp_y[None, None, :, None]
    return scaled.astype(jnp.bfloat16)


def block_levels(key, extent, pieces, least, largest):
    factor_of = 1.0
    for axis_at, blocks in pieces:
        draws = jax.random.uniform(jax.random.fold_in(jax.random.fold_in(key, 6), axis_at), (blocks,), jnp.float32, least / len(pieces), largest / len(pieces))
        factor_of = factor_of * jnp.repeat(jnp.exp(draws), extent[axis_at] // blocks).reshape((-1,) + (1,) * (len(extent) - 1 - axis_at))
    return factor_of


def centred(rng, shape, scale, reach, cuts=(), kind=jnp.bfloat16):
    drawn = jax.random.normal(rng, shape, jnp.float32) * scale
    if len(cuts) > 0:
        drawn = block_levels(rng, shape, cuts, -0.22, 0.18) * drawn
    return jnp.clip(drawn, min=-reach, max=reach).astype(kind)


def setup_inputs(seed: int = 0, part: int = 0) -> dict:
    seeds = jax.random.split(jax.random.key(seed), 6)
    part_splits = jax.random.split(jax.random.fold_in(seeds[5], part), 6)
    field = draw_field(jax.random.fold_in(jax.random.fold_in(seeds[5], part), 71), part)
    cotangent = centred(part_splits[1], (WIDTH, GRID_X, GRID_Y, GRID_Z), 1.0, 6.0, ((1, 4), (2, 4)))
    qk_weight = centred(seeds[2], (3, 2, WIDTH, WIDTH), WIDTH ** -0.5, 0.75, (), jnp.float32)
    w_value = centred(seeds[3], (WIDTH, WIDTH), WIDTH ** -0.5, 0.75)
    w_out = centred(seeds[4], (WIDTH, WIDTH), WIDTH ** -0.5, 0.75)
    return dict(field=field, cotangent=cotangent, qk_weight=qk_weight, w_value=w_value, w_out=w_out)


EPSILON = 1e-06
PRECISE = lax.Precision.HIGHEST

def axis_features(pooled, weights):
    inverse = lax.rsqrt(lax.optimization_barrier(jnp.mean(pooled * pooled, axis=0, keepdims=True)) + EPSILON)
    normed = pooled * inverse
    length = pooled.shape[1]
    factor = 1.0 / math.sqrt(HEAD_DIM * length)
    queries = jnp.dot(weights[0].T, normed, precision=PRECISE).reshape(HEADS, HEAD_DIM, length)
    keyset = jnp.dot(weights[1].T, normed, precision=PRECISE).reshape(HEADS, HEAD_DIM, length)
    kernel = (jnp.einsum('hdm,hdn->hmn', queries, keyset, precision=PRECISE) * factor).astype(jnp.bfloat16)
    return (kernel, normed, inverse, queries, keyset, factor)

def kernel_backward(gram, queries, keyset, factor):
    grad_query = factor * jnp.einsum('hmn,hdn->hdm', gram, keyset, precision=PRECISE)
    grad_keyset = factor * jnp.einsum('hmn,hdm->hdn', gram, queries, precision=PRECISE)
    return (grad_query, grad_keyset)

def pooled_grad(normed, inverse, weights, grad_query, grad_keyset):
    length = normed.shape[1]
    grad_normed = jnp.dot(weights[0], grad_query.reshape(WIDTH, length), precision=PRECISE)
    grad_normed = grad_normed + jnp.dot(weights[1], grad_keyset.reshape(WIDTH, length), precision=PRECISE)
    return inverse * (grad_normed - normed * lax.optimization_barrier(jnp.mean(grad_normed * normed, axis=0, keepdims=True)))

def mix_heads(pattern, kernel, tensor):

    def single(operands):
        return jnp.einsum(pattern, operands[0].astype(jnp.float32), operands[1].astype(jnp.float32)).astype(jnp.bfloat16)
    return lax.map(single, (kernel, tensor))

def gram_heads(pattern, left_side, right_side):

    def single(operands):
        return jnp.einsum(pattern, operands[0].astype(jnp.float32), operands[1].astype(jnp.float32))
    return lax.map(single, (left_side, right_side))

def reference(field, cotangent, qk_weight, w_value, w_out):
    cell_count = GRID_X * GRID_Y * GRID_Z
    pooled_x = lax.optimization_barrier(jnp.sum(field, axis=(2, 3), dtype=jnp.float32)) / (GRID_Y * GRID_Z)
    pooled_y = lax.optimization_barrier(jnp.sum(field, axis=(1, 3), dtype=jnp.float32)) / (GRID_X * GRID_Z)
    pooled_z = lax.optimization_barrier(jnp.sum(field, axis=(1, 2), dtype=jnp.float32)) / (GRID_X * GRID_Y)
    kernel_x, normed_x, inverse_x, query_x, keyset_x, factor_x = axis_features(pooled_x, qk_weight[0])
    kernel_y, normed_y, inverse_y, query_y, keyset_y, factor_y = axis_features(pooled_y, qk_weight[1])
    kernel_z, normed_z, inverse_z, query_z, keyset_z, factor_z = axis_features(pooled_z, qk_weight[2])
    values = jnp.dot(w_value.T, field.reshape(WIDTH, cell_count), preferred_element_type=jnp.float32).astype(jnp.bfloat16)
    values = values.reshape(HEADS, HEAD_DIM, GRID_X, GRID_Y, GRID_Z)
    after_z = mix_heads('zk,dxyk->dxyz', kernel_z, values)
    after_y = mix_heads('yj,dxjz->dxyz', kernel_y, after_z)
    after_x = mix_heads('xi,diyz->dxyz', kernel_x, after_y)
    projected = jnp.dot(w_out.T, after_x.reshape(WIDTH, cell_count), preferred_element_type=jnp.float32)
    layer_output = (projected + field.reshape(WIDTH, cell_count)).astype(jnp.bfloat16).reshape(WIDTH, GRID_X, GRID_Y, GRID_Z)
    upstream = jnp.dot(w_out, cotangent.reshape(WIDTH, cell_count), preferred_element_type=jnp.float32).astype(jnp.bfloat16)
    upstream = upstream.reshape(HEADS, HEAD_DIM, GRID_X, GRID_Y, GRID_Z)
    down_y = mix_heads('xi,dxyz->diyz', kernel_x, upstream)
    gram_x = gram_heads('dmyz,dnyz->mn', upstream, after_y)
    down_z = mix_heads('yj,dxyz->dxjz', kernel_y, down_y)
    gram_y = gram_heads('dxmz,dxnz->mn', down_y, after_z)
    grad_values = mix_heads('zk,dxyz->dxyk', kernel_z, down_z)
    gram_z = gram_heads('dxym,dxyn->mn', down_z, values)
    grads_x = kernel_backward(gram_x, query_x, keyset_x, factor_x)
    grads_y = kernel_backward(gram_y, query_y, keyset_y, factor_y)
    grads_z = kernel_backward(gram_z, query_z, keyset_z, factor_z)
    pull_x = pooled_grad(normed_x, inverse_x, qk_weight[0], grads_x[0], grads_x[1]) / (GRID_Y * GRID_Z)
    pull_y = pooled_grad(normed_y, inverse_y, qk_weight[1], grads_y[0], grads_y[1]) / (GRID_X * GRID_Z)
    pull_z = pooled_grad(normed_z, inverse_z, qk_weight[2], grads_z[0], grads_z[1]) / (GRID_X * GRID_Y)
    through_values = jnp.dot(w_value, grad_values.reshape(WIDTH, cell_count), preferred_element_type=jnp.float32)
    through_values = through_values.reshape(WIDTH, GRID_X, GRID_Y, GRID_Z)
    field_grad = (cotangent.astype(jnp.float32) + through_values + pull_x[:, :, None, None] + pull_y[:, None, :, None] + pull_z[:, None, None, :]).astype(jnp.bfloat16)
    return (layer_output, field_grad)
```

```python
import math

import jax
import jax.numpy as jnp
from jax import lax
from jax.sharding import PartitionSpec as P

WIDTH = 64
HEADS = 8
HEAD_DIM = 8
LANES = 128

EPSILON = 1e-06
PRECISE = lax.Precision.HIGHEST
AXES = ("gx", "gy")


def swap(part, axis, size, step):
    return lax.ppermute(part, axis, [(i, i ^ step) for i in range(size)])


def swap_gather(part, axis, size):
    found = jnp.stack([part] + [swap(part, axis, size, step) for step in range(1, size)])
    return found[jnp.arange(size) ^ lax.axis_index(axis)]


def swap_scatter(parts, axis, size):
    me = lax.axis_index(axis)
    total = parts[me]
    for step in range(1, size):
        total = total + swap(parts[me ^ step], axis, size, step)
    return total


def gather(part, count, flat=True):
    if flat:
        return swap_gather(part, AXES, count)
    size_x, size_y = lax.axis_size("gx"), lax.axis_size("gy")
    found = swap_gather(swap_gather(part, "gy", size_y), "gx", size_x)
    return found.reshape((count,) + part.shape)


def reduce_blocks(total, count):
    width, depth = total.shape
    blocks = total.reshape(width, depth // LANES, LANES).transpose(1, 0, 2)
    blocks = blocks.reshape(count, width * depth // LANES // count, LANES)
    size_x, size_y = lax.axis_size("gx"), lax.axis_size("gy")
    mine = swap_scatter(blocks.reshape((size_x, size_y) + blocks.shape[1:]), "gx", size_x)
    mine = swap_scatter(mine, "gy", size_y)
    whole = gather(mine, count).reshape(depth // LANES, width, LANES)
    return whole.transpose(1, 0, 2).reshape(width, depth)


def axis_features(pooled, weights):
    inverse = lax.rsqrt(jnp.mean(pooled * pooled, axis=0, keepdims=True) + EPSILON)
    normed = pooled * inverse
    length = pooled.shape[1]
    factor = 1.0 / math.sqrt(HEAD_DIM * length)
    queries = jnp.dot(weights[0].T, normed, precision=PRECISE).reshape(HEADS, HEAD_DIM, length)
    keyset = jnp.dot(weights[1].T, normed, precision=PRECISE).reshape(HEADS, HEAD_DIM, length)
    return (normed, inverse, queries, keyset, factor)


def axis_kernel(queries, keyset, factor):
    scores = jnp.einsum("hdm,hdn->hmn", queries, keyset, precision=PRECISE)
    return (scores * factor).astype(jnp.bfloat16)


def kernel_backward(gram, queries, keyset, factor):
    grad_query = factor * jnp.einsum("hmn,hdn->hdm", gram, keyset, precision=PRECISE)
    grad_keyset = factor * jnp.einsum("hmn,hdm->hdn", gram, queries, precision=PRECISE)
    return (grad_query, grad_keyset)


def grad_of_normed(weights, grad_query, grad_keyset):
    length = grad_query.shape[-1]
    grad_normed = jnp.dot(weights[0], grad_query.reshape(WIDTH, length), precision=PRECISE)
    return grad_normed + jnp.dot(
        weights[1], grad_keyset.reshape(WIDTH, length), precision=PRECISE
    )


def pooled_grad(normed, inverse, grad_normed):
    return inverse * (grad_normed - normed * jnp.mean(grad_normed * normed, axis=0, keepdims=True))


def f32_einsum(pattern, left, right):
    return jnp.einsum(pattern, left, right, preferred_element_type=jnp.float32)


def per_device(field, cotangent, qk_weight, w_value, w_out):
    span_x = lax.axis_size("gx")
    span_y = lax.axis_size("gy")
    count = span_x * span_y
    rows_x, rows_y, depth = field.shape[1:]
    cells = rows_x * rows_y
    grid_x = rows_x * span_x
    grid_y = rows_y * span_y
    start_x = lax.axis_index("gx") * rows_x
    start_y = lax.axis_index("gy") * rows_y
    bf16 = jnp.bfloat16

    cols = field.reshape(WIDTH, cells, depth)
    cots = cotangent.reshape(WIDTH, cells, depth)

    sum_z = jnp.sum(cols, axis=1, dtype=jnp.float32)
    sum_rows = jnp.sum(cols, axis=2, dtype=jnp.float32)
    rows_all = gather(sum_rows.T, count).reshape(span_x, span_y, rows_x, rows_y, WIDTH)
    total_x = jnp.sum(rows_all, axis=(1, 3)).reshape(grid_x, WIDTH).T
    total_y = jnp.sum(rows_all, axis=(0, 2)).reshape(grid_y, WIDTH).T
    total_z = reduce_blocks(sum_z, count)

    normed_x, inverse_x, query_x, keyset_x, factor_x = axis_features(
        total_x / (grid_y * depth), qk_weight[0]
    )
    normed_y, inverse_y, query_y, keyset_y, factor_y = axis_features(
        total_y / (grid_x * depth), qk_weight[1]
    )
    normed_z, inverse_z, query_z, keyset_z, factor_z = axis_features(
        total_z / (grid_x * grid_y), qk_weight[2]
    )
    kernel_x = axis_kernel(query_x, keyset_x, factor_x)
    kernel_y = axis_kernel(query_y, keyset_y, factor_y)
    query_b = query_z.astype(bf16)
    keyset_b = keyset_z.astype(bf16)

    wv = w_value.reshape(WIDTH, HEADS, HEAD_DIM)
    wo = w_out.reshape(HEADS, HEAD_DIM, WIDTH)
    coef_f = f32_einsum("cpk,hgk->cphg", cols, keyset_b)
    coef_c = f32_einsum("cpz,hgz->cphg", cots, query_b)
    low_f = jnp.einsum("chd,cphg->phdg", wv.astype(jnp.float32), coef_f, precision=PRECISE)
    low_c = jnp.einsum("hdc,cphg->phdg", wo.astype(jnp.float32), coef_c, precision=PRECISE)
    squares = HEAD_DIM * HEAD_DIM
    both = jnp.stack([low_f, low_c]).astype(bf16).reshape(2, cells, HEADS * squares)
    both = gather(both, count, False).reshape(span_x, span_y, 2, rows_x, rows_y, HEADS * squares)
    both = both.transpose(2, 0, 3, 1, 4, 5).reshape(2, grid_x, grid_y, HEADS, squares)
    low_f, low_c = both[0], both[1]

    mid_f = f32_einsum("hyj,xjhq->xyhq", kernel_y, low_f).astype(bf16)
    top_f = f32_einsum("hxi,iyhq->xyhq", kernel_x, mid_f)
    mid_c = f32_einsum("hxi,xyhq->iyhq", kernel_x, low_c).astype(bf16)
    top_c = f32_einsum("hyj,xyhq->xjhq", kernel_y, mid_c)
    gram_x = factor_z * f32_einsum("myhq,nyhq->hmn", low_c, mid_f)
    gram_y = factor_z * f32_einsum("xmhq,xnhq->hmn", mid_c, low_f)

    def here(top):
        top = lax.dynamic_slice_in_dim(top, start_x, rows_x, 0)
        top = lax.dynamic_slice_in_dim(top, start_y, rows_y, 1)
        return top.reshape(cells, HEADS, HEAD_DIM, HEAD_DIM)

    left_f = factor_z * jnp.einsum(
        "hdc,phdg->cphg", wo.astype(jnp.float32), here(top_f), precision=PRECISE
    )
    left_c = factor_z * jnp.einsum(
        "chd,phdg->cphg", wv.astype(jnp.float32), here(top_c), precision=PRECISE
    )
    left_f = left_f.astype(bf16)
    left_c = left_c.astype(bf16)

    grad_query_z = f32_einsum("cphg,cpz->hgz", left_f, cots)
    grad_keyset_z = f32_einsum("cphg,cpz->hgz", left_c, cols)
    gn_z = reduce_blocks(grad_of_normed(qk_weight[2], grad_query_z, grad_keyset_z), count)

    layer_output = (cols.astype(jnp.float32) + f32_einsum("cphg,hgz->cpz", left_f, query_b)).astype(bf16)
    through = f32_einsum("cphg,hgz->cpz", left_c, keyset_b)

    gn_x = grad_of_normed(qk_weight[0], *kernel_backward(gram_x, query_x, keyset_x, factor_x))
    gn_y = grad_of_normed(qk_weight[1], *kernel_backward(gram_y, query_y, keyset_y, factor_y))
    pull_x = pooled_grad(normed_x, inverse_x, gn_x)
    pull_y = pooled_grad(normed_y, inverse_y, gn_y)
    pull_z = pooled_grad(normed_z, inverse_z, gn_z)
    local_x = lax.dynamic_slice_in_dim(pull_x, start_x, rows_x, 1) / (grid_y * depth)
    local_y = lax.dynamic_slice_in_dim(pull_y, start_y, rows_y, 1) / (grid_x * depth)
    local_xy = (local_x[:, :, None] + local_y[:, None, :]).reshape(WIDTH, cells)
    local_z = pull_z / (grid_x * grid_y)
    field_grad = (
        cots.astype(jnp.float32) + through + local_xy[:, :, None] + local_z[:, None, :]
    ).astype(bf16)
    return (layer_output.reshape(field.shape), field_grad.reshape(field.shape))


def solution(mesh):
    placed = P(None, ("groups", "gx"), "gy", None)
    return jax.shard_map(
        per_device,
        mesh=mesh,
        in_specs=(placed, placed, P(), P(), P()),
        out_specs=(placed, placed),
        check_vma=False,
    )
```

```python
import functools
import math

import jax
import jax.numpy as jnp
import numpy as np
from jax import lax
from jax.experimental import pallas as pl
from jax.experimental.pallas import tpu as pltpu
from jax.sharding import PartitionSpec as P

WIDTH = 64
HEADS = 8
HEAD_DIM = 8
LANES = 128

EPSILON = 1e-06
PRECISE = lax.Precision.HIGHEST
AXES = ("gx", "gy")


def exchange(parts):
    return lax.all_to_all(parts, AXES, split_axis=0, concat_axis=0, tiled=True)


def gather(part, count):
    return exchange(jnp.broadcast_to(part[None], (count,) + part.shape))


def reduce_blocks(total, count):
    width, depth = total.shape
    blocks = total.reshape(width, depth // LANES, LANES).transpose(1, 0, 2)
    blocks = blocks.reshape(count, width * depth // LANES // count, LANES)
    mine = jnp.sum(exchange(blocks), axis=0)
    whole = gather(mine, count).reshape(depth // LANES, width, LANES)
    return whole.transpose(1, 0, 2).reshape(width, depth)


def axis_features(pooled, weights):
    inverse = lax.rsqrt(jnp.mean(pooled * pooled, axis=0, keepdims=True) + EPSILON)
    normed = pooled * inverse
    length = pooled.shape[1]
    factor = 1.0 / math.sqrt(HEAD_DIM * length)
    queries = jnp.dot(weights[0].T, normed, precision=PRECISE).reshape(HEADS, HEAD_DIM, length)
    keyset = jnp.dot(weights[1].T, normed, precision=PRECISE).reshape(HEADS, HEAD_DIM, length)
    return (normed, inverse, queries, keyset, factor)


def axis_kernel(queries, keyset, factor):
    scores = jnp.einsum("hdm,hdn->hmn", queries, keyset, precision=PRECISE)
    return (scores * factor).astype(jnp.bfloat16)


def kernel_backward(gram, queries, keyset, factor):
    grad_query = factor * jnp.einsum("hmn,hdn->hdm", gram, keyset, precision=PRECISE)
    grad_keyset = factor * jnp.einsum("hmn,hdm->hdn", gram, queries, precision=PRECISE)
    return (grad_query, grad_keyset)


def grad_of_normed(weights, grad_query, grad_keyset):
    length = grad_query.shape[-1]
    grad_normed = jnp.dot(weights[0], grad_query.reshape(WIDTH, length), precision=PRECISE)
    return grad_normed + jnp.dot(
        weights[1], grad_keyset.reshape(WIDTH, length), precision=PRECISE
    )


def pooled_grad(normed, inverse, grad_normed):
    return inverse * (grad_normed - normed * jnp.mean(grad_normed * normed, axis=0, keepdims=True))


def f32_einsum(pattern, left, right):
    return jnp.einsum(pattern, left, right, preferred_element_type=jnp.float32)


def per_device(field, cotangent, qk_weight, w_value, w_out):
    span_x = lax.axis_size("gx")
    span_y = lax.axis_size("gy")
    count = span_x * span_y
    rows_x, rows_y, depth = field.shape[1:]
    cells = rows_x * rows_y
    grid_x = rows_x * span_x
    grid_y = rows_y * span_y
    start_x = lax.axis_index("gx") * rows_x
    start_y = lax.axis_index("gy") * rows_y
    bf16 = jnp.bfloat16

    cols = field.reshape(WIDTH, cells, depth)
    cots = cotangent.reshape(WIDTH, cells, depth)

    sum_z = jnp.sum(cols, axis=1, dtype=jnp.float32)
    sum_rows = jnp.sum(cols, axis=2, dtype=jnp.float32)
    rows_all = gather(sum_rows.T, count).reshape(span_x, span_y, rows_x, rows_y, WIDTH)
    total_x = jnp.sum(rows_all, axis=(1, 3)).reshape(grid_x, WIDTH).T
    total_y = jnp.sum(rows_all, axis=(0, 2)).reshape(grid_y, WIDTH).T
    total_z = reduce_blocks(sum_z, count)

    normed_x, inverse_x, query_x, keyset_x, factor_x = axis_features(
        total_x / (grid_y * depth), qk_weight[0]
    )
    normed_y, inverse_y, query_y, keyset_y, factor_y = axis_features(
        total_y / (grid_x * depth), qk_weight[1]
    )
    normed_z, inverse_z, query_z, keyset_z, factor_z = axis_features(
        total_z / (grid_x * grid_y), qk_weight[2]
    )
    kernel_x = axis_kernel(query_x, keyset_x, factor_x)
    kernel_y = axis_kernel(query_y, keyset_y, factor_y)
    query_b = query_z.astype(bf16)
    keyset_b = keyset_z.astype(bf16)

    wv = w_value.reshape(WIDTH, HEADS, HEAD_DIM)
    wo = w_out.reshape(HEADS, HEAD_DIM, WIDTH)
    coef_f = f32_einsum("cpk,hgk->cphg", cols, keyset_b)
    coef_c = f32_einsum("cpz,hgz->cphg", cots, query_b)
    low_f = jnp.einsum("chd,cphg->phdg", wv.astype(jnp.float32), coef_f, precision=PRECISE)
    low_c = jnp.einsum("hdc,cphg->phdg", wo.astype(jnp.float32), coef_c, precision=PRECISE)
    squares = HEAD_DIM * HEAD_DIM
    both = jnp.stack([low_f, low_c]).astype(bf16).reshape(2, cells, HEADS * squares)
    both = gather(both, count).reshape(span_x, span_y, 2, rows_x, rows_y, HEADS * squares)
    both = both.transpose(2, 0, 3, 1, 4, 5).reshape(2, grid_x, grid_y, HEADS, squares)
    low_f, low_c = both[0], both[1]

    mid_f = f32_einsum("hyj,xjhq->xyhq", kernel_y, low_f).astype(bf16)
    top_f = f32_einsum("hxi,iyhq->xyhq", kernel_x, mid_f)
    mid_c = f32_einsum("hxi,xyhq->iyhq", kernel_x, low_c).astype(bf16)
    top_c = f32_einsum("hyj,xyhq->xjhq", kernel_y, mid_c)
    gram_x = factor_z * f32_einsum("myhq,nyhq->hmn", low_c, mid_f)
    gram_y = factor_z * f32_einsum("xmhq,xnhq->hmn", mid_c, low_f)

    def here(top):
        top = lax.dynamic_slice_in_dim(top, start_x, rows_x, 0)
        top = lax.dynamic_slice_in_dim(top, start_y, rows_y, 1)
        return top.reshape(cells, HEADS, HEAD_DIM, HEAD_DIM)

    left_f = factor_z * jnp.einsum(
        "hdc,phdg->cphg", wo.astype(jnp.float32), here(top_f), precision=PRECISE
    )
    left_c = factor_z * jnp.einsum(
        "chd,phdg->cphg", wv.astype(jnp.float32), here(top_c), precision=PRECISE
    )
    left_f = left_f.astype(bf16)
    left_c = left_c.astype(bf16)

    grad_query_z = f32_einsum("cphg,cpz->hgz", left_f, cots)
    grad_keyset_z = f32_einsum("cphg,cpz->hgz", left_c, cols)
    gn_z = reduce_blocks(grad_of_normed(qk_weight[2], grad_query_z, grad_keyset_z), count)

    layer_output = (cols.astype(jnp.float32) + f32_einsum("cphg,hgz->cpz", left_f, query_b)).astype(bf16)
    through = f32_einsum("cphg,hgz->cpz", left_c, keyset_b)

    gn_x = grad_of_normed(qk_weight[0], *kernel_backward(gram_x, query_x, keyset_x, factor_x))
    gn_y = grad_of_normed(qk_weight[1], *kernel_backward(gram_y, query_y, keyset_y, factor_y))
    pull_x = pooled_grad(normed_x, inverse_x, gn_x)
    pull_y = pooled_grad(normed_y, inverse_y, gn_y)
    pull_z = pooled_grad(normed_z, inverse_z, gn_z)
    local_x = lax.dynamic_slice_in_dim(pull_x, start_x, rows_x, 1) / (grid_y * depth)
    local_y = lax.dynamic_slice_in_dim(pull_y, start_y, rows_y, 1) / (grid_x * depth)
    local_xy = (local_x[:, :, None] + local_y[:, None, :]).reshape(WIDTH, cells)
    local_z = pull_z / (grid_x * grid_y)
    field_grad = (
        cots.astype(jnp.float32) + through + local_xy[:, :, None] + local_z[:, None, :]
    ).astype(bf16)
    return (layer_output.reshape(field.shape), field_grad.reshape(field.shape))


def split(x):
    high = x.astype(jnp.bfloat16)
    return high, (x - high.astype(jnp.float32)).astype(jnp.bfloat16)


NN = (((1,), (0,)), ((), ()))
NT = (((1,), (1,)), ((), ()))
TN = (((0,), (0,)), ((), ()))


def mul(left, right, dims=NN):
    return lax.dot_general(left, right, dims, preferred_element_type=jnp.float32)


def mul_near(left, right, dims=NN):
    left_high, left_low = split(left)
    right_high, right_low = split(right)
    return (
        mul(left_high, right_high, dims)
        + mul(left_low, right_high, dims)
        + mul(left_high, right_low, dims)
    )


def mul_left(left, right, dims=NN):
    high, low = split(left)
    return mul(high, right, dims) + mul(low, right, dims)


def number(shape, dim):
    return lax.broadcasted_iota(jnp.int32, shape, dim)


def put_blocks(ref, total):
    count = ref.shape[0]
    columns = total.shape[1] // LANES
    groups = count // columns
    rows = WIDTH // groups
    for block in range(count):
        column, group = block // groups, block % groups
        ref[block, 0:rows, :] = total[
            group * rows : (group + 1) * rows, column * LANES : (column + 1) * LANES
        ]


def whole_blocks(ref, depth):
    columns = depth // LANES
    blocks = ref[...].reshape(columns, WIDTH, LANES)
    return jnp.concatenate([blocks[i] for i in range(columns)], axis=1)


def prepare_kernel(wv_ref, wo_ref, qk_ref, wv_out, wo_out, wq_out, wk_out, wz_out):
    wide = HEADS * HEAD_DIM * HEAD_DIM
    row = number((WIDTH, wide), 0)
    lane = number((WIDTH, wide), 1)
    by_channel = ((lane >> 3) == row).astype(jnp.bfloat16)
    by_factor = (((lane >> 6) * HEAD_DIM + (lane & 7)) == row).astype(jnp.bfloat16)
    wv_out[...] = mul(wv_ref[...], by_channel)
    wo_out[...] = mul(wo_ref[...], by_channel, TN)
    for index, out in ((0, wq_out), (1, wk_out)):
        high, low = split(qk_ref[2, index])
        out[0:WIDTH, :] = mul(high, by_factor).astype(jnp.bfloat16)
        out[WIDTH : 2 * WIDTH, :] = mul(low, by_factor).astype(jnp.bfloat16)
        wz_out[index * WIDTH : (index + 1) * WIDTH, :] = qk_ref[2, index].T


def sums_kernel(field_ref, out_ref):
    data = field_ref[...]
    rows, depth = data.shape
    cells = rows // WIDTH
    pick = (number((WIDTH, rows), 1) // cells == number((WIDTH, rows), 0)).astype(jnp.bfloat16)
    part = mul(pick, data)
    row_sums = mul(data, jnp.ones((depth, LANES), jnp.bfloat16)).reshape(WIDTH, cells, LANES)
    shape = row_sums.shape
    own = jnp.sum(jnp.where(number(shape, 0) == number(shape, 2), row_sums, 0.0), axis=0)
    put_blocks(out_ref, part)
    for block in range(out_ref.shape[0]):
        out_ref[block, out_ref.shape[1] - cells :, :] = own


def add_kernel(recv_ref, out_ref):
    rows = out_ref.shape[1]
    total = jnp.sum(recv_ref[:, 0:rows, :], axis=0)
    out_ref[...] = jnp.broadcast_to(total[None], out_ref.shape)


def plane_kernel(cells, lengths, me_ref, recv_ref, same_ref, qk_ref, mix_ref, feat_ref):
    places = recv_ref.shape[0] * cells
    totals = recv_ref[:, recv_ref.shape[1] - cells :, :].reshape(places, LANES)[:, :WIDTH]
    here = pl.ds(pl.multiple_of(me_ref[0] * cells, cells), cells)
    head = (number((HEADS * cells, WIDTH), 0) // cells) == (number((HEADS * cells, WIDTH), 1) >> 3)
    high, low = split(totals)
    forward = backward = None
    for axis in range(2):
        same = same_ref[axis]
        pooled = (mul(same, high) + mul(same, low)) * (1.0 / lengths[axis][1])
        inverse = lax.rsqrt(jnp.mean(pooled * pooled, axis=1, keepdims=True) + EPSILON)
        normed = pooled * inverse
        query = mul_near(normed, qk_ref[axis, 0])
        keyset = mul_near(normed, qk_ref[axis, 1])
        feat_ref[4 * axis] = normed
        feat_ref[4 * axis + 1] = query
        feat_ref[4 * axis + 2] = keyset
        feat_ref[4 * axis + 3] = jnp.broadcast_to(inverse, (places, WIDTH))
        factor = 1.0 / math.sqrt(HEAD_DIM * lengths[axis][0])

        def local(index, other):
            rows = feat_ref[4 * axis + index, here, :]
            rows = jnp.broadcast_to(rows[None], (HEADS, cells, WIDTH)).reshape(-1, WIDTH)
            scores = mul_near(jnp.where(head, rows, 0.0), other, NT) * factor
            return scores.astype(jnp.bfloat16).astype(jnp.float32)

        one, two = local(1, keyset), local(2, query)
        forward = one if forward is None else forward * one
        backward = two if backward is None else backward * two
    mix_ref[0] = forward
    mix_ref[1] = backward


def coef_kernel(places, recv_ref, wz_ref, field_ref, cot_ref, wv_ref, wo_ref,
                send_ref, feat_ref, query_ref, keyset_ref):
    rows, depth = field_ref.shape
    cells = rows // WIDTH
    wide = HEADS * HEAD_DIM * HEAD_DIM
    pooled = whole_blocks(recv_ref, depth) * (1.0 / places)
    inverse = lax.rsqrt(jnp.mean(pooled * pooled, axis=0, keepdims=True) + EPSILON)
    normed = pooled * inverse
    feat_ref[0:WIDTH, :] = normed
    feat_ref[WIDTH:, :] = jnp.broadcast_to(inverse, (HEAD_DIM, depth))
    both = mul_near(wz_ref[...], normed)

    def expand(part):
        part = part.reshape(HEADS, 1, HEAD_DIM, depth)
        part = jnp.broadcast_to(part, (HEADS, HEAD_DIM, HEAD_DIM, depth))
        return part.reshape(wide, depth).astype(jnp.bfloat16)

    query = expand(both[:WIDTH])
    keyset = expand(both[WIDTH:])
    query_ref[...] = query
    keyset_ref[...] = keyset
    low_f = mul(field_ref[...], keyset, NT).reshape(WIDTH, cells, wide)
    low_f = jnp.sum(wv_ref[...][:, None, :] * low_f, axis=0)
    low_c = mul(cot_ref[...], query, NT).reshape(WIDTH, cells, wide)
    low_c = jnp.sum(wo_ref[...][:, None, :] * low_c, axis=0)
    low = jnp.concatenate([low_f, low_c], axis=0).astype(jnp.bfloat16)
    send_ref[...] = jnp.broadcast_to(low[None], send_ref.shape)


def mix_kernel(factor, recv_ref, mix_ref, wv_ref, wo_ref, wq_ref, wk_ref, field_ref, cot_ref,
               send_ref, left_f_ref, left_c_ref):
    rows = field_ref.shape[0]
    cells = rows // WIDTH
    places = recv_ref.shape[0] * cells
    wide = recv_ref.shape[2]
    both = recv_ref[...].astype(jnp.float32)
    shape = (HEADS, cells, wide)
    head = number(shape, 0) == (number(shape, 2) >> 6)

    def top(mix, low):
        low = low.reshape(places, wide).astype(jnp.bfloat16)
        found = mul_left(mix, low).reshape(shape)
        return jnp.sum(jnp.where(head, found, 0.0), axis=0) * factor

    left_f = wo_ref[...][:, None, :] * top(mix_ref[0], both[:, :cells])[None]
    left_f = left_f.reshape(rows, wide).astype(jnp.bfloat16)
    left_c = wv_ref[...][:, None, :] * top(mix_ref[1], both[:, cells:])[None]
    left_c = left_c.reshape(rows, wide).astype(jnp.bfloat16)
    left_f_ref[...] = left_f
    left_c_ref[...] = left_c

    def pull(weights, left, right):
        found = mul(weights, left, NT)
        return mul_left(found[:WIDTH] + found[WIDTH:], right)

    put_blocks(
        send_ref,
        pull(wq_ref[...], left_f, cot_ref[...]) + pull(wk_ref[...], left_c, field_ref[...]),
    )


def output_kernel(left_ref, query_ref, field_ref, out_ref):
    found = mul(left_ref[...], query_ref[...]) + field_ref[...].astype(jnp.float32)
    out_ref[...] = found.astype(jnp.bfloat16)


def gram_kernel(cells, lengths, factor_z, me_ref, recv_ref, feat_ref, same_ref, qk_ref, out_ref,
                found_ref):
    places = recv_ref.shape[0] * cells
    wide = recv_ref.shape[2]
    squares = HEAD_DIM * HEAD_DIM
    both = recv_ref[...].astype(jnp.float32)
    low_f = both[:, :cells].reshape(places, wide).astype(jnp.bfloat16)
    low_c = both[:, cells:].reshape(places, wide).astype(jnp.bfloat16)
    here = pl.ds(pl.multiple_of(me_ref[0] * cells, cells), cells)
    lane = number((places, LANES), 1)
    products = []
    for pair in range(wide // LANES):
        part_f = low_f[:, pair * LANES : (pair + 1) * LANES]
        part_c = low_c[:, pair * LANES : (pair + 1) * LANES]
        for half in range(LANES // squares):
            mine = (lane >> 6) == half
            products.append(mul(jnp.where(mine, part_c, jnp.zeros_like(part_c)), part_f, NT))
    product = jnp.concatenate(products, axis=0)
    heads = number((HEADS * places, WIDTH), 0) // places == number((HEADS * places, WIDTH), 1) >> 3

    def stack(part):
        part = jnp.broadcast_to(part[None], (HEADS, places, WIDTH)).reshape(-1, WIDTH)
        return jnp.where(heads, part, 0.0)

    factors = [1.0 / math.sqrt(HEAD_DIM * lengths[axis][0]) for axis in range(2)]
    queries = [stack(feat_ref[4 * axis + 1]) for axis in range(2)]
    keysets = [stack(feat_ref[4 * axis + 2]) for axis in range(2)]
    kernels = []
    for axis in range(2):
        scores = mul_near(queries[axis], feat_ref[4 * axis + 2], NT) * factors[axis]
        kernels.append(scores.astype(jnp.bfloat16).astype(jnp.float32))
    total = jnp.zeros((cells, WIDTH), jnp.float32)
    for axis in range(2):
        gram = (product * kernels[1 - axis]).astype(jnp.bfloat16)
        across = jnp.concatenate(
            [gram[h * places : (h + 1) * places] for h in range(HEADS)], axis=1
        )
        scale = factors[axis] * factor_z
        grad_query = mul(across, keysets[axis].astype(jnp.bfloat16)) * scale
        grad_keyset = mul(gram, queries[axis].astype(jnp.bfloat16), TN) * scale
        found = mul_near(grad_query, qk_ref[axis, 0], NT) + mul_near(grad_keyset, qk_ref[axis, 1], NT)
        high, low = split(found)
        found_ref[...] = mul(same_ref[axis], high) + mul(same_ref[axis], low)
        found = found_ref[here, :]
        normed = feat_ref[4 * axis, here, :]
        inverse = feat_ref[4 * axis + 3, here, :]
        found = found - normed * jnp.mean(found * normed, axis=1, keepdims=True)
        total = total + inverse * found * (1.0 / lengths[axis][1])
    out_ref[...] = total


def base_kernel(left_ref, keyset_ref, cot_ref, plane_ref, out_ref):
    rows = cot_ref.shape[0]
    cells = rows // WIDTH
    shape = (WIDTH, cells, WIDTH)
    own = jnp.where(number(shape, 0) == number(shape, 2), plane_ref[...][None], 0.0)
    plane = mul_left(own.reshape(rows, WIDTH), jnp.ones((WIDTH, LANES), jnp.bfloat16))
    found = mul(left_ref[...], keyset_ref[...]) + cot_ref[...].astype(jnp.float32)
    columns = found.shape[1] // LANES
    out_ref[...] = found + jnp.concatenate([plane] * columns, axis=1)


def final_kernel(places, recv_ref, feat_ref, base_ref, out_ref):
    rows, depth = base_ref.shape
    cells = rows // WIDTH
    found = whole_blocks(recv_ref, depth)
    normed = feat_ref[0:WIDTH, :]
    inverse = feat_ref[WIDTH : WIDTH + 1, :]
    found = inverse * (found - normed * jnp.mean(found * normed, axis=0, keepdims=True))
    found = found * (1.0 / places)
    total = base_ref[...].reshape(WIDTH, cells, depth) + found[:, None, :]
    out_ref[...] = total.reshape(rows, depth).astype(jnp.bfloat16)


def run(kernel, outs, operands, scalars=0, flops=0, scratch=()):
    vmem = pl.BlockSpec(memory_space=pltpu.VMEM)
    smem = pl.BlockSpec(memory_space=pltpu.SMEM)
    moved = sum(x.size * x.dtype.itemsize for x in tuple(operands) + tuple(outs))
    found = pl.pallas_call(
        kernel,
        out_shape=tuple(outs),
        in_specs=[smem] * scalars + [vmem] * (len(operands) - scalars),
        out_specs=tuple(vmem for _ in outs),
        scratch_shapes=list(scratch),
        compiler_params=pltpu.CompilerParams(vmem_limit_bytes=48 * 1024 * 1024),
        cost_estimate=pl.CostEstimate(flops=flops, bytes_accessed=moved, transcendentals=0),
    )(*operands)
    return found[0] if len(outs) == 1 else found


def per_device_kernels(field, cotangent, qk_weight, w_value, w_out):
    span_x = lax.axis_size("gx")
    span_y = lax.axis_size("gy")
    count = span_x * span_y
    rows_x, rows_y, depth = field.shape[1:]
    cells = rows_x * rows_y
    places = count * cells
    grid_x = rows_x * span_x
    grid_y = rows_y * span_y
    rows = WIDTH * cells
    wide = WIDTH * HEAD_DIM
    f32, bf16 = jnp.float32, jnp.bfloat16
    like = jax.ShapeDtypeStruct
    lengths = ((grid_x, grid_y * depth), (grid_y, grid_x * depth))
    me = (lax.axis_index("gx") * span_y + lax.axis_index("gy")).astype(jnp.int32).reshape(1)

    place = np.arange(places)
    at_x = place // cells // span_y * rows_x + place % cells // rows_y
    at_y = place // cells % span_y * rows_y + place % rows_y
    same = jnp.asarray(
        np.stack([at_x[:, None] == at_x[None], at_y[:, None] == at_y[None]]), dtype=bf16
    )

    cols = field.reshape(rows, depth)
    cots = cotangent.reshape(rows, depth)
    share = WIDTH * depth // LANES // count
    block = like((count, share, LANES), f32)
    factor_z = 1.0 / math.sqrt(HEAD_DIM * depth)
    cube = rows * wide * depth * 2

    sums = run(sums_kernel, [like((count, share + cells, LANES), f32)], (cols,), flops=cube // 4)
    recv = exchange(sums)
    wv, wo, wq, wk, wz = run(
        prepare_kernel,
        [like((WIDTH, wide), f32)] * 2 + [like((2 * WIDTH, wide), bf16)] * 2
        + [like((2 * WIDTH, WIDTH), f32)],
        (w_value, w_out, qk_weight),
        flops=cube // 8,
    )
    pooled = exchange(run(add_kernel, [block], (recv,)))
    mix, feat = run(
        functools.partial(plane_kernel, cells, lengths),
        [like((2, HEADS * cells, places), f32), like((8, places, WIDTH), f32)],
        (me, recv, same, qk_weight),
        scalars=1,
        flops=cube // 2,
    )
    send, feat_z, query, keyset = run(
        functools.partial(coef_kernel, grid_x * grid_y),
        [like((count, 2 * cells, wide), bf16), like((WIDTH + HEAD_DIM, depth), f32)]
        + [like((wide, depth), bf16)] * 2,
        (pooled, wz, cols, cots, wv, wo),
        flops=2 * cube,
    )
    low = exchange(send)
    send, left_f, left_c = run(
        functools.partial(mix_kernel, factor_z),
        [block, like((rows, wide), bf16), like((rows, wide), bf16)],
        (low, mix, wv, wo, wq, wk, cols, cots),
        flops=cube,
    )
    recv = exchange(send)
    layer_output = run(output_kernel, [like((rows, depth), bf16)], (left_f, query, cols), flops=cube)
    plane = run(
        functools.partial(gram_kernel, cells, lengths, factor_z),
        [like((cells, WIDTH), f32)],
        (me, low, feat, same, qk_weight),
        scalars=1,
        flops=2 * cube,
        scratch=[pltpu.VMEM((places, WIDTH), f32)],
    )
    pulled = exchange(run(add_kernel, [block], (recv,)))
    base = run(base_kernel, [like((rows, depth), f32)], (left_c, keyset, cots, plane), flops=cube)
    field_grad = run(
        functools.partial(final_kernel, grid_x * grid_y),
        [like((rows, depth), bf16)],
        (pulled, feat_z, base),
    )
    return (layer_output.reshape(field.shape), field_grad.reshape(field.shape))


def solution(mesh):
    placed = P(None, ("groups", "gx"), "gy", None)
    count = mesh.shape["gx"] * mesh.shape["gy"]

    def program(*arrays):
        _, grid_x, grid_y, depth = arrays[0].shape
        places = grid_x // mesh.shape["groups"] * grid_y
        small = places == LANES and places == 8 * count and depth % LANES == 0
        small = small and count % (depth // LANES) == 0
        return jax.shard_map(
            per_device_kernels if small else per_device,
            mesh=mesh,
            in_specs=(placed, placed, P(), P(), P()),
            out_specs=(placed, placed),
            check_vma=False,
        )(*arrays)

    return program
```

```python
import functools
import math

import jax
import jax.numpy as jnp
import numpy as np
from jax import lax
from jax.experimental import pallas as pl
from jax.experimental.pallas import tpu as pltpu
from jax.sharding import PartitionSpec as P

WIDTH = 64
HEADS = 8
HEAD_DIM = 8
LANES = 128

EPSILON = 1e-06
PRECISE = lax.Precision.HIGHEST
AXES = ("gx", "gy")


def exchange(parts):
    return lax.all_to_all(parts, AXES, split_axis=0, concat_axis=0, tiled=True)


def gather(part, count):
    return exchange(jnp.broadcast_to(part[None], (count,) + part.shape))


def reduce_blocks(total, count):
    width, depth = total.shape
    blocks = total.reshape(width, depth // LANES, LANES).transpose(1, 0, 2)
    blocks = blocks.reshape(count, width * depth // LANES // count, LANES)
    mine = jnp.sum(exchange(blocks), axis=0)
    whole = gather(mine, count).reshape(depth // LANES, width, LANES)
    return whole.transpose(1, 0, 2).reshape(width, depth)


def axis_features(pooled, weights):
    inverse = lax.rsqrt(jnp.mean(pooled * pooled, axis=0, keepdims=True) + EPSILON)
    normed = pooled * inverse
    length = pooled.shape[1]
    factor = 1.0 / math.sqrt(HEAD_DIM * length)
    queries = jnp.dot(weights[0].T, normed, precision=PRECISE).reshape(HEADS, HEAD_DIM, length)
    keyset = jnp.dot(weights[1].T, normed, precision=PRECISE).reshape(HEADS, HEAD_DIM, length)
    return (normed, inverse, queries, keyset, factor)


def axis_kernel(queries, keyset, factor):
    scores = jnp.einsum("hdm,hdn->hmn", queries, keyset, precision=PRECISE)
    return (scores * factor).astype(jnp.bfloat16)


def kernel_backward(gram, queries, keyset, factor):
    grad_query = factor * jnp.einsum("hmn,hdn->hdm", gram, keyset, precision=PRECISE)
    grad_keyset = factor * jnp.einsum("hmn,hdm->hdn", gram, queries, precision=PRECISE)
    return (grad_query, grad_keyset)


def grad_of_normed(weights, grad_query, grad_keyset):
    length = grad_query.shape[-1]
    grad_normed = jnp.dot(weights[0], grad_query.reshape(WIDTH, length), precision=PRECISE)
    return grad_normed + jnp.dot(
        weights[1], grad_keyset.reshape(WIDTH, length), precision=PRECISE
    )


def pooled_grad(normed, inverse, grad_normed):
    return inverse * (grad_normed - normed * jnp.mean(grad_normed * normed, axis=0, keepdims=True))


def f32_einsum(pattern, left, right):
    return jnp.einsum(pattern, left, right, preferred_element_type=jnp.float32)


def per_device(field, cotangent, qk_weight, w_value, w_out):
    span_x = lax.axis_size("gx")
    span_y = lax.axis_size("gy")
    count = span_x * span_y
    rows_x, rows_y, depth = field.shape[1:]
    cells = rows_x * rows_y
    grid_x = rows_x * span_x
    grid_y = rows_y * span_y
    start_x = lax.axis_index("gx") * rows_x
    start_y = lax.axis_index("gy") * rows_y
    bf16 = jnp.bfloat16

    cols = field.reshape(WIDTH, cells, depth)
    cots = cotangent.reshape(WIDTH, cells, depth)

    sum_z = jnp.sum(cols, axis=1, dtype=jnp.float32)
    sum_rows = jnp.sum(cols, axis=2, dtype=jnp.float32)
    rows_all = gather(sum_rows.T, count).reshape(span_x, span_y, rows_x, rows_y, WIDTH)
    total_x = jnp.sum(rows_all, axis=(1, 3)).reshape(grid_x, WIDTH).T
    total_y = jnp.sum(rows_all, axis=(0, 2)).reshape(grid_y, WIDTH).T
    total_z = reduce_blocks(sum_z, count)

    normed_x, inverse_x, query_x, keyset_x, factor_x = axis_features(
        total_x / (grid_y * depth), qk_weight[0]
    )
    normed_y, inverse_y, query_y, keyset_y, factor_y = axis_features(
        total_y / (grid_x * depth), qk_weight[1]
    )
    normed_z, inverse_z, query_z, keyset_z, factor_z = axis_features(
        total_z / (grid_x * grid_y), qk_weight[2]
    )
    kernel_x = axis_kernel(query_x, keyset_x, factor_x)
    kernel_y = axis_kernel(query_y, keyset_y, factor_y)
    query_b = query_z.astype(bf16)
    keyset_b = keyset_z.astype(bf16)

    wv = w_value.reshape(WIDTH, HEADS, HEAD_DIM)
    wo = w_out.reshape(HEADS, HEAD_DIM, WIDTH)
    coef_f = f32_einsum("cpk,hgk->cphg", cols, keyset_b)
    coef_c = f32_einsum("cpz,hgz->cphg", cots, query_b)
    low_f = jnp.einsum("chd,cphg->phdg", wv.astype(jnp.float32), coef_f, precision=PRECISE)
    low_c = jnp.einsum("hdc,cphg->phdg", wo.astype(jnp.float32), coef_c, precision=PRECISE)
    squares = HEAD_DIM * HEAD_DIM
    both = jnp.stack([low_f, low_c]).astype(bf16).reshape(2, cells, HEADS * squares)
    both = gather(both, count).reshape(span_x, span_y, 2, rows_x, rows_y, HEADS * squares)
    both = both.transpose(2, 0, 3, 1, 4, 5).reshape(2, grid_x, grid_y, HEADS, squares)
    low_f, low_c = both[0], both[1]

    mid_f = f32_einsum("hyj,xjhq->xyhq", kernel_y, low_f).astype(bf16)
    top_f = f32_einsum("hxi,iyhq->xyhq", kernel_x, mid_f)
    mid_c = f32_einsum("hxi,xyhq->iyhq", kernel_x, low_c).astype(bf16)
    top_c = f32_einsum("hyj,xyhq->xjhq", kernel_y, mid_c)
    gram_x = factor_z * f32_einsum("myhq,nyhq->hmn", low_c, mid_f)
    gram_y = factor_z * f32_einsum("xmhq,xnhq->hmn", mid_c, low_f)

    def here(top):
        top = lax.dynamic_slice_in_dim(top, start_x, rows_x, 0)
        top = lax.dynamic_slice_in_dim(top, start_y, rows_y, 1)
        return top.reshape(cells, HEADS, HEAD_DIM, HEAD_DIM)

    left_f = factor_z * jnp.einsum(
        "hdc,phdg->cphg", wo.astype(jnp.float32), here(top_f), precision=PRECISE
    )
    left_c = factor_z * jnp.einsum(
        "chd,phdg->cphg", wv.astype(jnp.float32), here(top_c), precision=PRECISE
    )
    left_f = left_f.astype(bf16)
    left_c = left_c.astype(bf16)

    grad_query_z = f32_einsum("cphg,cpz->hgz", left_f, cots)
    grad_keyset_z = f32_einsum("cphg,cpz->hgz", left_c, cols)
    gn_z = reduce_blocks(grad_of_normed(qk_weight[2], grad_query_z, grad_keyset_z), count)

    layer_output = (cols.astype(jnp.float32) + f32_einsum("cphg,hgz->cpz", left_f, query_b)).astype(bf16)
    through = f32_einsum("cphg,hgz->cpz", left_c, keyset_b)

    gn_x = grad_of_normed(qk_weight[0], *kernel_backward(gram_x, query_x, keyset_x, factor_x))
    gn_y = grad_of_normed(qk_weight[1], *kernel_backward(gram_y, query_y, keyset_y, factor_y))
    pull_x = pooled_grad(normed_x, inverse_x, gn_x)
    pull_y = pooled_grad(normed_y, inverse_y, gn_y)
    pull_z = pooled_grad(normed_z, inverse_z, gn_z)
    local_x = lax.dynamic_slice_in_dim(pull_x, start_x, rows_x, 1) / (grid_y * depth)
    local_y = lax.dynamic_slice_in_dim(pull_y, start_y, rows_y, 1) / (grid_x * depth)
    local_xy = (local_x[:, :, None] + local_y[:, None, :]).reshape(WIDTH, cells)
    local_z = pull_z / (grid_x * grid_y)
    field_grad = (
        cots.astype(jnp.float32) + through + local_xy[:, :, None] + local_z[:, None, :]
    ).astype(bf16)
    return (layer_output.reshape(field.shape), field_grad.reshape(field.shape))


def split(x):
    high = x.astype(jnp.bfloat16)
    return high, (x - high.astype(jnp.float32)).astype(jnp.bfloat16)


NN = (((1,), (0,)), ((), ()))
NT = (((1,), (1,)), ((), ()))
TN = (((0,), (0,)), ((), ()))


def mul(left, right, dims=NN):
    return lax.dot_general(left, right, dims, preferred_element_type=jnp.float32)


def mul_near(left, right, dims=NN):
    left_high, left_low = split(left)
    right_high, right_low = split(right)
    return (
        mul(left_high, right_high, dims)
        + mul(left_low, right_high, dims)
        + mul(left_high, right_low, dims)
    )


def mul_left(left, right, dims=NN):
    high, low = split(left)
    return mul(high, right, dims) + mul(low, right, dims)


def number(shape, dim):
    return lax.broadcasted_iota(jnp.int32, shape, dim)


def put_blocks(ref, total):
    count = ref.shape[0]
    columns = total.shape[1] // LANES
    groups = count // columns
    rows = WIDTH // groups
    for block in range(count):
        column, group = block // groups, block % groups
        ref[block, 0:rows, :] = total[
            group * rows : (group + 1) * rows, column * LANES : (column + 1) * LANES
        ]


def whole_blocks(ref, depth):
    columns = depth // LANES
    blocks = ref[...].reshape(columns, WIDTH, LANES)
    return jnp.concatenate([blocks[i] for i in range(columns)], axis=1)


def prepare_kernel(wv_ref, wo_ref, qk_ref, wv_out, wo_out, wq_out, wk_out, wz_out):
    wide = HEADS * HEAD_DIM * HEAD_DIM
    row = number((WIDTH, wide), 0)
    lane = number((WIDTH, wide), 1)
    by_channel = ((lane >> 3) == row).astype(jnp.bfloat16)
    by_factor = (((lane >> 6) * HEAD_DIM + (lane & 7)) == row).astype(jnp.bfloat16)
    wv_out[...] = mul(wv_ref[...], by_channel)
    wo_out[...] = mul(wo_ref[...], by_channel, TN)
    for index, out in ((0, wq_out), (1, wk_out)):
        high, low = split(qk_ref[2, index])
        out[0:WIDTH, :] = mul(high, by_factor).astype(jnp.bfloat16)
        out[WIDTH : 2 * WIDTH, :] = mul(low, by_factor).astype(jnp.bfloat16)
        wz_out[index * WIDTH : (index + 1) * WIDTH, :] = qk_ref[2, index].T


def sums_kernel(field_ref, out_ref):
    data = field_ref[...]
    rows, depth = data.shape
    cells = rows // WIDTH
    pick = (number((WIDTH, rows), 1) // cells == number((WIDTH, rows), 0)).astype(jnp.bfloat16)
    part = mul(pick, data)
    row_sums = mul(data, jnp.ones((depth, LANES), jnp.bfloat16)).reshape(WIDTH, cells, LANES)
    shape = row_sums.shape
    own = jnp.sum(jnp.where(number(shape, 0) == number(shape, 2), row_sums, 0.0), axis=0)
    put_blocks(out_ref, part)
    for block in range(out_ref.shape[0]):
        out_ref[block, out_ref.shape[1] - cells :, :] = own


def add_kernel(recv_ref, out_ref):
    rows = out_ref.shape[1]
    total = jnp.sum(recv_ref[:, 0:rows, :], axis=0)
    out_ref[...] = jnp.broadcast_to(total[None], out_ref.shape)


def plane_kernel(cells, lengths, me_ref, recv_ref, same_ref, qk_ref, mix_ref, feat_ref):
    places = recv_ref.shape[0] * cells
    totals = recv_ref[:, recv_ref.shape[1] - cells :, :].reshape(places, LANES)[:, :WIDTH]
    here = pl.ds(pl.multiple_of(me_ref[0] * cells, cells), cells)
    head = (number((HEADS * cells, WIDTH), 0) // cells) == (number((HEADS * cells, WIDTH), 1) >> 3)
    high, low = split(totals)
    forward = backward = None
    for axis in range(2):
        same = same_ref[axis]
        pooled = (mul(same, high) + mul(same, low)) * (1.0 / lengths[axis][1])
        inverse = lax.rsqrt(jnp.mean(pooled * pooled, axis=1, keepdims=True) + EPSILON)
        normed = pooled * inverse
        query = mul_near(normed, qk_ref[axis, 0])
        keyset = mul_near(normed, qk_ref[axis, 1])
        feat_ref[4 * axis] = normed
        feat_ref[4 * axis + 1] = query
        feat_ref[4 * axis + 2] = keyset
        feat_ref[4 * axis + 3] = jnp.broadcast_to(inverse, (places, WIDTH))
        factor = 1.0 / math.sqrt(HEAD_DIM * lengths[axis][0])

        def local(index, other):
            rows = feat_ref[4 * axis + index, here, :]
            rows = jnp.broadcast_to(rows[None], (HEADS, cells, WIDTH)).reshape(-1, WIDTH)
            scores = mul_near(jnp.where(head, rows, 0.0), other, NT) * factor
            return scores.astype(jnp.bfloat16).astype(jnp.float32)

        one, two = local(1, keyset), local(2, query)
        forward = one if forward is None else forward * one
        backward = two if backward is None else backward * two
    mix_ref[0] = forward
    mix_ref[1] = backward


def coef_kernel(places, recv_ref, wz_ref, field_ref, cot_ref, wv_ref, wo_ref,
                send_ref, feat_ref, query_ref, keyset_ref):
    rows, depth = field_ref.shape
    cells = rows // WIDTH
    wide = HEADS * HEAD_DIM * HEAD_DIM
    pooled = whole_blocks(recv_ref, depth) * (1.0 / places)
    inverse = lax.rsqrt(jnp.mean(pooled * pooled, axis=0, keepdims=True) + EPSILON)
    normed = pooled * inverse
    feat_ref[0:WIDTH, :] = normed
    feat_ref[WIDTH:, :] = jnp.broadcast_to(inverse, (HEAD_DIM, depth))
    both = mul_near(wz_ref[...], normed)

    def expand(part):
        part = part.reshape(HEADS, 1, HEAD_DIM, depth)
        part = jnp.broadcast_to(part, (HEADS, HEAD_DIM, HEAD_DIM, depth))
        return part.reshape(wide, depth).astype(jnp.bfloat16)

    query = expand(both[:WIDTH])
    keyset = expand(both[WIDTH:])
    query_ref[...] = query
    keyset_ref[...] = keyset
    low_f = mul(field_ref[...], keyset, NT).reshape(WIDTH, cells, wide)
    low_f = jnp.sum(wv_ref[...][:, None, :] * low_f, axis=0)
    low_c = mul(cot_ref[...], query, NT).reshape(WIDTH, cells, wide)
    low_c = jnp.sum(wo_ref[...][:, None, :] * low_c, axis=0)
    low = jnp.concatenate([low_f, low_c], axis=0).astype(jnp.bfloat16)
    send_ref[...] = jnp.broadcast_to(low[None], send_ref.shape)


def mix_kernel(factor, recv_ref, mix_ref, wv_ref, wo_ref, wq_ref, wk_ref, field_ref, cot_ref,
               send_ref, left_f_ref, left_c_ref):
    rows = field_ref.shape[0]
    cells = rows // WIDTH
    places = recv_ref.shape[0] * cells
    wide = recv_ref.shape[2]
    both = recv_ref[...].astype(jnp.float32)
    shape = (HEADS, cells, wide)
    head = number(shape, 0) == (number(shape, 2) >> 6)

    def top(mix, low):
        low = low.reshape(places, wide).astype(jnp.bfloat16)
        found = mul_left(mix, low).reshape(shape)
        return jnp.sum(jnp.where(head, found, 0.0), axis=0) * factor

    left_f = wo_ref[...][:, None, :] * top(mix_ref[0], both[:, :cells])[None]
    left_f = left_f.reshape(rows, wide).astype(jnp.bfloat16)
    left_c = wv_ref[...][:, None, :] * top(mix_ref[1], both[:, cells:])[None]
    left_c = left_c.reshape(rows, wide).astype(jnp.bfloat16)
    left_f_ref[...] = left_f
    left_c_ref[...] = left_c

    def pull(weights, left, right):
        found = mul(weights, left, NT)
        return mul_left(found[:WIDTH] + found[WIDTH:], right)

    put_blocks(
        send_ref,
        pull(wq_ref[...], left_f, cot_ref[...]) + pull(wk_ref[...], left_c, field_ref[...]),
    )


def output_kernel(left_ref, query_ref, field_ref, out_ref):
    found = mul(left_ref[...], query_ref[...]) + field_ref[...].astype(jnp.float32)
    out_ref[...] = found.astype(jnp.bfloat16)


def gram_kernel(cells, lengths, factor_z, me_ref, recv_ref, feat_ref, same_ref, qk_ref, out_ref,
                found_ref):
    places = recv_ref.shape[0] * cells
    wide = recv_ref.shape[2]
    squares = HEAD_DIM * HEAD_DIM
    both = recv_ref[...].astype(jnp.float32)
    low_f = both[:, :cells].reshape(places, wide).astype(jnp.bfloat16)
    low_c = both[:, cells:].reshape(places, wide).astype(jnp.bfloat16)
    here = pl.ds(pl.multiple_of(me_ref[0] * cells, cells), cells)
    lane = number((places, LANES), 1)
    products = []
    for pair in range(wide // LANES):
        part_f = low_f[:, pair * LANES : (pair + 1) * LANES]
        part_c = low_c[:, pair * LANES : (pair + 1) * LANES]
        for half in range(LANES // squares):
            mine = (lane >> 6) == half
            products.append(mul(jnp.where(mine, part_c, jnp.zeros_like(part_c)), part_f, NT))
    product = jnp.concatenate(products, axis=0)
    heads = number((HEADS * places, WIDTH), 0) // places == number((HEADS * places, WIDTH), 1) >> 3

    def stack(part):
        part = jnp.broadcast_to(part[None], (HEADS, places, WIDTH)).reshape(-1, WIDTH)
        return jnp.where(heads, part, 0.0)

    factors = [1.0 / math.sqrt(HEAD_DIM * lengths[axis][0]) for axis in range(2)]
    queries = [stack(feat_ref[4 * axis + 1]) for axis in range(2)]
    keysets = [stack(feat_ref[4 * axis + 2]) for axis in range(2)]
    kernels = []
    for axis in range(2):
        scores = mul_near(queries[axis], feat_ref[4 * axis + 2], NT) * factors[axis]
        kernels.append(scores.astype(jnp.bfloat16).astype(jnp.float32))
    total = jnp.zeros((cells, WIDTH), jnp.float32)
    for axis in range(2):
        gram = (product * kernels[1 - axis]).astype(jnp.bfloat16)
        across = jnp.concatenate(
            [gram[h * places : (h + 1) * places] for h in range(HEADS)], axis=1
        )
        scale = factors[axis] * factor_z
        grad_query = mul(across, keysets[axis].astype(jnp.bfloat16)) * scale
        grad_keyset = mul(gram, queries[axis].astype(jnp.bfloat16), TN) * scale
        found = mul_near(grad_query, qk_ref[axis, 0], NT) + mul_near(grad_keyset, qk_ref[axis, 1], NT)
        high, low = split(found)
        found_ref[...] = mul(same_ref[axis], high) + mul(same_ref[axis], low)
        found = found_ref[here, :]
        normed = feat_ref[4 * axis, here, :]
        inverse = feat_ref[4 * axis + 3, here, :]
        found = found - normed * jnp.mean(found * normed, axis=1, keepdims=True)
        total = total + inverse * found * (1.0 / lengths[axis][1])
    out_ref[...] = total


def base_kernel(left_ref, keyset_ref, cot_ref, plane_ref, out_ref):
    rows = cot_ref.shape[0]
    cells = rows // WIDTH
    shape = (WIDTH, cells, WIDTH)
    own = jnp.where(number(shape, 0) == number(shape, 2), plane_ref[...][None], 0.0)
    plane = mul_left(own.reshape(rows, WIDTH), jnp.ones((WIDTH, LANES), jnp.bfloat16))
    found = mul(left_ref[...], keyset_ref[...]) + cot_ref[...].astype(jnp.float32)
    columns = found.shape[1] // LANES
    out_ref[...] = found + jnp.concatenate([plane] * columns, axis=1)


def final_kernel(places, recv_ref, feat_ref, base_ref, out_ref):
    rows, depth = base_ref.shape
    cells = rows // WIDTH
    found = whole_blocks(recv_ref, depth)
    normed = feat_ref[0:WIDTH, :]
    inverse = feat_ref[WIDTH : WIDTH + 1, :]
    found = inverse * (found - normed * jnp.mean(found * normed, axis=0, keepdims=True))
    found = found * (1.0 / places)
    total = base_ref[...].reshape(WIDTH, cells, depth) + found[:, None, :]
    out_ref[...] = total.reshape(rows, depth).astype(jnp.bfloat16)


def run(kernel, outs, operands, scalars=0, flops=0, scratch=()):
    vmem = pl.BlockSpec(memory_space=pltpu.VMEM)
    smem = pl.BlockSpec(memory_space=pltpu.SMEM)
    moved = sum(x.size * x.dtype.itemsize for x in tuple(operands) + tuple(outs))
    found = pl.pallas_call(
        kernel,
        out_shape=tuple(outs),
        in_specs=[smem] * scalars + [vmem] * (len(operands) - scalars),
        out_specs=tuple(vmem for _ in outs),
        scratch_shapes=list(scratch),
        compiler_params=pltpu.CompilerParams(vmem_limit_bytes=16 * 1024 * 1024),
        cost_estimate=pl.CostEstimate(flops=flops, bytes_accessed=moved, transcendentals=0),
    )(*operands)
    return found[0] if len(outs) == 1 else found


def per_device_kernels(field, cotangent, qk_weight, w_value, w_out):
    span_x = lax.axis_size("gx")
    span_y = lax.axis_size("gy")
    count = span_x * span_y
    rows_x, rows_y, depth = field.shape[1:]
    cells = rows_x * rows_y
    places = count * cells
    grid_x = rows_x * span_x
    grid_y = rows_y * span_y
    rows = WIDTH * cells
    wide = WIDTH * HEAD_DIM
    f32, bf16 = jnp.float32, jnp.bfloat16
    like = jax.ShapeDtypeStruct
    lengths = ((grid_x, grid_y * depth), (grid_y, grid_x * depth))
    me = (lax.axis_index("gx") * span_y + lax.axis_index("gy")).astype(jnp.int32).reshape(1)

    place = np.arange(places)
    at_x = place // cells // span_y * rows_x + place % cells // rows_y
    at_y = place // cells % span_y * rows_y + place % rows_y
    same = jnp.asarray(
        np.stack([at_x[:, None] == at_x[None], at_y[:, None] == at_y[None]]), dtype=bf16
    )

    cols = field.reshape(rows, depth)
    cots = cotangent.reshape(rows, depth)
    share = WIDTH * depth // LANES // count
    block = like((count, share, LANES), f32)
    factor_z = 1.0 / math.sqrt(HEAD_DIM * depth)
    cube = rows * wide * depth * 2

    sums = run(sums_kernel, [like((count, share + cells, LANES), f32)], (cols,), flops=cube // 4)
    recv = exchange(sums)
    wv, wo, wq, wk, wz = run(
        prepare_kernel,
        [like((WIDTH, wide), f32)] * 2 + [like((2 * WIDTH, wide), bf16)] * 2
        + [like((2 * WIDTH, WIDTH), f32)],
        (w_value, w_out, qk_weight),
        flops=cube // 8,
    )
    pooled = exchange(run(add_kernel, [block], (recv,)))
    mix, feat = run(
        functools.partial(plane_kernel, cells, lengths),
        [like((2, HEADS * cells, places), f32), like((8, places, WIDTH), f32)],
        (me, recv, same, qk_weight),
        scalars=1,
        flops=cube // 2,
    )
    send, feat_z, query, keyset = run(
        functools.partial(coef_kernel, grid_x * grid_y),
        [like((count, 2 * cells, wide), bf16), like((WIDTH + HEAD_DIM, depth), f32)]
        + [like((wide, depth), bf16)] * 2,
        (pooled, wz, cols, cots, wv, wo),
        flops=2 * cube,
    )
    low = exchange(send)
    send, left_f, left_c = run(
        functools.partial(mix_kernel, factor_z),
        [block, like((rows, wide), bf16), like((rows, wide), bf16)],
        (low, mix, wv, wo, wq, wk, cols, cots),
        flops=cube,
    )
    recv = exchange(send)
    layer_output = run(output_kernel, [like((rows, depth), bf16)], (left_f, query, cols), flops=cube)
    plane = run(
        functools.partial(gram_kernel, cells, lengths, factor_z),
        [like((cells, WIDTH), f32)],
        (me, low, feat, same, qk_weight),
        scalars=1,
        flops=2 * cube,
        scratch=[pltpu.VMEM((places, WIDTH), f32)],
    )
    pulled = exchange(run(add_kernel, [block], (recv,)))
    base = run(base_kernel, [like((rows, depth), f32)], (left_c, keyset, cots, plane), flops=cube)
    field_grad = run(
        functools.partial(final_kernel, grid_x * grid_y),
        [like((rows, depth), bf16)],
        (pulled, feat_z, base),
    )
    return (layer_output.reshape(field.shape), field_grad.reshape(field.shape))


def solution(mesh):
    placed = P(None, ("groups", "gx"), "gy", None)
    count = mesh.shape["gx"] * mesh.shape["gy"]

    def program(*arrays):
        _, grid_x, grid_y, depth = arrays[0].shape
        places = grid_x // mesh.shape["groups"] * grid_y
        small = places == LANES and places == 8 * count and depth % LANES == 0
        small = small and count % (depth // LANES) == 0
        return jax.shard_map(
            per_device_kernels if small else per_device,
            mesh=mesh,
            in_specs=(placed, placed, P(), P(), P()),
            out_specs=(placed, placed),
            check_vma=False,
        )(*arrays)

    return program
```

```python
import functools
import math

import jax
import jax.numpy as jnp
import numpy as np
from jax import lax
from jax.experimental import pallas as pl
from jax.experimental.pallas import tpu as pltpu
from jax.sharding import PartitionSpec as P

WIDTH = 64
HEADS = 8
HEAD_DIM = 8
LANES = 128

EPSILON = 1e-06
PRECISE = lax.Precision.HIGHEST
AXES = ("gx", "gy")


def exchange(parts):
    return lax.all_to_all(parts, AXES, split_axis=0, concat_axis=0, tiled=True)


def swap(part, axis, size, step):
    return lax.ppermute(part, axis, [(i, i ^ step) for i in range(size)])


def gather(part, count):
    return exchange(jnp.broadcast_to(part[None], (count,) + part.shape))


def reduce_blocks(total, count):
    width, depth = total.shape
    blocks = total.reshape(width, depth // LANES, LANES).transpose(1, 0, 2)
    blocks = blocks.reshape(count, width * depth // LANES // count, LANES)
    mine = jnp.sum(exchange(blocks), axis=0)
    whole = gather(mine, count).reshape(depth // LANES, width, LANES)
    return whole.transpose(1, 0, 2).reshape(width, depth)


def axis_features(pooled, weights):
    inverse = lax.rsqrt(jnp.mean(pooled * pooled, axis=0, keepdims=True) + EPSILON)
    normed = pooled * inverse
    length = pooled.shape[1]
    factor = 1.0 / math.sqrt(HEAD_DIM * length)
    queries = jnp.dot(weights[0].T, normed, precision=PRECISE).reshape(HEADS, HEAD_DIM, length)
    keyset = jnp.dot(weights[1].T, normed, precision=PRECISE).reshape(HEADS, HEAD_DIM, length)
    return (normed, inverse, queries, keyset, factor)


def axis_kernel(queries, keyset, factor):
    scores = jnp.einsum("hdm,hdn->hmn", queries, keyset, precision=PRECISE)
    return (scores * factor).astype(jnp.bfloat16)


def kernel_backward(gram, queries, keyset, factor):
    grad_query = factor * jnp.einsum("hmn,hdn->hdm", gram, keyset, precision=PRECISE)
    grad_keyset = factor * jnp.einsum("hmn,hdm->hdn", gram, queries, precision=PRECISE)
    return (grad_query, grad_keyset)


def grad_of_normed(weights, grad_query, grad_keyset):
    length = grad_query.shape[-1]
    grad_normed = jnp.dot(weights[0], grad_query.reshape(WIDTH, length), precision=PRECISE)
    return grad_normed + jnp.dot(
        weights[1], grad_keyset.reshape(WIDTH, length), precision=PRECISE
    )


def pooled_grad(normed, inverse, grad_normed):
    return inverse * (grad_normed - normed * jnp.mean(grad_normed * normed, axis=0, keepdims=True))


def f32_einsum(pattern, left, right):
    return jnp.einsum(pattern, left, right, preferred_element_type=jnp.float32)


def per_device(field, cotangent, qk_weight, w_value, w_out):
    span_x = lax.axis_size("gx")
    span_y = lax.axis_size("gy")
    count = span_x * span_y
    rows_x, rows_y, depth = field.shape[1:]
    cells = rows_x * rows_y
    grid_x = rows_x * span_x
    grid_y = rows_y * span_y
    start_x = lax.axis_index("gx") * rows_x
    start_y = lax.axis_index("gy") * rows_y
    bf16 = jnp.bfloat16

    cols = field.reshape(WIDTH, cells, depth)
    cots = cotangent.reshape(WIDTH, cells, depth)

    sum_z = jnp.sum(cols, axis=1, dtype=jnp.float32)
    sum_rows = jnp.sum(cols, axis=2, dtype=jnp.float32)
    rows_all = gather(sum_rows.T, count).reshape(span_x, span_y, rows_x, rows_y, WIDTH)
    total_x = jnp.sum(rows_all, axis=(1, 3)).reshape(grid_x, WIDTH).T
    total_y = jnp.sum(rows_all, axis=(0, 2)).reshape(grid_y, WIDTH).T
    total_z = reduce_blocks(sum_z, count)

    normed_x, inverse_x, query_x, keyset_x, factor_x = axis_features(
        total_x / (grid_y * depth), qk_weight[0]
    )
    normed_y, inverse_y, query_y, keyset_y, factor_y = axis_features(
        total_y / (grid_x * depth), qk_weight[1]
    )
    normed_z, inverse_z, query_z, keyset_z, factor_z = axis_features(
        total_z / (grid_x * grid_y), qk_weight[2]
    )
    kernel_x = axis_kernel(query_x, keyset_x, factor_x)
    kernel_y = axis_kernel(query_y, keyset_y, factor_y)
    query_b = query_z.astype(bf16)
    keyset_b = keyset_z.astype(bf16)

    wv = w_value.reshape(WIDTH, HEADS, HEAD_DIM)
    wo = w_out.reshape(HEADS, HEAD_DIM, WIDTH)
    coef_f = f32_einsum("cpk,hgk->cphg", cols, keyset_b)
    coef_c = f32_einsum("cpz,hgz->cphg", cots, query_b)
    low_f = jnp.einsum("chd,cphg->phdg", wv.astype(jnp.float32), coef_f, precision=PRECISE)
    low_c = jnp.einsum("hdc,cphg->phdg", wo.astype(jnp.float32), coef_c, precision=PRECISE)
    squares = HEAD_DIM * HEAD_DIM
    both = jnp.stack([low_f, low_c]).astype(bf16).reshape(2, cells, HEADS * squares)
    both = gather(both, count).reshape(span_x, span_y, 2, rows_x, rows_y, HEADS * squares)
    both = both.transpose(2, 0, 3, 1, 4, 5).reshape(2, grid_x, grid_y, HEADS, squares)
    low_f, low_c = both[0], both[1]

    mid_f = f32_einsum("hyj,xjhq->xyhq", kernel_y, low_f).astype(bf16)
    top_f = f32_einsum("hxi,iyhq->xyhq", kernel_x, mid_f)
    mid_c = f32_einsum("hxi,xyhq->iyhq", kernel_x, low_c).astype(bf16)
    top_c = f32_einsum("hyj,xyhq->xjhq", kernel_y, mid_c)
    gram_x = factor_z * f32_einsum("myhq,nyhq->hmn", low_c, mid_f)
    gram_y = factor_z * f32_einsum("xmhq,xnhq->hmn", mid_c, low_f)

    def here(top):
        top = lax.dynamic_slice_in_dim(top, start_x, rows_x, 0)
        top = lax.dynamic_slice_in_dim(top, start_y, rows_y, 1)
        return top.reshape(cells, HEADS, HEAD_DIM, HEAD_DIM)

    left_f = factor_z * jnp.einsum(
        "hdc,phdg->cphg", wo.astype(jnp.float32), here(top_f), precision=PRECISE
    )
    left_c = factor_z * jnp.einsum(
        "chd,phdg->cphg", wv.astype(jnp.float32), here(top_c), precision=PRECISE
    )
    left_f = left_f.astype(bf16)
    left_c = left_c.astype(bf16)

    grad_query_z = f32_einsum("cphg,cpz->hgz", left_f, cots)
    grad_keyset_z = f32_einsum("cphg,cpz->hgz", left_c, cols)
    gn_z = reduce_blocks(grad_of_normed(qk_weight[2], grad_query_z, grad_keyset_z), count)

    layer_output = (cols.astype(jnp.float32) + f32_einsum("cphg,hgz->cpz", left_f, query_b)).astype(bf16)
    through = f32_einsum("cphg,hgz->cpz", left_c, keyset_b)

    gn_x = grad_of_normed(qk_weight[0], *kernel_backward(gram_x, query_x, keyset_x, factor_x))
    gn_y = grad_of_normed(qk_weight[1], *kernel_backward(gram_y, query_y, keyset_y, factor_y))
    pull_x = pooled_grad(normed_x, inverse_x, gn_x)
    pull_y = pooled_grad(normed_y, inverse_y, gn_y)
    pull_z = pooled_grad(normed_z, inverse_z, gn_z)
    local_x = lax.dynamic_slice_in_dim(pull_x, start_x, rows_x, 1) / (grid_y * depth)
    local_y = lax.dynamic_slice_in_dim(pull_y, start_y, rows_y, 1) / (grid_x * depth)
    local_xy = (local_x[:, :, None] + local_y[:, None, :]).reshape(WIDTH, cells)
    local_z = pull_z / (grid_x * grid_y)
    field_grad = (
        cots.astype(jnp.float32) + through + local_xy[:, :, None] + local_z[:, None, :]
    ).astype(bf16)
    return (layer_output.reshape(field.shape), field_grad.reshape(field.shape))


def split(x):
    high = x.astype(jnp.bfloat16)
    return high, (x - high.astype(jnp.float32)).astype(jnp.bfloat16)


NN = (((1,), (0,)), ((), ()))
NT = (((1,), (1,)), ((), ()))
TN = (((0,), (0,)), ((), ()))


def mul(left, right, dims=NN):
    return lax.dot_general(left, right, dims, preferred_element_type=jnp.float32)


def mul_near(left, right, dims=NN):
    left_high, left_low = split(left)
    right_high, right_low = split(right)
    return (
        mul(left_high, right_high, dims)
        + mul(left_low, right_high, dims)
        + mul(left_high, right_low, dims)
    )


def mul_left(left, right, dims=NN):
    high, low = split(left)
    return mul(high, right, dims) + mul(low, right, dims)


def number(shape, dim):
    return lax.broadcasted_iota(jnp.int32, shape, dim)


def put_quarters(place_ref, part_ref, total, outs):
    for index in range(part_ref.shape[0]):
        part_ref[index] = total[:, index * LANES : (index + 1) * LANES]
    for step, out in enumerate(outs):
        out[0:WIDTH, :] = part_ref[place_ref[0] ^ step]


def join_quarters(place_ref, part_ref, quarters):
    for step, quarter in enumerate(quarters):
        part_ref[place_ref[0] ^ step] = quarter[...]
    return jnp.concatenate([part_ref[index] for index in range(part_ref.shape[0])], axis=1)


def expand(part):
    depth = part.shape[1]
    part = part.reshape(HEADS, 1, HEAD_DIM, depth)
    part = jnp.broadcast_to(part, (HEADS, HEAD_DIM, HEAD_DIM, depth))
    return part.reshape(WIDTH * HEAD_DIM, depth).astype(jnp.bfloat16)


def spread(weights, top):
    left = weights[:, None, :] * top[None]
    return left.reshape(-1, left.shape[2]).astype(jnp.bfloat16)


def prepare_kernel(wv_ref, wo_ref, qk_ref, wv_out, wo_out, wq_out, wk_out, wz_out):
    wide = HEADS * HEAD_DIM * HEAD_DIM
    row = number((WIDTH, wide), 0)
    lane = number((WIDTH, wide), 1)
    by_channel = ((lane >> 3) == row).astype(jnp.bfloat16)
    by_factor = (((lane >> 6) * HEAD_DIM + (lane & 7)) == row).astype(jnp.bfloat16)
    wv_out[...] = mul(wv_ref[...], by_channel)
    wo_out[...] = mul(wo_ref[...], by_channel, TN)
    for index, out in ((0, wq_out), (1, wk_out)):
        high, low = split(qk_ref[2, index])
        out[0:WIDTH, :] = mul(high, by_factor).astype(jnp.bfloat16)
        out[WIDTH : 2 * WIDTH, :] = mul(low, by_factor).astype(jnp.bfloat16)
        wz_out[index * WIDTH : (index + 1) * WIDTH, :] = qk_ref[2, index].T


def sums_kernel(place_ref, field_ref, *refs):
    outs, part_ref = refs[:-1], refs[-1]
    data = field_ref[...]
    rows, depth = data.shape
    cells = rows // WIDTH
    pick = (number((WIDTH, rows), 1) // cells == number((WIDTH, rows), 0)).astype(jnp.bfloat16)
    part = mul(pick, data)
    row_sums = mul(data, jnp.ones((depth, LANES), jnp.bfloat16)).reshape(WIDTH, cells, LANES)
    shape = row_sums.shape
    own = jnp.sum(jnp.where(number(shape, 0) == number(shape, 2), row_sums, 0.0), axis=0)
    put_quarters(place_ref, part_ref, part, outs)
    for out in outs:
        out[WIDTH:, :] = own


def add_kernel(*refs):
    parts, out_ref = refs[:-1], refs[-1]
    total = parts[0][0:WIDTH, :]
    for part in parts[1:]:
        total = total + part[0:WIDTH, :]
    out_ref[0:WIDTH, :] = total
    cells = parts[0].shape[0] - WIDTH
    for step, part in enumerate(parts):
        start = WIDTH + step * cells
        out_ref[start : start + cells, :] = part[WIDTH:, :]


def factor_kernel(places, *refs):
    parts, (wz_ref, both_ref, feat_ref) = refs[:-3], refs[-3:]
    total = parts[0][0:WIDTH, :]
    for part in parts[1:]:
        total = total + part[0:WIDTH, :]
    pooled = total * (1.0 / places)
    inverse = lax.rsqrt(jnp.mean(pooled * pooled, axis=0, keepdims=True) + EPSILON)
    normed = pooled * inverse
    feat_ref[0:WIDTH, :] = normed
    feat_ref[WIDTH:, :] = jnp.broadcast_to(inverse, (HEAD_DIM, LANES))
    both_ref[...] = mul_near(wz_ref[...], normed).astype(jnp.bfloat16)


def pull_kernel(places, *refs):
    parts, (feat_ref, out_ref) = refs[:-2], refs[-2:]
    found = parts[0][...]
    for part in parts[1:]:
        found = found + part[...]
    normed = feat_ref[0:WIDTH, :]
    inverse = feat_ref[WIDTH : WIDTH + 1, :]
    found = inverse * (found - normed * jnp.mean(found * normed, axis=0, keepdims=True))
    out_ref[...] = found * (1.0 / places)


def plane_kernel(cells, lengths, place_ref, *refs):
    parts, (same_ref, qk_ref, mix_ref, feat_ref, total_ref) = refs[:-5], refs[-5:]
    span_y = len(parts)
    count = total_ref.shape[0]
    places = count * cells
    for block in range(count):
        step_x, step_y = block // span_y, block % span_y
        start = WIDTH + step_x * cells
        index = (place_ref[0] ^ step_x) * span_y + (place_ref[1] ^ step_y)
        total_ref[index] = parts[step_y][start : start + cells, :]
    totals = total_ref[...].reshape(places, LANES)[:, :WIDTH]
    me = place_ref[0] * span_y + place_ref[1]
    here = pl.ds(pl.multiple_of(me * cells, cells), cells)
    head = (number((HEADS * cells, WIDTH), 0) // cells) == (number((HEADS * cells, WIDTH), 1) >> 3)
    high, low = split(totals)
    forward = backward = None
    for axis in range(2):
        same = same_ref[axis]
        pooled = (mul(same, high) + mul(same, low)) * (1.0 / lengths[axis][1])
        inverse = lax.rsqrt(jnp.mean(pooled * pooled, axis=1, keepdims=True) + EPSILON)
        normed = pooled * inverse
        query = mul_near(normed, qk_ref[axis, 0])
        keyset = mul_near(normed, qk_ref[axis, 1])
        feat_ref[4 * axis] = normed
        feat_ref[4 * axis + 1] = query
        feat_ref[4 * axis + 2] = keyset
        feat_ref[4 * axis + 3] = jnp.broadcast_to(inverse, (places, WIDTH))
        factor = 1.0 / math.sqrt(HEAD_DIM * lengths[axis][0])

        def local(index, other):
            rows = feat_ref[4 * axis + index, here, :]
            rows = jnp.broadcast_to(rows[None], (HEADS, cells, WIDTH)).reshape(-1, WIDTH)
            scores = mul_near(jnp.where(head, rows, 0.0), other, NT) * factor
            return scores.astype(jnp.bfloat16).astype(jnp.float32)

        one, two = local(1, keyset), local(2, query)
        forward = one if forward is None else forward * one
        backward = two if backward is None else backward * two
    mix_ref[0] = forward
    mix_ref[1] = backward


def coef_kernel(place_ref, *refs):
    quarters, rest = refs[:-8], refs[-8:]
    field_ref, cot_ref, wv_ref, wo_ref, send_ref, both_ref, part_ref = rest[1:]
    quarters = quarters + rest[:1]
    rows, depth = field_ref.shape
    cells = rows // WIDTH
    wide = HEADS * HEAD_DIM * HEAD_DIM
    both = join_quarters(place_ref, part_ref, [q[...].astype(jnp.float32) for q in quarters])
    both_ref[...] = both.astype(jnp.bfloat16)
    query = expand(both[:WIDTH])
    keyset = expand(both[WIDTH:])
    low_f = mul(field_ref[...], keyset, NT).reshape(WIDTH, cells, wide)
    low_f = jnp.sum(wv_ref[...][:, None, :] * low_f, axis=0)
    low_c = mul(cot_ref[...], query, NT).reshape(WIDTH, cells, wide)
    low_c = jnp.sum(wo_ref[...][:, None, :] * low_c, axis=0)
    low = jnp.concatenate([low_f, low_c], axis=0).astype(jnp.bfloat16)
    send_ref[...] = jnp.broadcast_to(low[None], send_ref.shape)


def mix_kernel(factor, place_ref, recv_ref, mix_ref, wv_ref, wo_ref, wq_ref, wk_ref, field_ref,
               cot_ref, top_ref, *refs):
    outs, part_ref = refs[:-1], refs[-1]
    rows = field_ref.shape[0]
    cells = rows // WIDTH
    places = recv_ref.shape[0] * cells
    wide = recv_ref.shape[2]
    both = recv_ref[...].astype(jnp.float32)
    shape = (HEADS, cells, wide)
    head = number(shape, 0) == (number(shape, 2) >> 6)

    def top(mix, low):
        low = low.reshape(places, wide).astype(jnp.bfloat16)
        found = mul_left(mix, low).reshape(shape)
        return jnp.sum(jnp.where(head, found, 0.0), axis=0) * factor

    top_f = top(mix_ref[0], both[:, :cells])
    top_c = top(mix_ref[1], both[:, cells:])
    top_ref[0] = top_f
    top_ref[1] = top_c
    left_f = spread(wo_ref[...], top_f)
    left_c = spread(wv_ref[...], top_c)

    def pull(weights, left, right):
        found = mul(weights, left, NT)
        return mul_left(found[:WIDTH] + found[WIDTH:], right)

    found = pull(wq_ref[...], left_f, cot_ref[...]) + pull(wk_ref[...], left_c, field_ref[...])
    put_quarters(place_ref, part_ref, found, outs)


def output_kernel(top_ref, wo_ref, both_ref, field_ref, out_ref):
    query = expand(both_ref[...].astype(jnp.float32)[:WIDTH])
    left = spread(wo_ref[...], top_ref[0])
    out_ref[...] = (mul(left, query) + field_ref[...].astype(jnp.float32)).astype(jnp.bfloat16)


def gram_kernel(cells, span_y, lengths, factor_z, place_ref, recv_ref, feat_ref, same_ref, qk_ref, out_ref,
                found_ref):
    places = recv_ref.shape[0] * cells
    wide = recv_ref.shape[2]
    squares = HEAD_DIM * HEAD_DIM
    both = recv_ref[...].astype(jnp.float32)
    low_f = both[:, :cells].reshape(places, wide).astype(jnp.bfloat16)
    low_c = both[:, cells:].reshape(places, wide).astype(jnp.bfloat16)
    me = place_ref[0] * span_y + place_ref[1]
    here = pl.ds(pl.multiple_of(me * cells, cells), cells)
    lane = number((places, LANES), 1)
    products = []
    for pair in range(wide // LANES):
        part_f = low_f[:, pair * LANES : (pair + 1) * LANES]
        part_c = low_c[:, pair * LANES : (pair + 1) * LANES]
        for half in range(LANES // squares):
            mine = (lane >> 6) == half
            products.append(mul(jnp.where(mine, part_c, jnp.zeros_like(part_c)), part_f, NT))
    product = jnp.concatenate(products, axis=0)
    heads = number((HEADS * places, WIDTH), 0) // places == number((HEADS * places, WIDTH), 1) >> 3

    def stack(part):
        part = jnp.broadcast_to(part[None], (HEADS, places, WIDTH)).reshape(-1, WIDTH)
        return jnp.where(heads, part, 0.0)

    factors = [1.0 / math.sqrt(HEAD_DIM * lengths[axis][0]) for axis in range(2)]
    queries = [stack(feat_ref[4 * axis + 1]) for axis in range(2)]
    keysets = [stack(feat_ref[4 * axis + 2]) for axis in range(2)]
    kernels = []
    for axis in range(2):
        scores = mul_near(queries[axis], feat_ref[4 * axis + 2], NT) * factors[axis]
        kernels.append(scores.astype(jnp.bfloat16).astype(jnp.float32))
    total = jnp.zeros((cells, WIDTH), jnp.float32)
    for axis in range(2):
        gram = (product * kernels[1 - axis]).astype(jnp.bfloat16)
        across = jnp.concatenate(
            [gram[h * places : (h + 1) * places] for h in range(HEADS)], axis=1
        )
        scale = factors[axis] * factor_z
        grad_query = mul(across, keysets[axis].astype(jnp.bfloat16)) * scale
        grad_keyset = mul(gram, queries[axis].astype(jnp.bfloat16), TN) * scale
        found = mul_near(grad_query, qk_ref[axis, 0], NT) + mul_near(grad_keyset, qk_ref[axis, 1], NT)
        high, low = split(found)
        found_ref[...] = mul(same_ref[axis], high) + mul(same_ref[axis], low)
        found = found_ref[here, :]
        normed = feat_ref[4 * axis, here, :]
        inverse = feat_ref[4 * axis + 3, here, :]
        found = found - normed * jnp.mean(found * normed, axis=1, keepdims=True)
        total = total + inverse * found * (1.0 / lengths[axis][1])
    out_ref[...] = total


def base_kernel(top_ref, wv_ref, both_ref, cot_ref, plane_ref, out_ref):
    rows = cot_ref.shape[0]
    cells = rows // WIDTH
    shape = (WIDTH, cells, WIDTH)
    own = jnp.where(number(shape, 0) == number(shape, 2), plane_ref[...][None], 0.0)
    plane = mul_left(own.reshape(rows, WIDTH), jnp.ones((WIDTH, LANES), jnp.bfloat16))
    keyset = expand(both_ref[...].astype(jnp.float32)[WIDTH:])
    left = spread(wv_ref[...], top_ref[1])
    found = mul(left, keyset) + cot_ref[...].astype(jnp.float32)
    columns = found.shape[1] // LANES
    out_ref[...] = found + jnp.concatenate([plane] * columns, axis=1)


def final_kernel(place_ref, *refs):
    quarters, (base_ref, out_ref, part_ref) = refs[:-3], refs[-3:]
    rows, depth = base_ref.shape
    cells = rows // WIDTH
    found = join_quarters(place_ref, part_ref, quarters)
    total = base_ref[...].reshape(WIDTH, cells, depth) + found[:, None, :]
    out_ref[...] = total.reshape(rows, depth).astype(jnp.bfloat16)


def run(kernel, outs, operands, scalars=0, flops=0, scratch=()):
    vmem = pl.BlockSpec(memory_space=pltpu.VMEM)
    smem = pl.BlockSpec(memory_space=pltpu.SMEM)
    moved = sum(x.size * x.dtype.itemsize for x in tuple(operands) + tuple(outs))
    found = pl.pallas_call(
        kernel,
        out_shape=tuple(outs),
        in_specs=[smem] * scalars + [vmem] * (len(operands) - scalars),
        out_specs=tuple(vmem for _ in outs),
        scratch_shapes=list(scratch),
        compiler_params=pltpu.CompilerParams(vmem_limit_bytes=16 * 1024 * 1024),
        cost_estimate=pl.CostEstimate(flops=flops, bytes_accessed=moved, transcendentals=0),
    )(*operands)
    return found[0] if len(outs) == 1 else found


def per_device_kernels(field, cotangent, qk_weight, w_value, w_out):
    span_x = lax.axis_size("gx")
    span_y = lax.axis_size("gy")
    count = span_x * span_y
    rows_x, rows_y, depth = field.shape[1:]
    cells = rows_x * rows_y
    places = count * cells
    grid_x = rows_x * span_x
    grid_y = rows_y * span_y
    rows = WIDTH * cells
    wide = WIDTH * HEAD_DIM
    f32, bf16 = jnp.float32, jnp.bfloat16
    like = jax.ShapeDtypeStruct
    lengths = ((grid_x, grid_y * depth), (grid_y, grid_x * depth))
    place = jnp.stack([lax.axis_index("gx"), lax.axis_index("gy")]).astype(jnp.int32)

    cell = np.arange(places)
    at_x = cell // cells // span_y * rows_x + cell % cells // rows_y
    at_y = cell // cells % span_y * rows_y + cell % rows_y
    same = jnp.asarray(
        np.stack([at_x[:, None] == at_x[None], at_y[:, None] == at_y[None]]), dtype=bf16
    )

    cols = field.reshape(rows, depth)
    cots = cotangent.reshape(rows, depth)
    block = like((WIDTH, LANES), f32)
    parts = pltpu.VMEM((span_x, WIDTH, LANES), f32)
    factor_z = 1.0 / math.sqrt(HEAD_DIM * depth)
    cube = rows * wide * depth * 2

    def swaps(sent, axis, size):
        if not isinstance(sent, (tuple, list)):
            sent = [sent] * size
        return tuple(sent[:1]) + tuple(
            swap(sent[step], axis, size, step) for step in range(1, size)
        )

    sums = run(
        sums_kernel, [like((WIDTH + cells, LANES), f32)] * span_x, (place, cols),
        scalars=1, flops=cube // 4, scratch=[parts],
    )
    wv, wo, wq, wk, wz = run(
        prepare_kernel,
        [like((WIDTH, wide), f32)] * 2 + [like((2 * WIDTH, wide), bf16)] * 2
        + [like((2 * WIDTH, WIDTH), f32)],
        (w_value, w_out, qk_weight),
        flops=cube // 8,
    )
    total = run(
        add_kernel, [like((WIDTH + span_x * cells, LANES), f32)], swaps(sums, "gx", span_x)
    )
    totals = swaps(total, "gy", span_y)
    mine, feat_z = run(
        functools.partial(factor_kernel, grid_x * grid_y),
        [like((2 * WIDTH, LANES), bf16), like((WIDTH + HEAD_DIM, LANES), f32)],
        totals + (wz,),
    )
    mix, feat = run(
        functools.partial(plane_kernel, cells, lengths),
        [like((2, HEADS * cells, places), f32), like((8, places, WIDTH), f32)],
        (place,) + totals + (same, qk_weight),
        scalars=1,
        flops=cube // 2,
        scratch=[pltpu.VMEM((count, cells, LANES), f32)],
    )
    send, both = run(
        coef_kernel,
        [like((count, 2 * cells, wide), bf16), like((2 * WIDTH, depth), bf16)],
        (place,) + swaps(mine, "gx", span_x) + (cols, cots, wv, wo),
        scalars=1,
        flops=2 * cube,
        scratch=[pltpu.VMEM((span_x, 2 * WIDTH, LANES), f32)],
    )
    low = exchange(send)
    top, *pulls = run(
        functools.partial(mix_kernel, factor_z),
        [like((2, cells, wide), f32)] + [block] * span_x,
        (place, low, mix, wv, wo, wq, wk, cols, cots),
        scalars=1,
        flops=cube,
        scratch=[parts],
    )
    total = sum(swaps(pulls, "gx", span_x))
    layer_output = run(
        output_kernel, [like((rows, depth), bf16)], (top, wo, both, cols), flops=cube
    )
    plane = run(
        functools.partial(gram_kernel, cells, span_y, lengths, factor_z),
        [like((cells, WIDTH), f32)],
        (place, low, feat, same, qk_weight),
        scalars=1,
        flops=2 * cube,
        scratch=[pltpu.VMEM((places, WIDTH), f32)],
    )
    mine = run(
        functools.partial(pull_kernel, grid_x * grid_y),
        [block],
        swaps(total, "gy", span_y) + (feat_z,),
    )
    base = run(base_kernel, [like((rows, depth), f32)], (top, wv, both, cots, plane), flops=cube)
    field_grad = run(
        final_kernel,
        [like((rows, depth), bf16)],
        (place,) + swaps(mine, "gx", span_x) + (base,),
        scalars=1,
        scratch=[parts],
    )
    return (layer_output.reshape(field.shape), field_grad.reshape(field.shape))


def solution(mesh):
    placed = P(None, ("groups", "gx"), "gy", None)
    count = mesh.shape["gx"] * mesh.shape["gy"]

    def program(*arrays):
        _, grid_x, grid_y, depth = arrays[0].shape
        places = grid_x // mesh.shape["groups"] * grid_y
        small = places == LANES and places == 8 * count
        small = small and depth == LANES * mesh.shape["gx"] and count & (count - 1) == 0
        return jax.shard_map(
            per_device_kernels if small else per_device,
            mesh=mesh,
            in_specs=(placed, placed, P(), P(), P()),
            out_specs=(placed, placed),
            check_vma=False,
        )(*arrays)

    return program
```

```python
import functools
import math

import jax
import jax.numpy as jnp
import numpy as np
from jax import lax
from jax.experimental import pallas as pl
from jax.experimental.pallas import tpu as pltpu
from jax.sharding import PartitionSpec as P

WIDTH = 64
HEADS = 8
HEAD_DIM = 8
LANES = 128

EPSILON = 1e-06
PRECISE = lax.Precision.HIGHEST
AXES = ("gx", "gy")


def exchange(parts):
    return lax.all_to_all(parts, AXES, split_axis=0, concat_axis=0, tiled=True)


def swap(part, axis, size, step):
    return lax.ppermute(part, axis, [(i, i ^ step) for i in range(size)])


def gather(part, count):
    return exchange(jnp.broadcast_to(part[None], (count,) + part.shape))


def reduce_blocks(total, count):
    width, depth = total.shape
    blocks = total.reshape(width, depth // LANES, LANES).transpose(1, 0, 2)
    blocks = blocks.reshape(count, width * depth // LANES // count, LANES)
    mine = jnp.sum(exchange(blocks), axis=0)
    whole = gather(mine, count).reshape(depth // LANES, width, LANES)
    return whole.transpose(1, 0, 2).reshape(width, depth)


def axis_features(pooled, weights):
    inverse = lax.rsqrt(jnp.mean(pooled * pooled, axis=0, keepdims=True) + EPSILON)
    normed = pooled * inverse
    length = pooled.shape[1]
    factor = 1.0 / math.sqrt(HEAD_DIM * length)
    queries = jnp.dot(weights[0].T, normed, precision=PRECISE).reshape(HEADS, HEAD_DIM, length)
    keyset = jnp.dot(weights[1].T, normed, precision=PRECISE).reshape(HEADS, HEAD_DIM, length)
    return (normed, inverse, queries, keyset, factor)


def axis_kernel(queries, keyset, factor):
    scores = jnp.einsum("hdm,hdn->hmn", queries, keyset, precision=PRECISE)
    return (scores * factor).astype(jnp.bfloat16)


def kernel_backward(gram, queries, keyset, factor):
    grad_query = factor * jnp.einsum("hmn,hdn->hdm", gram, keyset, precision=PRECISE)
    grad_keyset = factor * jnp.einsum("hmn,hdm->hdn", gram, queries, precision=PRECISE)
    return (grad_query, grad_keyset)


def grad_of_normed(weights, grad_query, grad_keyset):
    length = grad_query.shape[-1]
    grad_normed = jnp.dot(weights[0], grad_query.reshape(WIDTH, length), precision=PRECISE)
    return grad_normed + jnp.dot(
        weights[1], grad_keyset.reshape(WIDTH, length), precision=PRECISE
    )


def pooled_grad(normed, inverse, grad_normed):
    return inverse * (grad_normed - normed * jnp.mean(grad_normed * normed, axis=0, keepdims=True))


def f32_einsum(pattern, left, right):
    return jnp.einsum(pattern, left, right, preferred_element_type=jnp.float32)


def per_device(field, cotangent, qk_weight, w_value, w_out):
    span_x = lax.axis_size("gx")
    span_y = lax.axis_size("gy")
    count = span_x * span_y
    rows_x, rows_y, depth = field.shape[1:]
    cells = rows_x * rows_y
    grid_x = rows_x * span_x
    grid_y = rows_y * span_y
    start_x = lax.axis_index("gx") * rows_x
    start_y = lax.axis_index("gy") * rows_y
    bf16 = jnp.bfloat16

    cols = field.reshape(WIDTH, cells, depth)
    cots = cotangent.reshape(WIDTH, cells, depth)

    sum_z = jnp.sum(cols, axis=1, dtype=jnp.float32)
    sum_rows = jnp.sum(cols, axis=2, dtype=jnp.float32)
    rows_all = gather(sum_rows.T, count).reshape(span_x, span_y, rows_x, rows_y, WIDTH)
    total_x = jnp.sum(rows_all, axis=(1, 3)).reshape(grid_x, WIDTH).T
    total_y = jnp.sum(rows_all, axis=(0, 2)).reshape(grid_y, WIDTH).T
    total_z = reduce_blocks(sum_z, count)

    normed_x, inverse_x, query_x, keyset_x, factor_x = axis_features(
        total_x / (grid_y * depth), qk_weight[0]
    )
    normed_y, inverse_y, query_y, keyset_y, factor_y = axis_features(
        total_y / (grid_x * depth), qk_weight[1]
    )
    normed_z, inverse_z, query_z, keyset_z, factor_z = axis_features(
        total_z / (grid_x * grid_y), qk_weight[2]
    )
    kernel_x = axis_kernel(query_x, keyset_x, factor_x)
    kernel_y = axis_kernel(query_y, keyset_y, factor_y)
    query_b = query_z.astype(bf16)
    keyset_b = keyset_z.astype(bf16)

    wv = w_value.reshape(WIDTH, HEADS, HEAD_DIM)
    wo = w_out.reshape(HEADS, HEAD_DIM, WIDTH)
    coef_f = f32_einsum("cpk,hgk->cphg", cols, keyset_b)
    coef_c = f32_einsum("cpz,hgz->cphg", cots, query_b)
    low_f = jnp.einsum("chd,cphg->phdg", wv.astype(jnp.float32), coef_f, precision=PRECISE)
    low_c = jnp.einsum("hdc,cphg->phdg", wo.astype(jnp.float32), coef_c, precision=PRECISE)
    squares = HEAD_DIM * HEAD_DIM
    both = jnp.stack([low_f, low_c]).astype(bf16).reshape(2, cells, HEADS * squares)
    both = gather(both, count).reshape(span_x, span_y, 2, rows_x, rows_y, HEADS * squares)
    both = both.transpose(2, 0, 3, 1, 4, 5).reshape(2, grid_x, grid_y, HEADS, squares)
    low_f, low_c = both[0], both[1]

    mid_f = f32_einsum("hyj,xjhq->xyhq", kernel_y, low_f).astype(bf16)
    top_f = f32_einsum("hxi,iyhq->xyhq", kernel_x, mid_f)
    mid_c = f32_einsum("hxi,xyhq->iyhq", kernel_x, low_c).astype(bf16)
    top_c = f32_einsum("hyj,xyhq->xjhq", kernel_y, mid_c)
    gram_x = factor_z * f32_einsum("myhq,nyhq->hmn", low_c, mid_f)
    gram_y = factor_z * f32_einsum("xmhq,xnhq->hmn", mid_c, low_f)

    def here(top):
        top = lax.dynamic_slice_in_dim(top, start_x, rows_x, 0)
        top = lax.dynamic_slice_in_dim(top, start_y, rows_y, 1)
        return top.reshape(cells, HEADS, HEAD_DIM, HEAD_DIM)

    left_f = factor_z * jnp.einsum(
        "hdc,phdg->cphg", wo.astype(jnp.float32), here(top_f), precision=PRECISE
    )
    left_c = factor_z * jnp.einsum(
        "chd,phdg->cphg", wv.astype(jnp.float32), here(top_c), precision=PRECISE
    )
    left_f = left_f.astype(bf16)
    left_c = left_c.astype(bf16)

    grad_query_z = f32_einsum("cphg,cpz->hgz", left_f, cots)
    grad_keyset_z = f32_einsum("cphg,cpz->hgz", left_c, cols)
    gn_z = reduce_blocks(grad_of_normed(qk_weight[2], grad_query_z, grad_keyset_z), count)

    layer_output = (cols.astype(jnp.float32) + f32_einsum("cphg,hgz->cpz", left_f, query_b)).astype(bf16)
    through = f32_einsum("cphg,hgz->cpz", left_c, keyset_b)

    gn_x = grad_of_normed(qk_weight[0], *kernel_backward(gram_x, query_x, keyset_x, factor_x))
    gn_y = grad_of_normed(qk_weight[1], *kernel_backward(gram_y, query_y, keyset_y, factor_y))
    pull_x = pooled_grad(normed_x, inverse_x, gn_x)
    pull_y = pooled_grad(normed_y, inverse_y, gn_y)
    pull_z = pooled_grad(normed_z, inverse_z, gn_z)
    local_x = lax.dynamic_slice_in_dim(pull_x, start_x, rows_x, 1) / (grid_y * depth)
    local_y = lax.dynamic_slice_in_dim(pull_y, start_y, rows_y, 1) / (grid_x * depth)
    local_xy = (local_x[:, :, None] + local_y[:, None, :]).reshape(WIDTH, cells)
    local_z = pull_z / (grid_x * grid_y)
    field_grad = (
        cots.astype(jnp.float32) + through + local_xy[:, :, None] + local_z[:, None, :]
    ).astype(bf16)
    return (layer_output.reshape(field.shape), field_grad.reshape(field.shape))


def split(x):
    high = x.astype(jnp.bfloat16)
    return high, (x - high.astype(jnp.float32)).astype(jnp.bfloat16)


NN = (((1,), (0,)), ((), ()))
NT = (((1,), (1,)), ((), ()))
TN = (((0,), (0,)), ((), ()))


def mul(left, right, dims=NN):
    return lax.dot_general(left, right, dims, preferred_element_type=jnp.float32)


def mul_near(left, right, dims=NN):
    left_high, left_low = split(left)
    right_high, right_low = split(right)
    return (
        mul(left_high, right_high, dims)
        + mul(left_low, right_high, dims)
        + mul(left_high, right_low, dims)
    )


def mul_left(left, right, dims=NN):
    rows = left.shape[0]
    both = mul(jnp.concatenate(split(left), axis=0), right, dims)
    return both[:rows] + both[rows:]


def number(shape, dim):
    return lax.broadcasted_iota(jnp.int32, shape, dim)


def put_quarters(place_ref, part_ref, total, outs):
    for index in range(part_ref.shape[0]):
        part_ref[index] = total[:, index * LANES : (index + 1) * LANES]
    for step, out in enumerate(outs):
        out[0:WIDTH, :] = part_ref[place_ref[0] ^ step]


def join_quarters(place_ref, part_ref, quarters):
    for step, quarter in enumerate(quarters):
        part_ref[place_ref[0] ^ step] = quarter[...]
    return jnp.concatenate([part_ref[index] for index in range(part_ref.shape[0])], axis=1)


def expand(part):
    depth = part.shape[1]
    part = part.reshape(HEADS, 1, HEAD_DIM, depth)
    part = jnp.broadcast_to(part, (HEADS, HEAD_DIM, HEAD_DIM, depth))
    return part.reshape(WIDTH * HEAD_DIM, depth).astype(jnp.bfloat16)


def spread(weights, top):
    left = weights[:, None, :] * top[None]
    return left.reshape(-1, left.shape[2]).astype(jnp.bfloat16)


def prepare_kernel(wv_ref, wo_ref, qk_ref, wv_out, wo_out, wq_out, wk_out, wz_out):
    wide = HEADS * HEAD_DIM * HEAD_DIM
    row = number((WIDTH, wide), 0)
    lane = number((WIDTH, wide), 1)
    by_channel = ((lane >> 3) == row).astype(jnp.bfloat16)
    by_factor = (((lane >> 6) * HEAD_DIM + (lane & 7)) == row).astype(jnp.bfloat16)
    wv_out[...] = mul(wv_ref[...], by_channel)
    wo_out[...] = mul(wo_ref[...], by_channel, TN)
    for index, out in ((0, wq_out), (1, wk_out)):
        high, low = split(qk_ref[2, index])
        out[0:WIDTH, :] = mul(high, by_factor).astype(jnp.bfloat16)
        out[WIDTH : 2 * WIDTH, :] = mul(low, by_factor).astype(jnp.bfloat16)
        wz_out[index * WIDTH : (index + 1) * WIDTH, :] = qk_ref[2, index].T


def sums_kernel(place_ref, field_ref, *refs):
    outs, part_ref = refs[:-1], refs[-1]
    data = field_ref[...].astype(jnp.float32)
    _, rows_x, rows_y, depth = data.shape
    part = jnp.sum(jnp.sum(data, axis=1), axis=1)
    lanes = data[..., :LANES]
    for start in range(LANES, depth, LANES):
        lanes = lanes + data[..., start : start + LANES]
    row_sums = jnp.sum(lanes, axis=3, keepdims=True)
    shape = lanes.shape
    own = jnp.sum(jnp.where(number(shape, 0) == number(shape, 3), row_sums, 0.0), axis=0)
    put_quarters(place_ref, part_ref, part, outs)
    for out in outs:
        for index in range(rows_x):
            start = WIDTH + index * rows_y
            out[start : start + rows_y, :] = own[index]


def add_kernel(*refs):
    parts, out_ref = refs[:-1], refs[-1]
    total = parts[0][0:WIDTH, :]
    for part in parts[1:]:
        total = total + part[0:WIDTH, :]
    out_ref[0:WIDTH, :] = total
    cells = parts[0].shape[0] - WIDTH
    for step, part in enumerate(parts):
        start = WIDTH + step * cells
        out_ref[start : start + cells, :] = part[WIDTH:, :]


def factor_kernel(places, *refs):
    parts, (wz_ref, both_ref, feat_ref) = refs[:-3], refs[-3:]
    total = parts[0][0:WIDTH, :]
    for part in parts[1:]:
        total = total + part[0:WIDTH, :]
    pooled = total * (1.0 / places)
    inverse = lax.rsqrt(jnp.mean(pooled * pooled, axis=0, keepdims=True) + EPSILON)
    normed = pooled * inverse
    feat_ref[0:WIDTH, :] = normed
    feat_ref[WIDTH:, :] = jnp.broadcast_to(inverse, (HEAD_DIM, LANES))
    both_ref[...] = mul_near(wz_ref[...], normed).astype(jnp.bfloat16)


def pull_kernel(places, *refs):
    parts, (feat_ref, out_ref) = refs[:-2], refs[-2:]
    found = parts[0][...]
    for part in parts[1:]:
        found = found + part[...]
    normed = feat_ref[0:WIDTH, :]
    inverse = feat_ref[WIDTH : WIDTH + 1, :]
    found = inverse * (found - normed * jnp.mean(found * normed, axis=0, keepdims=True))
    out_ref[...] = found * (1.0 / places)


def by_head(part):
    shape = (HEADS, part.shape[0], WIDTH)
    mine = number(shape, 0) == (number(shape, 2) >> 3)
    return jnp.where(mine, part[None], 0.0).reshape(-1, WIDTH)


def plane_kernel(cells, lengths, *refs):
    parts, (same_ref, qk_ref, mix_ref, feat_ref, full_ref) = refs[:-5], refs[-5:]
    totals = jnp.concatenate(
        [
            part[WIDTH + step * cells : WIDTH + (step + 1) * cells, :]
            for step in range((parts[0].shape[0] - WIDTH) // cells)
            for part in parts
        ],
        axis=0,
    )[:, :WIDTH]
    places = totals.shape[0]
    high, low = split(totals)
    forward = backward = None
    for axis in range(2):
        same = same_ref[axis]
        pooled = (mul(same, high) + mul(same, low)) * (1.0 / lengths[axis][1])
        inverse = lax.rsqrt(jnp.mean(pooled * pooled, axis=1, keepdims=True) + EPSILON)
        normed = pooled * inverse
        query = mul_near(normed, qk_ref[axis, 0])
        keyset = mul_near(normed, qk_ref[axis, 1])
        feat_ref[4 * axis] = normed
        feat_ref[4 * axis + 1] = query
        feat_ref[4 * axis + 2] = keyset
        feat_ref[4 * axis + 3] = jnp.broadcast_to(inverse, (places, WIDTH))
        factor = 1.0 / math.sqrt(HEAD_DIM * lengths[axis][0])

        def scores(rows, other):
            found = mul_near(by_head(rows), other, NT) * factor
            return found.astype(jnp.bfloat16).astype(jnp.float32)

        full = scores(query, keyset)
        full_ref[axis] = full
        one = full.reshape(HEADS, places, places)[:, :cells].reshape(-1, places)
        two = scores(keyset[:cells], query)
        forward = one if forward is None else forward * one
        backward = two if backward is None else backward * two
    mix_ref[0] = forward
    mix_ref[1] = backward


def coef_kernel(place_ref, *refs):
    quarters, rest = refs[:-8], refs[-8:]
    field_ref, cot_ref, wv_ref, wo_ref, send_ref, both_ref, part_ref = rest[1:]
    quarters = quarters + rest[:1]
    rows, depth = field_ref.shape
    cells = rows // WIDTH
    wide = HEADS * HEAD_DIM * HEAD_DIM
    both = join_quarters(place_ref, part_ref, [q[...].astype(jnp.float32) for q in quarters])
    both_ref[...] = both.astype(jnp.bfloat16)
    query = expand(both[:WIDTH])
    keyset = expand(both[WIDTH:])
    low_f = mul(field_ref[...], keyset, NT).reshape(WIDTH, cells, wide)
    low_f = jnp.sum(wv_ref[...][:, None, :] * low_f, axis=0)
    low_c = mul(cot_ref[...], query, NT).reshape(WIDTH, cells, wide)
    low_c = jnp.sum(wo_ref[...][:, None, :] * low_c, axis=0)
    low = jnp.concatenate([low_f, low_c], axis=0).astype(jnp.bfloat16)
    send_ref[...] = low


def join_low(refs, cells):
    low = jnp.concatenate([ref[...].astype(jnp.float32) for ref in refs], axis=0)
    wide = low.shape[1]
    low = low.reshape(-1, 2 * cells, wide)
    return [
        low[:, start : start + cells].reshape(-1, wide).astype(jnp.bfloat16)
        for start in (0, cells)
    ]


def mix_kernel(factor, spans, place_ref, *refs):
    lows, refs = refs[:spans], refs[spans:]
    mix_ref, wv_ref, wo_ref, wq_ref, wk_ref, field_ref, cot_ref, top_ref = refs[:8]
    outs, part_ref = refs[8:-1], refs[-1]
    cells = field_ref.shape[0] // WIDTH
    low_f, low_c = join_low(lows, cells)
    wide = low_f.shape[1]
    shape = (HEADS, cells, wide)
    head = number(shape, 0) == (number(shape, 2) >> 6)

    def top(mix, low):
        found = mul_left(mix, low).reshape(shape)
        return jnp.sum(jnp.where(head, found, 0.0), axis=0) * factor

    top_f = top(mix_ref[0], low_f)
    top_c = top(mix_ref[1], low_c)
    top_ref[0] = top_f
    top_ref[1] = top_c
    left_f = spread(wo_ref[...], top_f)
    left_c = spread(wv_ref[...], top_c)

    def pull(weights, left, right):
        found = mul(weights, left, NT)
        return mul_left(found[:WIDTH] + found[WIDTH:], right)

    found = pull(wq_ref[...], left_f, cot_ref[...]) + pull(wk_ref[...], left_c, field_ref[...])
    put_quarters(place_ref, part_ref, found, outs)


def put_cells(ref, total):
    _, rows_x, rows_y, depth = ref.shape
    total = total.reshape(WIDTH, rows_x * rows_y, depth)
    for index in range(rows_x):
        rows = total[:, index * rows_y : (index + 1) * rows_y, :]
        ref[:, index, :, :] = rows.astype(jnp.bfloat16)


def output_kernel(top_ref, wo_ref, both_ref, field_ref, out_ref):
    query = expand(both_ref[...].astype(jnp.float32)[:WIDTH])
    left = spread(wo_ref[...], top_ref[0])
    put_cells(out_ref, mul(left, query) + field_ref[...].astype(jnp.float32))


def gram_kernel(cells, lengths, factor_z, *refs):
    lows, (feat_ref, full_ref, same_ref, qk_ref, out_ref) = refs[:-5], refs[-5:]
    low_f, low_c = join_low(lows, cells)
    places, wide = low_f.shape
    squares = HEAD_DIM * HEAD_DIM
    lane = number((places, LANES), 1)
    products = []
    for pair in range(wide // LANES):
        part_f = low_f[:, pair * LANES : (pair + 1) * LANES]
        part_c = low_c[:, pair * LANES : (pair + 1) * LANES]
        for half in range(LANES // squares):
            mine = (lane >> 6) == half
            products.append(mul(jnp.where(mine, part_c, jnp.zeros_like(part_c)), part_f, NT))
    product = jnp.concatenate(products, axis=0)
    factors = [1.0 / math.sqrt(HEAD_DIM * lengths[axis][0]) for axis in range(2)]
    queries = [by_head(feat_ref[4 * axis + 1]).astype(jnp.bfloat16) for axis in range(2)]
    keysets = [by_head(feat_ref[4 * axis + 2]).astype(jnp.bfloat16) for axis in range(2)]
    total = jnp.zeros((cells, WIDTH), jnp.float32)
    for axis in range(2):
        gram = (product * full_ref[1 - axis]).astype(jnp.bfloat16)
        across = jnp.concatenate(
            [gram[h * places : (h + 1) * places] for h in range(HEADS)], axis=1
        )
        scale = factors[axis] * factor_z
        grad_query = mul(across, keysets[axis]) * scale
        grad_keyset = mul(gram, queries[axis], TN) * scale
        found = mul_near(grad_query, qk_ref[axis, 0], NT) + mul_near(grad_keyset, qk_ref[axis, 1], NT)
        high, low = split(found)
        own = same_ref[axis, 0 : 2 * cells, :]
        found = (mul(own, high) + mul(own, low))[:cells]
        normed = feat_ref[4 * axis, 0:cells, :]
        inverse = feat_ref[4 * axis + 3, 0:cells, :]
        found = found - normed * jnp.mean(found * normed, axis=1, keepdims=True)
        total = total + inverse * found * (1.0 / lengths[axis][1])
    out_ref[...] = total


def base_kernel(top_ref, wv_ref, both_ref, cot_ref, plane_ref, out_ref):
    rows = cot_ref.shape[0]
    cells = rows // WIDTH
    shape = (WIDTH, cells, WIDTH)
    own = jnp.where(number(shape, 0) == number(shape, 2), plane_ref[...][None], 0.0)
    plane = mul_left(own.reshape(rows, WIDTH), jnp.ones((WIDTH, LANES), jnp.bfloat16))
    keyset = expand(both_ref[...].astype(jnp.float32)[WIDTH:])
    left = spread(wv_ref[...], top_ref[1])
    found = mul(left, keyset) + cot_ref[...].astype(jnp.float32)
    columns = found.shape[1] // LANES
    out_ref[...] = found + jnp.concatenate([plane] * columns, axis=1)


def final_kernel(place_ref, *refs):
    quarters, (base_ref, out_ref, part_ref) = refs[:-3], refs[-3:]
    rows, depth = base_ref.shape
    cells = rows // WIDTH
    found = join_quarters(place_ref, part_ref, quarters)
    total = base_ref[...].reshape(WIDTH, cells, depth) + found[:, None, :]
    put_cells(out_ref, total)


def run(kernel, outs, operands, scalars=0, flops=0, scratch=()):
    vmem = pl.BlockSpec(memory_space=pltpu.VMEM)
    smem = pl.BlockSpec(memory_space=pltpu.SMEM)
    moved = sum(x.size * x.dtype.itemsize for x in tuple(operands) + tuple(outs))
    found = pl.pallas_call(
        kernel,
        out_shape=tuple(outs),
        in_specs=[smem] * scalars + [vmem] * (len(operands) - scalars),
        out_specs=tuple(vmem for _ in outs),
        scratch_shapes=list(scratch),
        compiler_params=pltpu.CompilerParams(vmem_limit_bytes=16 * 1024 * 1024),
        cost_estimate=pl.CostEstimate(flops=flops, bytes_accessed=moved, transcendentals=0),
    )(*operands)
    return found[0] if len(outs) == 1 else found


def per_device_kernels(field, cotangent, qk_weight, w_value, w_out):
    span_x = lax.axis_size("gx")
    span_y = lax.axis_size("gy")
    count = span_x * span_y
    rows_x, rows_y, depth = field.shape[1:]
    cells = rows_x * rows_y
    places = count * cells
    grid_x = rows_x * span_x
    grid_y = rows_y * span_y
    rows = WIDTH * cells
    wide = WIDTH * HEAD_DIM
    f32, bf16 = jnp.float32, jnp.bfloat16
    like = jax.ShapeDtypeStruct
    lengths = ((grid_x, grid_y * depth), (grid_y, grid_x * depth))
    place = jnp.stack([lax.axis_index("gx"), lax.axis_index("gy")]).astype(jnp.int32)

    cell = np.arange(places)
    at_x = cell // cells // span_y * rows_x + cell % cells // rows_y
    at_y = cell // cells % span_y * rows_y + cell % rows_y
    same = jnp.asarray(
        np.stack([at_x[:, None] == at_x[None], at_y[:, None] == at_y[None]]), dtype=bf16
    )

    cols = field.reshape(rows, depth)
    cots = cotangent.reshape(rows, depth)
    block = like((WIDTH, LANES), f32)
    parts = pltpu.VMEM((span_x, WIDTH, LANES), f32)
    factor_z = 1.0 / math.sqrt(HEAD_DIM * depth)
    cube = rows * wide * depth * 2

    def swaps(sent, axis, size):
        if not isinstance(sent, (tuple, list)):
            sent = [sent] * size
        return tuple(sent[:1]) + tuple(
            swap(sent[step], axis, size, step) for step in range(1, size)
        )

    sums = run(
        sums_kernel, [like((WIDTH + cells, LANES), f32)] * span_x, (place, field),
        scalars=1, flops=cube // 4, scratch=[parts],
    )
    wv, wo, wq, wk, wz = run(
        prepare_kernel,
        [like((WIDTH, wide), f32)] * 2 + [like((2 * WIDTH, wide), bf16)] * 2
        + [like((2 * WIDTH, WIDTH), f32)],
        (w_value, w_out, qk_weight),
        flops=cube // 8,
    )
    total = run(
        add_kernel, [like((WIDTH + span_x * cells, LANES), f32)], swaps(sums, "gx", span_x)
    )
    totals = swaps(total, "gy", span_y)
    mine, feat_z = run(
        functools.partial(factor_kernel, grid_x * grid_y),
        [like((2 * WIDTH, LANES), bf16), like((WIDTH + HEAD_DIM, LANES), f32)],
        totals + (wz,),
    )
    mix, feat, full = run(
        functools.partial(plane_kernel, cells, lengths),
        [like((2, HEADS * cells, places), f32), like((8, places, WIDTH), f32),
         like((2, HEADS * places, places), f32)],
        totals + (same, qk_weight),
        flops=cube // 2,
    )
    send, both = run(
        coef_kernel,
        [like((2 * cells, wide), bf16), like((2 * WIDTH, depth), bf16)],
        (place,) + swaps(mine, "gx", span_x) + (cols, cots, wv, wo),
        scalars=1,
        flops=2 * cube,
        scratch=[pltpu.VMEM((span_x, 2 * WIDTH, LANES), f32)],
    )
    low = jnp.concatenate(swaps(send, "gy", span_y), axis=0)
    lows = swaps(low, "gx", span_x)
    top, *pulls = run(
        functools.partial(mix_kernel, factor_z, span_x),
        [like((2, cells, wide), f32)] + [block] * span_x,
        (place,) + lows + (mix, wv, wo, wq, wk, cols, cots),
        scalars=1,
        flops=cube,
        scratch=[parts],
    )
    total = sum(swaps(pulls, "gx", span_x))
    layer_output = run(
        output_kernel, [like(field.shape, bf16)], (top, wo, both, cols), flops=cube
    )
    plane = run(
        functools.partial(gram_kernel, cells, lengths, factor_z),
        [like((cells, WIDTH), f32)],
        lows + (feat, full, same, qk_weight),
        flops=2 * cube,
    )
    mine = run(
        functools.partial(pull_kernel, grid_x * grid_y),
        [block],
        swaps(total, "gy", span_y) + (feat_z,),
    )
    base = run(base_kernel, [like((rows, depth), f32)], (top, wv, both, cots, plane), flops=cube)
    field_grad = run(
        final_kernel,
        [like(field.shape, bf16)],
        (place,) + swaps(mine, "gx", span_x) + (base,),
        scalars=1,
        scratch=[parts],
    )
    return (layer_output, field_grad)


def solution(mesh):
    placed = P(None, ("groups", "gx"), "gy", None)
    count = mesh.shape["gx"] * mesh.shape["gy"]

    def program(*arrays):
        _, grid_x, grid_y, depth = arrays[0].shape
        places = grid_x // mesh.shape["groups"] * grid_y
        small = places == LANES and places == 8 * count
        small = small and depth == LANES * mesh.shape["gx"] and count & (count - 1) == 0
        return jax.shard_map(
            per_device_kernels if small else per_device,
            mesh=mesh,
            in_specs=(placed, placed, P(), P(), P()),
            out_specs=(placed, placed),
            check_vma=False,
        )(*arrays)

    return program
```

```python
import functools
import math

import jax
import jax.numpy as jnp
import numpy as np
from jax import lax
from jax.experimental import pallas as pl
from jax.experimental.pallas import tpu as pltpu
from jax.sharding import PartitionSpec as P

WIDTH = 64
HEADS = 8
HEAD_DIM = 8
LANES = 128

EPSILON = 1e-06
PRECISE = lax.Precision.HIGHEST
AXES = ("gx", "gy")


def exchange(parts):
    return lax.all_to_all(parts, AXES, split_axis=0, concat_axis=0, tiled=True)


def swap(part, axis, size, step):
    return lax.ppermute(part, axis, [(i, i ^ step) for i in range(size)])


def gather(part, count):
    return exchange(jnp.broadcast_to(part[None], (count,) + part.shape))


def reduce_blocks(total, count):
    width, depth = total.shape
    blocks = total.reshape(width, depth // LANES, LANES).transpose(1, 0, 2)
    blocks = blocks.reshape(count, width * depth // LANES // count, LANES)
    mine = jnp.sum(exchange(blocks), axis=0)
    whole = gather(mine, count).reshape(depth // LANES, width, LANES)
    return whole.transpose(1, 0, 2).reshape(width, depth)


def axis_features(pooled, weights):
    inverse = lax.rsqrt(jnp.mean(pooled * pooled, axis=0, keepdims=True) + EPSILON)
    normed = pooled * inverse
    length = pooled.shape[1]
    factor = 1.0 / math.sqrt(HEAD_DIM * length)
    queries = jnp.dot(weights[0].T, normed, precision=PRECISE).reshape(HEADS, HEAD_DIM, length)
    keyset = jnp.dot(weights[1].T, normed, precision=PRECISE).reshape(HEADS, HEAD_DIM, length)
    return (normed, inverse, queries, keyset, factor)


def axis_kernel(queries, keyset, factor):
    scores = jnp.einsum("hdm,hdn->hmn", queries, keyset, precision=PRECISE)
    return (scores * factor).astype(jnp.bfloat16)


def kernel_backward(gram, queries, keyset, factor):
    grad_query = factor * jnp.einsum("hmn,hdn->hdm", gram, keyset, precision=PRECISE)
    grad_keyset = factor * jnp.einsum("hmn,hdm->hdn", gram, queries, precision=PRECISE)
    return (grad_query, grad_keyset)


def grad_of_normed(weights, grad_query, grad_keyset):
    length = grad_query.shape[-1]
    grad_normed = jnp.dot(weights[0], grad_query.reshape(WIDTH, length), precision=PRECISE)
    return grad_normed + jnp.dot(
        weights[1], grad_keyset.reshape(WIDTH, length), precision=PRECISE
    )


def pooled_grad(normed, inverse, grad_normed):
    return inverse * (grad_normed - normed * jnp.mean(grad_normed * normed, axis=0, keepdims=True))


def f32_einsum(pattern, left, right):
    return jnp.einsum(pattern, left, right, preferred_element_type=jnp.float32)


def per_device(field, cotangent, qk_weight, w_value, w_out):
    span_x = lax.axis_size("gx")
    span_y = lax.axis_size("gy")
    count = span_x * span_y
    rows_x, rows_y, depth = field.shape[1:]
    cells = rows_x * rows_y
    grid_x = rows_x * span_x
    grid_y = rows_y * span_y
    start_x = lax.axis_index("gx") * rows_x
    start_y = lax.axis_index("gy") * rows_y
    bf16 = jnp.bfloat16

    cols = field.reshape(WIDTH, cells, depth)
    cots = cotangent.reshape(WIDTH, cells, depth)

    sum_z = jnp.sum(cols, axis=1, dtype=jnp.float32)
    sum_rows = jnp.sum(cols, axis=2, dtype=jnp.float32)
    rows_all = gather(sum_rows.T, count).reshape(span_x, span_y, rows_x, rows_y, WIDTH)
    total_x = jnp.sum(rows_all, axis=(1, 3)).reshape(grid_x, WIDTH).T
    total_y = jnp.sum(rows_all, axis=(0, 2)).reshape(grid_y, WIDTH).T
    total_z = reduce_blocks(sum_z, count)

    normed_x, inverse_x, query_x, keyset_x, factor_x = axis_features(
        total_x / (grid_y * depth), qk_weight[0]
    )
    normed_y, inverse_y, query_y, keyset_y, factor_y = axis_features(
        total_y / (grid_x * depth), qk_weight[1]
    )
    normed_z, inverse_z, query_z, keyset_z, factor_z = axis_features(
        total_z / (grid_x * grid_y), qk_weight[2]
    )
    kernel_x = axis_kernel(query_x, keyset_x, factor_x)
    kernel_y = axis_kernel(query_y, keyset_y, factor_y)
    query_b = query_z.astype(bf16)
    keyset_b = keyset_z.astype(bf16)

    wv = w_value.reshape(WIDTH, HEADS, HEAD_DIM)
    wo = w_out.reshape(HEADS, HEAD_DIM, WIDTH)
    coef_f = f32_einsum("cpk,hgk->cphg", cols, keyset_b)
    coef_c = f32_einsum("cpz,hgz->cphg", cots, query_b)
    low_f = jnp.einsum("chd,cphg->phdg", wv.astype(jnp.float32), coef_f, precision=PRECISE)
    low_c = jnp.einsum("hdc,cphg->phdg", wo.astype(jnp.float32), coef_c, precision=PRECISE)
    squares = HEAD_DIM * HEAD_DIM
    both = jnp.stack([low_f, low_c]).astype(bf16).reshape(2, cells, HEADS * squares)
    both = gather(both, count).reshape(span_x, span_y, 2, rows_x, rows_y, HEADS * squares)
    both = both.transpose(2, 0, 3, 1, 4, 5).reshape(2, grid_x, grid_y, HEADS, squares)
    low_f, low_c = both[0], both[1]

    mid_f = f32_einsum("hyj,xjhq->xyhq", kernel_y, low_f).astype(bf16)
    top_f = f32_einsum("hxi,iyhq->xyhq", kernel_x, mid_f)
    mid_c = f32_einsum("hxi,xyhq->iyhq", kernel_x, low_c).astype(bf16)
    top_c = f32_einsum("hyj,xyhq->xjhq", kernel_y, mid_c)
    gram_x = factor_z * f32_einsum("myhq,nyhq->hmn", low_c, mid_f)
    gram_y = factor_z * f32_einsum("xmhq,xnhq->hmn", mid_c, low_f)

    def here(top):
        top = lax.dynamic_slice_in_dim(top, start_x, rows_x, 0)
        top = lax.dynamic_slice_in_dim(top, start_y, rows_y, 1)
        return top.reshape(cells, HEADS, HEAD_DIM, HEAD_DIM)

    left_f = factor_z * jnp.einsum(
        "hdc,phdg->cphg", wo.astype(jnp.float32), here(top_f), precision=PRECISE
    )
    left_c = factor_z * jnp.einsum(
        "chd,phdg->cphg", wv.astype(jnp.float32), here(top_c), precision=PRECISE
    )
    left_f = left_f.astype(bf16)
    left_c = left_c.astype(bf16)

    grad_query_z = f32_einsum("cphg,cpz->hgz", left_f, cots)
    grad_keyset_z = f32_einsum("cphg,cpz->hgz", left_c, cols)
    gn_z = reduce_blocks(grad_of_normed(qk_weight[2], grad_query_z, grad_keyset_z), count)

    layer_output = (cols.astype(jnp.float32) + f32_einsum("cphg,hgz->cpz", left_f, query_b)).astype(bf16)
    through = f32_einsum("cphg,hgz->cpz", left_c, keyset_b)

    gn_x = grad_of_normed(qk_weight[0], *kernel_backward(gram_x, query_x, keyset_x, factor_x))
    gn_y = grad_of_normed(qk_weight[1], *kernel_backward(gram_y, query_y, keyset_y, factor_y))
    pull_x = pooled_grad(normed_x, inverse_x, gn_x)
    pull_y = pooled_grad(normed_y, inverse_y, gn_y)
    pull_z = pooled_grad(normed_z, inverse_z, gn_z)
    local_x = lax.dynamic_slice_in_dim(pull_x, start_x, rows_x, 1) / (grid_y * depth)
    local_y = lax.dynamic_slice_in_dim(pull_y, start_y, rows_y, 1) / (grid_x * depth)
    local_xy = (local_x[:, :, None] + local_y[:, None, :]).reshape(WIDTH, cells)
    local_z = pull_z / (grid_x * grid_y)
    field_grad = (
        cots.astype(jnp.float32) + through + local_xy[:, :, None] + local_z[:, None, :]
    ).astype(bf16)
    return (layer_output.reshape(field.shape), field_grad.reshape(field.shape))


def split(x):
    high = x.astype(jnp.bfloat16)
    return high, (x - high.astype(jnp.float32)).astype(jnp.bfloat16)


NN = (((1,), (0,)), ((), ()))
NT = (((1,), (1,)), ((), ()))
TN = (((0,), (0,)), ((), ()))


def mul(left, right, dims=NN):
    return lax.dot_general(left, right, dims, preferred_element_type=jnp.float32)


def mul_near(left, right, dims=NN):
    left_high, left_low = split(left)
    right_high, right_low = split(right)
    return (
        mul(left_high, right_high, dims)
        + mul(left_low, right_high, dims)
        + mul(left_high, right_low, dims)
    )


def mul_left(left, right, dims=NN):
    rows = left.shape[0]
    both = mul(jnp.concatenate(split(left), axis=0), right, dims)
    return both[:rows] + both[rows:]


def number(shape, dim):
    return lax.broadcasted_iota(jnp.int32, shape, dim)


def put_quarters(part_ref, total, outs):
    for index in range(part_ref.shape[0]):
        part_ref[index] = total[:, index * LANES : (index + 1) * LANES]
    for step, out in enumerate(outs):
        out[0:WIDTH, :] = part_ref[lax.axis_index("gx") ^ step]


def join_quarters(part_ref, quarters):
    for step, quarter in enumerate(quarters):
        part_ref[lax.axis_index("gx") ^ step] = quarter[...]
    return jnp.concatenate([part_ref[index] for index in range(part_ref.shape[0])], axis=1)


def expand(part):
    depth = part.shape[1]
    part = part.reshape(HEADS, 1, HEAD_DIM, depth)
    part = jnp.broadcast_to(part, (HEADS, HEAD_DIM, HEAD_DIM, depth))
    return part.reshape(WIDTH * HEAD_DIM, depth).astype(jnp.bfloat16)


def spread(weights, top):
    left = weights[:, None, :] * top[None]
    return left.reshape(-1, left.shape[2]).astype(jnp.bfloat16)


def prepare_kernel(wv_ref, wo_ref, qk_ref, wv_out, wo_out, wq_out, wk_out, wz_out):
    wide = HEADS * HEAD_DIM * HEAD_DIM
    row = number((WIDTH, wide), 0)
    lane = number((WIDTH, wide), 1)
    by_channel = ((lane >> 3) == row).astype(jnp.bfloat16)
    by_factor = (((lane >> 6) * HEAD_DIM + (lane & 7)) == row).astype(jnp.bfloat16)
    wv_out[...] = mul(wv_ref[...], by_channel)
    wo_out[...] = mul(wo_ref[...], by_channel, TN)
    for index, out in ((0, wq_out), (1, wk_out)):
        high, low = split(qk_ref[2, index])
        out[0:WIDTH, :] = mul(high, by_factor).astype(jnp.bfloat16)
        out[WIDTH : 2 * WIDTH, :] = mul(low, by_factor).astype(jnp.bfloat16)
        wz_out[index * WIDTH : (index + 1) * WIDTH, :] = qk_ref[2, index].T


def sums_kernel(field_ref, *refs):
    outs, (part_ref, data_ref, semaphores) = refs[:-3], refs[-3:]
    _, rows_x, rows_y, depth = data_ref.shape
    chunks = semaphores.shape[0]
    size = WIDTH // chunks
    copies = [
        pltpu.make_async_copy(
            field_ref.at[pl.ds(index * size, size)],
            data_ref.at[pl.ds(index * size, size)],
            semaphores.at[index],
        )
        for index in range(chunks)
    ]
    for copy in copies:
        copy.start()
    own = jnp.zeros((rows_x, rows_y, LANES), jnp.float32)
    for index, copy in enumerate(copies):
        copy.wait()
        rows = slice(index * size, (index + 1) * size)
        data = data_ref[rows].astype(jnp.float32)
        part = jnp.sum(jnp.sum(data, axis=1), axis=1)
        for quarter in range(part_ref.shape[0]):
            part_ref[quarter, rows, :] = part[:, quarter * LANES : (quarter + 1) * LANES]
        lanes = data[..., :LANES]
        for start in range(LANES, depth, LANES):
            lanes = lanes + data[..., start : start + LANES]
        row_sums = jnp.sum(lanes, axis=3, keepdims=True)
        shape = lanes.shape
        mine = number(shape, 0) + index * size == number(shape, 3)
        own = own + jnp.sum(jnp.where(mine, row_sums, 0.0), axis=0)
    for step, out in enumerate(outs):
        out[0:WIDTH, :] = part_ref[lax.axis_index("gx") ^ step]
        for index in range(rows_x):
            start = WIDTH + index * rows_y
            out[start : start + rows_y, :] = own[index]


def add_kernel(*refs):
    parts, out_ref = refs[:-1], refs[-1]
    total = parts[0][0:WIDTH, :]
    for part in parts[1:]:
        total = total + part[0:WIDTH, :]
    out_ref[0:WIDTH, :] = total
    cells = parts[0].shape[0] - WIDTH
    for step, part in enumerate(parts):
        start = WIDTH + step * cells
        out_ref[start : start + cells, :] = part[WIDTH:, :]


def factor_kernel(places, *refs):
    parts, (wz_ref, both_ref, feat_ref) = refs[:-3], refs[-3:]
    total = parts[0][0:WIDTH, :]
    for part in parts[1:]:
        total = total + part[0:WIDTH, :]
    pooled = total * (1.0 / places)
    inverse = lax.rsqrt(jnp.mean(pooled * pooled, axis=0, keepdims=True) + EPSILON)
    normed = pooled * inverse
    feat_ref[0:WIDTH, :] = normed
    feat_ref[WIDTH:, :] = jnp.broadcast_to(inverse, (HEAD_DIM, LANES))
    both_ref[...] = mul_near(wz_ref[...], normed).astype(jnp.bfloat16)


def pull_kernel(places, *refs):
    parts, (feat_ref, out_ref) = refs[:-2], refs[-2:]
    found = parts[0][...]
    for part in parts[1:]:
        found = found + part[...]
    normed = feat_ref[0:WIDTH, :]
    inverse = feat_ref[WIDTH : WIDTH + 1, :]
    found = inverse * (found - normed * jnp.mean(found * normed, axis=0, keepdims=True))
    out_ref[...] = found * (1.0 / places)


def by_head(part):
    shape = (HEADS, part.shape[0], WIDTH)
    mine = number(shape, 0) == (number(shape, 2) >> 3)
    return jnp.where(mine, part[None], 0.0).reshape(-1, WIDTH)


def plane_kernel(cells, span_x, lengths, *refs):
    parts, (same_ref, qk_ref, mix_ref, feat_ref, full_ref) = refs[:-5], refs[-5:]
    totals = jnp.concatenate(
        [
            part[WIDTH + step * cells : WIDTH + (step + 1) * cells, :]
            for first in range(span_x)
            for part in parts
            for step in range(first, (parts[0].shape[0] - WIDTH) // cells, span_x)
        ],
        axis=0,
    )[:, :WIDTH]
    places = totals.shape[0]
    high, low = split(totals)
    forward = backward = None
    for axis in range(2):
        same = same_ref[axis]
        pooled = (mul(same, high) + mul(same, low)) * (1.0 / lengths[axis][1])
        inverse = lax.rsqrt(jnp.mean(pooled * pooled, axis=1, keepdims=True) + EPSILON)
        normed = pooled * inverse
        query = mul_near(normed, qk_ref[axis, 0])
        keyset = mul_near(normed, qk_ref[axis, 1])
        feat_ref[4 * axis] = normed
        feat_ref[4 * axis + 1] = query
        feat_ref[4 * axis + 2] = keyset
        feat_ref[4 * axis + 3] = jnp.broadcast_to(inverse, (places, WIDTH))
        factor = 1.0 / math.sqrt(HEAD_DIM * lengths[axis][0])

        def scores(rows, other):
            found = mul_near(by_head(rows), other, NT) * factor
            return found.astype(jnp.bfloat16).astype(jnp.float32)

        full = scores(query, keyset)
        full_ref[axis] = full
        one = full.reshape(HEADS, places, places)[:, :cells].reshape(-1, places)
        two = scores(keyset[:cells], query)
        forward = one if forward is None else forward * one
        backward = two if backward is None else backward * two
    mix_ref[0] = forward
    mix_ref[1] = backward


def coef_kernel(*refs):
    quarters, rest = refs[:-8], refs[-8:]
    field_ref, cot_ref, wv_ref, wo_ref, send_ref, both_ref, part_ref = rest[1:]
    quarters = quarters + rest[:1]
    rows, depth = field_ref.shape
    cells = rows // WIDTH
    wide = HEADS * HEAD_DIM * HEAD_DIM
    both = join_quarters(part_ref, [q[...].astype(jnp.float32) for q in quarters])
    both_ref[...] = both.astype(jnp.bfloat16)
    query = expand(both[:WIDTH])
    keyset = expand(both[WIDTH:])
    low_f = mul(field_ref[...], keyset, NT).reshape(WIDTH, cells, wide)
    low_f = jnp.sum(wv_ref[...][:, None, :] * low_f, axis=0)
    low_c = mul(cot_ref[...], query, NT).reshape(WIDTH, cells, wide)
    low_c = jnp.sum(wo_ref[...][:, None, :] * low_c, axis=0)
    low = jnp.concatenate([low_f, low_c], axis=0).astype(jnp.bfloat16)
    send_ref[...] = low


def join_low(refs, cells):
    low = jnp.concatenate([ref[...].astype(jnp.float32) for ref in refs], axis=0)
    wide = low.shape[1]
    low = low.reshape(-1, 2 * cells, wide)
    return [
        low[:, start : start + cells].reshape(-1, wide).astype(jnp.bfloat16)
        for start in (0, cells)
    ]


def mix_kernel(factor, spans, *refs):
    lows, refs = refs[:spans], refs[spans:]
    mix_ref, wv_ref, wo_ref, wq_ref, wk_ref, field_ref, cot_ref, top_ref = refs[:8]
    outs, part_ref = refs[8:-1], refs[-1]
    cells = field_ref.shape[0] // WIDTH
    low_f, low_c = join_low(lows, cells)
    wide = low_f.shape[1]
    shape = (HEADS, cells, wide)
    head = number(shape, 0) == (number(shape, 2) >> 6)

    def top(mix, low):
        found = mul_left(mix, low).reshape(shape)
        return jnp.sum(jnp.where(head, found, 0.0), axis=0) * factor

    top_f = top(mix_ref[0], low_f)
    top_c = top(mix_ref[1], low_c)
    top_ref[0] = top_f
    top_ref[1] = top_c
    left_f = spread(wo_ref[...], top_f)
    left_c = spread(wv_ref[...], top_c)

    def pull(weights, left, right):
        found = mul(weights, left, NT)
        return mul_left(found[:WIDTH] + found[WIDTH:], right)

    found = pull(wq_ref[...], left_f, cot_ref[...]) + pull(wk_ref[...], left_c, field_ref[...])
    put_quarters(part_ref, found, outs)


def put_cells(ref, total):
    _, rows_x, rows_y, depth = ref.shape
    total = total.reshape(WIDTH, rows_x * rows_y, depth)
    for index in range(rows_x):
        rows = total[:, index * rows_y : (index + 1) * rows_y, :]
        ref[:, index, :, :] = rows.astype(jnp.bfloat16)


def output_kernel(top_ref, wo_ref, both_ref, field_ref, out_ref):
    query = expand(both_ref[...].astype(jnp.float32)[:WIDTH])
    left = spread(wo_ref[...], top_ref[0])
    put_cells(out_ref, mul(left, query) + field_ref[...].astype(jnp.float32))


def gram_kernel(cells, lengths, factor_z, *refs):
    lows, (feat_ref, full_ref, same_ref, qk_ref, out_ref) = refs[:-5], refs[-5:]
    low_f, low_c = join_low(lows, cells)
    places, wide = low_f.shape
    squares = HEAD_DIM * HEAD_DIM
    lane = number((places, LANES), 1)
    products = []
    for pair in range(wide // LANES):
        part_f = low_f[:, pair * LANES : (pair + 1) * LANES]
        part_c = low_c[:, pair * LANES : (pair + 1) * LANES]
        for half in range(LANES // squares):
            mine = (lane >> 6) == half
            products.append(mul(jnp.where(mine, part_c, jnp.zeros_like(part_c)), part_f, NT))
    product = jnp.concatenate(products, axis=0)
    factors = [1.0 / math.sqrt(HEAD_DIM * lengths[axis][0]) for axis in range(2)]
    queries = [by_head(feat_ref[4 * axis + 1]).astype(jnp.bfloat16) for axis in range(2)]
    keysets = [by_head(feat_ref[4 * axis + 2]).astype(jnp.bfloat16) for axis in range(2)]
    total = jnp.zeros((cells, WIDTH), jnp.float32)
    for axis in range(2):
        gram = (product * full_ref[1 - axis]).astype(jnp.bfloat16)
        across = jnp.concatenate(
            [gram[h * places : (h + 1) * places] for h in range(HEADS)], axis=1
        )
        scale = factors[axis] * factor_z
        grad_query = mul(across, keysets[axis]) * scale
        grad_keyset = mul(gram, queries[axis], TN) * scale
        found = mul_near(grad_query, qk_ref[axis, 0], NT) + mul_near(grad_keyset, qk_ref[axis, 1], NT)
        high, low = split(found)
        own = same_ref[axis, 0 : 2 * cells, :]
        found = (mul(own, high) + mul(own, low))[:cells]
        normed = feat_ref[4 * axis, 0:cells, :]
        inverse = feat_ref[4 * axis + 3, 0:cells, :]
        found = found - normed * jnp.mean(found * normed, axis=1, keepdims=True)
        total = total + inverse * found * (1.0 / lengths[axis][1])
    out_ref[...] = total


def base_kernel(top_ref, wv_ref, both_ref, cot_ref, plane_ref, out_ref):
    rows = cot_ref.shape[0]
    cells = rows // WIDTH
    shape = (WIDTH, cells, WIDTH)
    own = jnp.where(number(shape, 0) == number(shape, 2), plane_ref[...][None], 0.0)
    plane = mul_left(own.reshape(rows, WIDTH), jnp.ones((WIDTH, LANES), jnp.bfloat16))
    keyset = expand(both_ref[...].astype(jnp.float32)[WIDTH:])
    left = spread(wv_ref[...], top_ref[1])
    found = mul(left, keyset) + cot_ref[...].astype(jnp.float32)
    columns = found.shape[1] // LANES
    out_ref[...] = found + jnp.concatenate([plane] * columns, axis=1)


def final_kernel(*refs):
    quarters, (base_ref, out_ref, part_ref) = refs[:-3], refs[-3:]
    rows, depth = base_ref.shape
    cells = rows // WIDTH
    found = join_quarters(part_ref, quarters)
    total = base_ref[...].reshape(WIDTH, cells, depth) + found[:, None, :]
    put_cells(out_ref, total)


def run(kernel, outs, operands, places=pltpu.VMEM, flops=0, scratch=()):
    vmem = pl.BlockSpec(memory_space=pltpu.VMEM)
    moved = sum(x.size * x.dtype.itemsize for x in tuple(operands) + tuple(outs))
    found = pl.pallas_call(
        kernel,
        out_shape=tuple(outs),
        in_specs=[pl.BlockSpec(memory_space=places)] * len(operands),
        out_specs=tuple(vmem for _ in outs),
        scratch_shapes=list(scratch),
        compiler_params=pltpu.CompilerParams(vmem_limit_bytes=16 * 1024 * 1024),
        cost_estimate=pl.CostEstimate(flops=flops, bytes_accessed=moved, transcendentals=0),
    )(*operands)
    return found[0] if len(outs) == 1 else found


def per_device_kernels(field, cotangent, qk_weight, w_value, w_out):
    span_x = lax.axis_size("gx")
    span_y = lax.axis_size("gy")
    count = span_x * span_y
    rows_x, rows_y, depth = field.shape[1:]
    cells = rows_x * rows_y
    places = count * cells
    grid_x = rows_x * span_x
    grid_y = rows_y * span_y
    rows = WIDTH * cells
    wide = WIDTH * HEAD_DIM
    f32, bf16 = jnp.float32, jnp.bfloat16
    like = jax.ShapeDtypeStruct
    lengths = ((grid_x, grid_y * depth), (grid_y, grid_x * depth))

    cell = np.arange(places)
    at_x = cell // cells // span_y * rows_x + cell % cells // rows_y
    at_y = cell // cells % span_y * rows_y + cell % rows_y
    same = jnp.asarray(
        np.stack([at_x[:, None] == at_x[None], at_y[:, None] == at_y[None]]), dtype=bf16
    )

    cols = field.reshape(rows, depth)
    cots = cotangent.reshape(rows, depth)
    block = like((WIDTH, LANES), f32)
    parts = pltpu.VMEM((span_x, WIDTH, LANES), f32)
    factor_z = 1.0 / math.sqrt(HEAD_DIM * depth)
    cube = rows * wide * depth * 2

    def swaps(sent, axis, size):
        if not isinstance(sent, (tuple, list)):
            sent = [sent] * size
        return tuple(sent[:1]) + tuple(
            swap(sent[step], axis, size, step) for step in range(1, size)
        )

    sums = run(
        sums_kernel, [like((WIDTH + cells, LANES), f32)] * span_x, (field,), places=pl.ANY,
        flops=cube // 4,
        scratch=[parts, pltpu.VMEM(field.shape, bf16), pltpu.SemaphoreType.DMA((4,))],
    )
    wv, wo, wq, wk, wz = run(
        prepare_kernel,
        [like((WIDTH, wide), f32)] * 2 + [like((2 * WIDTH, wide), bf16)] * 2
        + [like((2 * WIDTH, WIDTH), f32)],
        (w_value, w_out, qk_weight),
        flops=cube // 8,
    )
    def add(sent, size):
        return run(add_kernel, [like((WIDTH + size * cells, LANES), f32)], sent)

    def pair(part, step):
        return part, swap(part, "gy", span_y, step)

    total = add(swaps(sums, "gx", span_x), span_x)
    steps = [1 << level for level in range(span_y.bit_length() - 1)]
    for step in steps[:-1]:
        total = add(pair(total, step), 2 * step * span_x)
    totals = pair(total, steps[-1])
    mine, feat_z = run(
        functools.partial(factor_kernel, grid_x * grid_y),
        [like((2 * WIDTH, LANES), bf16), like((WIDTH + HEAD_DIM, LANES), f32)],
        totals + (wz,),
    )
    mix, feat, full = run(
        functools.partial(plane_kernel, cells, span_x, lengths),
        [like((2, HEADS * cells, places), f32), like((8, places, WIDTH), f32),
         like((2, HEADS * places, places), f32)],
        totals + (same, qk_weight),
        flops=cube // 2,
    )
    send, both = run(
        coef_kernel,
        [like((2 * cells, wide), bf16), like((2 * WIDTH, depth), bf16)],
        swaps(mine, "gx", span_x) + (cols, cots, wv, wo),
        flops=2 * cube,
        scratch=[pltpu.VMEM((span_x, 2 * WIDTH, LANES), f32)],
    )
    low = send
    for step in steps:
        low = jnp.concatenate(pair(low, step), axis=0)
    lows = swaps(low, "gx", span_x)
    top, *pulls = run(
        functools.partial(mix_kernel, factor_z, span_x),
        [like((2, cells, wide), f32)] + [block] * span_x,
        lows + (mix, wv, wo, wq, wk, cols, cots),
        flops=cube,
        scratch=[parts],
    )
    total = sum(swaps(pulls, "gx", span_x))
    for step in steps[:-1]:
        total = sum(pair(total, step))
    layer_output = run(
        output_kernel, [like(field.shape, bf16)], (top, wo, both, cols), flops=cube
    )
    plane = run(
        functools.partial(gram_kernel, cells, lengths, factor_z),
        [like((cells, WIDTH), f32)],
        lows + (feat, full, same, qk_weight),
        flops=2 * cube,
    )
    mine = run(
        functools.partial(pull_kernel, grid_x * grid_y),
        [block],
        pair(total, steps[-1]) + (feat_z,),
    )
    base = run(base_kernel, [like((rows, depth), f32)], (top, wv, both, cots, plane), flops=cube)
    field_grad = run(
        final_kernel,
        [like(field.shape, bf16)],
        swaps(mine, "gx", span_x) + (base,),
        scratch=[parts],
    )
    return (layer_output, field_grad)


def solution(mesh):
    placed = P(None, ("groups", "gx"), "gy", None)
    count = mesh.shape["gx"] * mesh.shape["gy"]

    def program(*arrays):
        _, grid_x, grid_y, depth = arrays[0].shape
        places = grid_x // mesh.shape["groups"] * grid_y
        small = places == LANES and places == 8 * count
        small = small and depth == LANES * mesh.shape["gx"] and count & (count - 1) == 0
        small = small and mesh.shape["gy"] > 1
        return jax.shard_map(
            per_device_kernels if small else per_device,
            mesh=mesh,
            in_specs=(placed, placed, P(), P(), P()),
            out_specs=(placed, placed),
            check_vma=False,
        )(*arrays)

    return program
```

```python
import functools
import math

import jax
import jax.numpy as jnp
import numpy as np
from jax import lax
from jax.experimental import pallas as pl
from jax.experimental.pallas import tpu as pltpu
from jax.sharding import PartitionSpec as P

WIDTH = 64
HEADS = 8
HEAD_DIM = 8
LANES = 128

EPSILON = 1e-06
PRECISE = lax.Precision.HIGHEST
AXES = ("gx", "gy")


def exchange(parts):
    return lax.all_to_all(parts, AXES, split_axis=0, concat_axis=0, tiled=True)


def swap(part, axis, size, step):
    return lax.ppermute(part, axis, [(i, i ^ step) for i in range(size)])


def gather(part, count):
    return exchange(jnp.broadcast_to(part[None], (count,) + part.shape))


def reduce_blocks(total, count):
    width, depth = total.shape
    blocks = total.reshape(width, depth // LANES, LANES).transpose(1, 0, 2)
    blocks = blocks.reshape(count, width * depth // LANES // count, LANES)
    mine = jnp.sum(exchange(blocks), axis=0)
    whole = gather(mine, count).reshape(depth // LANES, width, LANES)
    return whole.transpose(1, 0, 2).reshape(width, depth)


def axis_features(pooled, weights):
    inverse = lax.rsqrt(jnp.mean(pooled * pooled, axis=0, keepdims=True) + EPSILON)
    normed = pooled * inverse
    length = pooled.shape[1]
    factor = 1.0 / math.sqrt(HEAD_DIM * length)
    queries = jnp.dot(weights[0].T, normed, precision=PRECISE).reshape(HEADS, HEAD_DIM, length)
    keyset = jnp.dot(weights[1].T, normed, precision=PRECISE).reshape(HEADS, HEAD_DIM, length)
    return (normed, inverse, queries, keyset, factor)


def axis_kernel(queries, keyset, factor):
    scores = jnp.einsum("hdm,hdn->hmn", queries, keyset, precision=PRECISE)
    return (scores * factor).astype(jnp.bfloat16)


def kernel_backward(gram, queries, keyset, factor):
    grad_query = factor * jnp.einsum("hmn,hdn->hdm", gram, keyset, precision=PRECISE)
    grad_keyset = factor * jnp.einsum("hmn,hdm->hdn", gram, queries, precision=PRECISE)
    return (grad_query, grad_keyset)


def grad_of_normed(weights, grad_query, grad_keyset):
    length = grad_query.shape[-1]
    grad_normed = jnp.dot(weights[0], grad_query.reshape(WIDTH, length), precision=PRECISE)
    return grad_normed + jnp.dot(
        weights[1], grad_keyset.reshape(WIDTH, length), precision=PRECISE
    )


def pooled_grad(normed, inverse, grad_normed):
    return inverse * (grad_normed - normed * jnp.mean(grad_normed * normed, axis=0, keepdims=True))


def f32_einsum(pattern, left, right):
    return jnp.einsum(pattern, left, right, preferred_element_type=jnp.float32)


def per_device(field, cotangent, qk_weight, w_value, w_out):
    span_x = lax.axis_size("gx")
    span_y = lax.axis_size("gy")
    count = span_x * span_y
    rows_x, rows_y, depth = field.shape[1:]
    cells = rows_x * rows_y
    grid_x = rows_x * span_x
    grid_y = rows_y * span_y
    start_x = lax.axis_index("gx") * rows_x
    start_y = lax.axis_index("gy") * rows_y
    bf16 = jnp.bfloat16

    cols = field.reshape(WIDTH, cells, depth)
    cots = cotangent.reshape(WIDTH, cells, depth)

    sum_z = jnp.sum(cols, axis=1, dtype=jnp.float32)
    sum_rows = jnp.sum(cols, axis=2, dtype=jnp.float32)
    rows_all = gather(sum_rows.T, count).reshape(span_x, span_y, rows_x, rows_y, WIDTH)
    total_x = jnp.sum(rows_all, axis=(1, 3)).reshape(grid_x, WIDTH).T
    total_y = jnp.sum(rows_all, axis=(0, 2)).reshape(grid_y, WIDTH).T
    total_z = reduce_blocks(sum_z, count)

    normed_x, inverse_x, query_x, keyset_x, factor_x = axis_features(
        total_x / (grid_y * depth), qk_weight[0]
    )
    normed_y, inverse_y, query_y, keyset_y, factor_y = axis_features(
        total_y / (grid_x * depth), qk_weight[1]
    )
    normed_z, inverse_z, query_z, keyset_z, factor_z = axis_features(
        total_z / (grid_x * grid_y), qk_weight[2]
    )
    kernel_x = axis_kernel(query_x, keyset_x, factor_x)
    kernel_y = axis_kernel(query_y, keyset_y, factor_y)
    query_b = query_z.astype(bf16)
    keyset_b = keyset_z.astype(bf16)

    wv = w_value.reshape(WIDTH, HEADS, HEAD_DIM)
    wo = w_out.reshape(HEADS, HEAD_DIM, WIDTH)
    coef_f = f32_einsum("cpk,hgk->cphg", cols, keyset_b)
    coef_c = f32_einsum("cpz,hgz->cphg", cots, query_b)
    low_f = jnp.einsum("chd,cphg->phdg", wv.astype(jnp.float32), coef_f, precision=PRECISE)
    low_c = jnp.einsum("hdc,cphg->phdg", wo.astype(jnp.float32), coef_c, precision=PRECISE)
    squares = HEAD_DIM * HEAD_DIM
    both = jnp.stack([low_f, low_c]).astype(bf16).reshape(2, cells, HEADS * squares)
    both = gather(both, count).reshape(span_x, span_y, 2, rows_x, rows_y, HEADS * squares)
    both = both.transpose(2, 0, 3, 1, 4, 5).reshape(2, grid_x, grid_y, HEADS, squares)
    low_f, low_c = both[0], both[1]

    mid_f = f32_einsum("hyj,xjhq->xyhq", kernel_y, low_f).astype(bf16)
    top_f = f32_einsum("hxi,iyhq->xyhq", kernel_x, mid_f)
    mid_c = f32_einsum("hxi,xyhq->iyhq", kernel_x, low_c).astype(bf16)
    top_c = f32_einsum("hyj,xyhq->xjhq", kernel_y, mid_c)
    gram_x = factor_z * f32_einsum("myhq,nyhq->hmn", low_c, mid_f)
    gram_y = factor_z * f32_einsum("xmhq,xnhq->hmn", mid_c, low_f)

    def here(top):
        top = lax.dynamic_slice_in_dim(top, start_x, rows_x, 0)
        top = lax.dynamic_slice_in_dim(top, start_y, rows_y, 1)
        return top.reshape(cells, HEADS, HEAD_DIM, HEAD_DIM)

    left_f = factor_z * jnp.einsum(
        "hdc,phdg->cphg", wo.astype(jnp.float32), here(top_f), precision=PRECISE
    )
    left_c = factor_z * jnp.einsum(
        "chd,phdg->cphg", wv.astype(jnp.float32), here(top_c), precision=PRECISE
    )
    left_f = left_f.astype(bf16)
    left_c = left_c.astype(bf16)

    grad_query_z = f32_einsum("cphg,cpz->hgz", left_f, cots)
    grad_keyset_z = f32_einsum("cphg,cpz->hgz", left_c, cols)
    gn_z = reduce_blocks(grad_of_normed(qk_weight[2], grad_query_z, grad_keyset_z), count)

    layer_output = (cols.astype(jnp.float32) + f32_einsum("cphg,hgz->cpz", left_f, query_b)).astype(bf16)
    through = f32_einsum("cphg,hgz->cpz", left_c, keyset_b)

    gn_x = grad_of_normed(qk_weight[0], *kernel_backward(gram_x, query_x, keyset_x, factor_x))
    gn_y = grad_of_normed(qk_weight[1], *kernel_backward(gram_y, query_y, keyset_y, factor_y))
    pull_x = pooled_grad(normed_x, inverse_x, gn_x)
    pull_y = pooled_grad(normed_y, inverse_y, gn_y)
    pull_z = pooled_grad(normed_z, inverse_z, gn_z)
    local_x = lax.dynamic_slice_in_dim(pull_x, start_x, rows_x, 1) / (grid_y * depth)
    local_y = lax.dynamic_slice_in_dim(pull_y, start_y, rows_y, 1) / (grid_x * depth)
    local_xy = (local_x[:, :, None] + local_y[:, None, :]).reshape(WIDTH, cells)
    local_z = pull_z / (grid_x * grid_y)
    field_grad = (
        cots.astype(jnp.float32) + through + local_xy[:, :, None] + local_z[:, None, :]
    ).astype(bf16)
    return (layer_output.reshape(field.shape), field_grad.reshape(field.shape))


def split(x):
    high = x.astype(jnp.bfloat16)
    return high, (x - high.astype(jnp.float32)).astype(jnp.bfloat16)


NN = (((1,), (0,)), ((), ()))
NT = (((1,), (1,)), ((), ()))
TN = (((0,), (0,)), ((), ()))


def mul(left, right, dims=NN):
    return lax.dot_general(left, right, dims, preferred_element_type=jnp.float32)


def mul_near(left, right, dims=NN):
    left_high, left_low = split(left)
    right_high, right_low = split(right)
    return (
        mul(left_high, right_high, dims)
        + mul(left_low, right_high, dims)
        + mul(left_high, right_low, dims)
    )


def mul_left(left, right, dims=NN):
    rows = left.shape[0]
    both = mul(jnp.concatenate(split(left), axis=0), right, dims)
    return both[:rows] + both[rows:]


def number(shape, dim):
    return lax.broadcasted_iota(jnp.int32, shape, dim)


def join_quarters(part_ref, quarters):
    for step, quarter in enumerate(quarters):
        part_ref[lax.axis_index("gx") ^ step] = quarter[...]
    return jnp.concatenate([part_ref[index] for index in range(part_ref.shape[0])], axis=1)


def expand(part):
    depth = part.shape[1]
    part = part.reshape(HEADS, 1, HEAD_DIM, depth)
    part = jnp.broadcast_to(part, (HEADS, HEAD_DIM, HEAD_DIM, depth))
    return part.reshape(WIDTH * HEAD_DIM, depth).astype(jnp.bfloat16)


def spread(weights, top):
    left = weights[:, None, :] * top[None]
    return left.reshape(-1, left.shape[2]).astype(jnp.bfloat16)


def prepare_kernel(wv_ref, wo_ref, qk_ref, wv_out, wo_out, wq_out, wk_out, wz_out):
    wide = HEADS * HEAD_DIM * HEAD_DIM
    row = number((WIDTH, wide), 0)
    lane = number((WIDTH, wide), 1)
    by_channel = ((lane >> 3) == row).astype(jnp.bfloat16)
    by_factor = (((lane >> 6) * HEAD_DIM + (lane & 7)) == row).astype(jnp.bfloat16)
    wv_out[...] = mul(wv_ref[...], by_channel)
    wo_out[...] = mul(wo_ref[...], by_channel, TN)
    for index, out in ((0, wq_out), (1, wk_out)):
        high, low = split(qk_ref[2, index])
        out[0:WIDTH, :] = mul(high, by_factor).astype(jnp.bfloat16)
        out[WIDTH : 2 * WIDTH, :] = mul(low, by_factor).astype(jnp.bfloat16)
        wz_out[index * WIDTH : (index + 1) * WIDTH, :] = qk_ref[2, index].T


def sums_kernel(field_ref, *refs):
    outs, (part_ref, data_ref, semaphores) = refs[:-3], refs[-3:]
    _, rows_x, rows_y, depth = data_ref.shape
    chunks = semaphores.shape[0]
    size = WIDTH // chunks
    copies = [
        pltpu.make_async_copy(
            field_ref.at[pl.ds(index * size, size)],
            data_ref.at[pl.ds(index * size, size)],
            semaphores.at[index],
        )
        for index in range(chunks)
    ]
    for copy in copies:
        copy.start()
    own = jnp.zeros((rows_x, rows_y, LANES), jnp.float32)
    for index, copy in enumerate(copies):
        copy.wait()
        rows = slice(index * size, (index + 1) * size)
        data = data_ref[rows].astype(jnp.float32)
        part = jnp.sum(jnp.sum(data, axis=1), axis=1)
        for quarter in range(part_ref.shape[0]):
            part_ref[quarter, rows, :] = part[:, quarter * LANES : (quarter + 1) * LANES]
        lanes = data[..., :LANES]
        for start in range(LANES, depth, LANES):
            lanes = lanes + data[..., start : start + LANES]
        row_sums = jnp.sum(lanes, axis=3, keepdims=True)
        shape = lanes.shape
        mine = number(shape, 0) + index * size == number(shape, 3)
        own = own + jnp.sum(jnp.where(mine, row_sums, 0.0), axis=0)
    for step, out in enumerate(outs):
        out[0:WIDTH, :] = part_ref[lax.axis_index("gx") ^ step]
        for index in range(rows_x):
            start = WIDTH + index * rows_y
            out[start : start + rows_y, :] = own[index]


def add_kernel(*refs):
    parts, out_ref = refs[:-1], refs[-1]
    total = parts[0][0:WIDTH, :]
    for part in parts[1:]:
        total = total + part[0:WIDTH, :]
    out_ref[0:WIDTH, :] = total
    cells = parts[0].shape[0] - WIDTH
    for step, part in enumerate(parts):
        start = WIDTH + step * cells
        out_ref[start : start + cells, :] = part[WIDTH:, :]


def factor_kernel(places, *refs):
    parts, feat_ref = refs[:-1], refs[-1]
    total = parts[0][0:WIDTH, :]
    for part in parts[1:]:
        total = total + part[0:WIDTH, :]
    pooled = total * (1.0 / places)
    inverse = lax.rsqrt(jnp.mean(pooled * pooled, axis=0, keepdims=True) + EPSILON)
    normed = pooled * inverse
    feat_ref[0:WIDTH, :] = normed
    feat_ref[WIDTH:, :] = jnp.broadcast_to(inverse, (HEAD_DIM, LANES))


def add_pull_kernel(*refs):
    total = refs[0][...].astype(jnp.float32)
    for part in refs[1:-1]:
        total = total + part[...].astype(jnp.float32)
    refs[-1][...] = total.astype(jnp.bfloat16)


def by_head(part):
    shape = (HEADS, part.shape[0], WIDTH)
    mine = number(shape, 0) == (number(shape, 2) >> 3)
    return jnp.where(mine, part[None], 0.0).reshape(-1, WIDTH)


def plane_kernel(cells, span_x, lengths, *refs):
    parts, (same_ref, qk_ref, mix_ref, feat_ref, full_ref) = refs[:-5], refs[-5:]
    totals = jnp.concatenate(
        [
            part[WIDTH + step * cells : WIDTH + (step + 1) * cells, :]
            for first in range(span_x)
            for part in parts
            for step in range(first, (parts[0].shape[0] - WIDTH) // cells, span_x)
        ],
        axis=0,
    )[:, :WIDTH]
    places = totals.shape[0]
    high, low = split(totals)
    forward = backward = None
    for axis in range(2):
        same = same_ref[axis]
        pooled = (mul(same, high) + mul(same, low)) * (1.0 / lengths[axis][1])
        inverse = lax.rsqrt(jnp.mean(pooled * pooled, axis=1, keepdims=True) + EPSILON)
        normed = pooled * inverse
        query = mul_near(normed, qk_ref[axis, 0])
        keyset = mul_near(normed, qk_ref[axis, 1])
        feat_ref[4 * axis] = normed
        feat_ref[4 * axis + 1] = query
        feat_ref[4 * axis + 2] = keyset
        feat_ref[4 * axis + 3] = jnp.broadcast_to(inverse, (places, WIDTH))
        factor = 1.0 / math.sqrt(HEAD_DIM * lengths[axis][0])

        def scores(rows, other):
            found = mul_near(by_head(rows), other, NT) * factor
            return found.astype(jnp.bfloat16).astype(jnp.float32)

        full = scores(query, keyset)
        full_ref[axis] = full
        one = full.reshape(HEADS, places, places)[:, :cells].reshape(-1, places)
        two = scores(keyset[:cells], query)
        forward = one if forward is None else forward * one
        backward = two if backward is None else backward * two
    mix_ref[0] = forward
    mix_ref[1] = backward


def coef_kernel(spans, *refs):
    quarters, refs = refs[:spans], refs[spans:]
    wz_ref, field_ref, cot_ref, wv_ref, wo_ref, send_ref, both_ref, feat_ref, part_ref = refs
    rows, depth = field_ref.shape
    cells = rows // WIDTH
    wide = HEADS * HEAD_DIM * HEAD_DIM
    feat = join_quarters(part_ref, quarters)
    feat_ref[...] = feat
    high, low = split(feat[:WIDTH])
    both = mul_left(wz_ref[...], high) + mul(wz_ref[...].astype(jnp.bfloat16), low)
    both_ref[...] = both.astype(jnp.bfloat16)
    query = expand(both[:WIDTH])
    keyset = expand(both[WIDTH:])
    low_f = mul(field_ref[...], keyset, NT).reshape(WIDTH, cells, wide)
    low_f = jnp.sum(wv_ref[...][:, None, :] * low_f, axis=0)
    low_c = mul(cot_ref[...], query, NT).reshape(WIDTH, cells, wide)
    low_c = jnp.sum(wo_ref[...][:, None, :] * low_c, axis=0)
    low = jnp.concatenate([low_f, low_c], axis=0).astype(jnp.bfloat16)
    send_ref[...] = low


def join_low(refs, cells):
    low = jnp.concatenate([ref[...].astype(jnp.float32) for ref in refs], axis=0)
    wide = low.shape[1]
    low = low.reshape(-1, 2 * cells, wide)
    return [
        low[:, start : start + cells].reshape(-1, wide).astype(jnp.bfloat16)
        for start in (0, cells)
    ]


def mix_kernel(factor, spans, *refs):
    lows, refs = refs[:spans], refs[spans:]
    mix_ref, wv_ref, wo_ref, wq_ref, wk_ref, field_ref, cot_ref, top_ref, out_ref = refs
    cells = field_ref.shape[0] // WIDTH
    low_f, low_c = join_low(lows, cells)
    wide = low_f.shape[1]
    shape = (HEADS, cells, wide)
    head = number(shape, 0) == (number(shape, 2) >> 6)

    def top(mix, low):
        found = mul_left(mix, low).reshape(shape)
        return jnp.sum(jnp.where(head, found, 0.0), axis=0) * factor

    top_f = top(mix_ref[0], low_f)
    top_c = top(mix_ref[1], low_c)
    top_ref[0] = top_f
    top_ref[1] = top_c
    left_f = spread(wo_ref[...], top_f)
    left_c = spread(wv_ref[...], top_c)

    def pull(weights, left, right):
        found = mul(weights, left, NT)
        return mul_left(found[:WIDTH] + found[WIDTH:], right)

    found = pull(wq_ref[...], left_f, cot_ref[...]) + pull(wk_ref[...], left_c, field_ref[...])
    out_ref[...] = found.astype(jnp.bfloat16)


def put_cells(ref, total):
    _, rows_x, rows_y, depth = ref.shape
    total = total.reshape(WIDTH, rows_x * rows_y, depth)
    for index in range(rows_x):
        rows = total[:, index * rows_y : (index + 1) * rows_y, :]
        ref[:, index, :, :] = rows.astype(jnp.bfloat16)


def output_kernel(top_ref, wo_ref, both_ref, field_ref, out_ref):
    query = expand(both_ref[...].astype(jnp.float32)[:WIDTH])
    left = spread(wo_ref[...], top_ref[0])
    put_cells(out_ref, mul(left, query) + field_ref[...].astype(jnp.float32))


def gram_kernel(cells, lengths, factor_z, *refs):
    lows, (feat_ref, full_ref, same_ref, qk_ref, out_ref) = refs[:-5], refs[-5:]
    low_f, low_c = join_low(lows, cells)
    places, wide = low_f.shape
    squares = HEAD_DIM * HEAD_DIM
    lane = number((places, LANES), 1)
    products = []
    for pair in range(wide // LANES):
        part_f = low_f[:, pair * LANES : (pair + 1) * LANES]
        part_c = low_c[:, pair * LANES : (pair + 1) * LANES]
        for half in range(LANES // squares):
            mine = (lane >> 6) == half
            products.append(mul(jnp.where(mine, part_c, jnp.zeros_like(part_c)), part_f, NT))
    product = jnp.concatenate(products, axis=0)
    factors = [1.0 / math.sqrt(HEAD_DIM * lengths[axis][0]) for axis in range(2)]
    queries = [by_head(feat_ref[4 * axis + 1]).astype(jnp.bfloat16) for axis in range(2)]
    keysets = [by_head(feat_ref[4 * axis + 2]).astype(jnp.bfloat16) for axis in range(2)]
    total = jnp.zeros((cells, WIDTH), jnp.float32)
    for axis in range(2):
        gram = (product * full_ref[1 - axis]).astype(jnp.bfloat16)
        across = jnp.concatenate(
            [gram[h * places : (h + 1) * places] for h in range(HEADS)], axis=1
        )
        scale = factors[axis] * factor_z
        grad_query = mul(across, keysets[axis]) * scale
        grad_keyset = mul(gram, queries[axis], TN) * scale
        found = mul_near(grad_query, qk_ref[axis, 0], NT) + mul_near(grad_keyset, qk_ref[axis, 1], NT)
        high, low = split(found)
        own = same_ref[axis, 0 : 2 * cells, :]
        found = (mul(own, high) + mul(own, low))[:cells]
        normed = feat_ref[4 * axis, 0:cells, :]
        inverse = feat_ref[4 * axis + 3, 0:cells, :]
        found = found - normed * jnp.mean(found * normed, axis=1, keepdims=True)
        total = total + inverse * found * (1.0 / lengths[axis][1])
    out_ref[...] = total


def base_kernel(top_ref, wv_ref, both_ref, cot_ref, plane_ref, out_ref):
    rows = cot_ref.shape[0]
    cells = rows // WIDTH
    shape = (WIDTH, cells, WIDTH)
    own = jnp.where(number(shape, 0) == number(shape, 2), plane_ref[...][None], 0.0)
    plane = mul_left(own.reshape(rows, WIDTH), jnp.ones((WIDTH, LANES), jnp.bfloat16))
    keyset = expand(both_ref[...].astype(jnp.float32)[WIDTH:])
    left = spread(wv_ref[...], top_ref[1])
    found = mul(left, keyset) + cot_ref[...].astype(jnp.float32)
    columns = found.shape[1] // LANES
    out_ref[...] = found + jnp.concatenate([plane] * columns, axis=1)


def final_kernel(places, *refs):
    parts, (feat_ref, base_ref, out_ref, data_ref, semaphores) = refs[:-5], refs[-5:]
    depth = base_ref.shape[1]
    _, rows_x, rows_y, _ = data_ref.shape
    found = parts[0][...].astype(jnp.float32)
    for part in parts[1:]:
        found = found + part[...].astype(jnp.float32)
    normed = feat_ref[0:WIDTH, :]
    inverse = feat_ref[WIDTH : WIDTH + 1, :]
    found = inverse * (found - normed * jnp.mean(found * normed, axis=0, keepdims=True))
    found = found * (1.0 / places)
    cells = rows_x * rows_y
    chunks = semaphores.shape[0]
    size = WIDTH // chunks
    copies = []
    for index in range(chunks):
        rows = slice(index * size, (index + 1) * size)
        base = base_ref[index * size * cells : (index + 1) * size * cells, :]
        total = base.reshape(size, cells, depth) + found[rows][:, None, :]
        for at_x in range(rows_x):
            part = total[:, at_x * rows_y : (at_x + 1) * rows_y, :]
            data_ref[rows, at_x, :, :] = part.astype(jnp.bfloat16)
        copy = pltpu.make_async_copy(
            data_ref.at[pl.ds(index * size, size)],
            out_ref.at[pl.ds(index * size, size)],
            semaphores.at[index],
        )
        copy.start()
        copies.append(copy)
    for copy in copies:
        copy.wait()


def run(kernel, outs, operands, places=pltpu.VMEM, target=pltpu.VMEM, flops=0, scratch=()):
    moved = sum(x.size * x.dtype.itemsize for x in tuple(operands) + tuple(outs))
    found = pl.pallas_call(
        kernel,
        out_shape=tuple(outs),
        in_specs=[pl.BlockSpec(memory_space=places)] * len(operands),
        out_specs=tuple(pl.BlockSpec(memory_space=target) for _ in outs),
        scratch_shapes=list(scratch),
        compiler_params=pltpu.CompilerParams(vmem_limit_bytes=16 * 1024 * 1024),
        cost_estimate=pl.CostEstimate(flops=flops, bytes_accessed=moved, transcendentals=0),
    )(*operands)
    return found[0] if len(outs) == 1 else found


def per_device_kernels(field, cotangent, qk_weight, w_value, w_out):
    span_x = lax.axis_size("gx")
    span_y = lax.axis_size("gy")
    count = span_x * span_y
    rows_x, rows_y, depth = field.shape[1:]
    cells = rows_x * rows_y
    places = count * cells
    grid_x = rows_x * span_x
    grid_y = rows_y * span_y
    rows = WIDTH * cells
    wide = WIDTH * HEAD_DIM
    f32, bf16 = jnp.float32, jnp.bfloat16
    like = jax.ShapeDtypeStruct
    lengths = ((grid_x, grid_y * depth), (grid_y, grid_x * depth))

    cell = np.arange(places)
    at_x = cell // cells // span_y * rows_x + cell % cells // rows_y
    at_y = cell // cells % span_y * rows_y + cell % rows_y
    same = jnp.asarray(
        np.stack([at_x[:, None] == at_x[None], at_y[:, None] == at_y[None]]), dtype=bf16
    )

    cols = field.reshape(rows, depth)
    cots = cotangent.reshape(rows, depth)
    parts = pltpu.VMEM((span_x, WIDTH, LANES), f32)
    chunked = [pltpu.VMEM(field.shape, bf16), pltpu.SemaphoreType.DMA((4,))]
    factor_z = 1.0 / math.sqrt(HEAD_DIM * depth)
    cube = rows * wide * depth * 2

    def swaps(sent, axis, size):
        if not isinstance(sent, (tuple, list)):
            sent = [sent] * size
        return tuple(sent[:1]) + tuple(
            swap(sent[step], axis, size, step) for step in range(1, size)
        )

    sums = run(
        sums_kernel, [like((WIDTH + cells, LANES), f32)] * span_x, (field,), places=pltpu.HBM,
        flops=cube // 4,
        scratch=[parts] + chunked,
    )
    wv, wo, wq, wk, wz = run(
        prepare_kernel,
        [like((WIDTH, wide), f32)] * 2 + [like((2 * WIDTH, wide), bf16)] * 2
        + [like((2 * WIDTH, WIDTH), f32)],
        (w_value, w_out, qk_weight),
        flops=cube // 8,
    )
    def add(sent, size):
        return run(add_kernel, [like((WIDTH + size * cells, LANES), f32)], sent)

    totals = swaps(add(swaps(sums, "gx", span_x), span_x), "gy", span_y)
    mine = run(
        functools.partial(factor_kernel, grid_x * grid_y),
        [like((WIDTH + HEAD_DIM, LANES), f32)],
        totals,
    )
    mix, feat, full = run(
        functools.partial(plane_kernel, cells, span_x, lengths),
        [like((2, HEADS * cells, places), f32), like((8, places, WIDTH), f32),
         like((2, HEADS * places, places), f32)],
        totals + (same, qk_weight),
        flops=cube // 2,
    )
    send, both, feat_z = run(
        functools.partial(coef_kernel, span_x),
        [like((2 * cells, wide), bf16), like((2 * WIDTH, depth), bf16),
         like((WIDTH + HEAD_DIM, depth), f32)],
        swaps(mine, "gx", span_x) + (wz, cols, cots, wv, wo),
        flops=2 * cube,
        scratch=[pltpu.VMEM((span_x, WIDTH + HEAD_DIM, LANES), f32)],
    )
    low = jnp.concatenate(swaps(send, "gy", span_y), axis=0)
    lows = swaps(low, "gx", span_x)
    pulled = like((WIDTH, depth), bf16)
    top, total = run(
        functools.partial(mix_kernel, factor_z, span_x),
        [like((2, cells, wide), f32), pulled],
        lows + (mix, wv, wo, wq, wk, cols, cots),
        flops=cube,
    )
    total = run(add_pull_kernel, [pulled], swaps(total, "gx", span_x))
    layer_output = run(
        output_kernel, [like(field.shape, bf16)], (top, wo, both, cols), flops=cube
    )
    plane = run(
        functools.partial(gram_kernel, cells, lengths, factor_z),
        [like((cells, WIDTH), f32)],
        lows + (feat, full, same, qk_weight),
        flops=2 * cube,
    )
    base = run(base_kernel, [like((rows, depth), f32)], (top, wv, both, cots, plane), flops=cube)
    field_grad = run(
        functools.partial(final_kernel, grid_x * grid_y),
        [like(field.shape, bf16)],
        swaps(total, "gy", span_y) + (feat_z, base),
        target=pltpu.HBM,
        scratch=chunked,
    )
    return (layer_output, field_grad)


def solution(mesh):
    placed = P(None, ("groups", "gx"), "gy", None)
    count = mesh.shape["gx"] * mesh.shape["gy"]

    def program(*arrays):
        _, grid_x, grid_y, depth = arrays[0].shape
        places = grid_x // mesh.shape["groups"] * grid_y
        small = places == LANES and places == 8 * count
        small = small and depth == LANES * mesh.shape["gx"] and count & (count - 1) == 0
        return jax.shard_map(
            per_device_kernels if small else per_device,
            mesh=mesh,
            in_specs=(placed, placed, P(), P(), P()),
            out_specs=(placed, placed),
            check_vma=False,
        )(*arrays)

    return program
```

```python
import functools
import math

import jax
import jax.numpy as jnp
import numpy as np
from jax import lax
from jax.experimental import pallas as pl
from jax.experimental.pallas import tpu as pltpu
from jax.sharding import PartitionSpec as P

WIDTH = 64
HEADS = 8
HEAD_DIM = 8
LANES = 128

EPSILON = 1e-06
PRECISE = lax.Precision.HIGHEST
AXES = ("gx", "gy")


def exchange(parts):
    return lax.all_to_all(parts, AXES, split_axis=0, concat_axis=0, tiled=True)


def swap(part, axis, size, step):
    return lax.ppermute(part, axis, [(i, i ^ step) for i in range(size)])


def gather(part, count):
    return exchange(jnp.broadcast_to(part[None], (count,) + part.shape))


def reduce_blocks(total, count):
    width, depth = total.shape
    blocks = total.reshape(width, depth // LANES, LANES).transpose(1, 0, 2)
    blocks = blocks.reshape(count, width * depth // LANES // count, LANES)
    mine = jnp.sum(exchange(blocks), axis=0)
    whole = gather(mine, count).reshape(depth // LANES, width, LANES)
    return whole.transpose(1, 0, 2).reshape(width, depth)


def axis_features(pooled, weights):
    inverse = lax.rsqrt(jnp.mean(pooled * pooled, axis=0, keepdims=True) + EPSILON)
    normed = pooled * inverse
    length = pooled.shape[1]
    factor = 1.0 / math.sqrt(HEAD_DIM * length)
    queries = jnp.dot(weights[0].T, normed, precision=PRECISE).reshape(HEADS, HEAD_DIM, length)
    keyset = jnp.dot(weights[1].T, normed, precision=PRECISE).reshape(HEADS, HEAD_DIM, length)
    return (normed, inverse, queries, keyset, factor)


def axis_kernel(queries, keyset, factor):
    scores = jnp.einsum("hdm,hdn->hmn", queries, keyset, precision=PRECISE)
    return (scores * factor).astype(jnp.bfloat16)


def kernel_backward(gram, queries, keyset, factor):
    grad_query = factor * jnp.einsum("hmn,hdn->hdm", gram, keyset, precision=PRECISE)
    grad_keyset = factor * jnp.einsum("hmn,hdm->hdn", gram, queries, precision=PRECISE)
    return (grad_query, grad_keyset)


def grad_of_normed(weights, grad_query, grad_keyset):
    length = grad_query.shape[-1]
    grad_normed = jnp.dot(weights[0], grad_query.reshape(WIDTH, length), precision=PRECISE)
    return grad_normed + jnp.dot(
        weights[1], grad_keyset.reshape(WIDTH, length), precision=PRECISE
    )


def pooled_grad(normed, inverse, grad_normed):
    return inverse * (grad_normed - normed * jnp.mean(grad_normed * normed, axis=0, keepdims=True))


def f32_einsum(pattern, left, right):
    return jnp.einsum(pattern, left, right, preferred_element_type=jnp.float32)


def per_device(field, cotangent, qk_weight, w_value, w_out):
    span_x = lax.axis_size("gx")
    span_y = lax.axis_size("gy")
    count = span_x * span_y
    rows_x, rows_y, depth = field.shape[1:]
    cells = rows_x * rows_y
    grid_x = rows_x * span_x
    grid_y = rows_y * span_y
    start_x = lax.axis_index("gx") * rows_x
    start_y = lax.axis_index("gy") * rows_y
    bf16 = jnp.bfloat16

    cols = field.reshape(WIDTH, cells, depth)
    cots = cotangent.reshape(WIDTH, cells, depth)

    sum_z = jnp.sum(cols, axis=1, dtype=jnp.float32)
    sum_rows = jnp.sum(cols, axis=2, dtype=jnp.float32)
    rows_all = gather(sum_rows.T, count).reshape(span_x, span_y, rows_x, rows_y, WIDTH)
    total_x = jnp.sum(rows_all, axis=(1, 3)).reshape(grid_x, WIDTH).T
    total_y = jnp.sum(rows_all, axis=(0, 2)).reshape(grid_y, WIDTH).T
    total_z = reduce_blocks(sum_z, count)

    normed_x, inverse_x, query_x, keyset_x, factor_x = axis_features(
        total_x / (grid_y * depth), qk_weight[0]
    )
    normed_y, inverse_y, query_y, keyset_y, factor_y = axis_features(
        total_y / (grid_x * depth), qk_weight[1]
    )
    normed_z, inverse_z, query_z, keyset_z, factor_z = axis_features(
        total_z / (grid_x * grid_y), qk_weight[2]
    )
    kernel_x = axis_kernel(query_x, keyset_x, factor_x)
    kernel_y = axis_kernel(query_y, keyset_y, factor_y)
    query_b = query_z.astype(bf16)
    keyset_b = keyset_z.astype(bf16)

    wv = w_value.reshape(WIDTH, HEADS, HEAD_DIM)
    wo = w_out.reshape(HEADS, HEAD_DIM, WIDTH)
    coef_f = f32_einsum("cpk,hgk->cphg", cols, keyset_b)
    coef_c = f32_einsum("cpz,hgz->cphg", cots, query_b)
    low_f = jnp.einsum("chd,cphg->phdg", wv.astype(jnp.float32), coef_f, precision=PRECISE)
    low_c = jnp.einsum("hdc,cphg->phdg", wo.astype(jnp.float32), coef_c, precision=PRECISE)
    squares = HEAD_DIM * HEAD_DIM
    both = jnp.stack([low_f, low_c]).astype(bf16).reshape(2, cells, HEADS * squares)
    both = gather(both, count).reshape(span_x, span_y, 2, rows_x, rows_y, HEADS * squares)
    both = both.transpose(2, 0, 3, 1, 4, 5).reshape(2, grid_x, grid_y, HEADS, squares)
    low_f, low_c = both[0], both[1]

    mid_f = f32_einsum("hyj,xjhq->xyhq", kernel_y, low_f).astype(bf16)
    top_f = f32_einsum("hxi,iyhq->xyhq", kernel_x, mid_f)
    mid_c = f32_einsum("hxi,xyhq->iyhq", kernel_x, low_c).astype(bf16)
    top_c = f32_einsum("hyj,xyhq->xjhq", kernel_y, mid_c)
    gram_x = factor_z * f32_einsum("myhq,nyhq->hmn", low_c, mid_f)
    gram_y = factor_z * f32_einsum("xmhq,xnhq->hmn", mid_c, low_f)

    def here(top):
        top = lax.dynamic_slice_in_dim(top, start_x, rows_x, 0)
        top = lax.dynamic_slice_in_dim(top, start_y, rows_y, 1)
        return top.reshape(cells, HEADS, HEAD_DIM, HEAD_DIM)

    left_f = factor_z * jnp.einsum(
        "hdc,phdg->cphg", wo.astype(jnp.float32), here(top_f), precision=PRECISE
    )
    left_c = factor_z * jnp.einsum(
        "chd,phdg->cphg", wv.astype(jnp.float32), here(top_c), precision=PRECISE
    )
    left_f = left_f.astype(bf16)
    left_c = left_c.astype(bf16)

    grad_query_z = f32_einsum("cphg,cpz->hgz", left_f, cots)
    grad_keyset_z = f32_einsum("cphg,cpz->hgz", left_c, cols)
    gn_z = reduce_blocks(grad_of_normed(qk_weight[2], grad_query_z, grad_keyset_z), count)

    layer_output = (cols.astype(jnp.float32) + f32_einsum("cphg,hgz->cpz", left_f, query_b)).astype(bf16)
    through = f32_einsum("cphg,hgz->cpz", left_c, keyset_b)

    gn_x = grad_of_normed(qk_weight[0], *kernel_backward(gram_x, query_x, keyset_x, factor_x))
    gn_y = grad_of_normed(qk_weight[1], *kernel_backward(gram_y, query_y, keyset_y, factor_y))
    pull_x = pooled_grad(normed_x, inverse_x, gn_x)
    pull_y = pooled_grad(normed_y, inverse_y, gn_y)
    pull_z = pooled_grad(normed_z, inverse_z, gn_z)
    local_x = lax.dynamic_slice_in_dim(pull_x, start_x, rows_x, 1) / (grid_y * depth)
    local_y = lax.dynamic_slice_in_dim(pull_y, start_y, rows_y, 1) / (grid_x * depth)
    local_xy = (local_x[:, :, None] + local_y[:, None, :]).reshape(WIDTH, cells)
    local_z = pull_z / (grid_x * grid_y)
    field_grad = (
        cots.astype(jnp.float32) + through + local_xy[:, :, None] + local_z[:, None, :]
    ).astype(bf16)
    return (layer_output.reshape(field.shape), field_grad.reshape(field.shape))


def split(x):
    high = x.astype(jnp.bfloat16)
    return high, (x - high.astype(jnp.float32)).astype(jnp.bfloat16)


NN = (((1,), (0,)), ((), ()))
NT = (((1,), (1,)), ((), ()))
TN = (((0,), (0,)), ((), ()))


def mul(left, right, dims=NN):
    return lax.dot_general(left, right, dims, preferred_element_type=jnp.float32)


def mul_near(left, right, dims=NN):
    left_high, left_low = split(left)
    right_high, right_low = split(right)
    return (
        mul(left_high, right_high, dims)
        + mul(left_low, right_high, dims)
        + mul(left_high, right_low, dims)
    )


def mul_left(left, right, dims=NN):
    rows = left.shape[0]
    both = mul(jnp.concatenate(split(left), axis=0), right, dims)
    return both[:rows] + both[rows:]


def number(shape, dim):
    return lax.broadcasted_iota(jnp.int32, shape, dim)


def join_quarters(part_ref, quarters):
    for step, quarter in enumerate(quarters):
        part_ref[lax.axis_index("gx") ^ step] = quarter[...]
    return jnp.concatenate([part_ref[index] for index in range(part_ref.shape[0])], axis=1)


def expand(part):
    depth = part.shape[1]
    part = part.reshape(HEADS, 1, HEAD_DIM, depth)
    part = jnp.broadcast_to(part, (HEADS, HEAD_DIM, HEAD_DIM, depth))
    return part.reshape(WIDTH * HEAD_DIM, depth).astype(jnp.bfloat16)


def spread(weights, top):
    left = weights[:, None, :] * top[None]
    return left.reshape(-1, left.shape[2]).astype(jnp.bfloat16)


def prepare_kernel(wv_ref, wo_ref, qk_ref, wv_out, wo_out, wq_out, wk_out, wz_out):
    wide = HEADS * HEAD_DIM * HEAD_DIM
    row = number((WIDTH, wide), 0)
    lane = number((WIDTH, wide), 1)
    by_channel = ((lane >> 3) == row).astype(jnp.bfloat16)
    by_factor = (((lane >> 6) * HEAD_DIM + (lane & 7)) == row).astype(jnp.bfloat16)
    wv_out[...] = mul(wv_ref[...], by_channel)
    wo_out[...] = mul(wo_ref[...], by_channel, TN)
    for index, out in ((0, wq_out), (1, wk_out)):
        high, low = split(qk_ref[2, index])
        out[0:WIDTH, :] = mul(high, by_factor).astype(jnp.bfloat16)
        out[WIDTH : 2 * WIDTH, :] = mul(low, by_factor).astype(jnp.bfloat16)
        wz_out[index * WIDTH : (index + 1) * WIDTH, :] = qk_ref[2, index].T


def sums_kernel(field_ref, *refs):
    outs, (part_ref, data_ref, semaphores) = refs[:-3], refs[-3:]
    _, rows_x, rows_y, depth = data_ref.shape
    chunks = semaphores.shape[0]
    size = WIDTH // chunks
    copies = [
        pltpu.make_async_copy(
            field_ref.at[pl.ds(index * size, size)],
            data_ref.at[pl.ds(index * size, size)],
            semaphores.at[index],
        )
        for index in range(chunks)
    ]
    for copy in copies:
        copy.start()
    own = jnp.zeros((rows_x, rows_y, LANES), jnp.float32)
    for index, copy in enumerate(copies):
        copy.wait()
        rows = slice(index * size, (index + 1) * size)
        data = data_ref[rows].astype(jnp.float32)
        part = jnp.sum(jnp.sum(data, axis=1), axis=1)
        for quarter in range(part_ref.shape[0]):
            part_ref[quarter, rows, :] = part[:, quarter * LANES : (quarter + 1) * LANES]
        lanes = data[..., :LANES]
        for start in range(LANES, depth, LANES):
            lanes = lanes + data[..., start : start + LANES]
        row_sums = jnp.sum(lanes, axis=3, keepdims=True)
        shape = lanes.shape
        mine = number(shape, 0) + index * size == number(shape, 3)
        own = own + jnp.sum(jnp.where(mine, row_sums, 0.0), axis=0)
    for step, out in enumerate(outs):
        out[0:WIDTH, :] = part_ref[lax.axis_index("gx") ^ step]
        for index in range(rows_x):
            start = WIDTH + index * rows_y
            out[start : start + rows_y, :] = own[index]


def add_kernel(*refs):
    parts, out_ref = refs[:-1], refs[-1]
    total = parts[0][0:WIDTH, :]
    for part in parts[1:]:
        total = total + part[0:WIDTH, :]
    out_ref[0:WIDTH, :] = total
    cells = parts[0].shape[0] - WIDTH
    for step, part in enumerate(parts):
        start = WIDTH + step * cells
        out_ref[start : start + cells, :] = part[WIDTH:, :]


def factor_kernel(places, *refs):
    parts, feat_ref = refs[:-1], refs[-1]
    total = parts[0][0:WIDTH, :]
    for part in parts[1:]:
        total = total + part[0:WIDTH, :]
    pooled = total * (1.0 / places)
    inverse = lax.rsqrt(jnp.mean(pooled * pooled, axis=0, keepdims=True) + EPSILON)
    normed = pooled * inverse
    feat_ref[0:WIDTH, :] = normed
    feat_ref[WIDTH:, :] = jnp.broadcast_to(inverse, (HEAD_DIM, LANES))


def add_pull_kernel(*refs):
    total = refs[0][...].astype(jnp.float32)
    for part in refs[1:-1]:
        total = total + part[...].astype(jnp.float32)
    refs[-1][...] = total.astype(jnp.bfloat16)


def by_head(part):
    shape = (HEADS, part.shape[0], WIDTH)
    mine = number(shape, 0) == (number(shape, 2) >> 3)
    return jnp.where(mine, part[None], 0.0).reshape(-1, WIDTH)


def plane_kernel(cells, span_x, lengths, *refs):
    parts, (same_ref, qk_ref, mix_ref, feat_ref, full_ref) = refs[:-5], refs[-5:]
    totals = jnp.concatenate(
        [
            part[WIDTH + step * cells : WIDTH + (step + 1) * cells, :]
            for first in range(span_x)
            for part in parts
            for step in range(first, (parts[0].shape[0] - WIDTH) // cells, span_x)
        ],
        axis=0,
    )[:, :WIDTH]
    places = totals.shape[0]
    high, low = split(totals)
    forward = backward = None
    for axis in range(2):
        same = same_ref[axis]
        pooled = (mul(same, high) + mul(same, low)) * (1.0 / lengths[axis][1])
        inverse = lax.rsqrt(jnp.mean(pooled * pooled, axis=1, keepdims=True) + EPSILON)
        normed = pooled * inverse
        query = mul_near(normed, qk_ref[axis, 0])
        keyset = mul_near(normed, qk_ref[axis, 1])
        feat_ref[4 * axis] = normed
        feat_ref[4 * axis + 1] = query
        feat_ref[4 * axis + 2] = keyset
        feat_ref[4 * axis + 3] = jnp.broadcast_to(inverse, (places, WIDTH))
        factor = 1.0 / math.sqrt(HEAD_DIM * lengths[axis][0])

        def scores(rows, other):
            found = mul_near(by_head(rows), other, NT) * factor
            return found.astype(jnp.bfloat16).astype(jnp.float32)

        full = scores(query, keyset)
        full_ref[axis] = full
        one = full.reshape(HEADS, places, places)[:, :cells].reshape(-1, places)
        two = scores(keyset[:cells], query)
        forward = one if forward is None else forward * one
        backward = two if backward is None else backward * two
    mix_ref[0] = forward
    mix_ref[1] = backward


def coef_kernel(spans, *refs):
    quarters, refs = refs[:spans], refs[spans:]
    wz_ref, field_ref, cot_ref, wv_ref, wo_ref, send_ref, both_ref, feat_ref, part_ref = refs
    rows, depth = field_ref.shape
    cells = rows // WIDTH
    wide = HEADS * HEAD_DIM * HEAD_DIM
    feat = join_quarters(part_ref, quarters)
    feat_ref[...] = feat
    high, low = split(feat[:WIDTH])
    both = mul_left(wz_ref[...], high) + mul(wz_ref[...].astype(jnp.bfloat16), low)
    both_ref[...] = both.astype(jnp.bfloat16)
    query = expand(both[:WIDTH])
    keyset = expand(both[WIDTH:])
    low_f = mul(field_ref[...], keyset, NT).reshape(WIDTH, cells, wide)
    low_f = jnp.sum(wv_ref[...][:, None, :] * low_f, axis=0)
    low_c = mul(cot_ref[...], query, NT).reshape(WIDTH, cells, wide)
    low_c = jnp.sum(wo_ref[...][:, None, :] * low_c, axis=0)
    low = jnp.concatenate([low_f, low_c], axis=0).astype(jnp.bfloat16)
    send_ref[...] = low


def join_low(refs, cells):
    low = jnp.concatenate([ref[...].astype(jnp.float32) for ref in refs], axis=0)
    wide = low.shape[1]
    low = low.reshape(-1, 2 * cells, wide)
    return [
        low[:, start : start + cells].reshape(-1, wide).astype(jnp.bfloat16)
        for start in (0, cells)
    ]


def mix_kernel(factor, spans, *refs):
    lows, refs = refs[:spans], refs[spans:]
    mix_ref, wv_ref, wo_ref, wq_ref, wk_ref, field_ref, cot_ref, top_ref, out_ref = refs
    cells = field_ref.shape[0] // WIDTH
    low_f, low_c = join_low(lows, cells)
    wide = low_f.shape[1]
    shape = (HEADS, cells, wide)
    head = number(shape, 0) == (number(shape, 2) >> 6)

    def top(mix, low):
        found = mul_left(mix, low).reshape(shape)
        return jnp.sum(jnp.where(head, found, 0.0), axis=0) * factor

    top_f = top(mix_ref[0], low_f)
    top_c = top(mix_ref[1], low_c)
    top_ref[0] = top_f
    top_ref[1] = top_c
    left_f = spread(wo_ref[...], top_f)
    left_c = spread(wv_ref[...], top_c)

    def pull(weights, left, right):
        found = mul(weights, left, NT)
        return mul_left(found[:WIDTH] + found[WIDTH:], right)

    found = pull(wq_ref[...], left_f, cot_ref[...]) + pull(wk_ref[...], left_c, field_ref[...])
    out_ref[...] = found.astype(jnp.bfloat16)


def put_cells(ref, total):
    _, rows_x, rows_y, depth = ref.shape
    total = total.reshape(WIDTH, rows_x * rows_y, depth)
    for index in range(rows_x):
        rows = total[:, index * rows_y : (index + 1) * rows_y, :]
        ref[:, index, :, :] = rows.astype(jnp.bfloat16)


def output_kernel(top_ref, wo_ref, both_ref, field_ref, out_ref):
    query = expand(both_ref[...].astype(jnp.float32)[:WIDTH])
    left = spread(wo_ref[...], top_ref[0])
    put_cells(out_ref, mul(left, query) + field_ref[...].astype(jnp.float32))


def gram_kernel(cells, lengths, factor_z, *refs):
    lows, (feat_ref, full_ref, same_ref, qk_ref, out_ref) = refs[:-5], refs[-5:]
    low_f, low_c = join_low(lows, cells)
    places, wide = low_f.shape
    squares = HEAD_DIM * HEAD_DIM
    lane = number((places, LANES), 1)
    products = []
    for pair in range(wide // LANES):
        part_f = low_f[:, pair * LANES : (pair + 1) * LANES]
        part_c = low_c[:, pair * LANES : (pair + 1) * LANES]
        for half in range(LANES // squares):
            mine = (lane >> 6) == half
            products.append(mul(jnp.where(mine, part_c, jnp.zeros_like(part_c)), part_f, NT))
    product = jnp.concatenate(products, axis=0)
    factors = [1.0 / math.sqrt(HEAD_DIM * lengths[axis][0]) for axis in range(2)]
    queries = [by_head(feat_ref[4 * axis + 1]).astype(jnp.bfloat16) for axis in range(2)]
    keysets = [by_head(feat_ref[4 * axis + 2]).astype(jnp.bfloat16) for axis in range(2)]
    total = jnp.zeros((cells, WIDTH), jnp.float32)
    for axis in range(2):
        gram = (product * full_ref[1 - axis]).astype(jnp.bfloat16)
        across = jnp.concatenate(
            [gram[h * places : (h + 1) * places] for h in range(HEADS)], axis=1
        )
        scale = factors[axis] * factor_z
        grad_query = mul(across, keysets[axis]) * scale
        grad_keyset = mul(gram, queries[axis], TN) * scale
        found = mul_near(grad_query, qk_ref[axis, 0], NT) + mul_near(grad_keyset, qk_ref[axis, 1], NT)
        high, low = split(found)
        own = same_ref[axis, 0 : 2 * cells, :]
        found = (mul(own, high) + mul(own, low))[:cells]
        normed = feat_ref[4 * axis, 0:cells, :]
        inverse = feat_ref[4 * axis + 3, 0:cells, :]
        found = found - normed * jnp.mean(found * normed, axis=1, keepdims=True)
        total = total + inverse * found * (1.0 / lengths[axis][1])
    out_ref[...] = total


def base_kernel(top_ref, wv_ref, both_ref, cot_ref, plane_ref, out_ref):
    rows = cot_ref.shape[0]
    cells = rows // WIDTH
    shape = (WIDTH, cells, WIDTH)
    own = jnp.where(number(shape, 0) == number(shape, 2), plane_ref[...][None], 0.0)
    plane = mul_left(own.reshape(rows, WIDTH), jnp.ones((WIDTH, LANES), jnp.bfloat16))
    keyset = expand(both_ref[...].astype(jnp.float32)[WIDTH:])
    left = spread(wv_ref[...], top_ref[1])
    found = mul(left, keyset) + cot_ref[...].astype(jnp.float32)
    columns = found.shape[1] // LANES
    out_ref[...] = found + jnp.concatenate([plane] * columns, axis=1)


def final_kernel(places, *refs):
    parts, (feat_ref, base_ref, out_ref, data_ref, semaphores) = refs[:-5], refs[-5:]
    depth = base_ref.shape[1]
    _, rows_x, rows_y, _ = data_ref.shape
    found = parts[0][...].astype(jnp.float32)
    for part in parts[1:]:
        found = found + part[...].astype(jnp.float32)
    normed = feat_ref[0:WIDTH, :]
    inverse = feat_ref[WIDTH : WIDTH + 1, :]
    found = inverse * (found - normed * jnp.mean(found * normed, axis=0, keepdims=True))
    found = found * (1.0 / places)
    cells = rows_x * rows_y
    chunks = semaphores.shape[0]
    size = WIDTH // chunks
    copies = []
    for index in range(chunks):
        rows = slice(index * size, (index + 1) * size)
        base = base_ref[index * size * cells : (index + 1) * size * cells, :]
        total = base.reshape(size, cells, depth) + found[rows][:, None, :]
        for at_x in range(rows_x):
            part = total[:, at_x * rows_y : (at_x + 1) * rows_y, :]
            data_ref[rows, at_x, :, :] = part.astype(jnp.bfloat16)
        copy = pltpu.make_async_copy(
            data_ref.at[pl.ds(index * size, size)],
            out_ref.at[pl.ds(index * size, size)],
            semaphores.at[index],
        )
        copy.start()
        copies.append(copy)
    for copy in copies:
        copy.wait()


def run(kernel, outs, operands, places=pltpu.VMEM, target=pltpu.VMEM, flops=0, scratch=(),
        mebibytes=16):
    moved = sum(x.size * x.dtype.itemsize for x in tuple(operands) + tuple(outs))
    found = pl.pallas_call(
        kernel,
        out_shape=tuple(outs),
        in_specs=[pl.BlockSpec(memory_space=places)] * len(operands),
        out_specs=tuple(pl.BlockSpec(memory_space=target) for _ in outs),
        scratch_shapes=list(scratch),
        compiler_params=pltpu.CompilerParams(vmem_limit_bytes=mebibytes * 1024 * 1024),
        cost_estimate=pl.CostEstimate(flops=flops, bytes_accessed=moved, transcendentals=0),
    )(*operands)
    return found[0] if len(outs) == 1 else found


def per_device_kernels(field, cotangent, qk_weight, w_value, w_out):
    span_x = lax.axis_size("gx")
    span_y = lax.axis_size("gy")
    count = span_x * span_y
    rows_x, rows_y, depth = field.shape[1:]
    cells = rows_x * rows_y
    places = count * cells
    grid_x = rows_x * span_x
    grid_y = rows_y * span_y
    rows = WIDTH * cells
    wide = WIDTH * HEAD_DIM
    f32, bf16 = jnp.float32, jnp.bfloat16
    like = jax.ShapeDtypeStruct
    lengths = ((grid_x, grid_y * depth), (grid_y, grid_x * depth))

    cell = np.arange(places)
    at_x = cell // cells // span_y * rows_x + cell % cells // rows_y
    at_y = cell // cells % span_y * rows_y + cell % rows_y
    same = jnp.asarray(
        np.stack([at_x[:, None] == at_x[None], at_y[:, None] == at_y[None]]), dtype=bf16
    )

    cols = field.reshape(rows, depth)
    cots = cotangent.reshape(rows, depth)
    parts = pltpu.VMEM((span_x, WIDTH, LANES), f32)
    chunked = [pltpu.VMEM(field.shape, bf16), pltpu.SemaphoreType.DMA((4,))]
    factor_z = 1.0 / math.sqrt(HEAD_DIM * depth)
    cube = rows * wide * depth * 2

    def swaps(sent, axis, size):
        if not isinstance(sent, (tuple, list)):
            sent = [sent] * size
        return tuple(sent[:1]) + tuple(
            swap(sent[step], axis, size, step) for step in range(1, size)
        )

    sums = run(
        sums_kernel, [like((WIDTH + cells, LANES), f32)] * span_x, (pltpu.with_memory_space_constraint(field, pltpu.HBM),), places=pltpu.HBM,
        flops=cube // 4,
        scratch=[parts] + chunked,
    )
    wv, wo, wq, wk, wz = run(
        prepare_kernel,
        [like((WIDTH, wide), f32)] * 2 + [like((2 * WIDTH, wide), bf16)] * 2
        + [like((2 * WIDTH, WIDTH), f32)],
        (w_value, w_out, qk_weight),
        flops=cube // 8,
    )
    def add(sent, size):
        return run(add_kernel, [like((WIDTH + size * cells, LANES), f32)], sent)

    totals = swaps(add(swaps(sums, "gx", span_x), span_x), "gy", span_y)
    mine = run(
        functools.partial(factor_kernel, grid_x * grid_y),
        [like((WIDTH + HEAD_DIM, LANES), f32)],
        totals,
    )
    mix, feat, full = run(
        functools.partial(plane_kernel, cells, span_x, lengths),
        [like((2, HEADS * cells, places), f32), like((8, places, WIDTH), f32),
         like((2, HEADS * places, places), f32)],
        totals + (same, qk_weight),
        flops=cube // 2,
    )
    send, both, feat_z = run(
        functools.partial(coef_kernel, span_x),
        [like((2 * cells, wide), bf16), like((2 * WIDTH, depth), bf16),
         like((WIDTH + HEAD_DIM, depth), f32)],
        swaps(mine, "gx", span_x) + (wz, cols, cots, wv, wo),
        flops=2 * cube,
        scratch=[pltpu.VMEM((span_x, WIDTH + HEAD_DIM, LANES), f32)],
    )
    low = jnp.concatenate(swaps(send, "gy", span_y), axis=0)
    lows = swaps(low, "gx", span_x)
    pulled = like((WIDTH, depth), bf16)
    top, total = run(
        functools.partial(mix_kernel, factor_z, span_x),
        [like((2, cells, wide), f32), pulled],
        lows + (mix, wv, wo, wq, wk, cols, cots),
        flops=cube,
    )
    total = run(add_pull_kernel, [pulled], swaps(total, "gx", span_x))
    layer_output = run(
        output_kernel, [like(field.shape, bf16)], (top, wo, both, cols), flops=cube
    )
    plane = run(
        functools.partial(gram_kernel, cells, lengths, factor_z),
        [like((cells, WIDTH), f32)],
        lows + (feat, full, same, qk_weight),
        flops=2 * cube,
    )
    base = run(base_kernel, [like((rows, depth), f32)], (top, wv, both, cots, plane), flops=cube)
    field_grad = run(
        functools.partial(final_kernel, grid_x * grid_y),
        [like(field.shape, bf16)],
        swaps(total, "gy", span_y) + (feat_z, base),
        target=pltpu.HBM,
        scratch=chunked,
    )
    return (layer_output, field_grad)


def solution(mesh):
    placed = P(None, ("groups", "gx"), "gy", None)
    count = mesh.shape["gx"] * mesh.shape["gy"]

    def program(*arrays):
        _, grid_x, grid_y, depth = arrays[0].shape
        places = grid_x // mesh.shape["groups"] * grid_y
        small = places == LANES and places == 8 * count
        small = small and depth == LANES * mesh.shape["gx"] and count & (count - 1) == 0
        return jax.shard_map(
            per_device_kernels if small else per_device,
            mesh=mesh,
            in_specs=(placed, placed, P(), P(), P()),
            out_specs=(placed, placed),
            check_vma=False,
        )(*arrays)

    return program
```

```python
import functools
import math

import jax
import jax.numpy as jnp
import numpy as np
from jax import lax
from jax.experimental import pallas as pl
from jax.experimental.pallas import tpu as pltpu
from jax.sharding import PartitionSpec as P

WIDTH = 64
HEADS = 8
HEAD_DIM = 8
LANES = 128

EPSILON = 1e-06
PRECISE = lax.Precision.HIGHEST
AXES = ("gx", "gy")


def exchange(parts):
    return lax.all_to_all(parts, AXES, split_axis=0, concat_axis=0, tiled=True)


def swap(part, axis, size, step):
    return lax.ppermute(part, axis, [(i, i ^ step) for i in range(size)])


def gather(part, count):
    return exchange(jnp.broadcast_to(part[None], (count,) + part.shape))


def reduce_blocks(total, count):
    width, depth = total.shape
    blocks = total.reshape(width, depth // LANES, LANES).transpose(1, 0, 2)
    blocks = blocks.reshape(count, width * depth // LANES // count, LANES)
    mine = jnp.sum(exchange(blocks), axis=0)
    whole = gather(mine, count).reshape(depth // LANES, width, LANES)
    return whole.transpose(1, 0, 2).reshape(width, depth)


def axis_features(pooled, weights):
    inverse = lax.rsqrt(jnp.mean(pooled * pooled, axis=0, keepdims=True) + EPSILON)
    normed = pooled * inverse
    length = pooled.shape[1]
    factor = 1.0 / math.sqrt(HEAD_DIM * length)
    queries = jnp.dot(weights[0].T, normed, precision=PRECISE).reshape(HEADS, HEAD_DIM, length)
    keyset = jnp.dot(weights[1].T, normed, precision=PRECISE).reshape(HEADS, HEAD_DIM, length)
    return (normed, inverse, queries, keyset, factor)


def axis_kernel(queries, keyset, factor):
    scores = jnp.einsum("hdm,hdn->hmn", queries, keyset, precision=PRECISE)
    return (scores * factor).astype(jnp.bfloat16)


def kernel_backward(gram, queries, keyset, factor):
    grad_query = factor * jnp.einsum("hmn,hdn->hdm", gram, keyset, precision=PRECISE)
    grad_keyset = factor * jnp.einsum("hmn,hdm->hdn", gram, queries, precision=PRECISE)
    return (grad_query, grad_keyset)


def grad_of_normed(weights, grad_query, grad_keyset):
    length = grad_query.shape[-1]
    grad_normed = jnp.dot(weights[0], grad_query.reshape(WIDTH, length), precision=PRECISE)
    return grad_normed + jnp.dot(
        weights[1], grad_keyset.reshape(WIDTH, length), precision=PRECISE
    )


def pooled_grad(normed, inverse, grad_normed):
    return inverse * (grad_normed - normed * jnp.mean(grad_normed * normed, axis=0, keepdims=True))


def f32_einsum(pattern, left, right):
    return jnp.einsum(pattern, left, right, preferred_element_type=jnp.float32)


def per_device(field, cotangent, qk_weight, w_value, w_out):
    span_x = lax.axis_size("gx")
    span_y = lax.axis_size("gy")
    count = span_x * span_y
    rows_x, rows_y, depth = field.shape[1:]
    cells = rows_x * rows_y
    grid_x = rows_x * span_x
    grid_y = rows_y * span_y
    start_x = lax.axis_index("gx") * rows_x
    start_y = lax.axis_index("gy") * rows_y
    bf16 = jnp.bfloat16

    cols = field.reshape(WIDTH, cells, depth)
    cots = cotangent.reshape(WIDTH, cells, depth)

    sum_z = jnp.sum(cols, axis=1, dtype=jnp.float32)
    sum_rows = jnp.sum(cols, axis=2, dtype=jnp.float32)
    rows_all = gather(sum_rows.T, count).reshape(span_x, span_y, rows_x, rows_y, WIDTH)
    total_x = jnp.sum(rows_all, axis=(1, 3)).reshape(grid_x, WIDTH).T
    total_y = jnp.sum(rows_all, axis=(0, 2)).reshape(grid_y, WIDTH).T
    total_z = reduce_blocks(sum_z, count)

    normed_x, inverse_x, query_x, keyset_x, factor_x = axis_features(
        total_x / (grid_y * depth), qk_weight[0]
    )
    normed_y, inverse_y, query_y, keyset_y, factor_y = axis_features(
        total_y / (grid_x * depth), qk_weight[1]
    )
    normed_z, inverse_z, query_z, keyset_z, factor_z = axis_features(
        total_z / (grid_x * grid_y), qk_weight[2]
    )
    kernel_x = axis_kernel(query_x, keyset_x, factor_x)
    kernel_y = axis_kernel(query_y, keyset_y, factor_y)
    query_b = query_z.astype(bf16)
    keyset_b = keyset_z.astype(bf16)

    wv = w_value.reshape(WIDTH, HEADS, HEAD_DIM)
    wo = w_out.reshape(HEADS, HEAD_DIM, WIDTH)
    coef_f = f32_einsum("cpk,hgk->cphg", cols, keyset_b)
    coef_c = f32_einsum("cpz,hgz->cphg", cots, query_b)
    low_f = jnp.einsum("chd,cphg->phdg", wv.astype(jnp.float32), coef_f, precision=PRECISE)
    low_c = jnp.einsum("hdc,cphg->phdg", wo.astype(jnp.float32), coef_c, precision=PRECISE)
    squares = HEAD_DIM * HEAD_DIM
    both = jnp.stack([low_f, low_c]).astype(bf16).reshape(2, cells, HEADS * squares)
    both = gather(both, count).reshape(span_x, span_y, 2, rows_x, rows_y, HEADS * squares)
    both = both.transpose(2, 0, 3, 1, 4, 5).reshape(2, grid_x, grid_y, HEADS, squares)
    low_f, low_c = both[0], both[1]

    mid_f = f32_einsum("hyj,xjhq->xyhq", kernel_y, low_f).astype(bf16)
    top_f = f32_einsum("hxi,iyhq->xyhq", kernel_x, mid_f)
    mid_c = f32_einsum("hxi,xyhq->iyhq", kernel_x, low_c).astype(bf16)
    top_c = f32_einsum("hyj,xyhq->xjhq", kernel_y, mid_c)
    gram_x = factor_z * f32_einsum("myhq,nyhq->hmn", low_c, mid_f)
    gram_y = factor_z * f32_einsum("xmhq,xnhq->hmn", mid_c, low_f)

    def here(top):
        top = lax.dynamic_slice_in_dim(top, start_x, rows_x, 0)
        top = lax.dynamic_slice_in_dim(top, start_y, rows_y, 1)
        return top.reshape(cells, HEADS, HEAD_DIM, HEAD_DIM)

    left_f = factor_z * jnp.einsum(
        "hdc,phdg->cphg", wo.astype(jnp.float32), here(top_f), precision=PRECISE
    )
    left_c = factor_z * jnp.einsum(
        "chd,phdg->cphg", wv.astype(jnp.float32), here(top_c), precision=PRECISE
    )
    left_f = left_f.astype(bf16)
    left_c = left_c.astype(bf16)

    grad_query_z = f32_einsum("cphg,cpz->hgz", left_f, cots)
    grad_keyset_z = f32_einsum("cphg,cpz->hgz", left_c, cols)
    gn_z = reduce_blocks(grad_of_normed(qk_weight[2], grad_query_z, grad_keyset_z), count)

    layer_output = (cols.astype(jnp.float32) + f32_einsum("cphg,hgz->cpz", left_f, query_b)).astype(bf16)
    through = f32_einsum("cphg,hgz->cpz", left_c, keyset_b)

    gn_x = grad_of_normed(qk_weight[0], *kernel_backward(gram_x, query_x, keyset_x, factor_x))
    gn_y = grad_of_normed(qk_weight[1], *kernel_backward(gram_y, query_y, keyset_y, factor_y))
    pull_x = pooled_grad(normed_x, inverse_x, gn_x)
    pull_y = pooled_grad(normed_y, inverse_y, gn_y)
    pull_z = pooled_grad(normed_z, inverse_z, gn_z)
    local_x = lax.dynamic_slice_in_dim(pull_x, start_x, rows_x, 1) / (grid_y * depth)
    local_y = lax.dynamic_slice_in_dim(pull_y, start_y, rows_y, 1) / (grid_x * depth)
    local_xy = (local_x[:, :, None] + local_y[:, None, :]).reshape(WIDTH, cells)
    local_z = pull_z / (grid_x * grid_y)
    field_grad = (
        cots.astype(jnp.float32) + through + local_xy[:, :, None] + local_z[:, None, :]
    ).astype(bf16)
    return (layer_output.reshape(field.shape), field_grad.reshape(field.shape))


def split(x):
    high = x.astype(jnp.bfloat16)
    return high, (x - high.astype(jnp.float32)).astype(jnp.bfloat16)


NN = (((1,), (0,)), ((), ()))
NT = (((1,), (1,)), ((), ()))
TN = (((0,), (0,)), ((), ()))


def mul(left, right, dims=NN):
    return lax.dot_general(left, right, dims, preferred_element_type=jnp.float32)


def mul_near(left, right, dims=NN):
    left_high, left_low = split(left)
    right_high, right_low = split(right)
    return (
        mul(left_high, right_high, dims)
        + mul(left_low, right_high, dims)
        + mul(left_high, right_low, dims)
    )


def mul_left(left, right, dims=NN):
    rows = left.shape[0]
    both = mul(jnp.concatenate(split(left), axis=0), right, dims)
    return both[:rows] + both[rows:]


def number(shape, dim):
    return lax.broadcasted_iota(jnp.int32, shape, dim)


def join_quarters(part_ref, quarters):
    for step, quarter in enumerate(quarters):
        part_ref[lax.axis_index("gx") ^ step] = quarter[...]
    return jnp.concatenate([part_ref[index] for index in range(part_ref.shape[0])], axis=1)


def expand(part):
    depth = part.shape[1]
    part = part.reshape(HEADS, 1, HEAD_DIM, depth)
    part = jnp.broadcast_to(part, (HEADS, HEAD_DIM, HEAD_DIM, depth))
    return part.reshape(WIDTH * HEAD_DIM, depth).astype(jnp.bfloat16)


def spread(weights, top):
    left = weights[:, None, :] * top[None]
    return left.reshape(-1, left.shape[2]).astype(jnp.bfloat16)


def prepare_kernel(wv_ref, wo_ref, qk_ref, wv_out, wo_out, wq_out, wk_out, wz_out):
    wide = HEADS * HEAD_DIM * HEAD_DIM
    row = number((WIDTH, wide), 0)
    lane = number((WIDTH, wide), 1)
    by_channel = ((lane >> 3) == row).astype(jnp.bfloat16)
    by_factor = (((lane >> 6) * HEAD_DIM + (lane & 7)) == row).astype(jnp.bfloat16)
    wv_out[...] = mul(wv_ref[...], by_channel)
    wo_out[...] = mul(wo_ref[...], by_channel, TN)
    for index, out in ((0, wq_out), (1, wk_out)):
        high, low = split(qk_ref[2, index])
        out[0:WIDTH, :] = mul(high, by_factor).astype(jnp.bfloat16)
        out[WIDTH : 2 * WIDTH, :] = mul(low, by_factor).astype(jnp.bfloat16)
        wz_out[index * WIDTH : (index + 1) * WIDTH, :] = qk_ref[2, index].T


def sums_kernel(field_ref, *refs):
    outs, (data_ref, part_ref, semaphores) = refs[:-3], refs[-3:]
    _, rows_x, rows_y, depth = data_ref.shape
    chunks = semaphores.shape[0]
    size = WIDTH // chunks
    copies = [
        pltpu.make_async_copy(
            field_ref.at[pl.ds(index * size, size)],
            data_ref.at[pl.ds(index * size, size)],
            semaphores.at[index],
        )
        for index in range(chunks)
    ]
    for copy in copies:
        copy.start()
    own = jnp.zeros((rows_x, rows_y, LANES), jnp.float32)
    for index, copy in enumerate(copies):
        copy.wait()
        rows = slice(index * size, (index + 1) * size)
        data = data_ref[rows].astype(jnp.float32)
        part = jnp.sum(jnp.sum(data, axis=1), axis=1)
        for quarter in range(part_ref.shape[0]):
            part_ref[quarter, rows, :] = part[:, quarter * LANES : (quarter + 1) * LANES]
        lanes = data[..., :LANES]
        for start in range(LANES, depth, LANES):
            lanes = lanes + data[..., start : start + LANES]
        row_sums = jnp.sum(lanes, axis=3, keepdims=True)
        shape = lanes.shape
        mine = number(shape, 0) + index * size == number(shape, 3)
        own = own + jnp.sum(jnp.where(mine, row_sums, 0.0), axis=0)
    for step, out in enumerate(outs):
        out[0:WIDTH, :] = part_ref[lax.axis_index("gx") ^ step]
        for index in range(rows_x):
            start = WIDTH + index * rows_y
            out[start : start + rows_y, :] = own[index]


def add_kernel(*refs):
    parts, out_ref = refs[:-1], refs[-1]
    total = parts[0][0:WIDTH, :]
    for part in parts[1:]:
        total = total + part[0:WIDTH, :]
    out_ref[0:WIDTH, :] = total
    cells = parts[0].shape[0] - WIDTH
    for step, part in enumerate(parts):
        start = WIDTH + step * cells
        out_ref[start : start + cells, :] = part[WIDTH:, :]


def factor_kernel(places, *refs):
    parts, feat_ref = refs[:-1], refs[-1]
    total = parts[0][0:WIDTH, :]
    for part in parts[1:]:
        total = total + part[0:WIDTH, :]
    pooled = total * (1.0 / places)
    inverse = lax.rsqrt(jnp.mean(pooled * pooled, axis=0, keepdims=True) + EPSILON)
    normed = pooled * inverse
    feat_ref[0:WIDTH, :] = normed
    feat_ref[WIDTH:, :] = jnp.broadcast_to(inverse, (HEAD_DIM, LANES))


def add_pull_kernel(*refs):
    total = refs[0][...].astype(jnp.float32)
    for part in refs[1:-1]:
        total = total + part[...].astype(jnp.float32)
    refs[-1][...] = total.astype(jnp.bfloat16)


def by_head(part):
    shape = (HEADS, part.shape[0], WIDTH)
    mine = number(shape, 0) == (number(shape, 2) >> 3)
    return jnp.where(mine, part[None], 0.0).reshape(-1, WIDTH)


def plane_kernel(cells, span_x, lengths, *refs):
    parts, (same_ref, qk_ref, mix_ref, feat_ref, full_ref) = refs[:-5], refs[-5:]
    totals = jnp.concatenate(
        [
            part[WIDTH + step * cells : WIDTH + (step + 1) * cells, :]
            for first in range(span_x)
            for part in parts
            for step in range(first, (parts[0].shape[0] - WIDTH) // cells, span_x)
        ],
        axis=0,
    )[:, :WIDTH]
    places = totals.shape[0]
    high, low = split(totals)
    forward = backward = None
    for axis in range(2):
        same = same_ref[axis]
        pooled = (mul(same, high) + mul(same, low)) * (1.0 / lengths[axis][1])
        inverse = lax.rsqrt(jnp.mean(pooled * pooled, axis=1, keepdims=True) + EPSILON)
        normed = pooled * inverse
        query = mul_near(normed, qk_ref[axis, 0])
        keyset = mul_near(normed, qk_ref[axis, 1])
        feat_ref[4 * axis] = normed
        feat_ref[4 * axis + 1] = query
        feat_ref[4 * axis + 2] = keyset
        feat_ref[4 * axis + 3] = jnp.broadcast_to(inverse, (places, WIDTH))
        factor = 1.0 / math.sqrt(HEAD_DIM * lengths[axis][0])

        def scores(rows, other):
            found = mul_near(by_head(rows), other, NT) * factor
            return found.astype(jnp.bfloat16).astype(jnp.float32)

        full = scores(query, keyset)
        full_ref[axis] = full
        one = full.reshape(HEADS, places, places)[:, :cells].reshape(-1, places)
        two = scores(keyset[:cells], query)
        forward = one if forward is None else forward * one
        backward = two if backward is None else backward * two
    mix_ref[0] = forward
    mix_ref[1] = backward


def coef_kernel(spans, *refs):
    quarters, refs = refs[:spans], refs[spans:]
    wz_ref, field_ref, cot_ref, wv_ref, wo_ref, send_ref, both_ref, feat_ref, part_ref = refs
    rows, depth = field_ref.shape
    cells = rows // WIDTH
    wide = HEADS * HEAD_DIM * HEAD_DIM
    feat = join_quarters(part_ref, quarters)
    feat_ref[...] = feat
    high, low = split(feat[:WIDTH])
    both = mul_left(wz_ref[...], high) + mul(wz_ref[...].astype(jnp.bfloat16), low)
    both_ref[...] = both.astype(jnp.bfloat16)
    query = expand(both[:WIDTH])
    keyset = expand(both[WIDTH:])
    low_f = mul(field_ref[...], keyset, NT).reshape(WIDTH, cells, wide)
    low_f = jnp.sum(wv_ref[...][:, None, :] * low_f, axis=0)
    low_c = mul(cot_ref[...], query, NT).reshape(WIDTH, cells, wide)
    low_c = jnp.sum(wo_ref[...][:, None, :] * low_c, axis=0)
    low = jnp.concatenate([low_f, low_c], axis=0).astype(jnp.bfloat16)
    send_ref[...] = low


def join_low(refs, cells):
    low = jnp.concatenate([ref[...].astype(jnp.float32) for ref in refs], axis=0)
    wide = low.shape[1]
    low = low.reshape(-1, 2 * cells, wide)
    return [
        low[:, start : start + cells].reshape(-1, wide).astype(jnp.bfloat16)
        for start in (0, cells)
    ]


def mix_kernel(factor, spans, *refs):
    lows, refs = refs[:spans], refs[spans:]
    mix_ref, wv_ref, wo_ref, wq_ref, wk_ref, field_ref, cot_ref, top_ref, out_ref = refs
    cells = field_ref.shape[0] // WIDTH
    low_f, low_c = join_low(lows, cells)
    wide = low_f.shape[1]
    shape = (HEADS, cells, wide)
    head = number(shape, 0) == (number(shape, 2) >> 6)

    def top(mix, low):
        found = mul_left(mix, low).reshape(shape)
        return jnp.sum(jnp.where(head, found, 0.0), axis=0) * factor

    top_f = top(mix_ref[0], low_f)
    top_c = top(mix_ref[1], low_c)
    top_ref[0] = top_f
    top_ref[1] = top_c
    left_f = spread(wo_ref[...], top_f)
    left_c = spread(wv_ref[...], top_c)

    def pull(weights, left, right):
        found = mul(weights, left, NT)
        return mul_left(found[:WIDTH] + found[WIDTH:], right)

    found = pull(wq_ref[...], left_f, cot_ref[...]) + pull(wk_ref[...], left_c, field_ref[...])
    out_ref[...] = found.astype(jnp.bfloat16)


def put_cells(ref, total):
    _, rows_x, rows_y, depth = ref.shape
    total = total.reshape(WIDTH, rows_x * rows_y, depth)
    for index in range(rows_x):
        rows = total[:, index * rows_y : (index + 1) * rows_y, :]
        ref[:, index, :, :] = rows.astype(jnp.bfloat16)


def output_kernel(top_ref, wo_ref, both_ref, field_ref, out_ref):
    query = expand(both_ref[...].astype(jnp.float32)[:WIDTH])
    left = spread(wo_ref[...], top_ref[0])
    put_cells(out_ref, mul(left, query) + field_ref[...].astype(jnp.float32))


def gram_kernel(cells, lengths, factor_z, *refs):
    lows, (feat_ref, full_ref, same_ref, qk_ref, out_ref) = refs[:-5], refs[-5:]
    low_f, low_c = join_low(lows, cells)
    places, wide = low_f.shape
    squares = HEAD_DIM * HEAD_DIM
    lane = number((places, LANES), 1)
    products = []
    for pair in range(wide // LANES):
        part_f = low_f[:, pair * LANES : (pair + 1) * LANES]
        part_c = low_c[:, pair * LANES : (pair + 1) * LANES]
        for half in range(LANES // squares):
            mine = (lane >> 6) == half
            products.append(mul(jnp.where(mine, part_c, jnp.zeros_like(part_c)), part_f, NT))
    product = jnp.concatenate(products, axis=0)
    factors = [1.0 / math.sqrt(HEAD_DIM * lengths[axis][0]) for axis in range(2)]
    queries = [by_head(feat_ref[4 * axis + 1]).astype(jnp.bfloat16) for axis in range(2)]
    keysets = [by_head(feat_ref[4 * axis + 2]).astype(jnp.bfloat16) for axis in range(2)]
    total = jnp.zeros((cells, WIDTH), jnp.float32)
    for axis in range(2):
        gram = (product * full_ref[1 - axis]).astype(jnp.bfloat16)
        across = jnp.concatenate(
            [gram[h * places : (h + 1) * places] for h in range(HEADS)], axis=1
        )
        scale = factors[axis] * factor_z
        grad_query = mul(across, keysets[axis]) * scale
        grad_keyset = mul(gram, queries[axis], TN) * scale
        found = mul_near(grad_query, qk_ref[axis, 0], NT) + mul_near(grad_keyset, qk_ref[axis, 1], NT)
        high, low = split(found)
        own = same_ref[axis, 0 : 2 * cells, :]
        found = (mul(own, high) + mul(own, low))[:cells]
        normed = feat_ref[4 * axis, 0:cells, :]
        inverse = feat_ref[4 * axis + 3, 0:cells, :]
        found = found - normed * jnp.mean(found * normed, axis=1, keepdims=True)
        total = total + inverse * found * (1.0 / lengths[axis][1])
    out_ref[...] = total


def base_kernel(top_ref, wv_ref, both_ref, cot_ref, plane_ref, out_ref):
    rows = cot_ref.shape[0]
    cells = rows // WIDTH
    shape = (WIDTH, cells, WIDTH)
    own = jnp.where(number(shape, 0) == number(shape, 2), plane_ref[...][None], 0.0)
    plane = mul_left(own.reshape(rows, WIDTH), jnp.ones((WIDTH, LANES), jnp.bfloat16))
    keyset = expand(both_ref[...].astype(jnp.float32)[WIDTH:])
    left = spread(wv_ref[...], top_ref[1])
    found = mul(left, keyset) + cot_ref[...].astype(jnp.float32)
    columns = found.shape[1] // LANES
    out_ref[...] = found + jnp.concatenate([plane] * columns, axis=1)


def final_kernel(places, *refs):
    parts, (feat_ref, base_ref, out_ref, data_ref, semaphores) = refs[:-5], refs[-5:]
    depth = base_ref.shape[1]
    _, rows_x, rows_y, _ = data_ref.shape
    found = parts[0][...].astype(jnp.float32)
    for part in parts[1:]:
        found = found + part[...].astype(jnp.float32)
    normed = feat_ref[0:WIDTH, :]
    inverse = feat_ref[WIDTH : WIDTH + 1, :]
    found = inverse * (found - normed * jnp.mean(found * normed, axis=0, keepdims=True))
    found = found * (1.0 / places)
    cells = rows_x * rows_y
    chunks = semaphores.shape[0]
    size = WIDTH // chunks
    copies = []
    for index in range(chunks):
        rows = slice(index * size, (index + 1) * size)
        base = base_ref[index * size * cells : (index + 1) * size * cells, :]
        total = base.reshape(size, cells, depth) + found[rows][:, None, :]
        for at_x in range(rows_x):
            part = total[:, at_x * rows_y : (at_x + 1) * rows_y, :]
            data_ref[rows, at_x, :, :] = part.astype(jnp.bfloat16)
        copy = pltpu.make_async_copy(
            data_ref.at[pl.ds(index * size, size)],
            out_ref.at[pl.ds(index * size, size)],
            semaphores.at[index],
        )
        copy.start()
        copies.append(copy)
    for copy in copies:
        copy.wait()


def run(kernel, outs, operands, places=pltpu.VMEM, target=pltpu.VMEM, flops=0, scratch=(),
        mebibytes=16):
    moved = sum(x.size * x.dtype.itemsize for x in tuple(operands) + tuple(outs))
    found = pl.pallas_call(
        kernel,
        out_shape=tuple(outs),
        in_specs=[pl.BlockSpec(memory_space=places)] * len(operands),
        out_specs=tuple(pl.BlockSpec(memory_space=target) for _ in outs),
        scratch_shapes=list(scratch),
        compiler_params=pltpu.CompilerParams(vmem_limit_bytes=mebibytes * 1024 * 1024),
        cost_estimate=pl.CostEstimate(flops=flops, bytes_accessed=moved, transcendentals=0),
    )(*operands)
    return found[0] if len(outs) == 1 else found


def per_device_kernels(field, cotangent, qk_weight, w_value, w_out):
    span_x = lax.axis_size("gx")
    span_y = lax.axis_size("gy")
    count = span_x * span_y
    rows_x, rows_y, depth = field.shape[1:]
    cells = rows_x * rows_y
    places = count * cells
    grid_x = rows_x * span_x
    grid_y = rows_y * span_y
    rows = WIDTH * cells
    wide = WIDTH * HEAD_DIM
    f32, bf16 = jnp.float32, jnp.bfloat16
    like = jax.ShapeDtypeStruct
    lengths = ((grid_x, grid_y * depth), (grid_y, grid_x * depth))

    cell = np.arange(places)
    at_x = cell // cells // span_y * rows_x + cell % cells // rows_y
    at_y = cell // cells % span_y * rows_y + cell % rows_y
    same = jnp.asarray(
        np.stack([at_x[:, None] == at_x[None], at_y[:, None] == at_y[None]]), dtype=bf16
    )

    cots = cotangent.reshape(rows, depth)
    parts = pltpu.VMEM((span_x, WIDTH, LANES), f32)
    chunked = [pltpu.VMEM(field.shape, bf16), pltpu.SemaphoreType.DMA((4,))]
    factor_z = 1.0 / math.sqrt(HEAD_DIM * depth)
    cube = rows * wide * depth * 2

    def swaps(sent, axis, size):
        if not isinstance(sent, (tuple, list)):
            sent = [sent] * size
        return tuple(sent[:1]) + tuple(
            swap(sent[step], axis, size, step) for step in range(1, size)
        )

    *sums, held = run(
        sums_kernel,
        [like((WIDTH + cells, LANES), f32)] * span_x + [like(field.shape, bf16)],
        (pltpu.with_memory_space_constraint(field, pltpu.HBM),),
        places=pltpu.HBM,
        flops=cube // 4,
        scratch=[parts, pltpu.SemaphoreType.DMA((4,))],
    )
    cols = held.reshape(rows, depth)
    wv, wo, wq, wk, wz = run(
        prepare_kernel,
        [like((WIDTH, wide), f32)] * 2 + [like((2 * WIDTH, wide), bf16)] * 2
        + [like((2 * WIDTH, WIDTH), f32)],
        (w_value, w_out, qk_weight),
        flops=cube // 8,
    )
    def add(sent, size):
        return run(add_kernel, [like((WIDTH + size * cells, LANES), f32)], sent)

    totals = swaps(add(swaps(sums, "gx", span_x), span_x), "gy", span_y)
    mine = run(
        functools.partial(factor_kernel, grid_x * grid_y),
        [like((WIDTH + HEAD_DIM, LANES), f32)],
        totals,
    )
    mix, feat, full = run(
        functools.partial(plane_kernel, cells, span_x, lengths),
        [like((2, HEADS * cells, places), f32), like((8, places, WIDTH), f32),
         like((2, HEADS * places, places), f32)],
        totals + (same, qk_weight),
        flops=cube // 2,
    )
    send, both, feat_z = run(
        functools.partial(coef_kernel, span_x),
        [like((2 * cells, wide), bf16), like((2 * WIDTH, depth), bf16),
         like((WIDTH + HEAD_DIM, depth), f32)],
        swaps(mine, "gx", span_x) + (wz, cols, cots, wv, wo),
        flops=2 * cube,
        scratch=[pltpu.VMEM((span_x, WIDTH + HEAD_DIM, LANES), f32)],
    )
    low = jnp.concatenate(swaps(send, "gy", span_y), axis=0)
    lows = swaps(low, "gx", span_x)
    pulled = like((WIDTH, depth), bf16)
    top, total = run(
        functools.partial(mix_kernel, factor_z, span_x),
        [like((2, cells, wide), f32), pulled],
        lows + (mix, wv, wo, wq, wk, cols, cots),
        flops=cube,
    )
    for level in range(span_x.bit_length() - 1):
        total = run(add_pull_kernel, [pulled], (total, swap(total, "gx", span_x, 1 << level)))
    layer_output = run(
        output_kernel, [like(field.shape, bf16)], (top, wo, both, cols), flops=cube
    )
    plane = run(
        functools.partial(gram_kernel, cells, lengths, factor_z),
        [like((cells, WIDTH), f32)],
        lows + (feat, full, same, qk_weight),
        flops=2 * cube,
    )
    base = run(base_kernel, [like((rows, depth), f32)], (top, wv, both, cots, plane), flops=cube)
    field_grad = run(
        functools.partial(final_kernel, grid_x * grid_y),
        [like(field.shape, bf16)],
        swaps(total, "gy", span_y) + (feat_z, base),
        target=pltpu.HBM,
        scratch=chunked,
    )
    return (layer_output, field_grad)


def solution(mesh):
    placed = P(None, ("groups", "gx"), "gy", None)
    count = mesh.shape["gx"] * mesh.shape["gy"]

    def program(*arrays):
        _, grid_x, grid_y, depth = arrays[0].shape
        places = grid_x // mesh.shape["groups"] * grid_y
        small = places == LANES and places == 8 * count
        small = small and depth == LANES * mesh.shape["gx"] and count & (count - 1) == 0
        return jax.shard_map(
            per_device_kernels if small else per_device,
            mesh=mesh,
            in_specs=(placed, placed, P(), P(), P()),
            out_specs=(placed, placed),
            check_vma=False,
        )(*arrays)

    return program
```

```python
import functools
import math

import jax
import jax.numpy as jnp
import numpy as np
from jax import lax
from jax.experimental import pallas as pl
from jax.experimental.pallas import tpu as pltpu
from jax.sharding import PartitionSpec as P

WIDTH = 64
HEADS = 8
HEAD_DIM = 8
LANES = 128

EPSILON = 1e-06
PRECISE = lax.Precision.HIGHEST
AXES = ("gx", "gy")


def exchange(parts):
    return lax.all_to_all(parts, AXES, split_axis=0, concat_axis=0, tiled=True)


def swap(part, axis, size, step):
    return lax.ppermute(part, axis, [(i, i ^ step) for i in range(size)])


def gather(part, count):
    return exchange(jnp.broadcast_to(part[None], (count,) + part.shape))


def reduce_blocks(total, count):
    width, depth = total.shape
    blocks = total.reshape(width, depth // LANES, LANES).transpose(1, 0, 2)
    blocks = blocks.reshape(count, width * depth // LANES // count, LANES)
    mine = jnp.sum(exchange(blocks), axis=0)
    whole = gather(mine, count).reshape(depth // LANES, width, LANES)
    return whole.transpose(1, 0, 2).reshape(width, depth)


def axis_features(pooled, weights):
    inverse = lax.rsqrt(jnp.mean(pooled * pooled, axis=0, keepdims=True) + EPSILON)
    normed = pooled * inverse
    length = pooled.shape[1]
    factor = 1.0 / math.sqrt(HEAD_DIM * length)
    queries = jnp.dot(weights[0].T, normed, precision=PRECISE).reshape(HEADS, HEAD_DIM, length)
    keyset = jnp.dot(weights[1].T, normed, precision=PRECISE).reshape(HEADS, HEAD_DIM, length)
    return (normed, inverse, queries, keyset, factor)


def axis_kernel(queries, keyset, factor):
    scores = jnp.einsum("hdm,hdn->hmn", queries, keyset, precision=PRECISE)
    return (scores * factor).astype(jnp.bfloat16)


def kernel_backward(gram, queries, keyset, factor):
    grad_query = factor * jnp.einsum("hmn,hdn->hdm", gram, keyset, precision=PRECISE)
    grad_keyset = factor * jnp.einsum("hmn,hdm->hdn", gram, queries, precision=PRECISE)
    return (grad_query, grad_keyset)


def grad_of_normed(weights, grad_query, grad_keyset):
    length = grad_query.shape[-1]
    grad_normed = jnp.dot(weights[0], grad_query.reshape(WIDTH, length), precision=PRECISE)
    return grad_normed + jnp.dot(
        weights[1], grad_keyset.reshape(WIDTH, length), precision=PRECISE
    )


def pooled_grad(normed, inverse, grad_normed):
    return inverse * (grad_normed - normed * jnp.mean(grad_normed * normed, axis=0, keepdims=True))


def f32_einsum(pattern, left, right):
    return jnp.einsum(pattern, left, right, preferred_element_type=jnp.float32)


def per_device(field, cotangent, qk_weight, w_value, w_out):
    span_x = lax.axis_size("gx")
    span_y = lax.axis_size("gy")
    count = span_x * span_y
    rows_x, rows_y, depth = field.shape[1:]
    cells = rows_x * rows_y
    grid_x = rows_x * span_x
    grid_y = rows_y * span_y
    start_x = lax.axis_index("gx") * rows_x
    start_y = lax.axis_index("gy") * rows_y
    bf16 = jnp.bfloat16

    cols = field.reshape(WIDTH, cells, depth)
    cots = cotangent.reshape(WIDTH, cells, depth)

    sum_z = jnp.sum(cols, axis=1, dtype=jnp.float32)
    sum_rows = jnp.sum(cols, axis=2, dtype=jnp.float32)
    rows_all = gather(sum_rows.T, count).reshape(span_x, span_y, rows_x, rows_y, WIDTH)
    total_x = jnp.sum(rows_all, axis=(1, 3)).reshape(grid_x, WIDTH).T
    total_y = jnp.sum(rows_all, axis=(0, 2)).reshape(grid_y, WIDTH).T
    total_z = reduce_blocks(sum_z, count)

    normed_x, inverse_x, query_x, keyset_x, factor_x = axis_features(
        total_x / (grid_y * depth), qk_weight[0]
    )
    normed_y, inverse_y, query_y, keyset_y, factor_y = axis_features(
        total_y / (grid_x * depth), qk_weight[1]
    )
    normed_z, inverse_z, query_z, keyset_z, factor_z = axis_features(
        total_z / (grid_x * grid_y), qk_weight[2]
    )
    kernel_x = axis_kernel(query_x, keyset_x, factor_x)
    kernel_y = axis_kernel(query_y, keyset_y, factor_y)
    query_b = query_z.astype(bf16)
    keyset_b = keyset_z.astype(bf16)

    wv = w_value.reshape(WIDTH, HEADS, HEAD_DIM)
    wo = w_out.reshape(HEADS, HEAD_DIM, WIDTH)
    coef_f = f32_einsum("cpk,hgk->cphg", cols, keyset_b)
    coef_c = f32_einsum("cpz,hgz->cphg", cots, query_b)
    low_f = jnp.einsum("chd,cphg->phdg", wv.astype(jnp.float32), coef_f, precision=PRECISE)
    low_c = jnp.einsum("hdc,cphg->phdg", wo.astype(jnp.float32), coef_c, precision=PRECISE)
    squares = HEAD_DIM * HEAD_DIM
    both = jnp.stack([low_f, low_c]).astype(bf16).reshape(2, cells, HEADS * squares)
    both = gather(both, count).reshape(span_x, span_y, 2, rows_x, rows_y, HEADS * squares)
    both = both.transpose(2, 0, 3, 1, 4, 5).reshape(2, grid_x, grid_y, HEADS, squares)
    low_f, low_c = both[0], both[1]

    mid_f = f32_einsum("hyj,xjhq->xyhq", kernel_y, low_f).astype(bf16)
    top_f = f32_einsum("hxi,iyhq->xyhq", kernel_x, mid_f)
    mid_c = f32_einsum("hxi,xyhq->iyhq", kernel_x, low_c).astype(bf16)
    top_c = f32_einsum("hyj,xyhq->xjhq", kernel_y, mid_c)
    gram_x = factor_z * f32_einsum("myhq,nyhq->hmn", low_c, mid_f)
    gram_y = factor_z * f32_einsum("xmhq,xnhq->hmn", mid_c, low_f)

    def here(top):
        top = lax.dynamic_slice_in_dim(top, start_x, rows_x, 0)
        top = lax.dynamic_slice_in_dim(top, start_y, rows_y, 1)
        return top.reshape(cells, HEADS, HEAD_DIM, HEAD_DIM)

    left_f = factor_z * jnp.einsum(
        "hdc,phdg->cphg", wo.astype(jnp.float32), here(top_f), precision=PRECISE
    )
    left_c = factor_z * jnp.einsum(
        "chd,phdg->cphg", wv.astype(jnp.float32), here(top_c), precision=PRECISE
    )
    left_f = left_f.astype(bf16)
    left_c = left_c.astype(bf16)

    grad_query_z = f32_einsum("cphg,cpz->hgz", left_f, cots)
    grad_keyset_z = f32_einsum("cphg,cpz->hgz", left_c, cols)
    gn_z = reduce_blocks(grad_of_normed(qk_weight[2], grad_query_z, grad_keyset_z), count)

    layer_output = (cols.astype(jnp.float32) + f32_einsum("cphg,hgz->cpz", left_f, query_b)).astype(bf16)
    through = f32_einsum("cphg,hgz->cpz", left_c, keyset_b)

    gn_x = grad_of_normed(qk_weight[0], *kernel_backward(gram_x, query_x, keyset_x, factor_x))
    gn_y = grad_of_normed(qk_weight[1], *kernel_backward(gram_y, query_y, keyset_y, factor_y))
    pull_x = pooled_grad(normed_x, inverse_x, gn_x)
    pull_y = pooled_grad(normed_y, inverse_y, gn_y)
    pull_z = pooled_grad(normed_z, inverse_z, gn_z)
    local_x = lax.dynamic_slice_in_dim(pull_x, start_x, rows_x, 1) / (grid_y * depth)
    local_y = lax.dynamic_slice_in_dim(pull_y, start_y, rows_y, 1) / (grid_x * depth)
    local_xy = (local_x[:, :, None] + local_y[:, None, :]).reshape(WIDTH, cells)
    local_z = pull_z / (grid_x * grid_y)
    field_grad = (
        cots.astype(jnp.float32) + through + local_xy[:, :, None] + local_z[:, None, :]
    ).astype(bf16)
    return (layer_output.reshape(field.shape), field_grad.reshape(field.shape))


def split(x):
    high = x.astype(jnp.bfloat16)
    return high, (x - high.astype(jnp.float32)).astype(jnp.bfloat16)


NN = (((1,), (0,)), ((), ()))
NT = (((1,), (1,)), ((), ()))
TN = (((0,), (0,)), ((), ()))


def mul(left, right, dims=NN):
    return lax.dot_general(left, right, dims, preferred_element_type=jnp.float32)


def mul_near(left, right, dims=NN):
    left_high, left_low = split(left)
    right_high, right_low = split(right)
    return (
        mul(left_high, right_high, dims)
        + mul(left_low, right_high, dims)
        + mul(left_high, right_low, dims)
    )


def mul_left(left, right, dims=NN):
    rows = left.shape[0]
    both = mul(jnp.concatenate(split(left), axis=0), right, dims)
    return both[:rows] + both[rows:]


def number(shape, dim):
    return lax.broadcasted_iota(jnp.int32, shape, dim)


def join_quarters(part_ref, quarters):
    size = len(quarters)
    for step, quarter in zip([0, *range(size - 1, 0, -1)], quarters):
        part_ref[lax.axis_index("gx") ^ step] = quarter[...]
    return jnp.concatenate([part_ref[index] for index in range(part_ref.shape[0])], axis=1)


def expand(part):
    depth = part.shape[1]
    part = part.reshape(HEADS, 1, HEAD_DIM, depth)
    part = jnp.broadcast_to(part, (HEADS, HEAD_DIM, HEAD_DIM, depth))
    return part.reshape(WIDTH * HEAD_DIM, depth).astype(jnp.bfloat16)


def spread(weights, top):
    left = weights[:, None, :] * top[None]
    return left.reshape(-1, left.shape[2]).astype(jnp.bfloat16)


def prepare_kernel(wv_ref, wo_ref, qk_ref, wv_out, wo_out, wq_out, wk_out, wz_out):
    wide = HEADS * HEAD_DIM * HEAD_DIM
    row = number((WIDTH, wide), 0)
    lane = number((WIDTH, wide), 1)
    by_channel = ((lane >> 3) == row).astype(jnp.bfloat16)
    by_factor = (((lane >> 6) * HEAD_DIM + (lane & 7)) == row).astype(jnp.bfloat16)
    wv_out[...] = mul(wv_ref[...], by_channel)
    wo_out[...] = mul(wo_ref[...], by_channel, TN)
    for index, out in ((0, wq_out), (1, wk_out)):
        high, low = split(qk_ref[2, index])
        out[0:WIDTH, :] = mul(high, by_factor).astype(jnp.bfloat16)
        out[WIDTH : 2 * WIDTH, :] = mul(low, by_factor).astype(jnp.bfloat16)
        wz_out[index * WIDTH : (index + 1) * WIDTH, :] = qk_ref[2, index].T


def sums_kernel(field_ref, *refs):
    outs, (cols_ref, data_ref, part_ref, semaphores) = refs[:-4], refs[-4:]
    _, rows_x, rows_y, depth = data_ref.shape
    cells = rows_x * rows_y
    chunks = semaphores.shape[0]
    size = WIDTH // chunks
    copies = [
        pltpu.make_async_copy(
            field_ref.at[pl.ds(index * size, size)],
            data_ref.at[pl.ds(index * size, size)],
            semaphores.at[index],
        )
        for index in range(chunks)
    ]
    for copy in copies:
        copy.start()
    own = jnp.zeros((cells, LANES), jnp.float32)
    pick = number((size, size * cells), 1) // cells == number((size, size * cells), 0)
    pick = pick.astype(jnp.bfloat16)
    ones = jnp.ones((depth, LANES), jnp.bfloat16)
    for index, copy in enumerate(copies):
        copy.wait()
        rows = slice(index * size, (index + 1) * size)
        data = data_ref[rows].astype(jnp.float32)
        data = jnp.concatenate([data[:, at_x] for at_x in range(rows_x)], axis=1)
        data = data.reshape(size * cells, depth).astype(jnp.bfloat16)
        cols_ref[index * size * cells : (index + 1) * size * cells, :] = data
        part = mul(pick, data)
        for quarter in range(part_ref.shape[0]):
            part_ref[quarter, rows, :] = part[:, quarter * LANES : (quarter + 1) * LANES]
        row_sums = mul(data, ones).reshape(size, cells, LANES)
        shape = row_sums.shape
        mine = number(shape, 0) + index * size == number(shape, 2)
        own = own + jnp.sum(jnp.where(mine, row_sums, 0.0), axis=0)
    for step, out in enumerate(outs):
        out[0:WIDTH, :] = part_ref[lax.axis_index("gx") ^ step]
        out[WIDTH:, :] = own


def add_kernel(*refs):
    parts, out_ref = refs[:-1], refs[-1]
    total = parts[0][0:WIDTH, :]
    for part in parts[1:]:
        total = total + part[0:WIDTH, :]
    out_ref[0:WIDTH, :] = total
    start = WIDTH
    for part in parts:
        more = part.shape[0] - WIDTH
        out_ref[start : start + more, :] = part[WIDTH:, :]
        start += more


def stack_kernel(*refs):
    refs[-1][...] = jnp.concatenate([ref[...] for ref in refs[:-1]], axis=0)


def factor_kernel(places, *refs):
    parts, feat_ref = refs[:-1], refs[-1]
    total = parts[0][0:WIDTH, :]
    for part in parts[1:]:
        total = total + part[0:WIDTH, :]
    pooled = total * (1.0 / places)
    inverse = lax.rsqrt(jnp.mean(pooled * pooled, axis=0, keepdims=True) + EPSILON)
    normed = pooled * inverse
    feat_ref[0:WIDTH, :] = normed
    feat_ref[WIDTH:, :] = jnp.broadcast_to(inverse, (HEAD_DIM, LANES))


def add_pull_kernel(*refs):
    total = refs[0][...].astype(jnp.float32)
    for part in refs[1:-1]:
        total = total + part[...].astype(jnp.float32)
    refs[-1][...] = total.astype(refs[-1].dtype)


def by_head(part):
    shape = (HEADS, part.shape[0], WIDTH)
    mine = number(shape, 0) == (number(shape, 2) >> 3)
    return jnp.where(mine, part[None], 0.0).reshape(-1, WIDTH)


def plane_kernel(cells, span_x, lengths, *refs):
    parts, (same_ref, qk_ref, mix_ref, feat_ref, full_ref) = refs[:-5], refs[-5:]
    totals = jnp.concatenate(
        [
            part[WIDTH + step * cells : WIDTH + (step + 1) * cells, :]
            for first in range(span_x)
            for part in parts
            for step in range(first, (part.shape[0] - WIDTH) // cells, span_x)
        ],
        axis=0,
    )[:, :WIDTH]
    places = totals.shape[0]
    high, low = split(totals)
    forward = backward = None
    for axis in range(2):
        same = same_ref[axis]
        pooled = (mul(same, high) + mul(same, low)) * (1.0 / lengths[axis][1])
        inverse = lax.rsqrt(jnp.mean(pooled * pooled, axis=1, keepdims=True) + EPSILON)
        normed = pooled * inverse
        query = mul_near(normed, qk_ref[axis, 0])
        keyset = mul_near(normed, qk_ref[axis, 1])
        feat_ref[4 * axis] = normed
        feat_ref[4 * axis + 1] = query
        feat_ref[4 * axis + 2] = keyset
        feat_ref[4 * axis + 3] = jnp.broadcast_to(inverse, (places, WIDTH))
        factor = 1.0 / math.sqrt(HEAD_DIM * lengths[axis][0])

        def scores(rows, other):
            found = mul_near(by_head(rows), other, NT) * factor
            return found.astype(jnp.bfloat16).astype(jnp.float32)

        full = scores(query, keyset)
        full_ref[axis] = full
        one = full.reshape(HEADS, places, places)[:, :cells].reshape(-1, places)
        two = scores(keyset[:cells], query)
        forward = one if forward is None else forward * one
        backward = two if backward is None else backward * two
    mix_ref[0] = forward
    mix_ref[1] = backward


def coef_kernel(spans, *refs):
    quarters, refs = refs[:spans], refs[spans:]
    wz_ref, field_ref, cot_ref, wv_ref, wo_ref, send_ref, both_ref, feat_ref, part_ref = refs
    rows, depth = field_ref.shape
    cells = rows // WIDTH
    wide = HEADS * HEAD_DIM * HEAD_DIM
    feat = join_quarters(part_ref, quarters)
    feat_ref[...] = feat
    high, low = split(feat[:WIDTH])
    both = mul_left(wz_ref[...], high) + mul(wz_ref[...].astype(jnp.bfloat16), low)
    both_ref[...] = both.astype(jnp.bfloat16)
    query = expand(both[:WIDTH])
    keyset = expand(both[WIDTH:])
    low_f = mul(field_ref[...], keyset, NT).reshape(WIDTH, cells, wide)
    low_f = jnp.sum(wv_ref[...][:, None, :] * low_f, axis=0)
    low_c = mul(cot_ref[...], query, NT).reshape(WIDTH, cells, wide)
    low_c = jnp.sum(wo_ref[...][:, None, :] * low_c, axis=0)
    low = jnp.concatenate([low_f, low_c], axis=0).astype(jnp.bfloat16)
    send_ref[...] = low


def join_low(refs, cells):
    low = jnp.concatenate([ref[...].astype(jnp.float32) for ref in refs], axis=0)
    wide = low.shape[1]
    low = low.reshape(-1, 2 * cells, wide)
    return [
        low[:, start : start + cells].reshape(-1, wide).astype(jnp.bfloat16)
        for start in (0, cells)
    ]


def mix_kernel(factor, spans, *refs):
    lows, refs = refs[:spans], refs[spans:]
    mix_ref, wv_ref, wo_ref, wq_ref, wk_ref, field_ref, cot_ref, top_ref, out_ref = refs
    cells = field_ref.shape[0] // WIDTH
    low_f, low_c = join_low(lows, cells)
    wide = low_f.shape[1]
    shape = (HEADS, cells, wide)
    head = number(shape, 0) == (number(shape, 2) >> 6)

    def top(mix, low):
        found = mul_left(mix, low).reshape(shape)
        return jnp.sum(jnp.where(head, found, 0.0), axis=0) * factor

    top_f = top(mix_ref[0], low_f)
    top_c = top(mix_ref[1], low_c)
    top_ref[0] = top_f
    top_ref[1] = top_c
    left_f = spread(wo_ref[...], top_f)
    left_c = spread(wv_ref[...], top_c)

    def pull(weights, left, right):
        found = mul(weights, left, NT)
        return mul_left(found[:WIDTH] + found[WIDTH:], right)

    found = pull(wq_ref[...], left_f, cot_ref[...]) + pull(wk_ref[...], left_c, field_ref[...])
    out_ref[...] = found.astype(jnp.bfloat16)


def put_cells(ref, total):
    _, rows_x, rows_y, depth = ref.shape
    total = total.reshape(WIDTH, rows_x * rows_y, depth)
    for index in range(rows_x):
        rows = total[:, index * rows_y : (index + 1) * rows_y, :]
        ref[:, index, :, :] = rows.astype(jnp.bfloat16)


def output_kernel(top_ref, wo_ref, both_ref, field_ref, out_ref):
    query = expand(both_ref[...].astype(jnp.float32)[:WIDTH])
    left = spread(wo_ref[...], top_ref[0])
    put_cells(out_ref, mul(left, query) + field_ref[...].astype(jnp.float32))


def gram_kernel(cells, lengths, factor_z, *refs):
    lows, (feat_ref, full_ref, same_ref, qk_ref, out_ref) = refs[:-5], refs[-5:]
    low_f, low_c = join_low(lows, cells)
    places, wide = low_f.shape
    squares = HEAD_DIM * HEAD_DIM
    lane = number((places, LANES), 1)
    products = []
    for pair in range(wide // LANES):
        part_f = low_f[:, pair * LANES : (pair + 1) * LANES]
        part_c = low_c[:, pair * LANES : (pair + 1) * LANES]
        for half in range(LANES // squares):
            mine = (lane >> 6) == half
            products.append(mul(jnp.where(mine, part_c, jnp.zeros_like(part_c)), part_f, NT))
    product = jnp.concatenate(products, axis=0)
    factors = [1.0 / math.sqrt(HEAD_DIM * lengths[axis][0]) for axis in range(2)]
    queries = [by_head(feat_ref[4 * axis + 1]).astype(jnp.bfloat16) for axis in range(2)]
    keysets = [by_head(feat_ref[4 * axis + 2]).astype(jnp.bfloat16) for axis in range(2)]
    total = jnp.zeros((cells, WIDTH), jnp.float32)
    for axis in range(2):
        gram = (product * full_ref[1 - axis]).astype(jnp.bfloat16)
        across = jnp.concatenate(
            [gram[h * places : (h + 1) * places] for h in range(HEADS)], axis=1
        )
        scale = factors[axis] * factor_z
        grad_query = mul(across, keysets[axis]) * scale
        grad_keyset = mul(gram, queries[axis], TN) * scale
        found = mul_near(grad_query, qk_ref[axis, 0], NT) + mul_near(grad_keyset, qk_ref[axis, 1], NT)
        high, low = split(found)
        own = same_ref[axis, 0 : 2 * cells, :]
        found = (mul(own, high) + mul(own, low))[:cells]
        normed = feat_ref[4 * axis, 0:cells, :]
        inverse = feat_ref[4 * axis + 3, 0:cells, :]
        found = found - normed * jnp.mean(found * normed, axis=1, keepdims=True)
        total = total + inverse * found * (1.0 / lengths[axis][1])
    out_ref[...] = total


def base_kernel(top_ref, wv_ref, both_ref, cot_ref, plane_ref, out_ref):
    rows = cot_ref.shape[0]
    cells = rows // WIDTH
    shape = (WIDTH, cells, WIDTH)
    own = jnp.where(number(shape, 0) == number(shape, 2), plane_ref[...][None], 0.0)
    plane = mul_left(own.reshape(rows, WIDTH), jnp.ones((WIDTH, LANES), jnp.bfloat16))
    keyset = expand(both_ref[...].astype(jnp.float32)[WIDTH:])
    left = spread(wv_ref[...], top_ref[1])
    found = mul(left, keyset) + cot_ref[...].astype(jnp.float32)
    columns = found.shape[1] // LANES
    out_ref[...] = found + jnp.concatenate([plane] * columns, axis=1)


def final_kernel(places, *refs):
    parts, (feat_ref, base_ref, out_ref, data_ref, semaphores) = refs[:-5], refs[-5:]
    depth = base_ref.shape[1]
    _, rows_x, rows_y, _ = data_ref.shape
    found = parts[0][...].astype(jnp.float32)
    for part in parts[1:]:
        found = found + part[...].astype(jnp.float32)
    normed = feat_ref[0:WIDTH, :]
    inverse = feat_ref[WIDTH : WIDTH + 1, :]
    found = inverse * (found - normed * jnp.mean(found * normed, axis=0, keepdims=True))
    found = found * (1.0 / places)
    cells = rows_x * rows_y
    chunks = semaphores.shape[0]
    size = WIDTH // chunks
    copies = []
    for index in range(chunks):
        rows = slice(index * size, (index + 1) * size)
        base = base_ref[index * size * cells : (index + 1) * size * cells, :]
        total = base.reshape(size, cells, depth) + found[rows][:, None, :]
        for at_x in range(rows_x):
            part = total[:, at_x * rows_y : (at_x + 1) * rows_y, :]
            data_ref[rows, at_x, :, :] = part.astype(jnp.bfloat16)
        copy = pltpu.make_async_copy(
            data_ref.at[pl.ds(index * size, size)],
            out_ref.at[pl.ds(index * size, size)],
            semaphores.at[index],
        )
        copy.start()
        copies.append(copy)
    for copy in copies:
        copy.wait()


def run(kernel, outs, operands, places=pltpu.VMEM, target=pltpu.VMEM, flops=0, scratch=(),
        mebibytes=16):
    moved = sum(x.size * x.dtype.itemsize for x in tuple(operands) + tuple(outs))
    found = pl.pallas_call(
        kernel,
        out_shape=tuple(outs),
        in_specs=[pl.BlockSpec(memory_space=places)] * len(operands),
        out_specs=tuple(pl.BlockSpec(memory_space=target) for _ in outs),
        scratch_shapes=list(scratch),
        compiler_params=pltpu.CompilerParams(vmem_limit_bytes=mebibytes * 1024 * 1024),
        cost_estimate=pl.CostEstimate(flops=flops, bytes_accessed=moved, transcendentals=0),
    )(*operands)
    return found[0] if len(outs) == 1 else found


def per_device_kernels(field, cotangent, qk_weight, w_value, w_out):
    span_x = lax.axis_size("gx")
    span_y = lax.axis_size("gy")
    count = span_x * span_y
    rows_x, rows_y, depth = field.shape[1:]
    cells = rows_x * rows_y
    places = count * cells
    grid_x = rows_x * span_x
    grid_y = rows_y * span_y
    rows = WIDTH * cells
    wide = WIDTH * HEAD_DIM
    f32, bf16 = jnp.float32, jnp.bfloat16
    like = jax.ShapeDtypeStruct
    lengths = ((grid_x, grid_y * depth), (grid_y, grid_x * depth))

    cell = np.arange(places)
    at_x = cell // cells // span_y * rows_x + cell % cells // rows_y
    at_y = cell // cells % span_y * rows_y + cell % rows_y
    same = jnp.asarray(
        np.stack([at_x[:, None] == at_x[None], at_y[:, None] == at_y[None]]), dtype=bf16
    )

    cots = cotangent.reshape(rows, depth)
    parts = pltpu.VMEM((span_x, WIDTH, LANES), f32)
    chunked = [pltpu.VMEM(field.shape, bf16), pltpu.SemaphoreType.DMA((4,))]
    factor_z = 1.0 / math.sqrt(HEAD_DIM * depth)
    cube = rows * wide * depth * 2

    def swaps(sent, axis, size):
        if not isinstance(sent, (tuple, list)):
            sent = [sent] * size
        return tuple(sent[:1]) + tuple(
            swap(sent[step], axis, size, step) for step in range(size - 1, 0, -1)
        )

    def taken(kernel, sent, dtype=None, last=False):
        found, *others = sent
        for part in others if last else others[:-1]:
            more = part.shape[0] if kernel is stack_kernel else part.shape[0] - WIDTH
            shape = (found.shape[0] + more,) + part.shape[1:]
            found = run(kernel, [like(shape, dtype or found.dtype)], (found, part))
        return (found,) if last else (found, others[-1])

    *sums, cols = run(
        sums_kernel,
        [like((WIDTH + cells, LANES), f32)] * span_x + [like((rows, depth), bf16)],
        (pltpu.with_memory_space_constraint(field, pltpu.HBM),),
        places=pltpu.HBM,
        flops=cube // 4,
        scratch=[chunked[0], parts, chunked[1]],
    )
    wv, wo, wq, wk, wz = run(
        prepare_kernel,
        [like((WIDTH, wide), f32)] * 2 + [like((2 * WIDTH, wide), bf16)] * 2
        + [like((2 * WIDTH, WIDTH), f32)],
        (w_value, w_out, qk_weight),
        flops=cube // 8,
    )
    total = run(
        add_kernel, [like((WIDTH + span_x * cells, LANES), f32)], swaps(sums, "gx", span_x)
    )
    totals = taken(add_kernel, swaps(total, "gy", span_y))
    mine = run(
        functools.partial(factor_kernel, grid_x * grid_y),
        [like((WIDTH + HEAD_DIM, LANES), f32)],
        totals,
    )
    mix, feat, full = run(
        functools.partial(plane_kernel, cells, span_x, lengths),
        [like((2, HEADS * cells, places), f32), like((8, places, WIDTH), f32),
         like((2, HEADS * places, places), f32)],
        totals + (same, qk_weight),
        flops=cube // 2,
    )
    send, both, feat_z = run(
        functools.partial(coef_kernel, span_x),
        [like((2 * cells, wide), bf16), like((2 * WIDTH, depth), bf16),
         like((WIDTH + HEAD_DIM, depth), f32)],
        swaps(mine, "gx", span_x) + (wz, cols, cots, wv, wo),
        flops=2 * cube,
        scratch=[pltpu.VMEM((span_x, WIDTH + HEAD_DIM, LANES), f32)],
    )
    (low,) = taken(stack_kernel, swaps(send, "gy", span_y), last=True)
    lows = swaps(low, "gx", span_x)
    pulled = like((WIDTH, depth), bf16)
    top, total = run(
        functools.partial(mix_kernel, factor_z, span_x),
        [like((2, cells, wide), f32), pulled],
        lows + (mix, wv, wo, wq, wk, cols, cots),
        flops=cube,
    )
    for level in range(span_x.bit_length() - 1):
        total = run(add_pull_kernel, [pulled], (total, swap(total, "gx", span_x, 1 << level)))
    layer_output = run(
        output_kernel, [like(field.shape, bf16)], (top, wo, both, cols), flops=cube
    )
    plane = run(
        functools.partial(gram_kernel, cells, lengths, factor_z),
        [like((cells, WIDTH), f32)],
        lows + (feat, full, same, qk_weight),
        flops=2 * cube,
    )
    base = run(base_kernel, [like((rows, depth), f32)], (top, wv, both, cots, plane), flops=cube)
    field_grad = run(
        functools.partial(final_kernel, grid_x * grid_y),
        [like(field.shape, bf16)],
        taken(add_pull_kernel, swaps(total, "gy", span_y), f32) + (feat_z, base),
        target=pltpu.HBM,
        scratch=chunked,
    )
    return (layer_output, field_grad)


def solution(mesh):
    placed = P(None, ("groups", "gx"), "gy", None)
    count = mesh.shape["gx"] * mesh.shape["gy"]

    def program(*arrays):
        _, grid_x, grid_y, depth = arrays[0].shape
        places = grid_x // mesh.shape["groups"] * grid_y
        small = places == LANES and places == 8 * count
        small = small and depth == LANES * mesh.shape["gx"] and count & (count - 1) == 0
        return jax.shard_map(
            per_device_kernels if small else per_device,
            mesh=mesh,
            in_specs=(placed, placed, P(), P(), P()),
            out_specs=(placed, placed),
            check_vma=False,
        )(*arrays)

    return program
```

```python
import functools
import math

import jax
import jax.numpy as jnp
import numpy as np
from jax import lax
from jax.experimental import pallas as pl
from jax.experimental.pallas import tpu as pltpu
from jax.sharding import PartitionSpec as P

WIDTH = 64
HEADS = 8
HEAD_DIM = 8
LANES = 128

EPSILON = 1e-06
PRECISE = lax.Precision.HIGHEST
AXES = ("gx", "gy")


def exchange(parts):
    return lax.all_to_all(parts, AXES, split_axis=0, concat_axis=0, tiled=True)


def swap(part, axis, size, step):
    return lax.ppermute(part, axis, [(i, i ^ step) for i in range(size)])


def gather(part, count):
    return exchange(jnp.broadcast_to(part[None], (count,) + part.shape))


def reduce_blocks(total, count):
    width, depth = total.shape
    blocks = total.reshape(width, depth // LANES, LANES).transpose(1, 0, 2)
    blocks = blocks.reshape(count, width * depth // LANES // count, LANES)
    mine = jnp.sum(exchange(blocks), axis=0)
    whole = gather(mine, count).reshape(depth // LANES, width, LANES)
    return whole.transpose(1, 0, 2).reshape(width, depth)


def axis_features(pooled, weights):
    inverse = lax.rsqrt(jnp.mean(pooled * pooled, axis=0, keepdims=True) + EPSILON)
    normed = pooled * inverse
    length = pooled.shape[1]
    factor = 1.0 / math.sqrt(HEAD_DIM * length)
    queries = jnp.dot(weights[0].T, normed, precision=PRECISE).reshape(HEADS, HEAD_DIM, length)
    keyset = jnp.dot(weights[1].T, normed, precision=PRECISE).reshape(HEADS, HEAD_DIM, length)
    return (normed, inverse, queries, keyset, factor)


def axis_kernel(queries, keyset, factor):
    scores = jnp.einsum("hdm,hdn->hmn", queries, keyset, precision=PRECISE)
    return (scores * factor).astype(jnp.bfloat16)


def kernel_backward(gram, queries, keyset, factor):
    grad_query = factor * jnp.einsum("hmn,hdn->hdm", gram, keyset, precision=PRECISE)
    grad_keyset = factor * jnp.einsum("hmn,hdm->hdn", gram, queries, precision=PRECISE)
    return (grad_query, grad_keyset)


def grad_of_normed(weights, grad_query, grad_keyset):
    length = grad_query.shape[-1]
    grad_normed = jnp.dot(weights[0], grad_query.reshape(WIDTH, length), precision=PRECISE)
    return grad_normed + jnp.dot(
        weights[1], grad_keyset.reshape(WIDTH, length), precision=PRECISE
    )


def pooled_grad(normed, inverse, grad_normed):
    return inverse * (grad_normed - normed * jnp.mean(grad_normed * normed, axis=0, keepdims=True))


def f32_einsum(pattern, left, right):
    return jnp.einsum(pattern, left, right, preferred_element_type=jnp.float32)


def per_device(field, cotangent, qk_weight, w_value, w_out):
    span_x = lax.axis_size("gx")
    span_y = lax.axis_size("gy")
    count = span_x * span_y
    rows_x, rows_y, depth = field.shape[1:]
    cells = rows_x * rows_y
    grid_x = rows_x * span_x
    grid_y = rows_y * span_y
    start_x = lax.axis_index("gx") * rows_x
    start_y = lax.axis_index("gy") * rows_y
    bf16 = jnp.bfloat16

    cols = field.reshape(WIDTH, cells, depth)
    cots = cotangent.reshape(WIDTH, cells, depth)

    sum_z = jnp.sum(cols, axis=1, dtype=jnp.float32)
    sum_rows = jnp.sum(cols, axis=2, dtype=jnp.float32)
    rows_all = gather(sum_rows.T, count).reshape(span_x, span_y, rows_x, rows_y, WIDTH)
    total_x = jnp.sum(rows_all, axis=(1, 3)).reshape(grid_x, WIDTH).T
    total_y = jnp.sum(rows_all, axis=(0, 2)).reshape(grid_y, WIDTH).T
    total_z = reduce_blocks(sum_z, count)

    normed_x, inverse_x, query_x, keyset_x, factor_x = axis_features(
        total_x / (grid_y * depth), qk_weight[0]
    )
    normed_y, inverse_y, query_y, keyset_y, factor_y = axis_features(
        total_y / (grid_x * depth), qk_weight[1]
    )
    normed_z, inverse_z, query_z, keyset_z, factor_z = axis_features(
        total_z / (grid_x * grid_y), qk_weight[2]
    )
    kernel_x = axis_kernel(query_x, keyset_x, factor_x)
    kernel_y = axis_kernel(query_y, keyset_y, factor_y)
    query_b = query_z.astype(bf16)
    keyset_b = keyset_z.astype(bf16)

    wv = w_value.reshape(WIDTH, HEADS, HEAD_DIM)
    wo = w_out.reshape(HEADS, HEAD_DIM, WIDTH)
    coef_f = f32_einsum("cpk,hgk->cphg", cols, keyset_b)
    coef_c = f32_einsum("cpz,hgz->cphg", cots, query_b)
    low_f = jnp.einsum("chd,cphg->phdg", wv.astype(jnp.float32), coef_f, precision=PRECISE)
    low_c = jnp.einsum("hdc,cphg->phdg", wo.astype(jnp.float32), coef_c, precision=PRECISE)
    squares = HEAD_DIM * HEAD_DIM
    both = jnp.stack([low_f, low_c]).astype(bf16).reshape(2, cells, HEADS * squares)
    both = gather(both, count).reshape(span_x, span_y, 2, rows_x, rows_y, HEADS * squares)
    both = both.transpose(2, 0, 3, 1, 4, 5).reshape(2, grid_x, grid_y, HEADS, squares)
    low_f, low_c = both[0], both[1]

    mid_f = f32_einsum("hyj,xjhq->xyhq", kernel_y, low_f).astype(bf16)
    top_f = f32_einsum("hxi,iyhq->xyhq", kernel_x, mid_f)
    mid_c = f32_einsum("hxi,xyhq->iyhq", kernel_x, low_c).astype(bf16)
    top_c = f32_einsum("hyj,xyhq->xjhq", kernel_y, mid_c)
    gram_x = factor_z * f32_einsum("myhq,nyhq->hmn", low_c, mid_f)
    gram_y = factor_z * f32_einsum("xmhq,xnhq->hmn", mid_c, low_f)

    def here(top):
        top = lax.dynamic_slice_in_dim(top, start_x, rows_x, 0)
        top = lax.dynamic_slice_in_dim(top, start_y, rows_y, 1)
        return top.reshape(cells, HEADS, HEAD_DIM, HEAD_DIM)

    left_f = factor_z * jnp.einsum(
        "hdc,phdg->cphg", wo.astype(jnp.float32), here(top_f), precision=PRECISE
    )
    left_c = factor_z * jnp.einsum(
        "chd,phdg->cphg", wv.astype(jnp.float32), here(top_c), precision=PRECISE
    )
    left_f = left_f.astype(bf16)
    left_c = left_c.astype(bf16)

    grad_query_z = f32_einsum("cphg,cpz->hgz", left_f, cots)
    grad_keyset_z = f32_einsum("cphg,cpz->hgz", left_c, cols)
    gn_z = reduce_blocks(grad_of_normed(qk_weight[2], grad_query_z, grad_keyset_z), count)

    layer_output = (cols.astype(jnp.float32) + f32_einsum("cphg,hgz->cpz", left_f, query_b)).astype(bf16)
    through = f32_einsum("cphg,hgz->cpz", left_c, keyset_b)

    gn_x = grad_of_normed(qk_weight[0], *kernel_backward(gram_x, query_x, keyset_x, factor_x))
    gn_y = grad_of_normed(qk_weight[1], *kernel_backward(gram_y, query_y, keyset_y, factor_y))
    pull_x = pooled_grad(normed_x, inverse_x, gn_x)
    pull_y = pooled_grad(normed_y, inverse_y, gn_y)
    pull_z = pooled_grad(normed_z, inverse_z, gn_z)
    local_x = lax.dynamic_slice_in_dim(pull_x, start_x, rows_x, 1) / (grid_y * depth)
    local_y = lax.dynamic_slice_in_dim(pull_y, start_y, rows_y, 1) / (grid_x * depth)
    local_xy = (local_x[:, :, None] + local_y[:, None, :]).reshape(WIDTH, cells)
    local_z = pull_z / (grid_x * grid_y)
    field_grad = (
        cots.astype(jnp.float32) + through + local_xy[:, :, None] + local_z[:, None, :]
    ).astype(bf16)
    return (layer_output.reshape(field.shape), field_grad.reshape(field.shape))


def split(x):
    high = x.astype(jnp.bfloat16)
    return high, (x - high.astype(jnp.float32)).astype(jnp.bfloat16)


NN = (((1,), (0,)), ((), ()))
NT = (((1,), (1,)), ((), ()))
TN = (((0,), (0,)), ((), ()))


def mul(left, right, dims=NN):
    return lax.dot_general(left, right, dims, preferred_element_type=jnp.float32)


def mul_near(left, right, dims=NN):
    left_high, left_low = split(left)
    right_high, right_low = split(right)
    return (
        mul(left_high, right_high, dims)
        + mul(left_low, right_high, dims)
        + mul(left_high, right_low, dims)
    )


def mul_left(left, right, dims=NN):
    rows = left.shape[0]
    both = mul(jnp.concatenate(split(left), axis=0), right, dims)
    return both[:rows] + both[rows:]


def number(shape, dim):
    return lax.broadcasted_iota(jnp.int32, shape, dim)


def join_quarters(part_ref, quarters):
    size = len(quarters)
    for step, quarter in zip([0, *range(size - 1, 0, -1)], quarters):
        part_ref[lax.axis_index("gx") ^ step] = quarter[...]
    return jnp.concatenate([part_ref[index] for index in range(part_ref.shape[0])], axis=1)


def expand(part):
    depth = part.shape[1]
    part = part.reshape(HEADS, 1, HEAD_DIM, depth)
    part = jnp.broadcast_to(part, (HEADS, HEAD_DIM, HEAD_DIM, depth))
    return part.reshape(WIDTH * HEAD_DIM, depth).astype(jnp.bfloat16)


def spread(weights, top):
    left = weights[:, None, :] * top[None]
    return left.reshape(-1, left.shape[2]).astype(jnp.bfloat16)


def prepare_kernel(wv_ref, wo_ref, qk_ref, wv_out, wo_out, wq_out, wk_out, wz_out):
    wide = HEADS * HEAD_DIM * HEAD_DIM
    row = number((WIDTH, wide), 0)
    lane = number((WIDTH, wide), 1)
    by_channel = ((lane >> 3) == row).astype(jnp.bfloat16)
    by_factor = (((lane >> 6) * HEAD_DIM + (lane & 7)) == row).astype(jnp.bfloat16)
    wv_out[...] = mul(wv_ref[...], by_channel)
    wo_out[...] = mul(wo_ref[...], by_channel, TN)
    for index, out in ((0, wq_out), (1, wk_out)):
        high, low = split(qk_ref[2, index])
        out[0:WIDTH, :] = mul(high, by_factor).astype(jnp.bfloat16)
        out[WIDTH : 2 * WIDTH, :] = mul(low, by_factor).astype(jnp.bfloat16)
        wz_out[index * WIDTH : (index + 1) * WIDTH, :] = qk_ref[2, index].T


def sums_kernel(field_ref, *refs):
    outs, (cols_ref, data_ref, part_ref, semaphores) = refs[:-4], refs[-4:]
    _, rows_x, rows_y, depth = data_ref.shape
    cells = rows_x * rows_y
    chunks = semaphores.shape[0]
    size = WIDTH // chunks
    copies = [
        pltpu.make_async_copy(
            field_ref.at[pl.ds(index * size, size)],
            data_ref.at[pl.ds(index * size, size)],
            semaphores.at[index],
        )
        for index in range(chunks)
    ]
    for copy in copies:
        copy.start()
    own = jnp.zeros((cells, LANES), jnp.float32)
    pick = number((size, size * cells), 1) // cells == number((size, size * cells), 0)
    pick = pick.astype(jnp.bfloat16)
    ones = jnp.ones((depth, LANES), jnp.bfloat16)
    for index, copy in enumerate(copies):
        copy.wait()
        rows = slice(index * size, (index + 1) * size)
        data = data_ref[rows].astype(jnp.float32)
        data = jnp.concatenate([data[:, at_x] for at_x in range(rows_x)], axis=1)
        data = data.reshape(size * cells, depth).astype(jnp.bfloat16)
        cols_ref[index * size * cells : (index + 1) * size * cells, :] = data
        part = mul(pick, data)
        for quarter in range(part_ref.shape[0]):
            part_ref[quarter, rows, :] = part[:, quarter * LANES : (quarter + 1) * LANES]
        row_sums = mul(data, ones).reshape(size, cells, LANES)
        shape = row_sums.shape
        mine = number(shape, 0) + index * size == number(shape, 2)
        own = own + jnp.sum(jnp.where(mine, row_sums, 0.0), axis=0)
    for step, out in enumerate(outs):
        out[0:WIDTH, :] = part_ref[lax.axis_index("gx") ^ step]
        out[WIDTH:, :] = own


def add_kernel(*refs):
    parts, out_ref = refs[:-1], refs[-1]
    total = parts[0][0:WIDTH, :]
    for part in parts[1:]:
        total = total + part[0:WIDTH, :]
    out_ref[0:WIDTH, :] = total
    start = WIDTH
    for part in parts:
        more = part.shape[0] - WIDTH
        out_ref[start : start + more, :] = part[WIDTH:, :]
        start += more


def stack_kernel(*refs):
    refs[-1][...] = jnp.concatenate([ref[...] for ref in refs[:-1]], axis=0)


def factor_kernel(places, *refs):
    parts, feat_ref = refs[:-1], refs[-1]
    total = parts[0][0:WIDTH, :]
    for part in parts[1:]:
        total = total + part[0:WIDTH, :]
    pooled = total * (1.0 / places)
    inverse = lax.rsqrt(jnp.mean(pooled * pooled, axis=0, keepdims=True) + EPSILON)
    normed = pooled * inverse
    feat_ref[0:WIDTH, :] = normed
    feat_ref[WIDTH:, :] = jnp.broadcast_to(inverse, (HEAD_DIM, LANES))


def add_pull_kernel(*refs):
    total = refs[0][...].astype(jnp.float32)
    for part in refs[1:-1]:
        total = total + part[...].astype(jnp.float32)
    refs[-1][...] = total.astype(refs[-1].dtype)


def by_head(part):
    shape = (HEADS, part.shape[0], WIDTH)
    mine = number(shape, 0) == (number(shape, 2) >> 3)
    return jnp.where(mine, part[None], 0.0).reshape(-1, WIDTH)


def plane_kernel(cells, span_x, lengths, *refs):
    parts, (same_ref, qk_ref, mix_ref, feat_ref, full_ref) = refs[:-5], refs[-5:]
    totals = jnp.concatenate(
        [
            part[WIDTH + step * cells : WIDTH + (step + 1) * cells, :]
            for first in range(span_x)
            for part in parts
            for step in range(first, (part.shape[0] - WIDTH) // cells, span_x)
        ],
        axis=0,
    )[:, :WIDTH]
    places = totals.shape[0]
    high, low = split(totals)
    forward = backward = None
    for axis in range(2):
        same = same_ref[axis]
        pooled = (mul(same, high) + mul(same, low)) * (1.0 / lengths[axis][1])
        inverse = lax.rsqrt(jnp.mean(pooled * pooled, axis=1, keepdims=True) + EPSILON)
        normed = pooled * inverse
        query = mul_near(normed, qk_ref[axis, 0])
        keyset = mul_near(normed, qk_ref[axis, 1])
        feat_ref[4 * axis] = normed
        feat_ref[4 * axis + 1] = query
        feat_ref[4 * axis + 2] = keyset
        feat_ref[4 * axis + 3] = jnp.broadcast_to(inverse, (places, WIDTH))
        factor = 1.0 / math.sqrt(HEAD_DIM * lengths[axis][0])

        def scores(rows, other):
            found = mul_near(by_head(rows), other, NT) * factor
            return found.astype(jnp.bfloat16).astype(jnp.float32)

        full = scores(query, keyset)
        full_ref[axis] = full
        one = full.reshape(HEADS, places, places)[:, :cells].reshape(-1, places)
        two = scores(keyset[:cells], query)
        forward = one if forward is None else forward * one
        backward = two if backward is None else backward * two
    mix_ref[0] = forward
    mix_ref[1] = backward


def coef_kernel(spans, *refs):
    quarters, refs = refs[:spans], refs[spans:]
    wz_ref, field_ref, cot_ref, wv_ref, wo_ref, send_ref, both_ref, feat_ref, part_ref = refs
    rows, depth = field_ref.shape
    cells = rows // WIDTH
    wide = HEADS * HEAD_DIM * HEAD_DIM
    feat = join_quarters(part_ref, quarters)
    feat_ref[...] = feat
    high, low = split(feat[:WIDTH])
    both = mul_left(wz_ref[...], high) + mul(wz_ref[...].astype(jnp.bfloat16), low)
    both_ref[...] = both.astype(jnp.bfloat16)
    query = expand(both[:WIDTH])
    keyset = expand(both[WIDTH:])
    low_f = mul(field_ref[...], keyset, NT).reshape(WIDTH, cells, wide)
    low_f = jnp.sum(wv_ref[...][:, None, :] * low_f, axis=0)
    low_c = mul(cot_ref[...], query, NT).reshape(WIDTH, cells, wide)
    low_c = jnp.sum(wo_ref[...][:, None, :] * low_c, axis=0)
    low = jnp.concatenate([low_f, low_c], axis=0).astype(jnp.bfloat16)
    send_ref[...] = low


def join_low(refs, cells):
    low = jnp.concatenate([ref[...].astype(jnp.float32) for ref in refs], axis=0)
    wide = low.shape[1]
    low = low.reshape(-1, 2 * cells, wide)
    return [
        low[:, start : start + cells].reshape(-1, wide).astype(jnp.bfloat16)
        for start in (0, cells)
    ]


def mix_kernel(factor, spans, *refs):
    lows, refs = refs[:spans], refs[spans:]
    mix_ref, wv_ref, wo_ref, wq_ref, wk_ref, field_ref, cot_ref, top_ref = refs[:8]
    mine_ref, other_ref, half_ref = refs[8:]
    cells = field_ref.shape[0] // WIDTH
    low_f, low_c = join_low(lows, cells)
    wide = low_f.shape[1]
    shape = (HEADS, cells, wide)
    head = number(shape, 0) == (number(shape, 2) >> 6)

    def top(mix, low):
        found = mul_left(mix, low).reshape(shape)
        return jnp.sum(jnp.where(head, found, 0.0), axis=0) * factor

    top_f = top(mix_ref[0], low_f)
    top_c = top(mix_ref[1], low_c)
    top_ref[0] = top_f
    top_ref[1] = top_c
    left_f = spread(wo_ref[...], top_f)
    left_c = spread(wv_ref[...], top_c)

    def pull(weights, left, right):
        found = mul(weights, left, NT)
        return mul_left(found[:WIDTH] + found[WIDTH:], right)

    found = pull(wq_ref[...], left_f, cot_ref[...]) + pull(wk_ref[...], left_c, field_ref[...])
    half = found.shape[1] // 2
    half_ref[0] = found[:, :half]
    half_ref[1] = found[:, half:]
    core = lax.axis_index("gx") & 1
    mine_ref[...] = half_ref[core].astype(jnp.bfloat16)
    other_ref[...] = half_ref[core ^ 1].astype(jnp.bfloat16)


def put_cells(ref, total):
    _, rows_x, rows_y, depth = ref.shape
    total = total.reshape(WIDTH, rows_x * rows_y, depth)
    for index in range(rows_x):
        rows = total[:, index * rows_y : (index + 1) * rows_y, :]
        ref[:, index, :, :] = rows.astype(jnp.bfloat16)


def output_kernel(top_ref, wo_ref, both_ref, field_ref, out_ref):
    query = expand(both_ref[...].astype(jnp.float32)[:WIDTH])
    left = spread(wo_ref[...], top_ref[0])
    put_cells(out_ref, mul(left, query) + field_ref[...].astype(jnp.float32))


def gram_kernel(cells, lengths, factor_z, *refs):
    lows, (feat_ref, full_ref, same_ref, qk_ref, out_ref) = refs[:-5], refs[-5:]
    low_f, low_c = join_low(lows, cells)
    places, wide = low_f.shape
    squares = HEAD_DIM * HEAD_DIM
    lane = number((places, LANES), 1)
    products = []
    for pair in range(wide // LANES):
        part_f = low_f[:, pair * LANES : (pair + 1) * LANES]
        part_c = low_c[:, pair * LANES : (pair + 1) * LANES]
        for half in range(LANES // squares):
            mine = (lane >> 6) == half
            products.append(mul(jnp.where(mine, part_c, jnp.zeros_like(part_c)), part_f, NT))
    product = jnp.concatenate(products, axis=0)
    factors = [1.0 / math.sqrt(HEAD_DIM * lengths[axis][0]) for axis in range(2)]
    queries = [by_head(feat_ref[4 * axis + 1]).astype(jnp.bfloat16) for axis in range(2)]
    keysets = [by_head(feat_ref[4 * axis + 2]).astype(jnp.bfloat16) for axis in range(2)]
    total = jnp.zeros((cells, WIDTH), jnp.float32)
    for axis in range(2):
        gram = (product * full_ref[1 - axis]).astype(jnp.bfloat16)
        across = jnp.concatenate(
            [gram[h * places : (h + 1) * places] for h in range(HEADS)], axis=1
        )
        scale = factors[axis] * factor_z
        grad_query = mul(across, keysets[axis]) * scale
        grad_keyset = mul(gram, queries[axis], TN) * scale
        found = mul_near(grad_query, qk_ref[axis, 0], NT) + mul_near(grad_keyset, qk_ref[axis, 1], NT)
        high, low = split(found)
        own = same_ref[axis, 0 : 2 * cells, :]
        found = (mul(own, high) + mul(own, low))[:cells]
        normed = feat_ref[4 * axis, 0:cells, :]
        inverse = feat_ref[4 * axis + 3, 0:cells, :]
        found = found - normed * jnp.mean(found * normed, axis=1, keepdims=True)
        total = total + inverse * found * (1.0 / lengths[axis][1])
    out_ref[...] = total


def base_kernel(top_ref, wv_ref, both_ref, cot_ref, plane_ref, out_ref):
    rows = cot_ref.shape[0]
    cells = rows // WIDTH
    shape = (WIDTH, cells, WIDTH)
    own = jnp.where(number(shape, 0) == number(shape, 2), plane_ref[...][None], 0.0)
    plane = mul_left(own.reshape(rows, WIDTH), jnp.ones((WIDTH, LANES), jnp.bfloat16))
    keyset = expand(both_ref[...].astype(jnp.float32)[WIDTH:])
    left = spread(wv_ref[...], top_ref[1])
    found = mul(left, keyset) + cot_ref[...].astype(jnp.float32)
    columns = found.shape[1] // LANES
    out_ref[...] = found + jnp.concatenate([plane] * columns, axis=1)


def final_kernel(places, mine_ref, other_ref, feat_ref, base_ref, out_ref, data_ref, half_ref, semaphores):
    depth = base_ref.shape[1]
    _, rows_x, rows_y, _ = data_ref.shape
    core = lax.axis_index("gx") & 1
    half_ref[core] = mine_ref[...]
    half_ref[core ^ 1] = other_ref[...]
    found = jnp.concatenate([half_ref[0], half_ref[1]], axis=1)
    normed = feat_ref[0:WIDTH, :]
    inverse = feat_ref[WIDTH : WIDTH + 1, :]
    found = inverse * (found - normed * jnp.mean(found * normed, axis=0, keepdims=True))
    found = found * (1.0 / places)
    cells = rows_x * rows_y
    chunks = semaphores.shape[0]
    size = WIDTH // chunks
    copies = []
    for index in range(chunks):
        rows = slice(index * size, (index + 1) * size)
        base = base_ref[index * size * cells : (index + 1) * size * cells, :]
        total = base.reshape(size, cells, depth) + found[rows][:, None, :]
        for at_x in range(rows_x):
            part = total[:, at_x * rows_y : (at_x + 1) * rows_y, :]
            data_ref[rows, at_x, :, :] = part.astype(jnp.bfloat16)
        copy = pltpu.make_async_copy(
            data_ref.at[pl.ds(index * size, size)],
            out_ref.at[pl.ds(index * size, size)],
            semaphores.at[index],
        )
        copy.start()
        copies.append(copy)
    for copy in copies:
        copy.wait()


def rows_kernel(cot_ref, rows_ref, data_ref, semaphores):
    _, rows_x, rows_y, depth = data_ref.shape
    cells = rows_x * rows_y
    chunks = semaphores.shape[0]
    size = WIDTH // chunks
    copies = [
        pltpu.make_async_copy(
            cot_ref.at[pl.ds(index * size, size)],
            data_ref.at[pl.ds(index * size, size)],
            semaphores.at[index],
        )
        for index in range(chunks)
    ]
    for copy in copies:
        copy.start()
    for index, copy in enumerate(copies):
        copy.wait()
        data = data_ref[index * size : (index + 1) * size].astype(jnp.float32)
        data = jnp.concatenate([data[:, at_x] for at_x in range(rows_x)], axis=1)
        data = data.reshape(size * cells, depth).astype(jnp.bfloat16)
        rows_ref[index * size * cells : (index + 1) * size * cells, :] = data


def run(kernel, outs, operands, places=pltpu.VMEM, target=pltpu.VMEM, flops=0, scratch=(),
        mebibytes=16):
    moved = sum(x.size * x.dtype.itemsize for x in tuple(operands) + tuple(outs))
    found = pl.pallas_call(
        kernel,
        out_shape=tuple(outs),
        in_specs=[pl.BlockSpec(memory_space=places)] * len(operands),
        out_specs=tuple(pl.BlockSpec(memory_space=target) for _ in outs),
        scratch_shapes=list(scratch),
        compiler_params=pltpu.CompilerParams(vmem_limit_bytes=mebibytes * 1024 * 1024),
        cost_estimate=pl.CostEstimate(flops=flops, bytes_accessed=moved, transcendentals=0),
    )(*operands)
    return found[0] if len(outs) == 1 else found


def per_device_kernels(field, cotangent, qk_weight, w_value, w_out):
    span_x = lax.axis_size("gx")
    span_y = lax.axis_size("gy")
    count = span_x * span_y
    rows_x, rows_y, depth = field.shape[1:]
    cells = rows_x * rows_y
    places = count * cells
    grid_x = rows_x * span_x
    grid_y = rows_y * span_y
    rows = WIDTH * cells
    wide = WIDTH * HEAD_DIM
    f32, bf16 = jnp.float32, jnp.bfloat16
    like = jax.ShapeDtypeStruct
    lengths = ((grid_x, grid_y * depth), (grid_y, grid_x * depth))

    cell = np.arange(places)
    at_x = cell // cells // span_y * rows_x + cell % cells // rows_y
    at_y = cell // cells % span_y * rows_y + cell % rows_y
    same = jnp.asarray(
        np.stack([at_x[:, None] == at_x[None], at_y[:, None] == at_y[None]]), dtype=bf16
    )

    parts = pltpu.VMEM((span_x, WIDTH, LANES), f32)
    chunked = [pltpu.VMEM(field.shape, bf16), pltpu.SemaphoreType.DMA((4,))]
    factor_z = 1.0 / math.sqrt(HEAD_DIM * depth)
    cube = rows * wide * depth * 2

    cots = run(
        rows_kernel,
        [like((rows, depth), bf16)],
        (pltpu.with_memory_space_constraint(cotangent, pltpu.HBM),),
        places=pltpu.HBM,
        flops=cube,
        scratch=chunked,
    )

    def swaps(sent, axis, size, farthest=True):
        if not isinstance(sent, (tuple, list)):
            sent = [sent] * size
        steps = range(size - 1, 0, -1)
        found = {}
        for step in steps if farthest else reversed(steps):
            found[step] = swap(sent[step], axis, size, step)
        return tuple(sent[:1]) + tuple(found[step] for step in steps)

    def taken(kernel, sent, dtype=None, last=False):
        found, *others = sent
        for part in others if last else others[:-1]:
            more = part.shape[0] if kernel is stack_kernel else part.shape[0] - WIDTH
            shape = (found.shape[0] + more,) + part.shape[1:]
            found = run(kernel, [like(shape, dtype or found.dtype)], (found, part))
        return (found,) if last else (found, others[-1])

    *sums, cols = run(
        sums_kernel,
        [like((WIDTH + cells, LANES), f32)] * span_x + [like((rows, depth), bf16)],
        (pltpu.with_memory_space_constraint(field, pltpu.HBM),),
        places=pltpu.HBM,
        flops=cube // 4,
        scratch=[chunked[0], parts, chunked[1]],
    )
    wv, wo, wq, wk, wz = run(
        prepare_kernel,
        [like((WIDTH, wide), f32)] * 2 + [like((2 * WIDTH, wide), bf16)] * 2
        + [like((2 * WIDTH, WIDTH), f32)],
        (w_value, w_out, qk_weight),
        flops=cube // 8,
    )
    total = run(
        add_kernel, [like((WIDTH + span_x * cells, LANES), f32)], swaps(sums, "gx", span_x)
    )
    totals = taken(add_kernel, swaps(total, "gy", span_y))
    mine = run(
        functools.partial(factor_kernel, grid_x * grid_y),
        [like((WIDTH + HEAD_DIM, LANES), f32)],
        totals,
    )
    mix, feat, full = run(
        functools.partial(plane_kernel, cells, span_x, lengths),
        [like((2, HEADS * cells, places), f32), like((8, places, WIDTH), f32),
         like((2, HEADS * places, places), f32)],
        totals + (same, qk_weight),
        flops=cube // 2,
    )
    send, both, feat_z = run(
        functools.partial(coef_kernel, span_x),
        [like((2 * cells, wide), bf16), like((2 * WIDTH, depth), bf16),
         like((WIDTH + HEAD_DIM, depth), f32)],
        swaps(mine, "gx", span_x, False) + (wz, cols, cots, wv, wo),
        flops=2 * cube,
        scratch=[pltpu.VMEM((span_x, WIDTH + HEAD_DIM, LANES), f32)],
    )
    (low,) = taken(stack_kernel, swaps(send, "gy", span_y), last=True)
    lows = swaps(low, "gx", span_x, False)
    pulled = like((WIDTH, depth // 2), bf16)
    halves = pltpu.VMEM((2, WIDTH, depth // 2), f32)
    top, mine, other = run(
        functools.partial(mix_kernel, factor_z, span_x),
        [like((2, cells, wide), f32), pulled, pulled],
        lows + (mix, wv, wo, wq, wk, cols, cots),
        flops=cube,
        scratch=[halves],
    )
    total = run(add_pull_kernel, [pulled], (mine, swap(other, "gx", span_x, 1)))
    for level in range(1, span_x.bit_length() - 1):
        total = run(add_pull_kernel, [pulled], (total, swap(total, "gx", span_x, 1 << level)))
    layer_output = run(
        output_kernel, [like(field.shape, bf16)], (top, wo, both, cols), flops=cube
    )
    total, layer_output = lax.optimization_barrier((total, layer_output))
    total = run(
        add_pull_kernel, [like(pulled.shape, f32)], swaps(total, "gy", span_y, False)
    )
    plane = run(
        functools.partial(gram_kernel, cells, lengths, factor_z),
        [like((cells, WIDTH), f32)],
        lows + (feat, full, same, qk_weight),
        flops=2 * cube,
    )
    base = run(base_kernel, [like((rows, depth), f32)], (top, wv, both, cots, plane), flops=cube)
    total, base = lax.optimization_barrier((total, base))
    other = swap(total, "gx", span_x, 1)
    field_grad = run(
        functools.partial(final_kernel, grid_x * grid_y),
        [like(field.shape, bf16)],
        (total, other, feat_z, base),
        target=pltpu.HBM,
        scratch=[chunked[0], halves, chunked[1]],
    )
    return (layer_output, field_grad)


def solution(mesh):
    placed = P(None, ("groups", "gx"), "gy", None)
    count = mesh.shape["gx"] * mesh.shape["gy"]

    def program(*arrays):
        _, grid_x, grid_y, depth = arrays[0].shape
        places = grid_x // mesh.shape["groups"] * grid_y
        small = places == LANES and places == 8 * count
        small = small and depth == LANES * mesh.shape["gx"] and count & (count - 1) == 0
        small = small and mesh.shape["gx"] > 1
        return jax.shard_map(
            per_device_kernels if small else per_device,
            mesh=mesh,
            in_specs=(placed, placed, P(), P(), P()),
            out_specs=(placed, placed),
            check_vma=False,
        )(*arrays)

    return program
```

```python
import functools
import math

import jax
import jax.numpy as jnp
import numpy as np
from jax import lax
from jax.experimental import pallas as pl
from jax.experimental.pallas import tpu as pltpu
from jax.sharding import PartitionSpec as P

WIDTH = 64
HEADS = 8
HEAD_DIM = 8
LANES = 128

EPSILON = 1e-06
PRECISE = lax.Precision.HIGHEST
AXES = ("gx", "gy")


def exchange(parts):
    return lax.all_to_all(parts, AXES, split_axis=0, concat_axis=0, tiled=True)


def swap(part, axis, size, step):
    return lax.ppermute(part, axis, [(i, i ^ step) for i in range(size)])


def gather(part, count):
    return exchange(jnp.broadcast_to(part[None], (count,) + part.shape))


def reduce_blocks(total, count):
    width, depth = total.shape
    blocks = total.reshape(width, depth // LANES, LANES).transpose(1, 0, 2)
    blocks = blocks.reshape(count, width * depth // LANES // count, LANES)
    mine = jnp.sum(exchange(blocks), axis=0)
    whole = gather(mine, count).reshape(depth // LANES, width, LANES)
    return whole.transpose(1, 0, 2).reshape(width, depth)


def axis_features(pooled, weights):
    inverse = lax.rsqrt(jnp.mean(pooled * pooled, axis=0, keepdims=True) + EPSILON)
    normed = pooled * inverse
    length = pooled.shape[1]
    factor = 1.0 / math.sqrt(HEAD_DIM * length)
    queries = jnp.dot(weights[0].T, normed, precision=PRECISE).reshape(HEADS, HEAD_DIM, length)
    keyset = jnp.dot(weights[1].T, normed, precision=PRECISE).reshape(HEADS, HEAD_DIM, length)
    return (normed, inverse, queries, keyset, factor)


def axis_kernel(queries, keyset, factor):
    scores = jnp.einsum("hdm,hdn->hmn", queries, keyset, precision=PRECISE)
    return (scores * factor).astype(jnp.bfloat16)


def kernel_backward(gram, queries, keyset, factor):
    grad_query = factor * jnp.einsum("hmn,hdn->hdm", gram, keyset, precision=PRECISE)
    grad_keyset = factor * jnp.einsum("hmn,hdm->hdn", gram, queries, precision=PRECISE)
    return (grad_query, grad_keyset)


def grad_of_normed(weights, grad_query, grad_keyset):
    length = grad_query.shape[-1]
    grad_normed = jnp.dot(weights[0], grad_query.reshape(WIDTH, length), precision=PRECISE)
    return grad_normed + jnp.dot(
        weights[1], grad_keyset.reshape(WIDTH, length), precision=PRECISE
    )


def pooled_grad(normed, inverse, grad_normed):
    return inverse * (grad_normed - normed * jnp.mean(grad_normed * normed, axis=0, keepdims=True))


def f32_einsum(pattern, left, right):
    return jnp.einsum(pattern, left, right, preferred_element_type=jnp.float32)


def per_device(field, cotangent, qk_weight, w_value, w_out):
    span_x = lax.axis_size("gx")
    span_y = lax.axis_size("gy")
    count = span_x * span_y
    rows_x, rows_y, depth = field.shape[1:]
    cells = rows_x * rows_y
    grid_x = rows_x * span_x
    grid_y = rows_y * span_y
    start_x = lax.axis_index("gx") * rows_x
    start_y = lax.axis_index("gy") * rows_y
    bf16 = jnp.bfloat16

    cols = field.reshape(WIDTH, cells, depth)
    cots = cotangent.reshape(WIDTH, cells, depth)

    sum_z = jnp.sum(cols, axis=1, dtype=jnp.float32)
    sum_rows = jnp.sum(cols, axis=2, dtype=jnp.float32)
    rows_all = gather(sum_rows.T, count).reshape(span_x, span_y, rows_x, rows_y, WIDTH)
    total_x = jnp.sum(rows_all, axis=(1, 3)).reshape(grid_x, WIDTH).T
    total_y = jnp.sum(rows_all, axis=(0, 2)).reshape(grid_y, WIDTH).T
    total_z = reduce_blocks(sum_z, count)

    normed_x, inverse_x, query_x, keyset_x, factor_x = axis_features(
        total_x / (grid_y * depth), qk_weight[0]
    )
    normed_y, inverse_y, query_y, keyset_y, factor_y = axis_features(
        total_y / (grid_x * depth), qk_weight[1]
    )
    normed_z, inverse_z, query_z, keyset_z, factor_z = axis_features(
        total_z / (grid_x * grid_y), qk_weight[2]
    )
    kernel_x = axis_kernel(query_x, keyset_x, factor_x)
    kernel_y = axis_kernel(query_y, keyset_y, factor_y)
    query_b = query_z.astype(bf16)
    keyset_b = keyset_z.astype(bf16)

    wv = w_value.reshape(WIDTH, HEADS, HEAD_DIM)
    wo = w_out.reshape(HEADS, HEAD_DIM, WIDTH)
    coef_f = f32_einsum("cpk,hgk->cphg", cols, keyset_b)
    coef_c = f32_einsum("cpz,hgz->cphg", cots, query_b)
    low_f = jnp.einsum("chd,cphg->phdg", wv.astype(jnp.float32), coef_f, precision=PRECISE)
    low_c = jnp.einsum("hdc,cphg->phdg", wo.astype(jnp.float32), coef_c, precision=PRECISE)
    squares = HEAD_DIM * HEAD_DIM
    both = jnp.stack([low_f, low_c]).astype(bf16).reshape(2, cells, HEADS * squares)
    both = gather(both, count).reshape(span_x, span_y, 2, rows_x, rows_y, HEADS * squares)
    both = both.transpose(2, 0, 3, 1, 4, 5).reshape(2, grid_x, grid_y, HEADS, squares)
    low_f, low_c = both[0], both[1]

    mid_f = f32_einsum("hyj,xjhq->xyhq", kernel_y, low_f).astype(bf16)
    top_f = f32_einsum("hxi,iyhq->xyhq", kernel_x, mid_f)
    mid_c = f32_einsum("hxi,xyhq->iyhq", kernel_x, low_c).astype(bf16)
    top_c = f32_einsum("hyj,xyhq->xjhq", kernel_y, mid_c)
    gram_x = factor_z * f32_einsum("myhq,nyhq->hmn", low_c, mid_f)
    gram_y = factor_z * f32_einsum("xmhq,xnhq->hmn", mid_c, low_f)

    def here(top):
        top = lax.dynamic_slice_in_dim(top, start_x, rows_x, 0)
        top = lax.dynamic_slice_in_dim(top, start_y, rows_y, 1)
        return top.reshape(cells, HEADS, HEAD_DIM, HEAD_DIM)

    left_f = factor_z * jnp.einsum(
        "hdc,phdg->cphg", wo.astype(jnp.float32), here(top_f), precision=PRECISE
    )
    left_c = factor_z * jnp.einsum(
        "chd,phdg->cphg", wv.astype(jnp.float32), here(top_c), precision=PRECISE
    )
    left_f = left_f.astype(bf16)
    left_c = left_c.astype(bf16)

    grad_query_z = f32_einsum("cphg,cpz->hgz", left_f, cots)
    grad_keyset_z = f32_einsum("cphg,cpz->hgz", left_c, cols)
    gn_z = reduce_blocks(grad_of_normed(qk_weight[2], grad_query_z, grad_keyset_z), count)

    layer_output = (cols.astype(jnp.float32) + f32_einsum("cphg,hgz->cpz", left_f, query_b)).astype(bf16)
    through = f32_einsum("cphg,hgz->cpz", left_c, keyset_b)

    gn_x = grad_of_normed(qk_weight[0], *kernel_backward(gram_x, query_x, keyset_x, factor_x))
    gn_y = grad_of_normed(qk_weight[1], *kernel_backward(gram_y, query_y, keyset_y, factor_y))
    pull_x = pooled_grad(normed_x, inverse_x, gn_x)
    pull_y = pooled_grad(normed_y, inverse_y, gn_y)
    pull_z = pooled_grad(normed_z, inverse_z, gn_z)
    local_x = lax.dynamic_slice_in_dim(pull_x, start_x, rows_x, 1) / (grid_y * depth)
    local_y = lax.dynamic_slice_in_dim(pull_y, start_y, rows_y, 1) / (grid_x * depth)
    local_xy = (local_x[:, :, None] + local_y[:, None, :]).reshape(WIDTH, cells)
    local_z = pull_z / (grid_x * grid_y)
    field_grad = (
        cots.astype(jnp.float32) + through + local_xy[:, :, None] + local_z[:, None, :]
    ).astype(bf16)
    return (layer_output.reshape(field.shape), field_grad.reshape(field.shape))


def split(x):
    high = x.astype(jnp.bfloat16)
    return high, (x - high.astype(jnp.float32)).astype(jnp.bfloat16)


NN = (((1,), (0,)), ((), ()))
NT = (((1,), (1,)), ((), ()))
TN = (((0,), (0,)), ((), ()))


def mul(left, right, dims=NN):
    return lax.dot_general(left, right, dims, preferred_element_type=jnp.float32)


def mul_near(left, right, dims=NN):
    left_high, left_low = split(left)
    right_high, right_low = split(right)
    return (
        mul(left_high, right_high, dims)
        + mul(left_low, right_high, dims)
        + mul(left_high, right_low, dims)
    )


def mul_left(left, right, dims=NN):
    rows = left.shape[0]
    both = mul(jnp.concatenate(split(left), axis=0), right, dims)
    return both[:rows] + both[rows:]


def number(shape, dim):
    return lax.broadcasted_iota(jnp.int32, shape, dim)


def join_halves(half_ref, mine_ref, other_ref):
    core = lax.axis_index("gx") & 1
    half_ref[core] = mine_ref[...]
    half_ref[core ^ 1] = other_ref[...]
    return jnp.concatenate([half_ref[0], half_ref[1]], axis=1)


def expand(part):
    depth = part.shape[1]
    part = part.reshape(HEADS, 1, HEAD_DIM, depth)
    part = jnp.broadcast_to(part, (HEADS, HEAD_DIM, HEAD_DIM, depth))
    return part.reshape(WIDTH * HEAD_DIM, depth).astype(jnp.bfloat16)


def spread(weights, top):
    left = weights[:, None, :] * top[None]
    return left.reshape(-1, left.shape[2]).astype(jnp.bfloat16)


def prepare_kernel(wv_ref, wo_ref, qk_ref, wv_out, wo_out, wq_out, wk_out, wz_out):
    wide = HEADS * HEAD_DIM * HEAD_DIM
    row = number((WIDTH, wide), 0)
    lane = number((WIDTH, wide), 1)
    by_channel = ((lane >> 3) == row).astype(jnp.bfloat16)
    by_factor = (((lane >> 6) * HEAD_DIM + (lane & 7)) == row).astype(jnp.bfloat16)
    wv_out[...] = mul(wv_ref[...], by_channel)
    wo_out[...] = mul(wo_ref[...], by_channel, TN)
    for index, out in ((0, wq_out), (1, wk_out)):
        high, low = split(qk_ref[2, index])
        out[0:WIDTH, :] = mul(high, by_factor).astype(jnp.bfloat16)
        out[WIDTH : 2 * WIDTH, :] = mul(low, by_factor).astype(jnp.bfloat16)
        wz_out[index * WIDTH : (index + 1) * WIDTH, :] = qk_ref[2, index].T


def sums_kernel(field_ref, *refs):
    outs, (cols_ref, data_ref, half_ref, semaphores) = refs[:-4], refs[-4:]
    _, rows_x, rows_y, depth = data_ref.shape
    cells = rows_x * rows_y
    chunks = semaphores.shape[0]
    size = WIDTH // chunks
    copies = [
        pltpu.make_async_copy(
            field_ref.at[pl.ds(index * size, size)],
            data_ref.at[pl.ds(index * size, size)],
            semaphores.at[index],
        )
        for index in range(chunks)
    ]
    for copy in copies:
        copy.start()
    own = jnp.zeros((cells, LANES), jnp.float32)
    pick = number((size, size * cells), 1) // cells == number((size, size * cells), 0)
    pick = pick.astype(jnp.bfloat16)
    ones = jnp.ones((depth, LANES), jnp.bfloat16)
    for index, copy in enumerate(copies):
        copy.wait()
        rows = slice(index * size, (index + 1) * size)
        data = data_ref[rows].astype(jnp.float32)
        data = jnp.concatenate([data[:, at_x] for at_x in range(rows_x)], axis=1)
        data = data.reshape(size * cells, depth).astype(jnp.bfloat16)
        cols_ref[index * size * cells : (index + 1) * size * cells, :] = data
        part = mul(pick, data)
        half_ref[0, rows, :] = part[:, : depth // 2]
        half_ref[1, rows, :] = part[:, depth // 2 :]
        row_sums = mul(data, ones).reshape(size, cells, LANES)
        shape = row_sums.shape
        mine = number(shape, 0) + index * size == number(shape, 2)
        own = own + jnp.sum(jnp.where(mine, row_sums, 0.0), axis=0)
    for step, out in enumerate(outs):
        out[0:WIDTH, :] = half_ref[(lax.axis_index("gx") & 1) ^ step]
        out[WIDTH:, :] = jnp.concatenate([own] * (depth // 2 // LANES), axis=1)


def add_kernel(*refs):
    parts, out_ref = refs[:-1], refs[-1]
    total = parts[0][0:WIDTH, :]
    for part in parts[1:]:
        total = total + part[0:WIDTH, :]
    out_ref[0:WIDTH, :] = total
    start = WIDTH
    for part in parts:
        more = part.shape[0] - WIDTH
        out_ref[start : start + more, :] = part[WIDTH:, :]
        start += more


def add_core_kernel(mine_ref, other_ref, out_ref):
    out_ref[0:WIDTH, :] = mine_ref[0:WIDTH, :] + other_ref[0:WIDTH, :]
    out_ref[WIDTH:, 0:LANES] = mine_ref[WIDTH:, 0:LANES]
    out_ref[WIDTH:, LANES : 2 * LANES] = other_ref[WIDTH:, 0:LANES]


def stack_kernel(*refs):
    refs[-1][...] = jnp.concatenate([ref[...] for ref in refs[:-1]], axis=0)


def factor_kernel(places, *refs):
    parts, feat_ref = refs[:-1], refs[-1]
    total = parts[0][0:WIDTH, :]
    for part in parts[1:]:
        total = total + part[0:WIDTH, :]
    pooled = total * (1.0 / places)
    inverse = lax.rsqrt(jnp.mean(pooled * pooled, axis=0, keepdims=True) + EPSILON)
    normed = pooled * inverse
    feat_ref[0:WIDTH, :] = normed
    feat_ref[WIDTH:, :] = jnp.broadcast_to(inverse, (HEAD_DIM, inverse.shape[1]))


def add_pull_kernel(*refs):
    total = refs[0][...].astype(jnp.float32)
    for part in refs[1:-1]:
        total = total + part[...].astype(jnp.float32)
    refs[-1][...] = total.astype(refs[-1].dtype)


def by_head(part):
    shape = (HEADS, part.shape[0], WIDTH)
    mine = number(shape, 0) == (number(shape, 2) >> 3)
    return jnp.where(mine, part[None], 0.0).reshape(-1, WIDTH)


def plane_kernel(cells, span_x, lengths, *refs):
    parts, (same_ref, qk_ref, mix_ref, feat_ref, full_ref) = refs[:-5], refs[-5:]
    chips = span_x // 2
    totals = jnp.concatenate(
        [
            part[WIDTH + step * cells : WIDTH + (step + 1) * cells, core * LANES : core * LANES + WIDTH]
            for chip in range(chips)
            for core in range(2)
            for part in parts
            for step in range(chip, (part.shape[0] - WIDTH) // cells, chips)
        ],
        axis=0,
    )
    places = totals.shape[0]
    high, low = split(totals)
    forward = backward = None
    for axis in range(2):
        same = same_ref[axis]
        pooled = (mul(same, high) + mul(same, low)) * (1.0 / lengths[axis][1])
        inverse = lax.rsqrt(jnp.mean(pooled * pooled, axis=1, keepdims=True) + EPSILON)
        normed = pooled * inverse
        query = mul_near(normed, qk_ref[axis, 0])
        keyset = mul_near(normed, qk_ref[axis, 1])
        feat_ref[4 * axis] = normed
        feat_ref[4 * axis + 1] = query
        feat_ref[4 * axis + 2] = keyset
        feat_ref[4 * axis + 3] = jnp.broadcast_to(inverse, (places, WIDTH))
        factor = 1.0 / math.sqrt(HEAD_DIM * lengths[axis][0])

        def scores(rows, other):
            found = mul_near(by_head(rows), other, NT) * factor
            return found.astype(jnp.bfloat16).astype(jnp.float32)

        full = scores(query, keyset)
        full_ref[axis] = full
        one = full.reshape(HEADS, places, places)[:, :cells].reshape(-1, places)
        two = scores(keyset[:cells], query)
        forward = one if forward is None else forward * one
        backward = two if backward is None else backward * two
    mix_ref[0] = forward
    mix_ref[1] = backward


def coef_kernel(mine_ref, other_ref, wz_ref, field_ref, cot_ref, wv_ref, wo_ref,
                send_ref, both_ref, feat_ref, half_ref):
    rows, depth = field_ref.shape
    cells = rows // WIDTH
    wide = HEADS * HEAD_DIM * HEAD_DIM
    feat = join_halves(half_ref, mine_ref, other_ref)
    feat_ref[...] = feat
    high, low = split(feat[:WIDTH])
    both = mul_left(wz_ref[...], high) + mul(wz_ref[...].astype(jnp.bfloat16), low)
    both_ref[...] = both.astype(jnp.bfloat16)
    query = expand(both[:WIDTH])
    keyset = expand(both[WIDTH:])
    low_f = mul(field_ref[...], keyset, NT).reshape(WIDTH, cells, wide)
    low_f = jnp.sum(wv_ref[...][:, None, :] * low_f, axis=0)
    low_c = mul(cot_ref[...], query, NT).reshape(WIDTH, cells, wide)
    low_c = jnp.sum(wo_ref[...][:, None, :] * low_c, axis=0)
    low = jnp.concatenate([low_f, low_c], axis=0).astype(jnp.bfloat16)
    send_ref[...] = low


def join_low(refs, cells):
    low = jnp.concatenate([ref[...].astype(jnp.float32) for ref in refs], axis=0)
    wide = low.shape[1]
    low = low.reshape(-1, 2 * cells, wide)
    return [
        low[:, start : start + cells].reshape(-1, wide).astype(jnp.bfloat16)
        for start in (0, cells)
    ]


def mix_kernel(factor, spans, *refs):
    lows, refs = refs[:spans], refs[spans:]
    mix_ref, wv_ref, wo_ref, wq_ref, wk_ref, field_ref, cot_ref, top_ref = refs[:8]
    mine_ref, other_ref, half_ref = refs[8:]
    cells = field_ref.shape[0] // WIDTH
    low_f, low_c = join_low(lows, cells)
    wide = low_f.shape[1]
    shape = (HEADS, cells, wide)
    head = number(shape, 0) == (number(shape, 2) >> 6)

    def top(mix, low):
        found = mul_left(mix, low).reshape(shape)
        return jnp.sum(jnp.where(head, found, 0.0), axis=0) * factor

    top_f = top(mix_ref[0], low_f)
    top_c = top(mix_ref[1], low_c)
    top_ref[0] = top_f
    top_ref[1] = top_c
    left_f = spread(wo_ref[...], top_f)
    left_c = spread(wv_ref[...], top_c)

    def pull(weights, left, right):
        found = mul(weights, left, NT)
        return mul_left(found[:WIDTH] + found[WIDTH:], right)

    found = pull(wq_ref[...], left_f, cot_ref[...]) + pull(wk_ref[...], left_c, field_ref[...])
    half = found.shape[1] // 2
    half_ref[0] = found[:, :half]
    half_ref[1] = found[:, half:]
    core = lax.axis_index("gx") & 1
    mine_ref[...] = half_ref[core].astype(jnp.bfloat16)
    other_ref[...] = half_ref[core ^ 1].astype(jnp.bfloat16)


def put_cells(ref, total):
    _, rows_x, rows_y, depth = ref.shape
    total = total.reshape(WIDTH, rows_x * rows_y, depth)
    for index in range(rows_x):
        rows = total[:, index * rows_y : (index + 1) * rows_y, :]
        ref[:, index, :, :] = rows.astype(jnp.bfloat16)


def output_kernel(top_ref, wo_ref, both_ref, field_ref, out_ref):
    query = expand(both_ref[...].astype(jnp.float32)[:WIDTH])
    left = spread(wo_ref[...], top_ref[0])
    put_cells(out_ref, mul(left, query) + field_ref[...].astype(jnp.float32))


def gram_kernel(cells, lengths, factor_z, *refs):
    lows, (feat_ref, full_ref, same_ref, qk_ref, out_ref) = refs[:-5], refs[-5:]
    low_f, low_c = join_low(lows, cells)
    places, wide = low_f.shape
    squares = HEAD_DIM * HEAD_DIM
    lane = number((places, LANES), 1)
    products = []
    for pair in range(wide // LANES):
        part_f = low_f[:, pair * LANES : (pair + 1) * LANES]
        part_c = low_c[:, pair * LANES : (pair + 1) * LANES]
        for half in range(LANES // squares):
            mine = (lane >> 6) == half
            products.append(mul(jnp.where(mine, part_c, jnp.zeros_like(part_c)), part_f, NT))
    product = jnp.concatenate(products, axis=0)
    factors = [1.0 / math.sqrt(HEAD_DIM * lengths[axis][0]) for axis in range(2)]
    queries = [by_head(feat_ref[4 * axis + 1]).astype(jnp.bfloat16) for axis in range(2)]
    keysets = [by_head(feat_ref[4 * axis + 2]).astype(jnp.bfloat16) for axis in range(2)]
    total = jnp.zeros((cells, WIDTH), jnp.float32)
    for axis in range(2):
        gram = (product * full_ref[1 - axis]).astype(jnp.bfloat16)
        across = jnp.concatenate(
            [gram[h * places : (h + 1) * places] for h in range(HEADS)], axis=1
        )
        scale = factors[axis] * factor_z
        grad_query = mul(across, keysets[axis]) * scale
        grad_keyset = mul(gram, queries[axis], TN) * scale
        found = mul_near(grad_query, qk_ref[axis, 0], NT) + mul_near(grad_keyset, qk_ref[axis, 1], NT)
        high, low = split(found)
        own = same_ref[axis, 0 : 2 * cells, :]
        found = (mul(own, high) + mul(own, low))[:cells]
        normed = feat_ref[4 * axis, 0:cells, :]
        inverse = feat_ref[4 * axis + 3, 0:cells, :]
        found = found - normed * jnp.mean(found * normed, axis=1, keepdims=True)
        total = total + inverse * found * (1.0 / lengths[axis][1])
    shape = (WIDTH, cells, WIDTH)
    own = jnp.where(number(shape, 0) == number(shape, 2), total[None], 0.0)
    out_ref[...] = mul_left(own.reshape(-1, WIDTH), jnp.ones((WIDTH, LANES), jnp.bfloat16))


def base_kernel(top_ref, wv_ref, both_ref, cot_ref, out_ref):
    keyset = expand(both_ref[...].astype(jnp.float32)[WIDTH:])
    left = spread(wv_ref[...], top_ref[1])
    out_ref[...] = mul(left, keyset) + cot_ref[...].astype(jnp.float32)


def final_kernel(places, mine_ref, other_ref, feat_ref, base_ref, plane_ref, out_ref, data_ref,
                 half_ref, semaphores):
    depth = base_ref.shape[1]
    _, rows_x, rows_y, _ = data_ref.shape
    found = join_halves(half_ref, mine_ref, other_ref)
    normed = feat_ref[0:WIDTH, :]
    inverse = feat_ref[WIDTH : WIDTH + 1, :]
    found = inverse * (found - normed * jnp.mean(found * normed, axis=0, keepdims=True))
    found = found * (1.0 / places)
    cells = rows_x * rows_y
    chunks = semaphores.shape[0]
    size = WIDTH // chunks
    copies = []
    for index in range(chunks):
        rows = slice(index * size, (index + 1) * size)
        base = base_ref[index * size * cells : (index + 1) * size * cells, :]
        plane = plane_ref[index * size * cells : (index + 1) * size * cells, :]
        base = base + jnp.concatenate([plane] * (depth // LANES), axis=1)
        total = base.reshape(size, cells, depth) + found[rows][:, None, :]
        for at_x in range(rows_x):
            part = total[:, at_x * rows_y : (at_x + 1) * rows_y, :]
            data_ref[rows, at_x, :, :] = part.astype(jnp.bfloat16)
        copy = pltpu.make_async_copy(
            data_ref.at[pl.ds(index * size, size)],
            out_ref.at[pl.ds(index * size, size)],
            semaphores.at[index],
        )
        copy.start()
        copies.append(copy)
    for copy in copies:
        copy.wait()


def rows_kernel(cot_ref, rows_ref, data_ref, semaphores):
    _, rows_x, rows_y, depth = data_ref.shape
    cells = rows_x * rows_y
    chunks = semaphores.shape[0]
    size = WIDTH // chunks
    copies = [
        pltpu.make_async_copy(
            cot_ref.at[pl.ds(index * size, size)],
            data_ref.at[pl.ds(index * size, size)],
            semaphores.at[index],
        )
        for index in range(chunks)
    ]
    for copy in copies:
        copy.start()
    for index, copy in enumerate(copies):
        copy.wait()
        data = data_ref[index * size : (index + 1) * size].astype(jnp.float32)
        data = jnp.concatenate([data[:, at_x] for at_x in range(rows_x)], axis=1)
        data = data.reshape(size * cells, depth).astype(jnp.bfloat16)
        rows_ref[index * size * cells : (index + 1) * size * cells, :] = data


def run(kernel, outs, operands, places=pltpu.VMEM, target=pltpu.VMEM, flops=0, scratch=(),
        mebibytes=16):
    moved = sum(x.size * x.dtype.itemsize for x in tuple(operands) + tuple(outs))
    found = pl.pallas_call(
        kernel,
        out_shape=tuple(outs),
        in_specs=[pl.BlockSpec(memory_space=places)] * len(operands),
        out_specs=tuple(pl.BlockSpec(memory_space=target) for _ in outs),
        scratch_shapes=list(scratch),
        compiler_params=pltpu.CompilerParams(vmem_limit_bytes=mebibytes * 1024 * 1024),
        cost_estimate=pl.CostEstimate(flops=flops, bytes_accessed=moved, transcendentals=0),
    )(*operands)
    return found[0] if len(outs) == 1 else found


def per_device_kernels(field, cotangent, qk_weight, w_value, w_out):
    span_x = lax.axis_size("gx")
    span_y = lax.axis_size("gy")
    count = span_x * span_y
    rows_x, rows_y, depth = field.shape[1:]
    cells = rows_x * rows_y
    places = count * cells
    grid_x = rows_x * span_x
    grid_y = rows_y * span_y
    rows = WIDTH * cells
    wide = WIDTH * HEAD_DIM
    f32, bf16 = jnp.float32, jnp.bfloat16
    like = jax.ShapeDtypeStruct
    lengths = ((grid_x, grid_y * depth), (grid_y, grid_x * depth))

    cell = np.arange(places)
    at_x = cell // cells // span_y * rows_x + cell % cells // rows_y
    at_y = cell // cells % span_y * rows_y + cell % rows_y
    same = jnp.asarray(
        np.stack([at_x[:, None] == at_x[None], at_y[:, None] == at_y[None]]), dtype=bf16
    )

    half = depth // 2
    halves = pltpu.VMEM((2, WIDTH, half), f32)
    chunked = [pltpu.VMEM(field.shape, bf16), pltpu.SemaphoreType.DMA((4,))]
    factor_z = 1.0 / math.sqrt(HEAD_DIM * depth)
    cube = rows * wide * depth * 2

    cots = run(
        rows_kernel,
        [like((rows, depth), bf16)],
        (pltpu.with_memory_space_constraint(cotangent, pltpu.HBM),),
        places=pltpu.HBM,
        flops=cube,
        scratch=chunked,
    )

    def swaps(sent, axis, size, farthest=True):
        if not isinstance(sent, (tuple, list)):
            sent = [sent] * size
        steps = range(size - 1, 0, -1)
        found = {}
        for step in steps if farthest else reversed(steps):
            found[step] = swap(sent[step], axis, size, step)
        return tuple(sent[:1]) + tuple(found[step] for step in steps)

    def taken(kernel, sent, dtype=None, last=False):
        found, *others = sent
        for part in others if last else others[:-1]:
            more = part.shape[0] if kernel is stack_kernel else part.shape[0] - WIDTH
            shape = (found.shape[0] + more,) + part.shape[1:]
            found = run(kernel, [like(shape, dtype or found.dtype)], (found, part))
        return (found,) if last else (found, others[-1])

    *sums, cols = run(
        sums_kernel,
        [like((WIDTH + cells, half), f32)] * 2 + [like((rows, depth), bf16)],
        (pltpu.with_memory_space_constraint(field, pltpu.HBM),),
        places=pltpu.HBM,
        flops=cube // 4,
        scratch=[chunked[0], halves, chunked[1]],
    )
    wv, wo, wq, wk, wz = run(
        prepare_kernel,
        [like((WIDTH, wide), f32)] * 2 + [like((2 * WIDTH, wide), bf16)] * 2
        + [like((2 * WIDTH, WIDTH), f32)],
        (w_value, w_out, qk_weight),
        flops=cube // 8,
    )
    total = run(
        add_core_kernel,
        [like((WIDTH + cells, half), f32)],
        (sums[0], swap(sums[1], "gx", span_x, 1)),
    )
    for level in range(1, span_x.bit_length() - 1):
        (total,) = taken(add_kernel, (total, swap(total, "gx", span_x, 1 << level)), last=True)
    totals = taken(add_kernel, swaps(total, "gy", span_y))
    totals, cots, wz = lax.optimization_barrier((totals, cots, wz))
    mine = run(
        functools.partial(factor_kernel, grid_x * grid_y),
        [like((WIDTH + HEAD_DIM, half), f32)],
        totals,
    )
    mix, feat, full = run(
        functools.partial(plane_kernel, cells, span_x, lengths),
        [like((2, HEADS * cells, places), f32), like((8, places, WIDTH), f32),
         like((2, HEADS * places, places), f32)],
        totals + (same, qk_weight),
        flops=cube // 2,
    )
    send, both, feat_z = run(
        coef_kernel,
        [like((2 * cells, wide), bf16), like((2 * WIDTH, depth), bf16),
         like((WIDTH + HEAD_DIM, depth), f32)],
        (mine, swap(mine, "gx", span_x, 1), wz, cols, cots, wv, wo),
        flops=2 * cube,
        scratch=[pltpu.VMEM((2, WIDTH + HEAD_DIM, half), f32)],
    )
    (low,) = taken(stack_kernel, swaps(send, "gy", span_y), last=True)
    first, *others = swaps(low, "gx", span_x, False)
    lows = (first,) + tuple(reversed(others))
    pulled = like((WIDTH, half), bf16)
    top, mine, other = run(
        functools.partial(mix_kernel, factor_z, span_x),
        [like((2, cells, wide), f32), pulled, pulled],
        lows + (mix, wv, wo, wq, wk, cols, cots),
        flops=cube,
        scratch=[halves],
    )
    total = run(add_pull_kernel, [pulled], (mine, swap(other, "gx", span_x, 1)))
    base = run(base_kernel, [like((rows, depth), f32)], (top, wv, both, cots), flops=cube)
    total, base = lax.optimization_barrier((total, base))
    for level in range(1, span_x.bit_length() - 1):
        total = run(add_pull_kernel, [pulled], (total, swap(total, "gx", span_x, 1 << level)))
    layer_output = run(
        output_kernel, [like(field.shape, bf16)], (top, wo, both, cols), flops=cube
    )
    plane = run(
        functools.partial(gram_kernel, cells, lengths, factor_z),
        [like((rows, LANES), f32)],
        lows + (feat, full, same, qk_weight),
        flops=2 * cube,
    )
    total, layer_output, plane = lax.optimization_barrier((total, layer_output, plane))
    total = run(
        add_pull_kernel, [like(pulled.shape, f32)], swaps(total, "gy", span_y, False)
    )
    field_grad = run(
        functools.partial(final_kernel, grid_x * grid_y),
        [like(field.shape, bf16)],
        (total, swap(total, "gx", span_x, 1), feat_z, base, plane),
        target=pltpu.HBM,
        scratch=[chunked[0], halves, chunked[1]],
    )
    return (layer_output, field_grad)


def solution(mesh):
    placed = P(None, ("groups", "gx"), "gy", None)
    count = mesh.shape["gx"] * mesh.shape["gy"]

    def program(*arrays):
        _, grid_x, grid_y, depth = arrays[0].shape
        places = grid_x // mesh.shape["groups"] * grid_y
        small = places == LANES and places == 8 * count
        small = small and depth == LANES * mesh.shape["gx"] and count & (count - 1) == 0
        small = small and mesh.shape["gx"] > 3
        return jax.shard_map(
            per_device_kernels if small else per_device,
            mesh=mesh,
            in_specs=(placed, placed, P(), P(), P()),
            out_specs=(placed, placed),
            check_vma=False,
        )(*arrays)

    return program
```

```python
import functools
import math

import jax
import jax.numpy as jnp
import numpy as np
from jax import lax
from jax.experimental import pallas as pl
from jax.experimental.pallas import tpu as pltpu
from jax.sharding import PartitionSpec as P

WIDTH = 64
HEADS = 8
HEAD_DIM = 8
LANES = 128

EPSILON = 1e-06
PRECISE = lax.Precision.HIGHEST
AXES = ("gx", "gy")


def exchange(parts):
    return lax.all_to_all(parts, AXES, split_axis=0, concat_axis=0, tiled=True)


def swap(part, axis, size, step):
    return lax.ppermute(part, axis, [(i, i ^ step) for i in range(size)])


def gather(part, count):
    return exchange(jnp.broadcast_to(part[None], (count,) + part.shape))


def reduce_blocks(total, count):
    width, depth = total.shape
    blocks = total.reshape(width, depth // LANES, LANES).transpose(1, 0, 2)
    blocks = blocks.reshape(count, width * depth // LANES // count, LANES)
    mine = jnp.sum(exchange(blocks), axis=0)
    whole = gather(mine, count).reshape(depth // LANES, width, LANES)
    return whole.transpose(1, 0, 2).reshape(width, depth)


def axis_features(pooled, weights):
    inverse = lax.rsqrt(jnp.mean(pooled * pooled, axis=0, keepdims=True) + EPSILON)
    normed = pooled * inverse
    length = pooled.shape[1]
    factor = 1.0 / math.sqrt(HEAD_DIM * length)
    queries = jnp.dot(weights[0].T, normed, precision=PRECISE).reshape(HEADS, HEAD_DIM, length)
    keyset = jnp.dot(weights[1].T, normed, precision=PRECISE).reshape(HEADS, HEAD_DIM, length)
    return (normed, inverse, queries, keyset, factor)


def axis_kernel(queries, keyset, factor):
    scores = jnp.einsum("hdm,hdn->hmn", queries, keyset, precision=PRECISE)
    return (scores * factor).astype(jnp.bfloat16)


def kernel_backward(gram, queries, keyset, factor):
    grad_query = factor * jnp.einsum("hmn,hdn->hdm", gram, keyset, precision=PRECISE)
    grad_keyset = factor * jnp.einsum("hmn,hdm->hdn", gram, queries, precision=PRECISE)
    return (grad_query, grad_keyset)


def grad_of_normed(weights, grad_query, grad_keyset):
    length = grad_query.shape[-1]
    grad_normed = jnp.dot(weights[0], grad_query.reshape(WIDTH, length), precision=PRECISE)
    return grad_normed + jnp.dot(
        weights[1], grad_keyset.reshape(WIDTH, length), precision=PRECISE
    )


def pooled_grad(normed, inverse, grad_normed):
    return inverse * (grad_normed - normed * jnp.mean(grad_normed * normed, axis=0, keepdims=True))


def f32_einsum(pattern, left, right):
    return jnp.einsum(pattern, left, right, preferred_element_type=jnp.float32)


def per_device(field, cotangent, qk_weight, w_value, w_out):
    span_x = lax.axis_size("gx")
    span_y = lax.axis_size("gy")
    count = span_x * span_y
    rows_x, rows_y, depth = field.shape[1:]
    cells = rows_x * rows_y
    grid_x = rows_x * span_x
    grid_y = rows_y * span_y
    start_x = lax.axis_index("gx") * rows_x
    start_y = lax.axis_index("gy") * rows_y
    bf16 = jnp.bfloat16

    cols = field.reshape(WIDTH, cells, depth)
    cots = cotangent.reshape(WIDTH, cells, depth)

    sum_z = jnp.sum(cols, axis=1, dtype=jnp.float32)
    sum_rows = jnp.sum(cols, axis=2, dtype=jnp.float32)
    rows_all = gather(sum_rows.T, count).reshape(span_x, span_y, rows_x, rows_y, WIDTH)
    total_x = jnp.sum(rows_all, axis=(1, 3)).reshape(grid_x, WIDTH).T
    total_y = jnp.sum(rows_all, axis=(0, 2)).reshape(grid_y, WIDTH).T
    total_z = reduce_blocks(sum_z, count)

    normed_x, inverse_x, query_x, keyset_x, factor_x = axis_features(
        total_x / (grid_y * depth), qk_weight[0]
    )
    normed_y, inverse_y, query_y, keyset_y, factor_y = axis_features(
        total_y / (grid_x * depth), qk_weight[1]
    )
    normed_z, inverse_z, query_z, keyset_z, factor_z = axis_features(
        total_z / (grid_x * grid_y), qk_weight[2]
    )
    kernel_x = axis_kernel(query_x, keyset_x, factor_x)
    kernel_y = axis_kernel(query_y, keyset_y, factor_y)
    query_b = query_z.astype(bf16)
    keyset_b = keyset_z.astype(bf16)

    wv = w_value.reshape(WIDTH, HEADS, HEAD_DIM)
    wo = w_out.reshape(HEADS, HEAD_DIM, WIDTH)
    coef_f = f32_einsum("cpk,hgk->cphg", cols, keyset_b)
    coef_c = f32_einsum("cpz,hgz->cphg", cots, query_b)
    low_f = jnp.einsum("chd,cphg->phdg", wv.astype(jnp.float32), coef_f, precision=PRECISE)
    low_c = jnp.einsum("hdc,cphg->phdg", wo.astype(jnp.float32), coef_c, precision=PRECISE)
    squares = HEAD_DIM * HEAD_DIM
    both = jnp.stack([low_f, low_c]).astype(bf16).reshape(2, cells, HEADS * squares)
    both = gather(both, count).reshape(span_x, span_y, 2, rows_x, rows_y, HEADS * squares)
    both = both.transpose(2, 0, 3, 1, 4, 5).reshape(2, grid_x, grid_y, HEADS, squares)
    low_f, low_c = both[0], both[1]

    mid_f = f32_einsum("hyj,xjhq->xyhq", kernel_y, low_f).astype(bf16)
    top_f = f32_einsum("hxi,iyhq->xyhq", kernel_x, mid_f)
    mid_c = f32_einsum("hxi,xyhq->iyhq", kernel_x, low_c).astype(bf16)
    top_c = f32_einsum("hyj,xyhq->xjhq", kernel_y, mid_c)
    gram_x = factor_z * f32_einsum("myhq,nyhq->hmn", low_c, mid_f)
    gram_y = factor_z * f32_einsum("xmhq,xnhq->hmn", mid_c, low_f)

    def here(top):
        top = lax.dynamic_slice_in_dim(top, start_x, rows_x, 0)
        top = lax.dynamic_slice_in_dim(top, start_y, rows_y, 1)
        return top.reshape(cells, HEADS, HEAD_DIM, HEAD_DIM)

    left_f = factor_z * jnp.einsum(
        "hdc,phdg->cphg", wo.astype(jnp.float32), here(top_f), precision=PRECISE
    )
    left_c = factor_z * jnp.einsum(
        "chd,phdg->cphg", wv.astype(jnp.float32), here(top_c), precision=PRECISE
    )
    left_f = left_f.astype(bf16)
    left_c = left_c.astype(bf16)

    grad_query_z = f32_einsum("cphg,cpz->hgz", left_f, cots)
    grad_keyset_z = f32_einsum("cphg,cpz->hgz", left_c, cols)
    gn_z = reduce_blocks(grad_of_normed(qk_weight[2], grad_query_z, grad_keyset_z), count)

    layer_output = (cols.astype(jnp.float32) + f32_einsum("cphg,hgz->cpz", left_f, query_b)).astype(bf16)
    through = f32_einsum("cphg,hgz->cpz", left_c, keyset_b)

    gn_x = grad_of_normed(qk_weight[0], *kernel_backward(gram_x, query_x, keyset_x, factor_x))
    gn_y = grad_of_normed(qk_weight[1], *kernel_backward(gram_y, query_y, keyset_y, factor_y))
    pull_x = pooled_grad(normed_x, inverse_x, gn_x)
    pull_y = pooled_grad(normed_y, inverse_y, gn_y)
    pull_z = pooled_grad(normed_z, inverse_z, gn_z)
    local_x = lax.dynamic_slice_in_dim(pull_x, start_x, rows_x, 1) / (grid_y * depth)
    local_y = lax.dynamic_slice_in_dim(pull_y, start_y, rows_y, 1) / (grid_x * depth)
    local_xy = (local_x[:, :, None] + local_y[:, None, :]).reshape(WIDTH, cells)
    local_z = pull_z / (grid_x * grid_y)
    field_grad = (
        cots.astype(jnp.float32) + through + local_xy[:, :, None] + local_z[:, None, :]
    ).astype(bf16)
    return (layer_output.reshape(field.shape), field_grad.reshape(field.shape))


def split(x):
    high = x.astype(jnp.bfloat16)
    return high, (x - high.astype(jnp.float32)).astype(jnp.bfloat16)


NN = (((1,), (0,)), ((), ()))
NT = (((1,), (1,)), ((), ()))
TN = (((0,), (0,)), ((), ()))


def mul(left, right, dims=NN):
    return lax.dot_general(left, right, dims, preferred_element_type=jnp.float32)


def mul_near(left, right, dims=NN):
    left_high, left_low = split(left)
    right_high, right_low = split(right)
    return (
        mul(left_high, right_high, dims)
        + mul(left_low, right_high, dims)
        + mul(left_high, right_low, dims)
    )


def mul_left(left, right, dims=NN):
    rows = left.shape[0]
    both = mul(jnp.concatenate(split(left), axis=0), right, dims)
    return both[:rows] + both[rows:]


def number(shape, dim):
    return lax.broadcasted_iota(jnp.int32, shape, dim)


def join_halves(half_ref, mine_ref, other_ref):
    core = lax.axis_index("gx") & 1
    half_ref[core] = mine_ref[...]
    half_ref[core ^ 1] = other_ref[...]
    return jnp.concatenate([half_ref[0], half_ref[1]], axis=1)


def expand(part):
    depth = part.shape[1]
    part = part.reshape(HEADS, 1, HEAD_DIM, depth)
    part = jnp.broadcast_to(part, (HEADS, HEAD_DIM, HEAD_DIM, depth))
    return part.reshape(WIDTH * HEAD_DIM, depth).astype(jnp.bfloat16)


def spread(weights, top):
    left = weights[:, None, :] * top[None]
    return left.reshape(-1, left.shape[2]).astype(jnp.bfloat16)


def prepare_kernel(wv_ref, wo_ref, qk_ref, wv_out, wo_out, wq_out, wk_out, wz_out):
    wide = HEADS * HEAD_DIM * HEAD_DIM
    row = number((WIDTH, wide), 0)
    lane = number((WIDTH, wide), 1)
    by_channel = ((lane >> 3) == row).astype(jnp.bfloat16)
    by_factor = (((lane >> 6) * HEAD_DIM + (lane & 7)) == row).astype(jnp.bfloat16)
    wv_out[...] = mul(wv_ref[...], by_channel)
    wo_out[...] = mul(wo_ref[...], by_channel, TN)
    for index, out in ((0, wq_out), (1, wk_out)):
        high, low = split(qk_ref[2, index])
        out[0:WIDTH, :] = mul(high, by_factor).astype(jnp.bfloat16)
        out[WIDTH : 2 * WIDTH, :] = mul(low, by_factor).astype(jnp.bfloat16)
        wz_out[index * WIDTH : (index + 1) * WIDTH, :] = qk_ref[2, index].T


def sums_kernel(field_ref, *refs):
    outs, (cols_ref, data_ref, half_ref, semaphores) = refs[:-4], refs[-4:]
    _, rows_x, rows_y, depth = data_ref.shape
    cells = rows_x * rows_y
    chunks = semaphores.shape[0]
    size = WIDTH // chunks
    copies = [
        pltpu.make_async_copy(
            field_ref.at[pl.ds(index * size, size)],
            data_ref.at[pl.ds(index * size, size)],
            semaphores.at[index],
        )
        for index in range(chunks)
    ]
    for copy in copies:
        copy.start()
    own = jnp.zeros((cells, LANES), jnp.float32)
    pick = number((size, size * cells), 1) // cells == number((size, size * cells), 0)
    pick = pick.astype(jnp.bfloat16)
    ones = jnp.ones((depth, LANES), jnp.bfloat16)
    for index, copy in enumerate(copies):
        copy.wait()
        rows = slice(index * size, (index + 1) * size)
        data = data_ref[rows].astype(jnp.float32)
        data = jnp.concatenate([data[:, at_x] for at_x in range(rows_x)], axis=1)
        data = data.reshape(size * cells, depth).astype(jnp.bfloat16)
        cols_ref[index * size * cells : (index + 1) * size * cells, :] = data
        part = mul(pick, data)
        half_ref[0, rows, :] = part[:, : depth // 2]
        half_ref[1, rows, :] = part[:, depth // 2 :]
        row_sums = mul(data, ones).reshape(size, cells, LANES)
        shape = row_sums.shape
        mine = number(shape, 0) + index * size == number(shape, 2)
        own = own + jnp.sum(jnp.where(mine, row_sums, 0.0), axis=0)
    for step, out in enumerate(outs):
        out[0:WIDTH, :] = half_ref[(lax.axis_index("gx") & 1) ^ step]
        out[WIDTH:, :] = jnp.concatenate([own] * (depth // 2 // LANES), axis=1)


def add_kernel(*refs):
    parts, out_ref = refs[:-1], refs[-1]
    total = parts[0][0:WIDTH, :]
    for part in parts[1:]:
        total = total + part[0:WIDTH, :]
    out_ref[0:WIDTH, :] = total
    start = WIDTH
    for part in parts:
        more = part.shape[0] - WIDTH
        out_ref[start : start + more, :] = part[WIDTH:, :]
        start += more


def add_beside_kernel(known, mine_ref, other_ref, out_ref):
    out_ref[0:WIDTH, :] = mine_ref[0:WIDTH, :] + other_ref[0:WIDTH, :]
    lanes = known * WIDTH
    rest = out_ref.shape[1] - 2 * lanes
    rows = [mine_ref[WIDTH:, 0:lanes], other_ref[WIDTH:, 0:lanes]]
    if rest > 0:
        rows.append(jnp.zeros((rows[0].shape[0], rest), jnp.float32))
    out_ref[WIDTH:, :] = jnp.concatenate(rows, axis=1)


def stack_kernel(*refs):
    refs[-1][...] = jnp.concatenate([ref[...] for ref in refs[:-1]], axis=0)


def factor_kernel(places, *refs):
    parts, feat_ref = refs[:-1], refs[-1]
    total = parts[0][0:WIDTH, :]
    for part in parts[1:]:
        total = total + part[0:WIDTH, :]
    pooled = total * (1.0 / places)
    inverse = lax.rsqrt(jnp.mean(pooled * pooled, axis=0, keepdims=True) + EPSILON)
    normed = pooled * inverse
    feat_ref[0:WIDTH, :] = normed
    feat_ref[WIDTH:, :] = jnp.broadcast_to(inverse, (HEAD_DIM, inverse.shape[1]))


def add_pull_kernel(*refs):
    total = refs[0][...].astype(jnp.float32)
    for part in refs[1:-1]:
        total = total + part[...].astype(jnp.float32)
    refs[-1][...] = total.astype(refs[-1].dtype)


def by_head(part):
    shape = (HEADS, part.shape[0], WIDTH)
    mine = number(shape, 0) == (number(shape, 2) >> 3)
    return jnp.where(mine, part[None], 0.0).reshape(-1, WIDTH)


def plane_kernel(cells, span_x, lengths, *refs):
    parts, (same_ref, qk_ref, mix_ref, feat_ref, full_ref) = refs[:-5], refs[-5:]
    totals = jnp.concatenate(
        [
            part[start : start + cells, step * WIDTH : (step + 1) * WIDTH]
            for step in range(span_x)
            for part in parts
            for start in range(WIDTH, part.shape[0], cells)
        ],
        axis=0,
    )
    places = totals.shape[0]
    high, low = split(totals)
    forward = backward = None
    for axis in range(2):
        same = same_ref[axis]
        pooled = (mul(same, high) + mul(same, low)) * (1.0 / lengths[axis][1])
        inverse = lax.rsqrt(jnp.mean(pooled * pooled, axis=1, keepdims=True) + EPSILON)
        normed = pooled * inverse
        query = mul_near(normed, qk_ref[axis, 0])
        keyset = mul_near(normed, qk_ref[axis, 1])
        feat_ref[4 * axis] = normed
        feat_ref[4 * axis + 1] = query
        feat_ref[4 * axis + 2] = keyset
        feat_ref[4 * axis + 3] = jnp.broadcast_to(inverse, (places, WIDTH))
        factor = 1.0 / math.sqrt(HEAD_DIM * lengths[axis][0])

        def scores(rows, other):
            found = mul_near(by_head(rows), other, NT) * factor
            return found.astype(jnp.bfloat16).astype(jnp.float32)

        full = scores(query, keyset)
        full_ref[axis] = full
        one = full.reshape(HEADS, places, places)[:, :cells].reshape(-1, places)
        two = scores(keyset[:cells], query)
        forward = one if forward is None else forward * one
        backward = two if backward is None else backward * two
    mix_ref[0] = forward
    mix_ref[1] = backward


def coef_kernel(mine_ref, other_ref, wz_ref, field_ref, cot_ref, wv_ref, wo_ref,
                send_ref, both_ref, feat_ref, half_ref):
    rows, depth = field_ref.shape
    cells = rows // WIDTH
    wide = HEADS * HEAD_DIM * HEAD_DIM
    feat = join_halves(half_ref, mine_ref, other_ref)
    feat_ref[...] = feat
    high, low = split(feat[:WIDTH])
    both = mul_left(wz_ref[...], high) + mul(wz_ref[...].astype(jnp.bfloat16), low)
    both_ref[...] = both.astype(jnp.bfloat16)
    query = expand(both[:WIDTH])
    keyset = expand(both[WIDTH:])
    low_f = mul(field_ref[...], keyset, NT).reshape(WIDTH, cells, wide)
    low_f = jnp.sum(wv_ref[...][:, None, :] * low_f, axis=0)
    low_c = mul(cot_ref[...], query, NT).reshape(WIDTH, cells, wide)
    low_c = jnp.sum(wo_ref[...][:, None, :] * low_c, axis=0)
    low = jnp.concatenate([low_f, low_c], axis=0).astype(jnp.bfloat16)
    send_ref[...] = low


def join_low(refs, cells):
    low = jnp.concatenate([ref[...].astype(jnp.float32) for ref in refs], axis=0)
    wide = low.shape[1]
    low = low.reshape(-1, 2 * cells, wide)
    return [
        low[:, start : start + cells].reshape(-1, wide).astype(jnp.bfloat16)
        for start in (0, cells)
    ]


def mix_kernel(factor, spans, *refs):
    lows, refs = refs[:spans], refs[spans:]
    mix_ref, wv_ref, wo_ref, wq_ref, wk_ref, field_ref, cot_ref, top_ref, out_ref = refs
    cells = field_ref.shape[0] // WIDTH
    low_f, low_c = join_low(lows, cells)
    wide = low_f.shape[1]
    shape = (HEADS, cells, wide)
    head = number(shape, 0) == (number(shape, 2) >> 6)

    def top(mix, low):
        found = mul_left(mix, low).reshape(shape)
        return jnp.sum(jnp.where(head, found, 0.0), axis=0) * factor

    top_f = top(mix_ref[0], low_f)
    top_c = top(mix_ref[1], low_c)
    top_ref[0] = top_f
    top_ref[1] = top_c
    left_f = spread(wo_ref[...], top_f)
    left_c = spread(wv_ref[...], top_c)

    def pull(weights, left, right):
        found = mul(weights, left, NT)
        return mul_left(found[:WIDTH] + found[WIDTH:], right)

    found = pull(wq_ref[...], left_f, cot_ref[...]) + pull(wk_ref[...], left_c, field_ref[...])
    out_ref[...] = found.astype(jnp.bfloat16)


def put_cells(ref, total):
    _, rows_x, rows_y, depth = ref.shape
    total = total.reshape(WIDTH, rows_x * rows_y, depth)
    for index in range(rows_x):
        rows = total[:, index * rows_y : (index + 1) * rows_y, :]
        ref[:, index, :, :] = rows.astype(jnp.bfloat16)


def output_kernel(top_ref, wo_ref, both_ref, field_ref, out_ref):
    query = expand(both_ref[...].astype(jnp.float32)[:WIDTH])
    left = spread(wo_ref[...], top_ref[0])
    put_cells(out_ref, mul(left, query) + field_ref[...].astype(jnp.float32))


def gram_kernel(cells, lengths, factor_z, *refs):
    lows, (feat_ref, full_ref, same_ref, qk_ref, out_ref) = refs[:-5], refs[-5:]
    low_f, low_c = join_low(lows, cells)
    places, wide = low_f.shape
    squares = HEAD_DIM * HEAD_DIM
    lane = number((places, LANES), 1)
    products = []
    for pair in range(wide // LANES):
        part_f = low_f[:, pair * LANES : (pair + 1) * LANES]
        part_c = low_c[:, pair * LANES : (pair + 1) * LANES]
        for half in range(LANES // squares):
            mine = (lane >> 6) == half
            products.append(mul(jnp.where(mine, part_c, jnp.zeros_like(part_c)), part_f, NT))
    product = jnp.concatenate(products, axis=0)
    factors = [1.0 / math.sqrt(HEAD_DIM * lengths[axis][0]) for axis in range(2)]
    queries = [by_head(feat_ref[4 * axis + 1]).astype(jnp.bfloat16) for axis in range(2)]
    keysets = [by_head(feat_ref[4 * axis + 2]).astype(jnp.bfloat16) for axis in range(2)]
    total = jnp.zeros((cells, WIDTH), jnp.float32)
    for axis in range(2):
        gram = (product * full_ref[1 - axis]).astype(jnp.bfloat16)
        across = jnp.concatenate(
            [gram[h * places : (h + 1) * places] for h in range(HEADS)], axis=1
        )
        scale = factors[axis] * factor_z
        grad_query = mul(across, keysets[axis]) * scale
        grad_keyset = mul(gram, queries[axis], TN) * scale
        found = mul_near(grad_query, qk_ref[axis, 0], NT) + mul_near(grad_keyset, qk_ref[axis, 1], NT)
        high, low = split(found)
        own = same_ref[axis, 0 : 2 * cells, :]
        found = (mul(own, high) + mul(own, low))[:cells]
        normed = feat_ref[4 * axis, 0:cells, :]
        inverse = feat_ref[4 * axis + 3, 0:cells, :]
        found = found - normed * jnp.mean(found * normed, axis=1, keepdims=True)
        total = total + inverse * found * (1.0 / lengths[axis][1])
    shape = (WIDTH, cells, WIDTH)
    own = jnp.where(number(shape, 0) == number(shape, 2), total[None], 0.0)
    out_ref[...] = mul_left(own.reshape(-1, WIDTH), jnp.ones((WIDTH, LANES), jnp.bfloat16))


def base_kernel(top_ref, wv_ref, both_ref, cot_ref, out_ref):
    keyset = expand(both_ref[...].astype(jnp.float32)[WIDTH:])
    left = spread(wv_ref[...], top_ref[1])
    out_ref[...] = mul(left, keyset) + cot_ref[...].astype(jnp.float32)


def final_kernel(places, *refs):
    parts, refs = refs[:-6], refs[-6:]
    feat_ref, base_ref, plane_ref, out_ref, data_ref, semaphores = refs
    depth = base_ref.shape[1]
    _, rows_x, rows_y, _ = data_ref.shape
    found = parts[0][...].astype(jnp.float32)
    for part in parts[1:]:
        found = found + part[...].astype(jnp.float32)
    normed = feat_ref[0:WIDTH, :]
    inverse = feat_ref[WIDTH : WIDTH + 1, :]
    found = inverse * (found - normed * jnp.mean(found * normed, axis=0, keepdims=True))
    found = found * (1.0 / places)
    cells = rows_x * rows_y
    chunks = semaphores.shape[0]
    size = WIDTH // chunks
    copies = []
    for index in range(chunks):
        rows = slice(index * size, (index + 1) * size)
        base = base_ref[index * size * cells : (index + 1) * size * cells, :]
        plane = plane_ref[index * size * cells : (index + 1) * size * cells, :]
        base = base + jnp.concatenate([plane] * (depth // LANES), axis=1)
        total = base.reshape(size, cells, depth) + found[rows][:, None, :]
        for at_x in range(rows_x):
            part = total[:, at_x * rows_y : (at_x + 1) * rows_y, :]
            data_ref[rows, at_x, :, :] = part.astype(jnp.bfloat16)
        copy = pltpu.make_async_copy(
            data_ref.at[pl.ds(index * size, size)],
            out_ref.at[pl.ds(index * size, size)],
            semaphores.at[index],
        )
        copy.start()
        copies.append(copy)
    for copy in copies:
        copy.wait()


def rows_kernel(cot_ref, rows_ref, data_ref, semaphores):
    _, rows_x, rows_y, depth = data_ref.shape
    cells = rows_x * rows_y
    chunks = semaphores.shape[0]
    size = WIDTH // chunks
    copies = [
        pltpu.make_async_copy(
            cot_ref.at[pl.ds(index * size, size)],
            data_ref.at[pl.ds(index * size, size)],
            semaphores.at[index],
        )
        for index in range(chunks)
    ]
    for copy in copies:
        copy.start()
    for index, copy in enumerate(copies):
        copy.wait()
        data = data_ref[index * size : (index + 1) * size].astype(jnp.float32)
        data = jnp.concatenate([data[:, at_x] for at_x in range(rows_x)], axis=1)
        data = data.reshape(size * cells, depth).astype(jnp.bfloat16)
        rows_ref[index * size * cells : (index + 1) * size * cells, :] = data


def run(kernel, outs, operands, places=pltpu.VMEM, target=pltpu.VMEM, flops=0, scratch=(),
        mebibytes=16):
    moved = sum(x.size * x.dtype.itemsize for x in tuple(operands) + tuple(outs))
    found = pl.pallas_call(
        kernel,
        out_shape=tuple(outs),
        in_specs=[pl.BlockSpec(memory_space=places)] * len(operands),
        out_specs=tuple(pl.BlockSpec(memory_space=target) for _ in outs),
        scratch_shapes=list(scratch),
        compiler_params=pltpu.CompilerParams(vmem_limit_bytes=mebibytes * 1024 * 1024),
        cost_estimate=pl.CostEstimate(flops=flops, bytes_accessed=moved, transcendentals=0),
    )(*operands)
    return found[0] if len(outs) == 1 else found


def per_device_kernels(field, cotangent, qk_weight, w_value, w_out):
    span_x = lax.axis_size("gx")
    span_y = lax.axis_size("gy")
    count = span_x * span_y
    rows_x, rows_y, depth = field.shape[1:]
    cells = rows_x * rows_y
    places = count * cells
    grid_x = rows_x * span_x
    grid_y = rows_y * span_y
    rows = WIDTH * cells
    wide = WIDTH * HEAD_DIM
    f32, bf16 = jnp.float32, jnp.bfloat16
    like = jax.ShapeDtypeStruct
    lengths = ((grid_x, grid_y * depth), (grid_y, grid_x * depth))

    cell = np.arange(places)
    at_x = cell // cells // span_y * rows_x + cell % cells // rows_y
    at_y = cell // cells % span_y * rows_y + cell % rows_y
    same = jnp.asarray(
        np.stack([at_x[:, None] == at_x[None], at_y[:, None] == at_y[None]]), dtype=bf16
    )

    half = depth // 2
    halves = pltpu.VMEM((2, WIDTH, half), f32)
    chunked = [pltpu.VMEM(field.shape, bf16), pltpu.SemaphoreType.DMA((4,))]
    factor_z = 1.0 / math.sqrt(HEAD_DIM * depth)
    cube = rows * wide * depth * 2

    cots = run(
        rows_kernel,
        [like((rows, depth), bf16)],
        (pltpu.with_memory_space_constraint(cotangent, pltpu.HBM),),
        places=pltpu.HBM,
        flops=cube,
        scratch=chunked,
    )

    def swaps(sent, axis, size, farthest=True):
        if not isinstance(sent, (tuple, list)):
            sent = [sent] * size
        steps = range(size - 1, 0, -1)
        found = {}
        for step in steps if farthest else reversed(steps):
            found[step] = swap(sent[step], axis, size, step)
        return tuple(sent[:1]) + tuple(found[step] for step in steps)

    def taken(kernel, sent, dtype=None, last=False):
        found, *others = sent
        for part in others if last else others[:-1]:
            more = part.shape[0] if kernel is stack_kernel else part.shape[0] - WIDTH
            shape = (found.shape[0] + more,) + part.shape[1:]
            found = run(kernel, [like(shape, dtype or found.dtype)], (found, part))
        return (found,) if last else (found, others[-1])

    *sums, cols = run(
        sums_kernel,
        [like((WIDTH + cells, half), f32)] * 2 + [like((rows, depth), bf16)],
        (pltpu.with_memory_space_constraint(field, pltpu.HBM),),
        places=pltpu.HBM,
        flops=cube // 4,
        scratch=[chunked[0], halves, chunked[1]],
    )
    wv, wo, wq, wk, wz = run(
        prepare_kernel,
        [like((WIDTH, wide), f32)] * 2 + [like((2 * WIDTH, wide), bf16)] * 2
        + [like((2 * WIDTH, WIDTH), f32)],
        (w_value, w_out, qk_weight),
        flops=cube // 8,
    )
    total, other = sums
    for level in range(span_x.bit_length() - 1):
        step = 1 << level
        total = run(
            functools.partial(add_beside_kernel, step),
            [like((WIDTH + cells, half), f32)],
            (total, swap(total if level else other, "gx", span_x, step)),
        )
    totals = taken(add_kernel, swaps(total, "gy", span_y))
    totals, cots, wz = lax.optimization_barrier((totals, cots, wz))
    mine = run(
        functools.partial(factor_kernel, grid_x * grid_y),
        [like((WIDTH + HEAD_DIM, half), f32)],
        totals,
    )
    mix, feat, full = run(
        functools.partial(plane_kernel, cells, span_x, lengths),
        [like((2, HEADS * cells, places), f32), like((8, places, WIDTH), f32),
         like((2, HEADS * places, places), f32)],
        totals + (same, qk_weight),
        flops=cube // 2,
    )
    send, both, feat_z = run(
        coef_kernel,
        [like((2 * cells, wide), bf16), like((2 * WIDTH, depth), bf16),
         like((WIDTH + HEAD_DIM, depth), f32)],
        (mine, swap(mine, "gx", span_x, 1), wz, cols, cots, wv, wo),
        flops=2 * cube,
        scratch=[pltpu.VMEM((2, WIDTH + HEAD_DIM, half), f32)],
    )
    (low,) = taken(stack_kernel, swaps(send, "gy", span_y), last=True)
    first, *others = swaps(low, "gx", span_x, False)
    lows = (first,) + tuple(reversed(others))
    pulled = like((WIDTH, depth), bf16)
    top, total = run(
        functools.partial(mix_kernel, factor_z, span_x),
        [like((2, cells, wide), f32), pulled],
        lows + (mix, wv, wo, wq, wk, cols, cots),
        flops=cube,
    )
    total = run(add_pull_kernel, [pulled], (total, swap(total, "gx", span_x, 1)))
    base = run(base_kernel, [like((rows, depth), f32)], (top, wv, both, cots), flops=cube)
    total, base = lax.optimization_barrier((total, base))
    for level in range(1, span_x.bit_length() - 1):
        total = run(add_pull_kernel, [pulled], (total, swap(total, "gx", span_x, 1 << level)))
    layer_output = run(
        output_kernel, [like(field.shape, bf16)], (top, wo, both, cols), flops=cube
    )
    plane = run(
        functools.partial(gram_kernel, cells, lengths, factor_z),
        [like((rows, LANES), f32)],
        lows + (feat, full, same, qk_weight),
        flops=2 * cube,
    )
    total, layer_output, plane = lax.optimization_barrier((total, layer_output, plane))
    field_grad = run(
        functools.partial(final_kernel, grid_x * grid_y),
        [like(field.shape, bf16)],
        swaps(total, "gy", span_y, False) + (feat_z, base, plane),
        target=pltpu.HBM,
        scratch=chunked,
    )
    return (layer_output, field_grad)


def solution(mesh):
    placed = P(None, ("groups", "gx"), "gy", None)
    count = mesh.shape["gx"] * mesh.shape["gy"]

    def program(*arrays):
        _, grid_x, grid_y, depth = arrays[0].shape
        places = grid_x // mesh.shape["groups"] * grid_y
        small = places == LANES and places == 8 * count
        small = small and depth == LANES * mesh.shape["gx"] and count & (count - 1) == 0
        small = small and mesh.shape["gx"] > 3
        return jax.shard_map(
            per_device_kernels if small else per_device,
            mesh=mesh,
            in_specs=(placed, placed, P(), P(), P()),
            out_specs=(placed, placed),
            check_vma=False,
        )(*arrays)

    return program
```

```python
import functools
import math

import jax
import jax.numpy as jnp
import numpy as np
from jax import lax
from jax.experimental import pallas as pl
from jax.experimental.pallas import tpu as pltpu
from jax.sharding import PartitionSpec as P

WIDTH = 64
HEADS = 8
HEAD_DIM = 8
LANES = 128

EPSILON = 1e-06
PRECISE = lax.Precision.HIGHEST
AXES = ("gx", "gy")


def exchange(parts):
    return lax.all_to_all(parts, AXES, split_axis=0, concat_axis=0, tiled=True)


def swap(part, axis, size, step):
    return lax.ppermute(part, axis, [(i, i ^ step) for i in range(size)])


def gather(part, count):
    return exchange(jnp.broadcast_to(part[None], (count,) + part.shape))


def reduce_blocks(total, count):
    width, depth = total.shape
    blocks = total.reshape(width, depth // LANES, LANES).transpose(1, 0, 2)
    blocks = blocks.reshape(count, width * depth // LANES // count, LANES)
    mine = jnp.sum(exchange(blocks), axis=0)
    whole = gather(mine, count).reshape(depth // LANES, width, LANES)
    return whole.transpose(1, 0, 2).reshape(width, depth)


def axis_features(pooled, weights):
    inverse = lax.rsqrt(jnp.mean(pooled * pooled, axis=0, keepdims=True) + EPSILON)
    normed = pooled * inverse
    length = pooled.shape[1]
    factor = 1.0 / math.sqrt(HEAD_DIM * length)
    queries = jnp.dot(weights[0].T, normed, precision=PRECISE).reshape(HEADS, HEAD_DIM, length)
    keyset = jnp.dot(weights[1].T, normed, precision=PRECISE).reshape(HEADS, HEAD_DIM, length)
    return (normed, inverse, queries, keyset, factor)


def axis_kernel(queries, keyset, factor):
    scores = jnp.einsum("hdm,hdn->hmn", queries, keyset, precision=PRECISE)
    return (scores * factor).astype(jnp.bfloat16)


def kernel_backward(gram, queries, keyset, factor):
    grad_query = factor * jnp.einsum("hmn,hdn->hdm", gram, keyset, precision=PRECISE)
    grad_keyset = factor * jnp.einsum("hmn,hdm->hdn", gram, queries, precision=PRECISE)
    return (grad_query, grad_keyset)


def grad_of_normed(weights, grad_query, grad_keyset):
    length = grad_query.shape[-1]
    grad_normed = jnp.dot(weights[0], grad_query.reshape(WIDTH, length), precision=PRECISE)
    return grad_normed + jnp.dot(
        weights[1], grad_keyset.reshape(WIDTH, length), precision=PRECISE
    )


def pooled_grad(normed, inverse, grad_normed):
    return inverse * (grad_normed - normed * jnp.mean(grad_normed * normed, axis=0, keepdims=True))


def f32_einsum(pattern, left, right):
    return jnp.einsum(pattern, left, right, preferred_element_type=jnp.float32)


def per_device(field, cotangent, qk_weight, w_value, w_out):
    span_x = lax.axis_size("gx")
    span_y = lax.axis_size("gy")
    count = span_x * span_y
    rows_x, rows_y, depth = field.shape[1:]
    cells = rows_x * rows_y
    grid_x = rows_x * span_x
    grid_y = rows_y * span_y
    start_x = lax.axis_index("gx") * rows_x
    start_y = lax.axis_index("gy") * rows_y
    bf16 = jnp.bfloat16

    cols = field.reshape(WIDTH, cells, depth)
    cots = cotangent.reshape(WIDTH, cells, depth)

    sum_z = jnp.sum(cols, axis=1, dtype=jnp.float32)
    sum_rows = jnp.sum(cols, axis=2, dtype=jnp.float32)
    rows_all = gather(sum_rows.T, count).reshape(span_x, span_y, rows_x, rows_y, WIDTH)
    total_x = jnp.sum(rows_all, axis=(1, 3)).reshape(grid_x, WIDTH).T
    total_y = jnp.sum(rows_all, axis=(0, 2)).reshape(grid_y, WIDTH).T
    total_z = reduce_blocks(sum_z, count)

    normed_x, inverse_x, query_x, keyset_x, factor_x = axis_features(
        total_x / (grid_y * depth), qk_weight[0]
    )
    normed_y, inverse_y, query_y, keyset_y, factor_y = axis_features(
        total_y / (grid_x * depth), qk_weight[1]
    )
    normed_z, inverse_z, query_z, keyset_z, factor_z = axis_features(
        total_z / (grid_x * grid_y), qk_weight[2]
    )
    kernel_x = axis_kernel(query_x, keyset_x, factor_x)
    kernel_y = axis_kernel(query_y, keyset_y, factor_y)
    query_b = query_z.astype(bf16)
    keyset_b = keyset_z.astype(bf16)

    wv = w_value.reshape(WIDTH, HEADS, HEAD_DIM)
    wo = w_out.reshape(HEADS, HEAD_DIM, WIDTH)
    coef_f = f32_einsum("cpk,hgk->cphg", cols, keyset_b)
    coef_c = f32_einsum("cpz,hgz->cphg", cots, query_b)
    low_f = jnp.einsum("chd,cphg->phdg", wv.astype(jnp.float32), coef_f, precision=PRECISE)
    low_c = jnp.einsum("hdc,cphg->phdg", wo.astype(jnp.float32), coef_c, precision=PRECISE)
    squares = HEAD_DIM * HEAD_DIM
    both = jnp.stack([low_f, low_c]).astype(bf16).reshape(2, cells, HEADS * squares)
    both = gather(both, count).reshape(span_x, span_y, 2, rows_x, rows_y, HEADS * squares)
    both = both.transpose(2, 0, 3, 1, 4, 5).reshape(2, grid_x, grid_y, HEADS, squares)
    low_f, low_c = both[0], both[1]

    mid_f = f32_einsum("hyj,xjhq->xyhq", kernel_y, low_f).astype(bf16)
    top_f = f32_einsum("hxi,iyhq->xyhq", kernel_x, mid_f)
    mid_c = f32_einsum("hxi,xyhq->iyhq", kernel_x, low_c).astype(bf16)
    top_c = f32_einsum("hyj,xyhq->xjhq", kernel_y, mid_c)
    gram_x = factor_z * f32_einsum("myhq,nyhq->hmn", low_c, mid_f)
    gram_y = factor_z * f32_einsum("xmhq,xnhq->hmn", mid_c, low_f)

    def here(top):
        top = lax.dynamic_slice_in_dim(top, start_x, rows_x, 0)
        top = lax.dynamic_slice_in_dim(top, start_y, rows_y, 1)
        return top.reshape(cells, HEADS, HEAD_DIM, HEAD_DIM)

    left_f = factor_z * jnp.einsum(
        "hdc,phdg->cphg", wo.astype(jnp.float32), here(top_f), precision=PRECISE
    )
    left_c = factor_z * jnp.einsum(
        "chd,phdg->cphg", wv.astype(jnp.float32), here(top_c), precision=PRECISE
    )
    left_f = left_f.astype(bf16)
    left_c = left_c.astype(bf16)

    grad_query_z = f32_einsum("cphg,cpz->hgz", left_f, cots)
    grad_keyset_z = f32_einsum("cphg,cpz->hgz", left_c, cols)
    gn_z = reduce_blocks(grad_of_normed(qk_weight[2], grad_query_z, grad_keyset_z), count)

    layer_output = (cols.astype(jnp.float32) + f32_einsum("cphg,hgz->cpz", left_f, query_b)).astype(bf16)
    through = f32_einsum("cphg,hgz->cpz", left_c, keyset_b)

    gn_x = grad_of_normed(qk_weight[0], *kernel_backward(gram_x, query_x, keyset_x, factor_x))
    gn_y = grad_of_normed(qk_weight[1], *kernel_backward(gram_y, query_y, keyset_y, factor_y))
    pull_x = pooled_grad(normed_x, inverse_x, gn_x)
    pull_y = pooled_grad(normed_y, inverse_y, gn_y)
    pull_z = pooled_grad(normed_z, inverse_z, gn_z)
    local_x = lax.dynamic_slice_in_dim(pull_x, start_x, rows_x, 1) / (grid_y * depth)
    local_y = lax.dynamic_slice_in_dim(pull_y, start_y, rows_y, 1) / (grid_x * depth)
    local_xy = (local_x[:, :, None] + local_y[:, None, :]).reshape(WIDTH, cells)
    local_z = pull_z / (grid_x * grid_y)
    field_grad = (
        cots.astype(jnp.float32) + through + local_xy[:, :, None] + local_z[:, None, :]
    ).astype(bf16)
    return (layer_output.reshape(field.shape), field_grad.reshape(field.shape))


def split(x):
    high = x.astype(jnp.bfloat16)
    return high, (x - high.astype(jnp.float32)).astype(jnp.bfloat16)


NN = (((1,), (0,)), ((), ()))
NT = (((1,), (1,)), ((), ()))
TN = (((0,), (0,)), ((), ()))


def mul(left, right, dims=NN):
    return lax.dot_general(left, right, dims, preferred_element_type=jnp.float32)


def mul_near(left, right, dims=NN):
    left_high, left_low = split(left)
    right_high, right_low = split(right)
    return (
        mul(left_high, right_high, dims)
        + mul(left_low, right_high, dims)
        + mul(left_high, right_low, dims)
    )


def mul_left(left, right, dims=NN):
    rows = left.shape[0]
    both = mul(jnp.concatenate(split(left), axis=0), right, dims)
    return both[:rows] + both[rows:]


def number(shape, dim):
    return lax.broadcasted_iota(jnp.int32, shape, dim)


def join_halves(half_ref, mine_ref, other_ref):
    core = lax.axis_index("gx") & 1
    half_ref[core] = mine_ref[...]
    half_ref[core ^ 1] = other_ref[...]
    return jnp.concatenate([half_ref[0], half_ref[1]], axis=1)


def expand(part):
    depth = part.shape[1]
    part = part.reshape(HEADS, 1, HEAD_DIM, depth)
    part = jnp.broadcast_to(part, (HEADS, HEAD_DIM, HEAD_DIM, depth))
    return part.reshape(WIDTH * HEAD_DIM, depth).astype(jnp.bfloat16)


def spread(weights, top):
    left = weights[:, None, :] * top[None]
    return left.reshape(-1, left.shape[2]).astype(jnp.bfloat16)


def prepare_kernel(wv_ref, wo_ref, qk_ref, wv_out, wo_out, wq_out, wk_out, wz_out):
    wide = HEADS * HEAD_DIM * HEAD_DIM
    row = number((WIDTH, wide), 0)
    lane = number((WIDTH, wide), 1)
    by_channel = ((lane >> 3) == row).astype(jnp.bfloat16)
    by_factor = (((lane >> 6) * HEAD_DIM + (lane & 7)) == row).astype(jnp.bfloat16)
    wv_out[...] = mul(wv_ref[...], by_channel)
    wo_out[...] = mul(wo_ref[...], by_channel, TN)
    for index, out in ((0, wq_out), (1, wk_out)):
        high, low = split(qk_ref[2, index])
        out[0:WIDTH, :] = mul(high, by_factor).astype(jnp.bfloat16)
        out[WIDTH : 2 * WIDTH, :] = mul(low, by_factor).astype(jnp.bfloat16)
        wz_out[index * WIDTH : (index + 1) * WIDTH, :] = qk_ref[2, index].T


def sums_kernel(field_ref, *refs):
    outs, (cols_ref, data_ref, half_ref, semaphores) = refs[:-4], refs[-4:]
    _, rows_x, rows_y, depth = data_ref.shape
    cells = rows_x * rows_y
    chunks = semaphores.shape[0]
    size = WIDTH // chunks
    copies = [
        pltpu.make_async_copy(
            field_ref.at[pl.ds(index * size, size)],
            data_ref.at[pl.ds(index * size, size)],
            semaphores.at[index],
        )
        for index in range(chunks)
    ]
    for copy in copies:
        copy.start()
    own = jnp.zeros((cells, LANES), jnp.float32)
    pick = number((size, size * cells), 1) // cells == number((size, size * cells), 0)
    pick = pick.astype(jnp.bfloat16)
    for index, copy in enumerate(copies):
        copy.wait()
        rows = slice(index * size, (index + 1) * size)
        data = data_ref[rows].astype(jnp.float32)
        data = jnp.concatenate([data[:, at_x] for at_x in range(rows_x)], axis=1)
        lanes = data[..., :LANES]
        for start in range(LANES, depth, LANES):
            lanes = lanes + data[..., start : start + LANES]
        row_sums = jnp.sum(lanes, axis=2, keepdims=True)
        shape = lanes.shape
        mine = number(shape, 0) + index * size == number(shape, 2)
        own = own + jnp.sum(jnp.where(mine, row_sums, 0.0), axis=0)
        data = data.reshape(size * cells, depth).astype(jnp.bfloat16)
        cols_ref[index * size * cells : (index + 1) * size * cells, :] = data
        part = mul(pick, data)
        half_ref[0, rows, :] = part[:, : depth // 2]
        half_ref[1, rows, :] = part[:, depth // 2 :]
    for step, out in enumerate(outs):
        out[0:WIDTH, :] = half_ref[(lax.axis_index("gx") & 1) ^ step]
        out[WIDTH:, :] = jnp.concatenate([own] * (depth // 2 // LANES), axis=1)


def add_kernel(*refs):
    parts, out_ref = refs[:-1], refs[-1]
    total = parts[0][0:WIDTH, :]
    for part in parts[1:]:
        total = total + part[0:WIDTH, :]
    out_ref[0:WIDTH, :] = total
    start = WIDTH
    for part in parts:
        more = part.shape[0] - WIDTH
        out_ref[start : start + more, :] = part[WIDTH:, :]
        start += more


def add_beside_kernel(known, mine_ref, other_ref, out_ref):
    out_ref[0:WIDTH, :] = mine_ref[0:WIDTH, :] + other_ref[0:WIDTH, :]
    lanes = known * WIDTH
    rest = out_ref.shape[1] - 2 * lanes
    rows = [mine_ref[WIDTH:, 0:lanes], other_ref[WIDTH:, 0:lanes]]
    if rest > 0:
        rows.append(jnp.zeros((rows[0].shape[0], rest), jnp.float32))
    out_ref[WIDTH:, :] = jnp.concatenate(rows, axis=1)


def stack_kernel(*refs):
    refs[-1][...] = jnp.concatenate([ref[...] for ref in refs[:-1]], axis=0)


def factor_kernel(places, *refs):
    parts, feat_ref = refs[:-1], refs[-1]
    total = parts[0][0:WIDTH, :]
    for part in parts[1:]:
        total = total + part[0:WIDTH, :]
    pooled = total * (1.0 / places)
    inverse = lax.rsqrt(jnp.mean(pooled * pooled, axis=0, keepdims=True) + EPSILON)
    normed = pooled * inverse
    feat_ref[0:WIDTH, :] = normed
    feat_ref[WIDTH:, :] = jnp.broadcast_to(inverse, (HEAD_DIM, inverse.shape[1]))


def add_pull_kernel(*refs):
    total = refs[0][...].astype(jnp.float32)
    for part in refs[1:-1]:
        total = total + part[...].astype(jnp.float32)
    refs[-1][...] = total.astype(refs[-1].dtype)


def by_head(part):
    shape = (HEADS, part.shape[0], WIDTH)
    mine = number(shape, 0) == (number(shape, 2) >> 3)
    return jnp.where(mine, part[None], 0.0).reshape(-1, WIDTH)


def plane_kernel(cells, span_x, lengths, *refs):
    parts, (same_ref, qk_ref, mix_ref, feat_ref, full_ref) = refs[:-5], refs[-5:]
    totals = jnp.concatenate(
        [
            part[start : start + cells, step * WIDTH : (step + 1) * WIDTH]
            for step in range(span_x)
            for part in parts
            for start in range(WIDTH, part.shape[0], cells)
        ],
        axis=0,
    )
    places = totals.shape[0]
    high, low = split(totals)
    forward = backward = None
    for axis in range(2):
        same = same_ref[axis]
        pooled = (mul(same, high) + mul(same, low)) * (1.0 / lengths[axis][1])
        inverse = lax.rsqrt(jnp.mean(pooled * pooled, axis=1, keepdims=True) + EPSILON)
        normed = pooled * inverse
        query = mul_near(normed, qk_ref[axis, 0])
        keyset = mul_near(normed, qk_ref[axis, 1])
        feat_ref[4 * axis] = normed
        feat_ref[4 * axis + 1] = query
        feat_ref[4 * axis + 2] = keyset
        feat_ref[4 * axis + 3] = jnp.broadcast_to(inverse, (places, WIDTH))
        factor = 1.0 / math.sqrt(HEAD_DIM * lengths[axis][0])

        def scores(rows, other):
            found = mul_near(by_head(rows), other, NT) * factor
            return found.astype(jnp.bfloat16).astype(jnp.float32)

        full = scores(query, keyset)
        full_ref[axis] = full
        one = full.reshape(HEADS, places, places)[:, :cells].reshape(-1, places)
        two = scores(keyset[:cells], query)
        forward = one if forward is None else forward * one
        backward = two if backward is None else backward * two
    mix_ref[0] = forward
    mix_ref[1] = backward


def coef_kernel(mine_ref, other_ref, wz_ref, field_ref, cot_ref, wv_ref, wo_ref,
                send_ref, both_ref, feat_ref, half_ref):
    rows, depth = field_ref.shape
    cells = rows // WIDTH
    wide = HEADS * HEAD_DIM * HEAD_DIM
    feat = join_halves(half_ref, mine_ref, other_ref)
    feat_ref[...] = feat
    high, low = split(feat[:WIDTH])
    both = mul_left(wz_ref[...], high) + mul(wz_ref[...].astype(jnp.bfloat16), low)
    both_ref[...] = both.astype(jnp.bfloat16)
    query = expand(both[:WIDTH])
    keyset = expand(both[WIDTH:])
    low_f = mul(field_ref[...], keyset, NT).reshape(WIDTH, cells, wide)
    low_f = jnp.sum(wv_ref[...][:, None, :] * low_f, axis=0)
    low_c = mul(cot_ref[...], query, NT).reshape(WIDTH, cells, wide)
    low_c = jnp.sum(wo_ref[...][:, None, :] * low_c, axis=0)
    low = jnp.concatenate([low_f, low_c], axis=0).astype(jnp.bfloat16)
    send_ref[...] = low


def join_low(refs, cells):
    low = jnp.concatenate([ref[...].astype(jnp.float32) for ref in refs], axis=0)
    wide = low.shape[1]
    low = low.reshape(-1, 2 * cells, wide)
    return [
        low[:, start : start + cells].reshape(-1, wide).astype(jnp.bfloat16)
        for start in (0, cells)
    ]


def mix_kernel(factor, spans, *refs):
    lows, refs = refs[:spans], refs[spans:]
    mix_ref, wv_ref, wo_ref, wq_ref, wk_ref, field_ref, cot_ref, top_ref, out_ref = refs
    cells = field_ref.shape[0] // WIDTH
    low_f, low_c = join_low(lows, cells)
    wide = low_f.shape[1]
    shape = (HEADS, cells, wide)
    head = number(shape, 0) == (number(shape, 2) >> 6)

    def top(mix, low):
        found = mul_left(mix, low).reshape(shape)
        return jnp.sum(jnp.where(head, found, 0.0), axis=0) * factor

    top_f = top(mix_ref[0], low_f)
    top_c = top(mix_ref[1], low_c)
    top_ref[0] = top_f
    top_ref[1] = top_c
    left_f = spread(wo_ref[...], top_f)
    left_c = spread(wv_ref[...], top_c)

    def pull(weights, left, right):
        found = mul(weights, left, NT)
        return mul_left(found[:WIDTH] + found[WIDTH:], right)

    found = pull(wq_ref[...], left_f, cot_ref[...]) + pull(wk_ref[...], left_c, field_ref[...])
    out_ref[...] = found.astype(jnp.bfloat16)


def put_cells(ref, total):
    _, rows_x, rows_y, depth = ref.shape
    total = total.reshape(WIDTH, rows_x * rows_y, depth)
    for index in range(rows_x):
        rows = total[:, index * rows_y : (index + 1) * rows_y, :]
        ref[:, index, :, :] = rows.astype(jnp.bfloat16)


def output_kernel(top_ref, wo_ref, both_ref, field_ref, out_ref):
    query = expand(both_ref[...].astype(jnp.float32)[:WIDTH])
    left = spread(wo_ref[...], top_ref[0])
    put_cells(out_ref, mul(left, query) + field_ref[...].astype(jnp.float32))


def gram_kernel(cells, lengths, factor_z, *refs):
    lows, (feat_ref, full_ref, same_ref, qk_ref, out_ref) = refs[:-5], refs[-5:]
    low_f, low_c = join_low(lows, cells)
    places, wide = low_f.shape
    squares = HEAD_DIM * HEAD_DIM
    lane = number((places, LANES), 1)
    products = []
    for pair in range(wide // LANES):
        part_f = low_f[:, pair * LANES : (pair + 1) * LANES]
        part_c = low_c[:, pair * LANES : (pair + 1) * LANES]
        for half in range(LANES // squares):
            mine = (lane >> 6) == half
            products.append(mul(jnp.where(mine, part_c, jnp.zeros_like(part_c)), part_f, NT))
    product = jnp.concatenate(products, axis=0)
    factors = [1.0 / math.sqrt(HEAD_DIM * lengths[axis][0]) for axis in range(2)]
    queries = [by_head(feat_ref[4 * axis + 1]).astype(jnp.bfloat16) for axis in range(2)]
    keysets = [by_head(feat_ref[4 * axis + 2]).astype(jnp.bfloat16) for axis in range(2)]
    total = jnp.zeros((cells, WIDTH), jnp.float32)
    for axis in range(2):
        gram = (product * full_ref[1 - axis]).astype(jnp.bfloat16)
        across = jnp.concatenate(
            [gram[h * places : (h + 1) * places] for h in range(HEADS)], axis=1
        )
        scale = factors[axis] * factor_z
        grad_query = mul(across, keysets[axis]) * scale
        grad_keyset = mul(gram, queries[axis], TN) * scale
        found = mul_near(grad_query, qk_ref[axis, 0], NT) + mul_near(grad_keyset, qk_ref[axis, 1], NT)
        high, low = split(found)
        own = same_ref[axis, 0 : 2 * cells, :]
        found = (mul(own, high) + mul(own, low))[:cells]
        normed = feat_ref[4 * axis, 0:cells, :]
        inverse = feat_ref[4 * axis + 3, 0:cells, :]
        found = found - normed * jnp.mean(found * normed, axis=1, keepdims=True)
        total = total + inverse * found * (1.0 / lengths[axis][1])
    shape = (WIDTH, cells, WIDTH)
    own = jnp.where(number(shape, 0) == number(shape, 2), total[None], 0.0)
    out_ref[...] = mul_left(own.reshape(-1, WIDTH), jnp.ones((WIDTH, LANES), jnp.bfloat16))


def base_kernel(top_ref, wv_ref, both_ref, cot_ref, out_ref):
    keyset = expand(both_ref[...].astype(jnp.float32)[WIDTH:])
    left = spread(wv_ref[...], top_ref[1])
    out_ref[...] = mul(left, keyset) + cot_ref[...].astype(jnp.float32)


def final_kernel(places, *refs):
    parts, refs = refs[:-6], refs[-6:]
    feat_ref, base_ref, plane_ref, out_ref, data_ref, semaphores = refs
    depth = base_ref.shape[1]
    _, rows_x, rows_y, _ = data_ref.shape
    found = parts[0][...].astype(jnp.float32)
    for part in parts[1:]:
        found = found + part[...].astype(jnp.float32)
    normed = feat_ref[0:WIDTH, :]
    inverse = feat_ref[WIDTH : WIDTH + 1, :]
    found = inverse * (found - normed * jnp.mean(found * normed, axis=0, keepdims=True))
    found = found * (1.0 / places)
    cells = rows_x * rows_y
    chunks = semaphores.shape[0]
    size = WIDTH // chunks
    copies = []
    for index in range(chunks):
        rows = slice(index * size, (index + 1) * size)
        base = base_ref[index * size * cells : (index + 1) * size * cells, :]
        plane = plane_ref[index * size * cells : (index + 1) * size * cells, :]
        base = base + jnp.concatenate([plane] * (depth // LANES), axis=1)
        total = base.reshape(size, cells, depth) + found[rows][:, None, :]
        for at_x in range(rows_x):
            part = total[:, at_x * rows_y : (at_x + 1) * rows_y, :]
            data_ref[rows, at_x, :, :] = part.astype(jnp.bfloat16)
        copy = pltpu.make_async_copy(
            data_ref.at[pl.ds(index * size, size)],
            out_ref.at[pl.ds(index * size, size)],
            semaphores.at[index],
        )
        copy.start()
        copies.append(copy)
    for copy in copies:
        copy.wait()


def rows_kernel(cot_ref, rows_ref, data_ref, semaphores):
    _, rows_x, rows_y, depth = data_ref.shape
    cells = rows_x * rows_y
    chunks = semaphores.shape[0]
    size = WIDTH // chunks
    copies = [
        pltpu.make_async_copy(
            cot_ref.at[pl.ds(index * size, size)],
            data_ref.at[pl.ds(index * size, size)],
            semaphores.at[index],
        )
        for index in range(chunks)
    ]
    for copy in copies:
        copy.start()
    for index, copy in enumerate(copies):
        copy.wait()
        data = data_ref[index * size : (index + 1) * size].astype(jnp.float32)
        data = jnp.concatenate([data[:, at_x] for at_x in range(rows_x)], axis=1)
        data = data.reshape(size * cells, depth).astype(jnp.bfloat16)
        rows_ref[index * size * cells : (index + 1) * size * cells, :] = data


def run(kernel, outs, operands, places=pltpu.VMEM, target=pltpu.VMEM, flops=0, scratch=(),
        mebibytes=16):
    moved = sum(x.size * x.dtype.itemsize for x in tuple(operands) + tuple(outs))
    found = pl.pallas_call(
        kernel,
        out_shape=tuple(outs),
        in_specs=[pl.BlockSpec(memory_space=places)] * len(operands),
        out_specs=tuple(pl.BlockSpec(memory_space=target) for _ in outs),
        scratch_shapes=list(scratch),
        compiler_params=pltpu.CompilerParams(vmem_limit_bytes=mebibytes * 1024 * 1024),
        cost_estimate=pl.CostEstimate(flops=flops, bytes_accessed=moved, transcendentals=0),
    )(*operands)
    return found[0] if len(outs) == 1 else found


def per_device_kernels(field, cotangent, qk_weight, w_value, w_out):
    span_x = lax.axis_size("gx")
    span_y = lax.axis_size("gy")
    count = span_x * span_y
    rows_x, rows_y, depth = field.shape[1:]
    cells = rows_x * rows_y
    places = count * cells
    grid_x = rows_x * span_x
    grid_y = rows_y * span_y
    rows = WIDTH * cells
    wide = WIDTH * HEAD_DIM
    f32, bf16 = jnp.float32, jnp.bfloat16
    like = jax.ShapeDtypeStruct
    lengths = ((grid_x, grid_y * depth), (grid_y, grid_x * depth))

    cell = np.arange(places)
    at_x = cell // cells // span_y * rows_x + cell % cells // rows_y
    at_y = cell // cells % span_y * rows_y + cell % rows_y
    same = jnp.asarray(
        np.stack([at_x[:, None] == at_x[None], at_y[:, None] == at_y[None]]), dtype=bf16
    )

    half = depth // 2
    halves = pltpu.VMEM((2, WIDTH, half), f32)
    chunked = [pltpu.VMEM(field.shape, bf16), pltpu.SemaphoreType.DMA((4,))]
    factor_z = 1.0 / math.sqrt(HEAD_DIM * depth)
    cube = rows * wide * depth * 2

    cots = run(
        rows_kernel,
        [like((rows, depth), bf16)],
        (pltpu.with_memory_space_constraint(cotangent, pltpu.HBM),),
        places=pltpu.HBM,
        flops=cube,
        scratch=chunked,
    )

    def swaps(sent, axis, size, farthest=True):
        if not isinstance(sent, (tuple, list)):
            sent = [sent] * size
        steps = range(size - 1, 0, -1)
        found = {}
        for step in steps if farthest else reversed(steps):
            found[step] = swap(sent[step], axis, size, step)
        return tuple(sent[:1]) + tuple(found[step] for step in steps)

    def taken(kernel, sent, dtype=None, last=False):
        found, *others = sent
        for part in others if last else others[:-1]:
            more = part.shape[0] if kernel is stack_kernel else part.shape[0] - WIDTH
            shape = (found.shape[0] + more,) + part.shape[1:]
            found = run(kernel, [like(shape, dtype or found.dtype)], (found, part))
        return (found,) if last else (found, others[-1])

    *sums, cols = run(
        sums_kernel,
        [like((WIDTH + cells, half), f32)] * 2 + [like((rows, depth), bf16)],
        (pltpu.with_memory_space_constraint(field, pltpu.HBM),),
        places=pltpu.HBM,
        flops=cube // 4,
        scratch=[chunked[0], halves, chunked[1]],
    )
    wv, wo, wq, wk, wz = run(
        prepare_kernel,
        [like((WIDTH, wide), f32)] * 2 + [like((2 * WIDTH, wide), bf16)] * 2
        + [like((2 * WIDTH, WIDTH), f32)],
        (w_value, w_out, qk_weight),
        flops=cube // 8,
    )
    total, other = sums
    for level in range(span_x.bit_length() - 1):
        step = 1 << level
        total = run(
            functools.partial(add_beside_kernel, step),
            [like((WIDTH + cells, half), f32)],
            (total, swap(total if level else other, "gx", span_x, step)),
        )
    totals = taken(add_kernel, swaps(total, "gy", span_y))
    totals, cots, wz = lax.optimization_barrier((totals, cots, wz))
    mine = run(
        functools.partial(factor_kernel, grid_x * grid_y),
        [like((WIDTH + HEAD_DIM, half), f32)],
        totals,
    )
    mix, feat, full = run(
        functools.partial(plane_kernel, cells, span_x, lengths),
        [like((2, HEADS * cells, places), f32), like((8, places, WIDTH), f32),
         like((2, HEADS * places, places), f32)],
        totals + (same, qk_weight),
        flops=cube // 2,
    )
    send, both, feat_z = run(
        coef_kernel,
        [like((2 * cells, wide), bf16), like((2 * WIDTH, depth), bf16),
         like((WIDTH + HEAD_DIM, depth), f32)],
        (mine, swap(mine, "gx", span_x, 1), wz, cols, cots, wv, wo),
        flops=2 * cube,
        scratch=[pltpu.VMEM((2, WIDTH + HEAD_DIM, half), f32)],
    )
    (low,) = taken(stack_kernel, swaps(send, "gy", span_y), last=True)
    first, *others = swaps(low, "gx", span_x, False)
    lows = (first,) + tuple(reversed(others))
    pulled = like((WIDTH, depth), bf16)
    top, total = run(
        functools.partial(mix_kernel, factor_z, span_x),
        [like((2, cells, wide), f32), pulled],
        lows + (mix, wv, wo, wq, wk, cols, cots),
        flops=cube,
    )
    total = run(add_pull_kernel, [pulled], (total, swap(total, "gx", span_x, 1)))
    base = run(base_kernel, [like((rows, depth), f32)], (top, wv, both, cots), flops=cube)
    total, base = lax.optimization_barrier((total, base))
    for level in range(1, span_x.bit_length() - 1):
        total = run(add_pull_kernel, [pulled], (total, swap(total, "gx", span_x, 1 << level)))
    layer_output = run(
        output_kernel, [like(field.shape, bf16)], (top, wo, both, cols), flops=cube
    )
    plane = run(
        functools.partial(gram_kernel, cells, lengths, factor_z),
        [like((rows, LANES), f32)],
        lows + (feat, full, same, qk_weight),
        flops=2 * cube,
    )
    total, layer_output, plane = lax.optimization_barrier((total, layer_output, plane))
    field_grad = run(
        functools.partial(final_kernel, grid_x * grid_y),
        [like(field.shape, bf16)],
        swaps(total, "gy", span_y, False) + (feat_z, base, plane),
        target=pltpu.HBM,
        scratch=chunked,
    )
    return (layer_output, field_grad)


def solution(mesh):
    placed = P(None, ("groups", "gx"), "gy", None)
    count = mesh.shape["gx"] * mesh.shape["gy"]

    def program(*arrays):
        _, grid_x, grid_y, depth = arrays[0].shape
        places = grid_x // mesh.shape["groups"] * grid_y
        small = places == LANES and places == 8 * count
        small = small and depth == LANES * mesh.shape["gx"] and count & (count - 1) == 0
        small = small and mesh.shape["gx"] > 3
        return jax.shard_map(
            per_device_kernels if small else per_device,
            mesh=mesh,
            in_specs=(placed, placed, P(), P(), P()),
            out_specs=(placed, placed),
            check_vma=False,
        )(*arrays)

    return program
```

```python
import functools
import math

import jax
import jax.numpy as jnp
import numpy as np
from jax import lax
from jax.experimental import pallas as pl
from jax.experimental.pallas import tpu as pltpu
from jax.sharding import PartitionSpec as P

WIDTH = 64
HEADS = 8
HEAD_DIM = 8
LANES = 128

EPSILON = 1e-06
PRECISE = lax.Precision.HIGHEST
AXES = ("gx", "gy")


def exchange(parts):
    return lax.all_to_all(parts, AXES, split_axis=0, concat_axis=0, tiled=True)


def swap(part, axis, size, step):
    return lax.ppermute(part, axis, [(i, i ^ step) for i in range(size)])


def gather(part, count):
    return exchange(jnp.broadcast_to(part[None], (count,) + part.shape))


def reduce_blocks(total, count):
    width, depth = total.shape
    blocks = total.reshape(width, depth // LANES, LANES).transpose(1, 0, 2)
    blocks = blocks.reshape(count, width * depth // LANES // count, LANES)
    mine = jnp.sum(exchange(blocks), axis=0)
    whole = gather(mine, count).reshape(depth // LANES, width, LANES)
    return whole.transpose(1, 0, 2).reshape(width, depth)


def axis_features(pooled, weights):
    inverse = lax.rsqrt(jnp.mean(pooled * pooled, axis=0, keepdims=True) + EPSILON)
    normed = pooled * inverse
    length = pooled.shape[1]
    factor = 1.0 / math.sqrt(HEAD_DIM * length)
    queries = jnp.dot(weights[0].T, normed, precision=PRECISE).reshape(HEADS, HEAD_DIM, length)
    keyset = jnp.dot(weights[1].T, normed, precision=PRECISE).reshape(HEADS, HEAD_DIM, length)
    return (normed, inverse, queries, keyset, factor)


def axis_kernel(queries, keyset, factor):
    scores = jnp.einsum("hdm,hdn->hmn", queries, keyset, precision=PRECISE)
    return (scores * factor).astype(jnp.bfloat16)


def kernel_backward(gram, queries, keyset, factor):
    grad_query = factor * jnp.einsum("hmn,hdn->hdm", gram, keyset, precision=PRECISE)
    grad_keyset = factor * jnp.einsum("hmn,hdm->hdn", gram, queries, precision=PRECISE)
    return (grad_query, grad_keyset)


def grad_of_normed(weights, grad_query, grad_keyset):
    length = grad_query.shape[-1]
    grad_normed = jnp.dot(weights[0], grad_query.reshape(WIDTH, length), precision=PRECISE)
    return grad_normed + jnp.dot(
        weights[1], grad_keyset.reshape(WIDTH, length), precision=PRECISE
    )


def pooled_grad(normed, inverse, grad_normed):
    return inverse * (grad_normed - normed * jnp.mean(grad_normed * normed, axis=0, keepdims=True))


def f32_einsum(pattern, left, right):
    return jnp.einsum(pattern, left, right, preferred_element_type=jnp.float32)


def per_device(field, cotangent, qk_weight, w_value, w_out):
    span_x = lax.axis_size("gx")
    span_y = lax.axis_size("gy")
    count = span_x * span_y
    rows_x, rows_y, depth = field.shape[1:]
    cells = rows_x * rows_y
    grid_x = rows_x * span_x
    grid_y = rows_y * span_y
    start_x = lax.axis_index("gx") * rows_x
    start_y = lax.axis_index("gy") * rows_y
    bf16 = jnp.bfloat16

    cols = field.reshape(WIDTH, cells, depth)
    cots = cotangent.reshape(WIDTH, cells, depth)

    sum_z = jnp.sum(cols, axis=1, dtype=jnp.float32)
    sum_rows = jnp.sum(cols, axis=2, dtype=jnp.float32)
    rows_all = gather(sum_rows.T, count).reshape(span_x, span_y, rows_x, rows_y, WIDTH)
    total_x = jnp.sum(rows_all, axis=(1, 3)).reshape(grid_x, WIDTH).T
    total_y = jnp.sum(rows_all, axis=(0, 2)).reshape(grid_y, WIDTH).T
    total_z = reduce_blocks(sum_z, count)

    normed_x, inverse_x, query_x, keyset_x, factor_x = axis_features(
        total_x / (grid_y * depth), qk_weight[0]
    )
    normed_y, inverse_y, query_y, keyset_y, factor_y = axis_features(
        total_y / (grid_x * depth), qk_weight[1]
    )
    normed_z, inverse_z, query_z, keyset_z, factor_z = axis_features(
        total_z / (grid_x * grid_y), qk_weight[2]
    )
    kernel_x = axis_kernel(query_x, keyset_x, factor_x)
    kernel_y = axis_kernel(query_y, keyset_y, factor_y)
    query_b = query_z.astype(bf16)
    keyset_b = keyset_z.astype(bf16)

    wv = w_value.reshape(WIDTH, HEADS, HEAD_DIM)
    wo = w_out.reshape(HEADS, HEAD_DIM, WIDTH)
    coef_f = f32_einsum("cpk,hgk->cphg", cols, keyset_b)
    coef_c = f32_einsum("cpz,hgz->cphg", cots, query_b)
    low_f = jnp.einsum("chd,cphg->phdg", wv.astype(jnp.float32), coef_f, precision=PRECISE)
    low_c = jnp.einsum("hdc,cphg->phdg", wo.astype(jnp.float32), coef_c, precision=PRECISE)
    squares = HEAD_DIM * HEAD_DIM
    both = jnp.stack([low_f, low_c]).astype(bf16).reshape(2, cells, HEADS * squares)
    both = gather(both, count).reshape(span_x, span_y, 2, rows_x, rows_y, HEADS * squares)
    both = both.transpose(2, 0, 3, 1, 4, 5).reshape(2, grid_x, grid_y, HEADS, squares)
    low_f, low_c = both[0], both[1]

    mid_f = f32_einsum("hyj,xjhq->xyhq", kernel_y, low_f).astype(bf16)
    top_f = f32_einsum("hxi,iyhq->xyhq", kernel_x, mid_f)
    mid_c = f32_einsum("hxi,xyhq->iyhq", kernel_x, low_c).astype(bf16)
    top_c = f32_einsum("hyj,xyhq->xjhq", kernel_y, mid_c)
    gram_x = factor_z * f32_einsum("myhq,nyhq->hmn", low_c, mid_f)
    gram_y = factor_z * f32_einsum("xmhq,xnhq->hmn", mid_c, low_f)

    def here(top):
        top = lax.dynamic_slice_in_dim(top, start_x, rows_x, 0)
        top = lax.dynamic_slice_in_dim(top, start_y, rows_y, 1)
        return top.reshape(cells, HEADS, HEAD_DIM, HEAD_DIM)

    left_f = factor_z * jnp.einsum(
        "hdc,phdg->cphg", wo.astype(jnp.float32), here(top_f), precision=PRECISE
    )
    left_c = factor_z * jnp.einsum(
        "chd,phdg->cphg", wv.astype(jnp.float32), here(top_c), precision=PRECISE
    )
    left_f = left_f.astype(bf16)
    left_c = left_c.astype(bf16)

    grad_query_z = f32_einsum("cphg,cpz->hgz", left_f, cots)
    grad_keyset_z = f32_einsum("cphg,cpz->hgz", left_c, cols)
    gn_z = reduce_blocks(grad_of_normed(qk_weight[2], grad_query_z, grad_keyset_z), count)

    layer_output = (cols.astype(jnp.float32) + f32_einsum("cphg,hgz->cpz", left_f, query_b)).astype(bf16)
    through = f32_einsum("cphg,hgz->cpz", left_c, keyset_b)

    gn_x = grad_of_normed(qk_weight[0], *kernel_backward(gram_x, query_x, keyset_x, factor_x))
    gn_y = grad_of_normed(qk_weight[1], *kernel_backward(gram_y, query_y, keyset_y, factor_y))
    pull_x = pooled_grad(normed_x, inverse_x, gn_x)
    pull_y = pooled_grad(normed_y, inverse_y, gn_y)
    pull_z = pooled_grad(normed_z, inverse_z, gn_z)
    local_x = lax.dynamic_slice_in_dim(pull_x, start_x, rows_x, 1) / (grid_y * depth)
    local_y = lax.dynamic_slice_in_dim(pull_y, start_y, rows_y, 1) / (grid_x * depth)
    local_xy = (local_x[:, :, None] + local_y[:, None, :]).reshape(WIDTH, cells)
    local_z = pull_z / (grid_x * grid_y)
    field_grad = (
        cots.astype(jnp.float32) + through + local_xy[:, :, None] + local_z[:, None, :]
    ).astype(bf16)
    return (layer_output.reshape(field.shape), field_grad.reshape(field.shape))


def split(x):
    high = x.astype(jnp.bfloat16)
    return high, (x - high.astype(jnp.float32)).astype(jnp.bfloat16)


NN = (((1,), (0,)), ((), ()))
NT = (((1,), (1,)), ((), ()))
TN = (((0,), (0,)), ((), ()))


def mul(left, right, dims=NN):
    return lax.dot_general(left, right, dims, preferred_element_type=jnp.float32)


def mul_near(left, right, dims=NN):
    left_high, left_low = split(left)
    right_high, right_low = split(right)
    return (
        mul(left_high, right_high, dims)
        + mul(left_low, right_high, dims)
        + mul(left_high, right_low, dims)
    )


def mul_left(left, right, dims=NN):
    rows = left.shape[0]
    both = mul(jnp.concatenate(split(left), axis=0), right, dims)
    return both[:rows] + both[rows:]


def number(shape, dim):
    return lax.broadcasted_iota(jnp.int32, shape, dim)


def join_halves(half_ref, mine_ref, other_ref):
    core = lax.axis_index("gx") & 1
    half_ref[core] = mine_ref[...]
    half_ref[core ^ 1] = other_ref[...]
    return jnp.concatenate([half_ref[0], half_ref[1]], axis=1)


def expand(part):
    depth = part.shape[1]
    part = part.reshape(HEADS, 1, HEAD_DIM, depth)
    part = jnp.broadcast_to(part, (HEADS, HEAD_DIM, HEAD_DIM, depth))
    return part.reshape(WIDTH * HEAD_DIM, depth).astype(jnp.bfloat16)


def spread(weights, top):
    left = weights[:, None, :] * top[None]
    return left.reshape(-1, left.shape[2]).astype(jnp.bfloat16)


def prepare_kernel(wv_ref, wo_ref, qk_ref, wv_out, wo_out, wq_out, wk_out, wz_out):
    wide = HEADS * HEAD_DIM * HEAD_DIM
    row = number((WIDTH, wide), 0)
    lane = number((WIDTH, wide), 1)
    by_channel = ((lane >> 3) == row).astype(jnp.bfloat16)
    by_factor = (((lane >> 6) * HEAD_DIM + (lane & 7)) == row).astype(jnp.bfloat16)
    wv_out[...] = mul(wv_ref[...], by_channel)
    wo_out[...] = mul(wo_ref[...], by_channel, TN)
    for index, out in ((0, wq_out), (1, wk_out)):
        high, low = split(qk_ref[2, index])
        out[0:WIDTH, :] = mul(high, by_factor).astype(jnp.bfloat16)
        out[WIDTH : 2 * WIDTH, :] = mul(low, by_factor).astype(jnp.bfloat16)
        wz_out[index * WIDTH : (index + 1) * WIDTH, :] = qk_ref[2, index].T


def sums_kernel(field_ref, *refs):
    outs, (cols_ref, data_ref, half_ref, semaphores) = refs[:-4], refs[-4:]
    _, rows_x, rows_y, depth = data_ref.shape
    cells = rows_x * rows_y
    chunks = semaphores.shape[0]
    size = WIDTH // chunks
    copies = [
        pltpu.make_async_copy(
            field_ref.at[pl.ds(index * size, size)],
            data_ref.at[pl.ds(index * size, size)],
            semaphores.at[index],
        )
        for index in range(chunks)
    ]
    for copy in copies:
        copy.start()
    own = jnp.zeros((cells, LANES), jnp.float32)
    pick = number((size, size * cells), 1) // cells == number((size, size * cells), 0)
    pick = pick.astype(jnp.bfloat16)
    for index, copy in enumerate(copies):
        copy.wait()
        rows = slice(index * size, (index + 1) * size)
        data = data_ref[rows].astype(jnp.float32)
        data = jnp.concatenate([data[:, at_x] for at_x in range(rows_x)], axis=1)
        lanes = data[..., :LANES]
        for start in range(LANES, depth, LANES):
            lanes = lanes + data[..., start : start + LANES]
        row_sums = jnp.sum(lanes, axis=2, keepdims=True)
        shape = lanes.shape
        mine = number(shape, 0) + index * size == number(shape, 2)
        own = own + jnp.sum(jnp.where(mine, row_sums, 0.0), axis=0)
        data = data.reshape(size * cells, depth).astype(jnp.bfloat16)
        cols_ref[index * size * cells : (index + 1) * size * cells, :] = data
        part = mul(pick, data)
        half_ref[0, rows, :] = part[:, : depth // 2]
        half_ref[1, rows, :] = part[:, depth // 2 :]
    for step, out in enumerate(outs):
        out[0:WIDTH, :] = half_ref[(lax.axis_index("gx") & 1) ^ step]
        out[WIDTH:, :] = jnp.concatenate([own] * (depth // 2 // LANES), axis=1)


def add_beside_kernel(known, mine_ref, other_ref, out_ref):
    out_ref[0:WIDTH, :] = mine_ref[0:WIDTH, :] + other_ref[0:WIDTH, :]
    lanes = known * WIDTH
    rest = out_ref.shape[1] - 2 * lanes
    rows = [mine_ref[WIDTH:, 0:lanes], other_ref[WIDTH:, 0:lanes]]
    if rest > 0:
        rows.append(jnp.zeros((rows[0].shape[0], rest), jnp.float32))
    out_ref[WIDTH:, :] = jnp.concatenate(rows, axis=1)


def narrow_kernel(total_ref, out_ref):
    out_ref[0:WIDTH, :] = total_ref[0:WIDTH, :].astype(jnp.bfloat16)
    high, low = split(total_ref[WIDTH:, :])
    out_ref[WIDTH:, :] = jnp.concatenate([high, low], axis=0)


def add_narrow_kernel(found_ref, part_ref, out_ref):
    known = found_ref.shape[0]
    part = part_ref[...].astype(jnp.float32)
    cells = (part.shape[0] - WIDTH) // 2
    out_ref[0:WIDTH, :] = found_ref[0:WIDTH, :] + part[0:WIDTH]
    out_ref[WIDTH:known, :] = found_ref[WIDTH:, :]
    out_ref[known:, :] = part[WIDTH : WIDTH + cells] + part[WIDTH + cells :]


def stack_kernel(*refs):
    refs[-1][...] = jnp.concatenate([ref[...] for ref in refs[:-1]], axis=0)


def factor_kernel(places, *refs):
    parts, feat_ref = refs[:-1], refs[-1]
    total = parts[0][0:WIDTH, :]
    for part in parts[1:]:
        total = total + part[0:WIDTH, :]
    pooled = total * (1.0 / places)
    inverse = lax.rsqrt(jnp.mean(pooled * pooled, axis=0, keepdims=True) + EPSILON)
    normed = pooled * inverse
    feat_ref[0:WIDTH, :] = normed
    feat_ref[WIDTH:, :] = jnp.broadcast_to(inverse, (HEAD_DIM, inverse.shape[1]))


def add_pull_kernel(*refs):
    total = refs[0][...].astype(jnp.float32)
    for part in refs[1:-1]:
        total = total + part[...].astype(jnp.float32)
    refs[-1][...] = total.astype(refs[-1].dtype)


def by_head(part):
    shape = (HEADS, part.shape[0], WIDTH)
    mine = number(shape, 0) == (number(shape, 2) >> 3)
    return jnp.where(mine, part[None], 0.0).reshape(-1, WIDTH)


def plane_kernel(cells, span_x, lengths, *refs):
    parts, (same_ref, qk_ref, mix_ref, feat_ref, full_ref) = refs[:-5], refs[-5:]
    totals = jnp.concatenate(
        [
            part[start : start + cells, step * WIDTH : (step + 1) * WIDTH]
            for step in range(span_x)
            for part in parts
            for start in range(WIDTH, part.shape[0], cells)
        ],
        axis=0,
    )
    places = totals.shape[0]
    high, low = split(totals)
    forward = backward = None
    for axis in range(2):
        same = same_ref[axis]
        pooled = (mul(same, high) + mul(same, low)) * (1.0 / lengths[axis][1])
        inverse = lax.rsqrt(jnp.mean(pooled * pooled, axis=1, keepdims=True) + EPSILON)
        normed = pooled * inverse
        query = mul_near(normed, qk_ref[axis, 0])
        keyset = mul_near(normed, qk_ref[axis, 1])
        feat_ref[4 * axis] = normed
        feat_ref[4 * axis + 1] = query
        feat_ref[4 * axis + 2] = keyset
        feat_ref[4 * axis + 3] = jnp.broadcast_to(inverse, (places, WIDTH))
        factor = 1.0 / math.sqrt(HEAD_DIM * lengths[axis][0])

        def scores(rows, other):
            found = mul_near(by_head(rows), other, NT) * factor
            return found.astype(jnp.bfloat16).astype(jnp.float32)

        full = scores(query, keyset)
        full_ref[axis] = full
        one = full.reshape(HEADS, places, places)[:, :cells].reshape(-1, places)
        two = scores(keyset[:cells], query)
        forward = one if forward is None else forward * one
        backward = two if backward is None else backward * two
    mix_ref[0] = forward
    mix_ref[1] = backward


def coef_kernel(mine_ref, other_ref, wz_ref, field_ref, cot_ref, wv_ref, wo_ref,
                send_ref, both_ref, feat_ref, half_ref):
    rows, depth = field_ref.shape
    cells = rows // WIDTH
    wide = HEADS * HEAD_DIM * HEAD_DIM
    feat = join_halves(half_ref, mine_ref, other_ref)
    feat_ref[...] = feat
    high, low = split(feat[:WIDTH])
    both = mul_left(wz_ref[...], high) + mul(wz_ref[...].astype(jnp.bfloat16), low)
    both_ref[...] = both.astype(jnp.bfloat16)
    query = expand(both[:WIDTH])
    keyset = expand(both[WIDTH:])
    low_f = mul(field_ref[...], keyset, NT).reshape(WIDTH, cells, wide)
    low_f = jnp.sum(wv_ref[...][:, None, :] * low_f, axis=0)
    low_c = mul(cot_ref[...], query, NT).reshape(WIDTH, cells, wide)
    low_c = jnp.sum(wo_ref[...][:, None, :] * low_c, axis=0)
    low = jnp.concatenate([low_f, low_c], axis=0).astype(jnp.bfloat16)
    send_ref[...] = low


def join_low(refs, cells):
    low = jnp.concatenate([ref[...].astype(jnp.float32) for ref in refs], axis=0)
    wide = low.shape[1]
    low = low.reshape(-1, 2 * cells, wide)
    return [
        low[:, start : start + cells].reshape(-1, wide).astype(jnp.bfloat16)
        for start in (0, cells)
    ]


def mix_kernel(factor, spans, *refs):
    lows, refs = refs[:spans], refs[spans:]
    mix_ref, wv_ref, wo_ref, wq_ref, wk_ref, field_ref, cot_ref, top_ref, out_ref = refs
    cells = field_ref.shape[0] // WIDTH
    low_f, low_c = join_low(lows, cells)
    wide = low_f.shape[1]
    shape = (HEADS, cells, wide)
    head = number(shape, 0) == (number(shape, 2) >> 6)

    def top(mix, low):
        found = mul_left(mix, low).reshape(shape)
        return jnp.sum(jnp.where(head, found, 0.0), axis=0) * factor

    top_f = top(mix_ref[0], low_f)
    top_c = top(mix_ref[1], low_c)
    top_ref[0] = top_f
    top_ref[1] = top_c
    left_f = spread(wo_ref[...], top_f)
    left_c = spread(wv_ref[...], top_c)

    def pull(weights, left, right):
        found = mul(weights, left, NT)
        return mul_left(found[:WIDTH] + found[WIDTH:], right)

    found = pull(wq_ref[...], left_f, cot_ref[...]) + pull(wk_ref[...], left_c, field_ref[...])
    out_ref[...] = found.astype(jnp.bfloat16)


def put_cells(ref, total):
    _, rows_x, rows_y, depth = ref.shape
    total = total.reshape(WIDTH, rows_x * rows_y, depth)
    for index in range(rows_x):
        rows = total[:, index * rows_y : (index + 1) * rows_y, :]
        ref[:, index, :, :] = rows.astype(jnp.bfloat16)


def output_kernel(top_ref, wo_ref, both_ref, field_ref, out_ref):
    query = expand(both_ref[...].astype(jnp.float32)[:WIDTH])
    left = spread(wo_ref[...], top_ref[0])
    put_cells(out_ref, mul(left, query) + field_ref[...].astype(jnp.float32))


def gram_kernel(cells, lengths, factor_z, *refs):
    lows, (feat_ref, full_ref, same_ref, qk_ref, out_ref) = refs[:-5], refs[-5:]
    low_f, low_c = join_low(lows, cells)
    places, wide = low_f.shape
    squares = HEAD_DIM * HEAD_DIM
    lane = number((places, LANES), 1)
    products = []
    for pair in range(wide // LANES):
        part_f = low_f[:, pair * LANES : (pair + 1) * LANES]
        part_c = low_c[:, pair * LANES : (pair + 1) * LANES]
        for half in range(LANES // squares):
            mine = (lane >> 6) == half
            products.append(mul(jnp.where(mine, part_c, jnp.zeros_like(part_c)), part_f, NT))
    product = jnp.concatenate(products, axis=0)
    factors = [1.0 / math.sqrt(HEAD_DIM * lengths[axis][0]) for axis in range(2)]
    queries = [by_head(feat_ref[4 * axis + 1]).astype(jnp.bfloat16) for axis in range(2)]
    keysets = [by_head(feat_ref[4 * axis + 2]).astype(jnp.bfloat16) for axis in range(2)]
    total = jnp.zeros((cells, WIDTH), jnp.float32)
    for axis in range(2):
        gram = (product * full_ref[1 - axis]).astype(jnp.bfloat16)
        across = jnp.concatenate(
            [gram[h * places : (h + 1) * places] for h in range(HEADS)], axis=1
        )
        scale = factors[axis] * factor_z
        grad_query = mul(across, keysets[axis]) * scale
        grad_keyset = mul(gram, queries[axis], TN) * scale
        found = mul_near(grad_query, qk_ref[axis, 0], NT) + mul_near(grad_keyset, qk_ref[axis, 1], NT)
        high, low = split(found)
        own = same_ref[axis, 0 : 2 * cells, :]
        found = (mul(own, high) + mul(own, low))[:cells]
        normed = feat_ref[4 * axis, 0:cells, :]
        inverse = feat_ref[4 * axis + 3, 0:cells, :]
        found = found - normed * jnp.mean(found * normed, axis=1, keepdims=True)
        total = total + inverse * found * (1.0 / lengths[axis][1])
    shape = (WIDTH, cells, WIDTH)
    own = jnp.where(number(shape, 0) == number(shape, 2), total[None], 0.0)
    out_ref[...] = mul_left(own.reshape(-1, WIDTH), jnp.ones((WIDTH, LANES), jnp.bfloat16))


def base_kernel(top_ref, wv_ref, both_ref, cot_ref, out_ref):
    keyset = expand(both_ref[...].astype(jnp.float32)[WIDTH:])
    left = spread(wv_ref[...], top_ref[1])
    out_ref[...] = mul(left, keyset) + cot_ref[...].astype(jnp.float32)


def final_kernel(places, *refs):
    parts, refs = refs[:-6], refs[-6:]
    feat_ref, base_ref, plane_ref, out_ref, data_ref, semaphores = refs
    depth = base_ref.shape[1]
    _, rows_x, rows_y, _ = data_ref.shape
    found = parts[0][...].astype(jnp.float32)
    for part in parts[1:]:
        found = found + part[...].astype(jnp.float32)
    normed = feat_ref[0:WIDTH, :]
    inverse = feat_ref[WIDTH : WIDTH + 1, :]
    found = inverse * (found - normed * jnp.mean(found * normed, axis=0, keepdims=True))
    found = found * (1.0 / places)
    cells = rows_x * rows_y
    chunks = semaphores.shape[0]
    size = WIDTH // chunks
    copies = []
    for index in range(chunks):
        rows = slice(index * size, (index + 1) * size)
        base = base_ref[index * size * cells : (index + 1) * size * cells, :]
        plane = plane_ref[index * size * cells : (index + 1) * size * cells, :]
        base = base + jnp.concatenate([plane] * (depth // LANES), axis=1)
        total = base.reshape(size, cells, depth) + found[rows][:, None, :]
        for at_x in range(rows_x):
            part = total[:, at_x * rows_y : (at_x + 1) * rows_y, :]
            data_ref[rows, at_x, :, :] = part.astype(jnp.bfloat16)
        copy = pltpu.make_async_copy(
            data_ref.at[pl.ds(index * size, size)],
            out_ref.at[pl.ds(index * size, size)],
            semaphores.at[index],
        )
        copy.start()
        copies.append(copy)
    for copy in copies:
        copy.wait()


def rows_kernel(cot_ref, rows_ref, data_ref, semaphores):
    _, rows_x, rows_y, depth = data_ref.shape
    cells = rows_x * rows_y
    chunks = semaphores.shape[0]
    size = WIDTH // chunks
    copies = [
        pltpu.make_async_copy(
            cot_ref.at[pl.ds(index * size, size)],
            data_ref.at[pl.ds(index * size, size)],
            semaphores.at[index],
        )
        for index in range(chunks)
    ]
    for copy in copies:
        copy.start()
    for index, copy in enumerate(copies):
        copy.wait()
        data = data_ref[index * size : (index + 1) * size].astype(jnp.float32)
        data = jnp.concatenate([data[:, at_x] for at_x in range(rows_x)], axis=1)
        data = data.reshape(size * cells, depth).astype(jnp.bfloat16)
        rows_ref[index * size * cells : (index + 1) * size * cells, :] = data


def run(kernel, outs, operands, places=pltpu.VMEM, target=pltpu.VMEM, flops=0, scratch=(),
        mebibytes=16):
    moved = sum(x.size * x.dtype.itemsize for x in tuple(operands) + tuple(outs))
    found = pl.pallas_call(
        kernel,
        out_shape=tuple(outs),
        in_specs=[pl.BlockSpec(memory_space=places)] * len(operands),
        out_specs=tuple(pl.BlockSpec(memory_space=target) for _ in outs),
        scratch_shapes=list(scratch),
        compiler_params=pltpu.CompilerParams(vmem_limit_bytes=mebibytes * 1024 * 1024),
        cost_estimate=pl.CostEstimate(flops=flops, bytes_accessed=moved, transcendentals=0),
    )(*operands)
    return found[0] if len(outs) == 1 else found


def per_device_kernels(field, cotangent, qk_weight, w_value, w_out):
    span_x = lax.axis_size("gx")
    span_y = lax.axis_size("gy")
    count = span_x * span_y
    rows_x, rows_y, depth = field.shape[1:]
    cells = rows_x * rows_y
    places = count * cells
    grid_x = rows_x * span_x
    grid_y = rows_y * span_y
    rows = WIDTH * cells
    wide = WIDTH * HEAD_DIM
    f32, bf16 = jnp.float32, jnp.bfloat16
    like = jax.ShapeDtypeStruct
    lengths = ((grid_x, grid_y * depth), (grid_y, grid_x * depth))

    cell = np.arange(places)
    at_x = cell // cells // span_y * rows_x + cell % cells // rows_y
    at_y = cell // cells % span_y * rows_y + cell % rows_y
    same = jnp.asarray(
        np.stack([at_x[:, None] == at_x[None], at_y[:, None] == at_y[None]]), dtype=bf16
    )

    half = depth // 2
    halves = pltpu.VMEM((2, WIDTH, half), f32)
    chunked = [pltpu.VMEM(field.shape, bf16), pltpu.SemaphoreType.DMA((4,))]
    factor_z = 1.0 / math.sqrt(HEAD_DIM * depth)
    cube = rows * wide * depth * 2

    cots = run(
        rows_kernel,
        [like((rows, depth), bf16)],
        (pltpu.with_memory_space_constraint(cotangent, pltpu.HBM),),
        places=pltpu.HBM,
        flops=cube,
        scratch=chunked,
    )

    def swaps(sent, axis, size, farthest=True):
        if not isinstance(sent, (tuple, list)):
            sent = [sent] * size
        steps = range(size - 1, 0, -1)
        found = {}
        for step in steps if farthest else reversed(steps):
            found[step] = swap(sent[step], axis, size, step)
        return tuple(sent[:1]) + tuple(found[step] for step in steps)

    def taken(kernel, sent, dtype=None, last=False):
        found, *others = sent
        for part in others if last else others[:-1]:
            more = part.shape[0] if kernel is stack_kernel else part.shape[0] - WIDTH
            shape = (found.shape[0] + more,) + part.shape[1:]
            found = run(kernel, [like(shape, dtype or found.dtype)], (found, part))
        return (found,) if last else (found, others[-1])

    *sums, cols = run(
        sums_kernel,
        [like((WIDTH + cells, half), f32)] * 2 + [like((rows, depth), bf16)],
        (pltpu.with_memory_space_constraint(field, pltpu.HBM),),
        places=pltpu.HBM,
        flops=cube // 4,
        scratch=[chunked[0], halves, chunked[1]],
    )
    wv, wo, wq, wk, wz = run(
        prepare_kernel,
        [like((WIDTH, wide), f32)] * 2 + [like((2 * WIDTH, wide), bf16)] * 2
        + [like((2 * WIDTH, WIDTH), f32)],
        (w_value, w_out, qk_weight),
        flops=cube // 8,
    )
    total, other = sums
    for level in range(span_x.bit_length() - 1):
        step = 1 << level
        total = run(
            functools.partial(add_beside_kernel, step),
            [like((WIDTH + cells, half), f32)],
            (total, swap(total if level else other, "gx", span_x, step)),
        )
    sent = run(narrow_kernel, [like((WIDTH + 2 * cells, half), bf16)], (total,))
    for part in swaps(sent, "gy", span_y)[1:]:
        shape = (total.shape[0] + cells, half)
        total = run(add_narrow_kernel, [like(shape, f32)], (total, part))
    totals = (total,)
    totals, cots, wz = lax.optimization_barrier((totals, cots, wz))
    mine = run(
        functools.partial(factor_kernel, grid_x * grid_y),
        [like((WIDTH + HEAD_DIM, half), f32)],
        totals,
    )
    mix, feat, full = run(
        functools.partial(plane_kernel, cells, span_x, lengths),
        [like((2, HEADS * cells, places), f32), like((8, places, WIDTH), f32),
         like((2, HEADS * places, places), f32)],
        totals + (same, qk_weight),
        flops=cube // 2,
    )
    send, both, feat_z = run(
        coef_kernel,
        [like((2 * cells, wide), bf16), like((2 * WIDTH, depth), bf16),
         like((WIDTH + HEAD_DIM, depth), f32)],
        (mine, swap(mine, "gx", span_x, 1), wz, cols, cots, wv, wo),
        flops=2 * cube,
        scratch=[pltpu.VMEM((2, WIDTH + HEAD_DIM, half), f32)],
    )
    (low,) = taken(stack_kernel, swaps(send, "gy", span_y), last=True)
    first, *others = swaps(low, "gx", span_x, False)
    lows = (first,) + tuple(reversed(others))
    pulled = like((WIDTH, depth), bf16)
    top, total = run(
        functools.partial(mix_kernel, factor_z, span_x),
        [like((2, cells, wide), f32), pulled],
        lows + (mix, wv, wo, wq, wk, cols, cots),
        flops=cube,
    )
    total = run(add_pull_kernel, [pulled], (total, swap(total, "gx", span_x, 1)))
    base = run(base_kernel, [like((rows, depth), f32)], (top, wv, both, cots), flops=cube)
    total, base = lax.optimization_barrier((total, base))
    for level in range(1, span_x.bit_length() - 1):
        total = run(add_pull_kernel, [pulled], (total, swap(total, "gx", span_x, 1 << level)))
    layer_output = run(
        output_kernel, [like(field.shape, bf16)], (top, wo, both, cols), flops=cube
    )
    plane = run(
        functools.partial(gram_kernel, cells, lengths, factor_z),
        [like((rows, LANES), f32)],
        lows + (feat, full, same, qk_weight),
        flops=2 * cube,
    )
    total, layer_output, plane = lax.optimization_barrier((total, layer_output, plane))
    field_grad = run(
        functools.partial(final_kernel, grid_x * grid_y),
        [like(field.shape, bf16)],
        swaps(total, "gy", span_y, False) + (feat_z, base, plane),
        target=pltpu.HBM,
        scratch=chunked,
    )
    return (layer_output, field_grad)


def solution(mesh):
    placed = P(None, ("groups", "gx"), "gy", None)
    count = mesh.shape["gx"] * mesh.shape["gy"]

    def program(*arrays):
        _, grid_x, grid_y, depth = arrays[0].shape
        places = grid_x // mesh.shape["groups"] * grid_y
        small = places == LANES and places == 8 * count
        small = small and depth == LANES * mesh.shape["gx"] and count & (count - 1) == 0
        small = small and mesh.shape["gx"] > 3
        return jax.shard_map(
            per_device_kernels if small else per_device,
            mesh=mesh,
            in_specs=(placed, placed, P(), P(), P()),
            out_specs=(placed, placed),
            check_vma=False,
        )(*arrays)

    return program
```

```python
import functools
import math

import jax
import jax.numpy as jnp
import numpy as np
from jax import lax
from jax.experimental import pallas as pl
from jax.experimental.pallas import tpu as pltpu
from jax.sharding import PartitionSpec as P

WIDTH = 64
HEADS = 8
HEAD_DIM = 8
LANES = 128

EPSILON = 1e-06
PRECISE = lax.Precision.HIGHEST
AXES = ("gx", "gy")


def exchange(parts):
    return lax.all_to_all(parts, AXES, split_axis=0, concat_axis=0, tiled=True)


def swap(part, axis, size, step):
    return lax.ppermute(part, axis, [(i, i ^ step) for i in range(size)])


def gather(part, count):
    return exchange(jnp.broadcast_to(part[None], (count,) + part.shape))


def reduce_blocks(total, count):
    width, depth = total.shape
    blocks = total.reshape(width, depth // LANES, LANES).transpose(1, 0, 2)
    blocks = blocks.reshape(count, width * depth // LANES // count, LANES)
    mine = jnp.sum(exchange(blocks), axis=0)
    whole = gather(mine, count).reshape(depth // LANES, width, LANES)
    return whole.transpose(1, 0, 2).reshape(width, depth)


def axis_features(pooled, weights):
    inverse = lax.rsqrt(jnp.mean(pooled * pooled, axis=0, keepdims=True) + EPSILON)
    normed = pooled * inverse
    length = pooled.shape[1]
    factor = 1.0 / math.sqrt(HEAD_DIM * length)
    queries = jnp.dot(weights[0].T, normed, precision=PRECISE).reshape(HEADS, HEAD_DIM, length)
    keyset = jnp.dot(weights[1].T, normed, precision=PRECISE).reshape(HEADS, HEAD_DIM, length)
    return (normed, inverse, queries, keyset, factor)


def axis_kernel(queries, keyset, factor):
    scores = jnp.einsum("hdm,hdn->hmn", queries, keyset, precision=PRECISE)
    return (scores * factor).astype(jnp.bfloat16)


def kernel_backward(gram, queries, keyset, factor):
    grad_query = factor * jnp.einsum("hmn,hdn->hdm", gram, keyset, precision=PRECISE)
    grad_keyset = factor * jnp.einsum("hmn,hdm->hdn", gram, queries, precision=PRECISE)
    return (grad_query, grad_keyset)


def grad_of_normed(weights, grad_query, grad_keyset):
    length = grad_query.shape[-1]
    grad_normed = jnp.dot(weights[0], grad_query.reshape(WIDTH, length), precision=PRECISE)
    return grad_normed + jnp.dot(
        weights[1], grad_keyset.reshape(WIDTH, length), precision=PRECISE
    )


def pooled_grad(normed, inverse, grad_normed):
    return inverse * (grad_normed - normed * jnp.mean(grad_normed * normed, axis=0, keepdims=True))


def f32_einsum(pattern, left, right):
    return jnp.einsum(pattern, left, right, preferred_element_type=jnp.float32)


def per_device(field, cotangent, qk_weight, w_value, w_out):
    span_x = lax.axis_size("gx")
    span_y = lax.axis_size("gy")
    count = span_x * span_y
    rows_x, rows_y, depth = field.shape[1:]
    cells = rows_x * rows_y
    grid_x = rows_x * span_x
    grid_y = rows_y * span_y
    start_x = lax.axis_index("gx") * rows_x
    start_y = lax.axis_index("gy") * rows_y
    bf16 = jnp.bfloat16

    cols = field.reshape(WIDTH, cells, depth)
    cots = cotangent.reshape(WIDTH, cells, depth)

    sum_z = jnp.sum(cols, axis=1, dtype=jnp.float32)
    sum_rows = jnp.sum(cols, axis=2, dtype=jnp.float32)
    rows_all = gather(sum_rows.T, count).reshape(span_x, span_y, rows_x, rows_y, WIDTH)
    total_x = jnp.sum(rows_all, axis=(1, 3)).reshape(grid_x, WIDTH).T
    total_y = jnp.sum(rows_all, axis=(0, 2)).reshape(grid_y, WIDTH).T
    total_z = reduce_blocks(sum_z, count)

    normed_x, inverse_x, query_x, keyset_x, factor_x = axis_features(
        total_x / (grid_y * depth), qk_weight[0]
    )
    normed_y, inverse_y, query_y, keyset_y, factor_y = axis_features(
        total_y / (grid_x * depth), qk_weight[1]
    )
    normed_z, inverse_z, query_z, keyset_z, factor_z = axis_features(
        total_z / (grid_x * grid_y), qk_weight[2]
    )
    kernel_x = axis_kernel(query_x, keyset_x, factor_x)
    kernel_y = axis_kernel(query_y, keyset_y, factor_y)
    query_b = query_z.astype(bf16)
    keyset_b = keyset_z.astype(bf16)

    wv = w_value.reshape(WIDTH, HEADS, HEAD_DIM)
    wo = w_out.reshape(HEADS, HEAD_DIM, WIDTH)
    coef_f = f32_einsum("cpk,hgk->cphg", cols, keyset_b)
    coef_c = f32_einsum("cpz,hgz->cphg", cots, query_b)
    low_f = jnp.einsum("chd,cphg->phdg", wv.astype(jnp.float32), coef_f, precision=PRECISE)
    low_c = jnp.einsum("hdc,cphg->phdg", wo.astype(jnp.float32), coef_c, precision=PRECISE)
    squares = HEAD_DIM * HEAD_DIM
    both = jnp.stack([low_f, low_c]).astype(bf16).reshape(2, cells, HEADS * squares)
    both = gather(both, count).reshape(span_x, span_y, 2, rows_x, rows_y, HEADS * squares)
    both = both.transpose(2, 0, 3, 1, 4, 5).reshape(2, grid_x, grid_y, HEADS, squares)
    low_f, low_c = both[0], both[1]

    mid_f = f32_einsum("hyj,xjhq->xyhq", kernel_y, low_f).astype(bf16)
    top_f = f32_einsum("hxi,iyhq->xyhq", kernel_x, mid_f)
    mid_c = f32_einsum("hxi,xyhq->iyhq", kernel_x, low_c).astype(bf16)
    top_c = f32_einsum("hyj,xyhq->xjhq", kernel_y, mid_c)
    gram_x = factor_z * f32_einsum("myhq,nyhq->hmn", low_c, mid_f)
    gram_y = factor_z * f32_einsum("xmhq,xnhq->hmn", mid_c, low_f)

    def here(top):
        top = lax.dynamic_slice_in_dim(top, start_x, rows_x, 0)
        top = lax.dynamic_slice_in_dim(top, start_y, rows_y, 1)
        return top.reshape(cells, HEADS, HEAD_DIM, HEAD_DIM)

    left_f = factor_z * jnp.einsum(
        "hdc,phdg->cphg", wo.astype(jnp.float32), here(top_f), precision=PRECISE
    )
    left_c = factor_z * jnp.einsum(
        "chd,phdg->cphg", wv.astype(jnp.float32), here(top_c), precision=PRECISE
    )
    left_f = left_f.astype(bf16)
    left_c = left_c.astype(bf16)

    grad_query_z = f32_einsum("cphg,cpz->hgz", left_f, cots)
    grad_keyset_z = f32_einsum("cphg,cpz->hgz", left_c, cols)
    gn_z = reduce_blocks(grad_of_normed(qk_weight[2], grad_query_z, grad_keyset_z), count)

    layer_output = (cols.astype(jnp.float32) + f32_einsum("cphg,hgz->cpz", left_f, query_b)).astype(bf16)
    through = f32_einsum("cphg,hgz->cpz", left_c, keyset_b)

    gn_x = grad_of_normed(qk_weight[0], *kernel_backward(gram_x, query_x, keyset_x, factor_x))
    gn_y = grad_of_normed(qk_weight[1], *kernel_backward(gram_y, query_y, keyset_y, factor_y))
    pull_x = pooled_grad(normed_x, inverse_x, gn_x)
    pull_y = pooled_grad(normed_y, inverse_y, gn_y)
    pull_z = pooled_grad(normed_z, inverse_z, gn_z)
    local_x = lax.dynamic_slice_in_dim(pull_x, start_x, rows_x, 1) / (grid_y * depth)
    local_y = lax.dynamic_slice_in_dim(pull_y, start_y, rows_y, 1) / (grid_x * depth)
    local_xy = (local_x[:, :, None] + local_y[:, None, :]).reshape(WIDTH, cells)
    local_z = pull_z / (grid_x * grid_y)
    field_grad = (
        cots.astype(jnp.float32) + through + local_xy[:, :, None] + local_z[:, None, :]
    ).astype(bf16)
    return (layer_output.reshape(field.shape), field_grad.reshape(field.shape))


def split(x):
    high = x.astype(jnp.bfloat16)
    return high, (x - high.astype(jnp.float32)).astype(jnp.bfloat16)


NN = (((1,), (0,)), ((), ()))
NT = (((1,), (1,)), ((), ()))
TN = (((0,), (0,)), ((), ()))


def mul(left, right, dims=NN):
    return lax.dot_general(left, right, dims, preferred_element_type=jnp.float32)


def mul_near(left, right, dims=NN):
    left_high, left_low = split(left)
    right_high, right_low = split(right)
    return (
        mul(left_high, right_high, dims)
        + mul(left_low, right_high, dims)
        + mul(left_high, right_low, dims)
    )


def mul_left(left, right, dims=NN):
    rows = left.shape[0]
    both = mul(jnp.concatenate(split(left), axis=0), right, dims)
    return both[:rows] + both[rows:]


def number(shape, dim):
    return lax.broadcasted_iota(jnp.int32, shape, dim)


def join_halves(half_ref, mine_ref, other_ref):
    core = lax.axis_index("gx") & 1
    half_ref[core] = mine_ref[...]
    half_ref[core ^ 1] = other_ref[...]
    return jnp.concatenate([half_ref[0], half_ref[1]], axis=1)


def expand(part):
    depth = part.shape[1]
    part = part.reshape(HEADS, 1, HEAD_DIM, depth)
    part = jnp.broadcast_to(part, (HEADS, HEAD_DIM, HEAD_DIM, depth))
    return part.reshape(WIDTH * HEAD_DIM, depth).astype(jnp.bfloat16)


def spread(weights, top):
    left = weights[:, None, :] * top[None]
    return left.reshape(-1, left.shape[2]).astype(jnp.bfloat16)


def prepare_kernel(wv_ref, wo_ref, qk_ref, wv_out, wo_out, wq_out, wk_out, wz_out):
    wide = HEADS * HEAD_DIM * HEAD_DIM
    row = number((WIDTH, wide), 0)
    lane = number((WIDTH, wide), 1)
    by_channel = ((lane >> 3) == row).astype(jnp.bfloat16)
    by_factor = (((lane >> 6) * HEAD_DIM + (lane & 7)) == row).astype(jnp.bfloat16)
    wv_out[...] = mul(wv_ref[...], by_channel)
    wo_out[...] = mul(wo_ref[...], by_channel, TN)
    for index, out in ((0, wq_out), (1, wk_out)):
        high, low = split(qk_ref[2, index])
        out[0:WIDTH, :] = mul(high, by_factor).astype(jnp.bfloat16)
        out[WIDTH : 2 * WIDTH, :] = mul(low, by_factor).astype(jnp.bfloat16)
        wz_out[index * WIDTH : (index + 1) * WIDTH, :] = qk_ref[2, index].T


def sums_kernel(field_ref, *refs):
    outs, (cols_ref, data_ref, half_ref, semaphores) = refs[:-4], refs[-4:]
    _, rows_x, rows_y, depth = data_ref.shape
    cells = rows_x * rows_y
    chunks = semaphores.shape[0]
    size = WIDTH // chunks
    copies = [
        pltpu.make_async_copy(
            field_ref.at[pl.ds(index * size, size)],
            data_ref.at[pl.ds(index * size, size)],
            semaphores.at[index],
        )
        for index in range(chunks)
    ]
    for copy in copies:
        copy.start()
    own = jnp.zeros((cells, LANES), jnp.float32)
    pick = number((size, size * cells), 1) // cells == number((size, size * cells), 0)
    pick = pick.astype(jnp.bfloat16)
    for index, copy in enumerate(copies):
        copy.wait()
        rows = slice(index * size, (index + 1) * size)
        data = data_ref[rows].astype(jnp.float32)
        data = jnp.concatenate([data[:, at_x] for at_x in range(rows_x)], axis=1)
        lanes = data[..., :LANES]
        for start in range(LANES, depth, LANES):
            lanes = lanes + data[..., start : start + LANES]
        row_sums = jnp.sum(lanes, axis=2, keepdims=True)
        shape = lanes.shape
        mine = number(shape, 0) + index * size == number(shape, 2)
        own = own + jnp.sum(jnp.where(mine, row_sums, 0.0), axis=0)
        data = data.reshape(size * cells, depth).astype(jnp.bfloat16)
        cols_ref[index * size * cells : (index + 1) * size * cells, :] = data
        part = mul(pick, data)
        half_ref[0, rows, :] = part[:, : depth // 2]
        half_ref[1, rows, :] = part[:, depth // 2 :]
    for step, out in enumerate(outs):
        out[0:WIDTH, :] = half_ref[(lax.axis_index("gx") & 1) ^ step]
        out[WIDTH:, :] = jnp.concatenate([own] * (depth // 2 // LANES), axis=1)


def add_beside_kernel(known, mine_ref, other_ref, out_ref):
    out_ref[0:WIDTH, :] = mine_ref[0:WIDTH, :] + other_ref[0:WIDTH, :]
    lanes = known * WIDTH
    rest = out_ref.shape[1] - 2 * lanes
    rows = [mine_ref[WIDTH:, 0:lanes], other_ref[WIDTH:, 0:lanes]]
    if rest > 0:
        rows.append(jnp.zeros((rows[0].shape[0], rest), jnp.float32))
    out_ref[WIDTH:, :] = jnp.concatenate(rows, axis=1)


def narrow_kernel(total_ref, out_ref):
    out_ref[0:WIDTH, :] = total_ref[0:WIDTH, :].astype(jnp.bfloat16)
    high, low = split(total_ref[WIDTH:, :])
    out_ref[WIDTH:, :] = jnp.concatenate([high, low], axis=0)


def add_narrow_kernel(found_ref, part_ref, out_ref):
    known = found_ref.shape[0]
    part = part_ref[...].astype(jnp.float32)
    cells = (part.shape[0] - WIDTH) // 2
    out_ref[0:WIDTH, :] = found_ref[0:WIDTH, :] + part[0:WIDTH]
    out_ref[WIDTH:known, :] = found_ref[WIDTH:, :]
    out_ref[known:, :] = part[WIDTH : WIDTH + cells] + part[WIDTH + cells :]


def stack_kernel(*refs):
    refs[-1][...] = jnp.concatenate([ref[...] for ref in refs[:-1]], axis=0)


def factor_kernel(places, *refs):
    parts, feat_ref = refs[:-1], refs[-1]
    total = parts[0][0:WIDTH, :]
    for part in parts[1:]:
        total = total + part[0:WIDTH, :]
    pooled = total * (1.0 / places)
    inverse = lax.rsqrt(jnp.mean(pooled * pooled, axis=0, keepdims=True) + EPSILON)
    normed = pooled * inverse
    feat_ref[0:WIDTH, :] = normed
    feat_ref[WIDTH:, :] = jnp.broadcast_to(inverse, (HEAD_DIM, inverse.shape[1]))


def add_pull_kernel(*refs):
    total = refs[0][...].astype(jnp.float32)
    for part in refs[1:-1]:
        total = total + part[...].astype(jnp.float32)
    refs[-1][...] = total.astype(refs[-1].dtype)


def by_head(part):
    shape = (HEADS, part.shape[0], WIDTH)
    mine = number(shape, 0) == (number(shape, 2) >> 3)
    return jnp.where(mine, part[None], 0.0).reshape(-1, WIDTH)


def plane_kernel(cells, span_x, lengths, *refs):
    parts, (same_ref, qk_ref, mix_ref, feat_ref, full_ref) = refs[:-5], refs[-5:]
    totals = jnp.concatenate(
        [
            part[start : start + cells, step * WIDTH : (step + 1) * WIDTH]
            for step in range(span_x)
            for part in parts
            for start in range(WIDTH, part.shape[0], cells)
        ],
        axis=0,
    )
    places = totals.shape[0]
    high, low = split(totals)
    forward = backward = None
    for axis in range(2):
        same = same_ref[axis]
        pooled = (mul(same, high) + mul(same, low)) * (1.0 / lengths[axis][1])
        inverse = lax.rsqrt(jnp.mean(pooled * pooled, axis=1, keepdims=True) + EPSILON)
        normed = pooled * inverse
        query = mul_near(normed, qk_ref[axis, 0])
        keyset = mul_near(normed, qk_ref[axis, 1])
        feat_ref[4 * axis] = normed
        feat_ref[4 * axis + 1] = query
        feat_ref[4 * axis + 2] = keyset
        feat_ref[4 * axis + 3] = jnp.broadcast_to(inverse, (places, WIDTH))
        factor = 1.0 / math.sqrt(HEAD_DIM * lengths[axis][0])

        def scores(rows, other):
            found = mul_near(by_head(rows), other, NT) * factor
            return found.astype(jnp.bfloat16).astype(jnp.float32)

        full = scores(query, keyset)
        full_ref[axis] = full
        one = full.reshape(HEADS, places, places)[:, :cells].reshape(-1, places)
        two = scores(keyset[:cells], query)
        forward = one if forward is None else forward * one
        backward = two if backward is None else backward * two
    mix_ref[0] = forward
    mix_ref[1] = backward


def coef_kernel(mine_ref, other_ref, wz_ref, field_ref, cot_ref, wv_ref, wo_ref,
                send_ref, both_ref, feat_ref, half_ref):
    rows, depth = field_ref.shape
    cells = rows // WIDTH
    wide = HEADS * HEAD_DIM * HEAD_DIM
    feat = join_halves(half_ref, mine_ref, other_ref)
    feat_ref[...] = feat
    high, low = split(feat[:WIDTH])
    both = mul_left(wz_ref[...], high) + mul(wz_ref[...].astype(jnp.bfloat16), low)
    both_ref[...] = both.astype(jnp.bfloat16)
    query = expand(both[:WIDTH])
    keyset = expand(both[WIDTH:])
    low_f = mul(field_ref[...], keyset, NT).reshape(WIDTH, cells, wide)
    low_f = jnp.sum(wv_ref[...][:, None, :] * low_f, axis=0)
    low_c = mul(cot_ref[...], query, NT).reshape(WIDTH, cells, wide)
    low_c = jnp.sum(wo_ref[...][:, None, :] * low_c, axis=0)
    low = jnp.concatenate([low_f, low_c], axis=0).astype(jnp.bfloat16)
    send_ref[...] = low


def join_low(refs, cells):
    low = jnp.concatenate([ref[...].astype(jnp.float32) for ref in refs], axis=0)
    wide = low.shape[1]
    low = low.reshape(-1, 2 * cells, wide)
    return [
        low[:, start : start + cells].reshape(-1, wide).astype(jnp.bfloat16)
        for start in (0, cells)
    ]


def mix_kernel(factor, spans, *refs):
    lows, refs = refs[:spans], refs[spans:]
    mix_ref, wv_ref, wo_ref, wq_ref, wk_ref, field_ref, cot_ref, top_ref = refs[:8]
    mine_ref, other_ref, half_ref = refs[8:]
    cells = field_ref.shape[0] // WIDTH
    low_f, low_c = join_low(lows, cells)
    wide = low_f.shape[1]
    shape = (HEADS, cells, wide)
    head = number(shape, 0) == (number(shape, 2) >> 6)

    def top(mix, low):
        found = mul_left(mix, low).reshape(shape)
        return jnp.sum(jnp.where(head, found, 0.0), axis=0) * factor

    top_f = top(mix_ref[0], low_f)
    top_c = top(mix_ref[1], low_c)
    top_ref[0] = top_f
    top_ref[1] = top_c
    left_f = spread(wo_ref[...], top_f)
    left_c = spread(wv_ref[...], top_c)

    def pull(weights, left, right):
        found = mul(weights, left, NT)
        return mul_left(found[:WIDTH] + found[WIDTH:], right)

    found = pull(wq_ref[...], left_f, cot_ref[...]) + pull(wk_ref[...], left_c, field_ref[...])
    half = found.shape[1] // 2
    half_ref[0] = found[:, :half]
    half_ref[1] = found[:, half:]
    core = lax.axis_index("gx") & 1
    mine_ref[...] = half_ref[core].astype(jnp.bfloat16)
    other_ref[...] = half_ref[core ^ 1].astype(jnp.bfloat16)


def put_cells(ref, total):
    _, rows_x, rows_y, depth = ref.shape
    total = total.reshape(WIDTH, rows_x * rows_y, depth)
    for index in range(rows_x):
        rows = total[:, index * rows_y : (index + 1) * rows_y, :]
        ref[:, index, :, :] = rows.astype(jnp.bfloat16)


def output_kernel(top_ref, wo_ref, both_ref, field_ref, out_ref):
    query = expand(both_ref[...].astype(jnp.float32)[:WIDTH])
    left = spread(wo_ref[...], top_ref[0])
    put_cells(out_ref, mul(left, query) + field_ref[...].astype(jnp.float32))


def gram_kernel(cells, lengths, factor_z, *refs):
    lows, (feat_ref, full_ref, same_ref, qk_ref, out_ref) = refs[:-5], refs[-5:]
    low_f, low_c = join_low(lows, cells)
    places, wide = low_f.shape
    squares = HEAD_DIM * HEAD_DIM
    lane = number((places, LANES), 1)
    products = []
    for pair in range(wide // LANES):
        part_f = low_f[:, pair * LANES : (pair + 1) * LANES]
        part_c = low_c[:, pair * LANES : (pair + 1) * LANES]
        for half in range(LANES // squares):
            mine = (lane >> 6) == half
            products.append(mul(jnp.where(mine, part_c, jnp.zeros_like(part_c)), part_f, NT))
    product = jnp.concatenate(products, axis=0)
    factors = [1.0 / math.sqrt(HEAD_DIM * lengths[axis][0]) for axis in range(2)]
    queries = [by_head(feat_ref[4 * axis + 1]).astype(jnp.bfloat16) for axis in range(2)]
    keysets = [by_head(feat_ref[4 * axis + 2]).astype(jnp.bfloat16) for axis in range(2)]
    total = jnp.zeros((cells, WIDTH), jnp.float32)
    for axis in range(2):
        gram = (product * full_ref[1 - axis]).astype(jnp.bfloat16)
        across = jnp.concatenate(
            [gram[h * places : (h + 1) * places] for h in range(HEADS)], axis=1
        )
        scale = factors[axis] * factor_z
        grad_query = mul(across, keysets[axis]) * scale
        grad_keyset = mul(gram, queries[axis], TN) * scale
        found = mul_near(grad_query, qk_ref[axis, 0], NT) + mul_near(grad_keyset, qk_ref[axis, 1], NT)
        high, low = split(found)
        own = same_ref[axis, 0 : 2 * cells, :]
        found = (mul(own, high) + mul(own, low))[:cells]
        normed = feat_ref[4 * axis, 0:cells, :]
        inverse = feat_ref[4 * axis + 3, 0:cells, :]
        found = found - normed * jnp.mean(found * normed, axis=1, keepdims=True)
        total = total + inverse * found * (1.0 / lengths[axis][1])
    shape = (WIDTH, cells, WIDTH)
    own = jnp.where(number(shape, 0) == number(shape, 2), total[None], 0.0)
    out_ref[...] = mul_left(own.reshape(-1, WIDTH), jnp.ones((WIDTH, LANES), jnp.bfloat16))


def base_kernel(top_ref, wv_ref, both_ref, cot_ref, out_ref):
    keyset = expand(both_ref[...].astype(jnp.float32)[WIDTH:])
    left = spread(wv_ref[...], top_ref[1])
    out_ref[...] = mul(left, keyset) + cot_ref[...].astype(jnp.float32)


def final_kernel(places, mine_ref, other_ref, feat_ref, base_ref, plane_ref, out_ref, data_ref,
                 half_ref, semaphores):
    depth = base_ref.shape[1]
    _, rows_x, rows_y, _ = data_ref.shape
    found = join_halves(half_ref, mine_ref, other_ref)
    normed = feat_ref[0:WIDTH, :]
    inverse = feat_ref[WIDTH : WIDTH + 1, :]
    found = inverse * (found - normed * jnp.mean(found * normed, axis=0, keepdims=True))
    found = found * (1.0 / places)
    cells = rows_x * rows_y
    chunks = semaphores.shape[0]
    size = WIDTH // chunks
    copies = []
    for index in range(chunks):
        rows = slice(index * size, (index + 1) * size)
        base = base_ref[index * size * cells : (index + 1) * size * cells, :]
        plane = plane_ref[index * size * cells : (index + 1) * size * cells, :]
        base = base + jnp.concatenate([plane] * (depth // LANES), axis=1)
        total = base.reshape(size, cells, depth) + found[rows][:, None, :]
        for at_x in range(rows_x):
            part = total[:, at_x * rows_y : (at_x + 1) * rows_y, :]
            data_ref[rows, at_x, :, :] = part.astype(jnp.bfloat16)
        copy = pltpu.make_async_copy(
            data_ref.at[pl.ds(index * size, size)],
            out_ref.at[pl.ds(index * size, size)],
            semaphores.at[index],
        )
        copy.start()
        copies.append(copy)
    for copy in copies:
        copy.wait()


def rows_kernel(cot_ref, rows_ref, data_ref, semaphores):
    _, rows_x, rows_y, depth = data_ref.shape
    cells = rows_x * rows_y
    chunks = semaphores.shape[0]
    size = WIDTH // chunks
    copies = [
        pltpu.make_async_copy(
            cot_ref.at[pl.ds(index * size, size)],
            data_ref.at[pl.ds(index * size, size)],
            semaphores.at[index],
        )
        for index in range(chunks)
    ]
    for copy in copies:
        copy.start()
    for index, copy in enumerate(copies):
        copy.wait()
        data = data_ref[index * size : (index + 1) * size].astype(jnp.float32)
        data = jnp.concatenate([data[:, at_x] for at_x in range(rows_x)], axis=1)
        data = data.reshape(size * cells, depth).astype(jnp.bfloat16)
        rows_ref[index * size * cells : (index + 1) * size * cells, :] = data


def run(kernel, outs, operands, places=pltpu.VMEM, target=pltpu.VMEM, flops=0, scratch=(),
        mebibytes=16):
    moved = sum(x.size * x.dtype.itemsize for x in tuple(operands) + tuple(outs))
    found = pl.pallas_call(
        kernel,
        out_shape=tuple(outs),
        in_specs=[pl.BlockSpec(memory_space=places)] * len(operands),
        out_specs=tuple(pl.BlockSpec(memory_space=target) for _ in outs),
        scratch_shapes=list(scratch),
        compiler_params=pltpu.CompilerParams(vmem_limit_bytes=mebibytes * 1024 * 1024),
        cost_estimate=pl.CostEstimate(flops=flops, bytes_accessed=moved, transcendentals=0),
    )(*operands)
    return found[0] if len(outs) == 1 else found


def per_device_kernels(field, cotangent, qk_weight, w_value, w_out):
    span_x = lax.axis_size("gx")
    span_y = lax.axis_size("gy")
    count = span_x * span_y
    rows_x, rows_y, depth = field.shape[1:]
    cells = rows_x * rows_y
    places = count * cells
    grid_x = rows_x * span_x
    grid_y = rows_y * span_y
    rows = WIDTH * cells
    wide = WIDTH * HEAD_DIM
    f32, bf16 = jnp.float32, jnp.bfloat16
    like = jax.ShapeDtypeStruct
    lengths = ((grid_x, grid_y * depth), (grid_y, grid_x * depth))

    cell = np.arange(places)
    at_x = cell // cells // span_y * rows_x + cell % cells // rows_y
    at_y = cell // cells % span_y * rows_y + cell % rows_y
    same = jnp.asarray(
        np.stack([at_x[:, None] == at_x[None], at_y[:, None] == at_y[None]]), dtype=bf16
    )

    half = depth // 2
    halves = pltpu.VMEM((2, WIDTH, half), f32)
    chunked = [pltpu.VMEM(field.shape, bf16), pltpu.SemaphoreType.DMA((4,))]
    factor_z = 1.0 / math.sqrt(HEAD_DIM * depth)
    cube = rows * wide * depth * 2

    cots = run(
        rows_kernel,
        [like((rows, depth), bf16)],
        (pltpu.with_memory_space_constraint(cotangent, pltpu.HBM),),
        places=pltpu.HBM,
        flops=cube,
        scratch=chunked,
    )

    def swaps(sent, axis, size, farthest=True):
        if not isinstance(sent, (tuple, list)):
            sent = [sent] * size
        steps = range(size - 1, 0, -1)
        found = {}
        for step in steps if farthest else reversed(steps):
            found[step] = swap(sent[step], axis, size, step)
        return tuple(sent[:1]) + tuple(found[step] for step in steps)

    def taken(kernel, sent, dtype=None, last=False):
        found, *others = sent
        for part in others if last else others[:-1]:
            more = part.shape[0] if kernel is stack_kernel else part.shape[0] - WIDTH
            shape = (found.shape[0] + more,) + part.shape[1:]
            found = run(kernel, [like(shape, dtype or found.dtype)], (found, part))
        return (found,) if last else (found, others[-1])

    *sums, cols = run(
        sums_kernel,
        [like((WIDTH + cells, half), f32)] * 2 + [like((rows, depth), bf16)],
        (pltpu.with_memory_space_constraint(field, pltpu.HBM),),
        places=pltpu.HBM,
        flops=cube // 4,
        scratch=[chunked[0], halves, chunked[1]],
    )
    wv, wo, wq, wk, wz = run(
        prepare_kernel,
        [like((WIDTH, wide), f32)] * 2 + [like((2 * WIDTH, wide), bf16)] * 2
        + [like((2 * WIDTH, WIDTH), f32)],
        (w_value, w_out, qk_weight),
        flops=cube // 8,
    )
    total, other = sums
    for level in range(span_x.bit_length() - 1):
        step = 1 << level
        total = run(
            functools.partial(add_beside_kernel, step),
            [like((WIDTH + cells, half), f32)],
            (total, swap(total if level else other, "gx", span_x, step)),
        )
    sent = run(narrow_kernel, [like((WIDTH + 2 * cells, half), bf16)], (total,))
    for part in swaps(sent, "gy", span_y)[1:]:
        shape = (total.shape[0] + cells, half)
        total = run(add_narrow_kernel, [like(shape, f32)], (total, part))
    totals = (total,)
    totals, cots, wz = lax.optimization_barrier((totals, cots, wz))
    mine = run(
        functools.partial(factor_kernel, grid_x * grid_y),
        [like((WIDTH + HEAD_DIM, half), f32)],
        totals,
    )
    mix, feat, full = run(
        functools.partial(plane_kernel, cells, span_x, lengths),
        [like((2, HEADS * cells, places), f32), like((8, places, WIDTH), f32),
         like((2, HEADS * places, places), f32)],
        totals + (same, qk_weight),
        flops=cube // 2,
    )
    send, both, feat_z = run(
        coef_kernel,
        [like((2 * cells, wide), bf16), like((2 * WIDTH, depth), bf16),
         like((WIDTH + HEAD_DIM, depth), f32)],
        (mine, swap(mine, "gx", span_x, 1), wz, cols, cots, wv, wo),
        flops=2 * cube,
        scratch=[pltpu.VMEM((2, WIDTH + HEAD_DIM, half), f32)],
    )
    (low,) = taken(stack_kernel, swaps(send, "gy", span_y), last=True)
    first, *others = swaps(low, "gx", span_x, False)
    lows = (first,) + tuple(reversed(others))
    pulled = like((WIDTH, half), bf16)
    top, mine, other = run(
        functools.partial(mix_kernel, factor_z, span_x),
        [like((2, cells, wide), f32), pulled, pulled],
        lows + (mix, wv, wo, wq, wk, cols, cots),
        flops=cube,
        scratch=[halves],
    )
    total = run(add_pull_kernel, [pulled], (mine, swap(other, "gx", span_x, 1)))
    base = run(base_kernel, [like((rows, depth), f32)], (top, wv, both, cots), flops=cube)
    total, base = lax.optimization_barrier((total, base))
    for level in range(1, span_x.bit_length() - 1):
        total = run(add_pull_kernel, [pulled], (total, swap(total, "gx", span_x, 1 << level)))
    plane = run(
        functools.partial(gram_kernel, cells, lengths, factor_z),
        [like((rows, LANES), f32)],
        lows + (feat, full, same, qk_weight),
        flops=2 * cube,
    )
    total, plane = lax.optimization_barrier((total, plane))
    layer_output = run(
        output_kernel, [like(field.shape, bf16)], (top, wo, both, cols), flops=cube
    )
    total = run(
        add_pull_kernel, [like(pulled.shape, f32)], swaps(total, "gy", span_y, False)
    )
    total, layer_output = lax.optimization_barrier((total, layer_output))
    field_grad = run(
        functools.partial(final_kernel, grid_x * grid_y),
        [like(field.shape, bf16)],
        (total, swap(total, "gx", span_x, 1), feat_z, base, plane),
        target=pltpu.HBM,
        scratch=[chunked[0], halves, chunked[1]],
    )
    return (layer_output, field_grad)


def solution(mesh):
    placed = P(None, ("groups", "gx"), "gy", None)
    count = mesh.shape["gx"] * mesh.shape["gy"]

    def program(*arrays):
        _, grid_x, grid_y, depth = arrays[0].shape
        places = grid_x // mesh.shape["groups"] * grid_y
        small = places == LANES and places == 8 * count
        small = small and depth == LANES * mesh.shape["gx"] and count & (count - 1) == 0
        small = small and mesh.shape["gx"] > 3
        return jax.shard_map(
            per_device_kernels if small else per_device,
            mesh=mesh,
            in_specs=(placed, placed, P(), P(), P()),
            out_specs=(placed, placed),
            check_vma=False,
        )(*arrays)

    return program
```

```python
import functools
import math

import jax
import jax.numpy as jnp
import numpy as np
from jax import lax
from jax.experimental import pallas as pl
from jax.experimental.pallas import tpu as pltpu
from jax.sharding import PartitionSpec as P

WIDTH = 64
HEADS = 8
HEAD_DIM = 8
LANES = 128

EPSILON = 1e-06
PRECISE = lax.Precision.HIGHEST
AXES = ("gx", "gy")


def exchange(parts):
    return lax.all_to_all(parts, AXES, split_axis=0, concat_axis=0, tiled=True)


def swap(part, axis, size, step):
    return lax.ppermute(part, axis, [(i, i ^ step) for i in range(size)])


def gather(part, count):
    return exchange(jnp.broadcast_to(part[None], (count,) + part.shape))


def reduce_blocks(total, count):
    width, depth = total.shape
    blocks = total.reshape(width, depth // LANES, LANES).transpose(1, 0, 2)
    blocks = blocks.reshape(count, width * depth // LANES // count, LANES)
    mine = jnp.sum(exchange(blocks), axis=0)
    whole = gather(mine, count).reshape(depth // LANES, width, LANES)
    return whole.transpose(1, 0, 2).reshape(width, depth)


def axis_features(pooled, weights):
    inverse = lax.rsqrt(jnp.mean(pooled * pooled, axis=0, keepdims=True) + EPSILON)
    normed = pooled * inverse
    length = pooled.shape[1]
    factor = 1.0 / math.sqrt(HEAD_DIM * length)
    queries = jnp.dot(weights[0].T, normed, precision=PRECISE).reshape(HEADS, HEAD_DIM, length)
    keyset = jnp.dot(weights[1].T, normed, precision=PRECISE).reshape(HEADS, HEAD_DIM, length)
    return (normed, inverse, queries, keyset, factor)


def axis_kernel(queries, keyset, factor):
    scores = jnp.einsum("hdm,hdn->hmn", queries, keyset, precision=PRECISE)
    return (scores * factor).astype(jnp.bfloat16)


def kernel_backward(gram, queries, keyset, factor):
    grad_query = factor * jnp.einsum("hmn,hdn->hdm", gram, keyset, precision=PRECISE)
    grad_keyset = factor * jnp.einsum("hmn,hdm->hdn", gram, queries, precision=PRECISE)
    return (grad_query, grad_keyset)


def grad_of_normed(weights, grad_query, grad_keyset):
    length = grad_query.shape[-1]
    grad_normed = jnp.dot(weights[0], grad_query.reshape(WIDTH, length), precision=PRECISE)
    return grad_normed + jnp.dot(
        weights[1], grad_keyset.reshape(WIDTH, length), precision=PRECISE
    )


def pooled_grad(normed, inverse, grad_normed):
    return inverse * (grad_normed - normed * jnp.mean(grad_normed * normed, axis=0, keepdims=True))


def f32_einsum(pattern, left, right):
    return jnp.einsum(pattern, left, right, preferred_element_type=jnp.float32)


def per_device(field, cotangent, qk_weight, w_value, w_out):
    span_x = lax.axis_size("gx")
    span_y = lax.axis_size("gy")
    count = span_x * span_y
    rows_x, rows_y, depth = field.shape[1:]
    cells = rows_x * rows_y
    grid_x = rows_x * span_x
    grid_y = rows_y * span_y
    start_x = lax.axis_index("gx") * rows_x
    start_y = lax.axis_index("gy") * rows_y
    bf16 = jnp.bfloat16

    cols = field.reshape(WIDTH, cells, depth)
    cots = cotangent.reshape(WIDTH, cells, depth)

    sum_z = jnp.sum(cols, axis=1, dtype=jnp.float32)
    sum_rows = jnp.sum(cols, axis=2, dtype=jnp.float32)
    rows_all = gather(sum_rows.T, count).reshape(span_x, span_y, rows_x, rows_y, WIDTH)
    total_x = jnp.sum(rows_all, axis=(1, 3)).reshape(grid_x, WIDTH).T
    total_y = jnp.sum(rows_all, axis=(0, 2)).reshape(grid_y, WIDTH).T
    total_z = reduce_blocks(sum_z, count)

    normed_x, inverse_x, query_x, keyset_x, factor_x = axis_features(
        total_x / (grid_y * depth), qk_weight[0]
    )
    normed_y, inverse_y, query_y, keyset_y, factor_y = axis_features(
        total_y / (grid_x * depth), qk_weight[1]
    )
    normed_z, inverse_z, query_z, keyset_z, factor_z = axis_features(
        total_z / (grid_x * grid_y), qk_weight[2]
    )
    kernel_x = axis_kernel(query_x, keyset_x, factor_x)
    kernel_y = axis_kernel(query_y, keyset_y, factor_y)
    query_b = query_z.astype(bf16)
    keyset_b = keyset_z.astype(bf16)

    wv = w_value.reshape(WIDTH, HEADS, HEAD_DIM)
    wo = w_out.reshape(HEADS, HEAD_DIM, WIDTH)
    coef_f = f32_einsum("cpk,hgk->cphg", cols, keyset_b)
    coef_c = f32_einsum("cpz,hgz->cphg", cots, query_b)
    low_f = jnp.einsum("chd,cphg->phdg", wv.astype(jnp.float32), coef_f, precision=PRECISE)
    low_c = jnp.einsum("hdc,cphg->phdg", wo.astype(jnp.float32), coef_c, precision=PRECISE)
    squares = HEAD_DIM * HEAD_DIM
    both = jnp.stack([low_f, low_c]).astype(bf16).reshape(2, cells, HEADS * squares)
    both = gather(both, count).reshape(span_x, span_y, 2, rows_x, rows_y, HEADS * squares)
    both = both.transpose(2, 0, 3, 1, 4, 5).reshape(2, grid_x, grid_y, HEADS, squares)
    low_f, low_c = both[0], both[1]

    mid_f = f32_einsum("hyj,xjhq->xyhq", kernel_y, low_f).astype(bf16)
    top_f = f32_einsum("hxi,iyhq->xyhq", kernel_x, mid_f)
    mid_c = f32_einsum("hxi,xyhq->iyhq", kernel_x, low_c).astype(bf16)
    top_c = f32_einsum("hyj,xyhq->xjhq", kernel_y, mid_c)
    gram_x = factor_z * f32_einsum("myhq,nyhq->hmn", low_c, mid_f)
    gram_y = factor_z * f32_einsum("xmhq,xnhq->hmn", mid_c, low_f)

    def here(top):
        top = lax.dynamic_slice_in_dim(top, start_x, rows_x, 0)
        top = lax.dynamic_slice_in_dim(top, start_y, rows_y, 1)
        return top.reshape(cells, HEADS, HEAD_DIM, HEAD_DIM)

    left_f = factor_z * jnp.einsum(
        "hdc,phdg->cphg", wo.astype(jnp.float32), here(top_f), precision=PRECISE
    )
    left_c = factor_z * jnp.einsum(
        "chd,phdg->cphg", wv.astype(jnp.float32), here(top_c), precision=PRECISE
    )
    left_f = left_f.astype(bf16)
    left_c = left_c.astype(bf16)

    grad_query_z = f32_einsum("cphg,cpz->hgz", left_f, cots)
    grad_keyset_z = f32_einsum("cphg,cpz->hgz", left_c, cols)
    gn_z = reduce_blocks(grad_of_normed(qk_weight[2], grad_query_z, grad_keyset_z), count)

    layer_output = (cols.astype(jnp.float32) + f32_einsum("cphg,hgz->cpz", left_f, query_b)).astype(bf16)
    through = f32_einsum("cphg,hgz->cpz", left_c, keyset_b)

    gn_x = grad_of_normed(qk_weight[0], *kernel_backward(gram_x, query_x, keyset_x, factor_x))
    gn_y = grad_of_normed(qk_weight[1], *kernel_backward(gram_y, query_y, keyset_y, factor_y))
    pull_x = pooled_grad(normed_x, inverse_x, gn_x)
    pull_y = pooled_grad(normed_y, inverse_y, gn_y)
    pull_z = pooled_grad(normed_z, inverse_z, gn_z)
    local_x = lax.dynamic_slice_in_dim(pull_x, start_x, rows_x, 1) / (grid_y * depth)
    local_y = lax.dynamic_slice_in_dim(pull_y, start_y, rows_y, 1) / (grid_x * depth)
    local_xy = (local_x[:, :, None] + local_y[:, None, :]).reshape(WIDTH, cells)
    local_z = pull_z / (grid_x * grid_y)
    field_grad = (
        cots.astype(jnp.float32) + through + local_xy[:, :, None] + local_z[:, None, :]
    ).astype(bf16)
    return (layer_output.reshape(field.shape), field_grad.reshape(field.shape))


def split(x):
    high = x.astype(jnp.bfloat16)
    return high, (x - high.astype(jnp.float32)).astype(jnp.bfloat16)


NN = (((1,), (0,)), ((), ()))
NT = (((1,), (1,)), ((), ()))
TN = (((0,), (0,)), ((), ()))


def mul(left, right, dims=NN):
    return lax.dot_general(left, right, dims, preferred_element_type=jnp.float32)


def mul_near(left, right, dims=NN):
    left_high, left_low = split(left)
    right_high, right_low = split(right)
    return (
        mul(left_high, right_high, dims)
        + mul(left_low, right_high, dims)
        + mul(left_high, right_low, dims)
    )


def mul_left(left, right, dims=NN):
    rows = left.shape[0]
    both = mul(jnp.concatenate(split(left), axis=0), right, dims)
    return both[:rows] + both[rows:]


def number(shape, dim):
    return lax.broadcasted_iota(jnp.int32, shape, dim)


def join_halves(half_ref, mine_ref, other_ref):
    core = lax.axis_index("gx") & 1
    half_ref[core] = mine_ref[...]
    half_ref[core ^ 1] = other_ref[...]
    return jnp.concatenate([half_ref[0], half_ref[1]], axis=1)


def expand(part):
    depth = part.shape[1]
    part = part.reshape(HEADS, 1, HEAD_DIM, depth)
    part = jnp.broadcast_to(part, (HEADS, HEAD_DIM, HEAD_DIM, depth))
    return part.reshape(WIDTH * HEAD_DIM, depth).astype(jnp.bfloat16)


def spread(weights, top):
    left = weights[:, None, :] * top[None]
    return left.reshape(-1, left.shape[2]).astype(jnp.bfloat16)


def prepare_kernel(wv_ref, wo_ref, qk_ref, wv_out, wo_out, wq_out, wk_out, wz_out):
    wide = HEADS * HEAD_DIM * HEAD_DIM
    row = number((WIDTH, wide), 0)
    lane = number((WIDTH, wide), 1)
    by_channel = ((lane >> 3) == row).astype(jnp.bfloat16)
    by_factor = (((lane >> 6) * HEAD_DIM + (lane & 7)) == row).astype(jnp.bfloat16)
    wv_out[...] = mul(wv_ref[...], by_channel)
    wo_out[...] = mul(wo_ref[...], by_channel, TN)
    for index, out in ((0, wq_out), (1, wk_out)):
        high, low = split(qk_ref[2, index])
        out[0:WIDTH, :] = mul(high, by_factor).astype(jnp.bfloat16)
        out[WIDTH : 2 * WIDTH, :] = mul(low, by_factor).astype(jnp.bfloat16)
        wz_out[index * WIDTH : (index + 1) * WIDTH, :] = qk_ref[2, index].T


def sums_kernel(field_ref, *refs):
    outs, (cols_ref, data_ref, half_ref, semaphores) = refs[:-4], refs[-4:]
    _, rows_x, rows_y, depth = data_ref.shape
    cells = rows_x * rows_y
    chunks = semaphores.shape[0]
    size = WIDTH // chunks
    copies = [
        pltpu.make_async_copy(
            field_ref.at[pl.ds(index * size, size)],
            data_ref.at[pl.ds(index * size, size)],
            semaphores.at[index],
        )
        for index in range(chunks)
    ]
    for copy in copies:
        copy.start()
    own = jnp.zeros((cells, LANES), jnp.float32)
    pick = number((size, size * cells), 1) // cells == number((size, size * cells), 0)
    pick = pick.astype(jnp.bfloat16)
    for index, copy in enumerate(copies):
        copy.wait()
        rows = slice(index * size, (index + 1) * size)
        data = data_ref[rows].astype(jnp.float32)
        data = jnp.concatenate([data[:, at_x] for at_x in range(rows_x)], axis=1)
        lanes = data[..., :LANES]
        for start in range(LANES, depth, LANES):
            lanes = lanes + data[..., start : start + LANES]
        row_sums = jnp.sum(lanes, axis=2, keepdims=True)
        shape = lanes.shape
        mine = number(shape, 0) + index * size == number(shape, 2)
        own = own + jnp.sum(jnp.where(mine, row_sums, 0.0), axis=0)
        data = data.reshape(size * cells, depth).astype(jnp.bfloat16)
        cols_ref[index * size * cells : (index + 1) * size * cells, :] = data
        part = mul(pick, data)
        half_ref[0, rows, :] = part[:, : depth // 2]
        half_ref[1, rows, :] = part[:, depth // 2 :]
    for step, out in enumerate(outs):
        out[0:WIDTH, :] = half_ref[(lax.axis_index("gx") & 1) ^ step]
        out[WIDTH:, :] = jnp.concatenate([own] * (depth // 2 // LANES), axis=1)


def add_beside_kernel(known, mine_ref, other_ref, out_ref):
    out_ref[0:WIDTH, :] = mine_ref[0:WIDTH, :] + other_ref[0:WIDTH, :]
    lanes = known * WIDTH
    rest = out_ref.shape[1] - 2 * lanes
    rows = [mine_ref[WIDTH:, 0:lanes], other_ref[WIDTH:, 0:lanes]]
    if rest > 0:
        rows.append(jnp.zeros((rows[0].shape[0], rest), jnp.float32))
    out_ref[WIDTH:, :] = jnp.concatenate(rows, axis=1)


def narrow_kernel(total_ref, out_ref):
    out_ref[0:WIDTH, :] = total_ref[0:WIDTH, :].astype(jnp.bfloat16)
    high, low = split(total_ref[WIDTH:, :])
    out_ref[WIDTH:, :] = jnp.concatenate([high, low], axis=0)


def add_narrow_kernel(found_ref, part_ref, out_ref):
    known = found_ref.shape[0]
    part = part_ref[...].astype(jnp.float32)
    cells = (part.shape[0] - WIDTH) // 2
    out_ref[0:WIDTH, :] = found_ref[0:WIDTH, :] + part[0:WIDTH]
    out_ref[WIDTH:known, :] = found_ref[WIDTH:, :]
    out_ref[known:, :] = part[WIDTH : WIDTH + cells] + part[WIDTH + cells :]


def stack_kernel(*refs):
    refs[-1][...] = jnp.concatenate([ref[...] for ref in refs[:-1]], axis=0)


def factor_kernel(places, *refs):
    parts, feat_ref = refs[:-1], refs[-1]
    total = parts[0][0:WIDTH, :]
    for part in parts[1:]:
        total = total + part[0:WIDTH, :]
    pooled = total * (1.0 / places)
    inverse = lax.rsqrt(jnp.mean(pooled * pooled, axis=0, keepdims=True) + EPSILON)
    normed = pooled * inverse
    feat_ref[0:WIDTH, :] = normed
    feat_ref[WIDTH:, :] = jnp.broadcast_to(inverse, (HEAD_DIM, inverse.shape[1]))


def add_pull_kernel(*refs):
    total = refs[0][...].astype(jnp.float32)
    for part in refs[1:-1]:
        total = total + part[...].astype(jnp.float32)
    refs[-1][...] = total.astype(refs[-1].dtype)


def by_head(part):
    shape = (HEADS, part.shape[0], WIDTH)
    mine = number(shape, 0) == (number(shape, 2) >> 3)
    return jnp.where(mine, part[None], 0.0).reshape(-1, WIDTH)


def plane_kernel(cells, span_x, lengths, *refs):
    parts, (same_ref, qk_ref, mix_ref, feat_ref, full_ref) = refs[:-5], refs[-5:]
    totals = jnp.concatenate(
        [
            part[start : start + cells, step * WIDTH : (step + 1) * WIDTH]
            for step in range(span_x)
            for part in parts
            for start in range(WIDTH, part.shape[0], cells)
        ],
        axis=0,
    )
    places = totals.shape[0]
    high, low = split(totals)
    forward = backward = None
    for axis in range(2):
        same = same_ref[axis]
        pooled = (mul(same, high) + mul(same, low)) * (1.0 / lengths[axis][1])
        inverse = lax.rsqrt(jnp.mean(pooled * pooled, axis=1, keepdims=True) + EPSILON)
        normed = pooled * inverse
        query = mul_near(normed, qk_ref[axis, 0])
        keyset = mul_near(normed, qk_ref[axis, 1])
        feat_ref[4 * axis] = normed
        feat_ref[4 * axis + 1] = query
        feat_ref[4 * axis + 2] = keyset
        feat_ref[4 * axis + 3] = jnp.broadcast_to(inverse, (places, WIDTH))
        factor = 1.0 / math.sqrt(HEAD_DIM * lengths[axis][0])

        def scores(rows, other):
            found = mul_near(by_head(rows), other, NT) * factor
            return found.astype(jnp.bfloat16).astype(jnp.float32)

        full = scores(query, keyset)
        full_ref[axis] = full
        one = full.reshape(HEADS, places, places)[:, :cells].reshape(-1, places)
        two = scores(keyset[:cells], query)
        forward = one if forward is None else forward * one
        backward = two if backward is None else backward * two
    mix_ref[0] = forward
    mix_ref[1] = backward


def coef_kernel(mine_ref, other_ref, wz_ref, field_ref, cot_ref, wv_ref, wo_ref,
                send_ref, both_ref, feat_ref, half_ref):
    rows, depth = field_ref.shape
    cells = rows // WIDTH
    wide = HEADS * HEAD_DIM * HEAD_DIM
    feat = join_halves(half_ref, mine_ref, other_ref)
    feat_ref[...] = feat
    high, low = split(feat[:WIDTH])
    both = mul_left(wz_ref[...], high) + mul(wz_ref[...].astype(jnp.bfloat16), low)
    both_ref[...] = both.astype(jnp.bfloat16)
    query = expand(both[:WIDTH])
    keyset = expand(both[WIDTH:])
    low_f = mul(field_ref[...], keyset, NT).reshape(WIDTH, cells, wide)
    low_f = jnp.sum(wv_ref[...][:, None, :] * low_f, axis=0)
    low_c = mul(cot_ref[...], query, NT).reshape(WIDTH, cells, wide)
    low_c = jnp.sum(wo_ref[...][:, None, :] * low_c, axis=0)
    low = jnp.concatenate([low_f, low_c], axis=0).astype(jnp.bfloat16)
    send_ref[...] = low


def join_low(refs, cells):
    low = jnp.concatenate([ref[...].astype(jnp.float32) for ref in refs], axis=0)
    wide = low.shape[1]
    low = low.reshape(-1, 2 * cells, wide)
    return [
        low[:, start : start + cells].reshape(-1, wide).astype(jnp.bfloat16)
        for start in (0, cells)
    ]


def mix_kernel(factor, spans, *refs):
    lows, refs = refs[:spans], refs[spans:]
    mix_ref, wv_ref, wo_ref, wq_ref, wk_ref, field_ref, cot_ref, top_ref, out_ref = refs
    cells = field_ref.shape[0] // WIDTH
    low_f, low_c = join_low(lows, cells)
    wide = low_f.shape[1]
    shape = (HEADS, cells, wide)
    head = number(shape, 0) == (number(shape, 2) >> 6)

    def top(mix, low):
        found = mul_left(mix, low).reshape(shape)
        return jnp.sum(jnp.where(head, found, 0.0), axis=0) * factor

    top_f = top(mix_ref[0], low_f)
    top_c = top(mix_ref[1], low_c)
    top_ref[0] = top_f
    top_ref[1] = top_c
    left_f = spread(wo_ref[...], top_f)
    left_c = spread(wv_ref[...], top_c)

    def pull(weights, left, right):
        found = mul(weights, left, NT)
        return mul_left(found[:WIDTH] + found[WIDTH:], right)

    found = pull(wq_ref[...], left_f, cot_ref[...]) + pull(wk_ref[...], left_c, field_ref[...])
    out_ref[...] = found.astype(jnp.bfloat16)


def put_cells(ref, total):
    _, rows_x, rows_y, depth = ref.shape
    total = total.reshape(WIDTH, rows_x * rows_y, depth)
    for index in range(rows_x):
        rows = total[:, index * rows_y : (index + 1) * rows_y, :]
        ref[:, index, :, :] = rows.astype(jnp.bfloat16)


def output_kernel(top_ref, wo_ref, both_ref, field_ref, out_ref):
    query = expand(both_ref[...].astype(jnp.float32)[:WIDTH])
    left = spread(wo_ref[...], top_ref[0])
    put_cells(out_ref, mul(left, query) + field_ref[...].astype(jnp.float32))


def gram_kernel(cells, lengths, factor_z, *refs):
    lows, (feat_ref, full_ref, same_ref, qk_ref, out_ref) = refs[:-5], refs[-5:]
    low_f, low_c = join_low(lows, cells)
    places, wide = low_f.shape
    squares = HEAD_DIM * HEAD_DIM
    lane = number((places, LANES), 1)
    products = []
    for pair in range(wide // LANES):
        part_f = low_f[:, pair * LANES : (pair + 1) * LANES]
        part_c = low_c[:, pair * LANES : (pair + 1) * LANES]
        for half in range(LANES // squares):
            mine = (lane >> 6) == half
            products.append(mul(jnp.where(mine, part_c, jnp.zeros_like(part_c)), part_f, NT))
    product = jnp.concatenate(products, axis=0)
    factors = [1.0 / math.sqrt(HEAD_DIM * lengths[axis][0]) for axis in range(2)]
    queries = [by_head(feat_ref[4 * axis + 1]).astype(jnp.bfloat16) for axis in range(2)]
    keysets = [by_head(feat_ref[4 * axis + 2]).astype(jnp.bfloat16) for axis in range(2)]
    total = jnp.zeros((cells, WIDTH), jnp.float32)
    for axis in range(2):
        gram = (product * full_ref[1 - axis]).astype(jnp.bfloat16)
        across = jnp.concatenate(
            [gram[h * places : (h + 1) * places] for h in range(HEADS)], axis=1
        )
        scale = factors[axis] * factor_z
        grad_query = mul(across, keysets[axis]) * scale
        grad_keyset = mul(gram, queries[axis], TN) * scale
        found = mul_near(grad_query, qk_ref[axis, 0], NT) + mul_near(grad_keyset, qk_ref[axis, 1], NT)
        high, low = split(found)
        own = same_ref[axis, 0 : 2 * cells, :]
        found = (mul(own, high) + mul(own, low))[:cells]
        normed = feat_ref[4 * axis, 0:cells, :]
        inverse = feat_ref[4 * axis + 3, 0:cells, :]
        found = found - normed * jnp.mean(found * normed, axis=1, keepdims=True)
        total = total + inverse * found * (1.0 / lengths[axis][1])
    shape = (WIDTH, cells, WIDTH)
    own = jnp.where(number(shape, 0) == number(shape, 2), total[None], 0.0)
    out_ref[...] = mul_left(own.reshape(-1, WIDTH), jnp.ones((WIDTH, LANES), jnp.bfloat16))


def base_kernel(top_ref, wv_ref, both_ref, cot_ref, plane_ref, out_ref):
    keyset = expand(both_ref[...].astype(jnp.float32)[WIDTH:])
    left = spread(wv_ref[...], top_ref[1])
    found = mul(left, keyset) + cot_ref[...].astype(jnp.float32)
    columns = found.shape[1] // LANES
    out_ref[...] = found + jnp.concatenate([plane_ref[...]] * columns, axis=1)


def final_kernel(places, *refs):
    parts, refs = refs[:-5], refs[-5:]
    feat_ref, base_ref, out_ref, data_ref, semaphores = refs
    depth = base_ref.shape[1]
    _, rows_x, rows_y, _ = data_ref.shape
    found = parts[0][...].astype(jnp.float32)
    for part in parts[1:]:
        found = found + part[...].astype(jnp.float32)
    normed = feat_ref[0:WIDTH, :]
    inverse = feat_ref[WIDTH : WIDTH + 1, :]
    found = inverse * (found - normed * jnp.mean(found * normed, axis=0, keepdims=True))
    found = found * (1.0 / places)
    cells = rows_x * rows_y
    chunks = semaphores.shape[0]
    size = WIDTH // chunks
    copies = []
    for index in range(chunks):
        rows = slice(index * size, (index + 1) * size)
        base = base_ref[index * size * cells : (index + 1) * size * cells, :]
        total = base.reshape(size, cells, depth) + found[rows][:, None, :]
        for at_x in range(rows_x):
            part = total[:, at_x * rows_y : (at_x + 1) * rows_y, :]
            data_ref[rows, at_x, :, :] = part.astype(jnp.bfloat16)
        copy = pltpu.make_async_copy(
            data_ref.at[pl.ds(index * size, size)],
            out_ref.at[pl.ds(index * size, size)],
            semaphores.at[index],
        )
        copy.start()
        copies.append(copy)
    for copy in copies:
        copy.wait()


def rows_kernel(cot_ref, rows_ref, data_ref, semaphores):
    _, rows_x, rows_y, depth = data_ref.shape
    cells = rows_x * rows_y
    chunks = semaphores.shape[0]
    size = WIDTH // chunks
    copies = [
        pltpu.make_async_copy(
            cot_ref.at[pl.ds(index * size, size)],
            data_ref.at[pl.ds(index * size, size)],
            semaphores.at[index],
        )
        for index in range(chunks)
    ]
    for copy in copies:
        copy.start()
    for index, copy in enumerate(copies):
        copy.wait()
        data = data_ref[index * size : (index + 1) * size].astype(jnp.float32)
        data = jnp.concatenate([data[:, at_x] for at_x in range(rows_x)], axis=1)
        data = data.reshape(size * cells, depth).astype(jnp.bfloat16)
        rows_ref[index * size * cells : (index + 1) * size * cells, :] = data


def run(kernel, outs, operands, places=pltpu.VMEM, target=pltpu.VMEM, flops=0, scratch=(),
        mebibytes=16):
    moved = sum(x.size * x.dtype.itemsize for x in tuple(operands) + tuple(outs))
    found = pl.pallas_call(
        kernel,
        out_shape=tuple(outs),
        in_specs=[pl.BlockSpec(memory_space=places)] * len(operands),
        out_specs=tuple(pl.BlockSpec(memory_space=target) for _ in outs),
        scratch_shapes=list(scratch),
        compiler_params=pltpu.CompilerParams(vmem_limit_bytes=mebibytes * 1024 * 1024),
        cost_estimate=pl.CostEstimate(flops=flops, bytes_accessed=moved, transcendentals=0),
    )(*operands)
    return found[0] if len(outs) == 1 else found


def per_device_kernels(field, cotangent, qk_weight, w_value, w_out):
    span_x = lax.axis_size("gx")
    span_y = lax.axis_size("gy")
    count = span_x * span_y
    rows_x, rows_y, depth = field.shape[1:]
    cells = rows_x * rows_y
    places = count * cells
    grid_x = rows_x * span_x
    grid_y = rows_y * span_y
    rows = WIDTH * cells
    wide = WIDTH * HEAD_DIM
    f32, bf16 = jnp.float32, jnp.bfloat16
    like = jax.ShapeDtypeStruct
    lengths = ((grid_x, grid_y * depth), (grid_y, grid_x * depth))

    cell = np.arange(places)
    at_x = cell // cells // span_y * rows_x + cell % cells // rows_y
    at_y = cell // cells % span_y * rows_y + cell % rows_y
    same = jnp.asarray(
        np.stack([at_x[:, None] == at_x[None], at_y[:, None] == at_y[None]]), dtype=bf16
    )

    half = depth // 2
    halves = pltpu.VMEM((2, WIDTH, half), f32)
    chunked = [pltpu.VMEM(field.shape, bf16), pltpu.SemaphoreType.DMA((8,))]
    factor_z = 1.0 / math.sqrt(HEAD_DIM * depth)
    cube = rows * wide * depth * 2

    cots = run(
        rows_kernel,
        [like((rows, depth), bf16)],
        (pltpu.with_memory_space_constraint(cotangent, pltpu.HBM),),
        places=pltpu.HBM,
        flops=cube,
        scratch=chunked,
    )

    def swaps(sent, axis, size, farthest=True):
        if not isinstance(sent, (tuple, list)):
            sent = [sent] * size
        steps = range(size - 1, 0, -1)
        found = {}
        for step in steps if farthest else reversed(steps):
            found[step] = swap(sent[step], axis, size, step)
        return tuple(sent[:1]) + tuple(found[step] for step in steps)

    def taken(kernel, sent, dtype=None, last=False):
        found, *others = sent
        for part in others if last else others[:-1]:
            more = part.shape[0] if kernel is stack_kernel else part.shape[0] - WIDTH
            shape = (found.shape[0] + more,) + part.shape[1:]
            found = run(kernel, [like(shape, dtype or found.dtype)], (found, part))
        return (found,) if last else (found, others[-1])

    *sums, cols = run(
        sums_kernel,
        [like((WIDTH + cells, half), f32)] * 2 + [like((rows, depth), bf16)],
        (pltpu.with_memory_space_constraint(field, pltpu.HBM),),
        places=pltpu.HBM,
        flops=cube // 4,
        scratch=[chunked[0], halves, chunked[1]],
    )
    wv, wo, wq, wk, wz = run(
        prepare_kernel,
        [like((WIDTH, wide), f32)] * 2 + [like((2 * WIDTH, wide), bf16)] * 2
        + [like((2 * WIDTH, WIDTH), f32)],
        (w_value, w_out, qk_weight),
        flops=cube // 8,
    )
    total, other = sums
    for level in range(span_x.bit_length() - 1):
        step = 1 << level
        total = run(
            functools.partial(add_beside_kernel, step),
            [like((WIDTH + cells, half), f32)],
            (total, swap(total if level else other, "gx", span_x, step)),
        )
    sent = run(narrow_kernel, [like((WIDTH + 2 * cells, half), bf16)], (total,))
    for part in swaps(sent, "gy", span_y)[1:]:
        shape = (total.shape[0] + cells, half)
        total = run(add_narrow_kernel, [like(shape, f32)], (total, part))
    totals = (total,)
    totals, cots, wz = lax.optimization_barrier((totals, cots, wz))
    mine = run(
        functools.partial(factor_kernel, grid_x * grid_y),
        [like((WIDTH + HEAD_DIM, half), f32)],
        totals,
    )
    mix, feat, full = run(
        functools.partial(plane_kernel, cells, span_x, lengths),
        [like((2, HEADS * cells, places), f32), like((8, places, WIDTH), f32),
         like((2, HEADS * places, places), f32)],
        totals + (same, qk_weight),
        flops=cube // 2,
    )
    send, both, feat_z = run(
        coef_kernel,
        [like((2 * cells, wide), bf16), like((2 * WIDTH, depth), bf16),
         like((WIDTH + HEAD_DIM, depth), f32)],
        (mine, swap(mine, "gx", span_x, 1), wz, cols, cots, wv, wo),
        flops=2 * cube,
        scratch=[pltpu.VMEM((2, WIDTH + HEAD_DIM, half), f32)],
    )
    (low,) = taken(stack_kernel, swaps(send, "gy", span_y), last=True)
    first, *others = swaps(low, "gx", span_x, False)
    lows = (first,) + tuple(reversed(others))
    pulled = like((WIDTH, depth), bf16)
    top, total = run(
        functools.partial(mix_kernel, factor_z, span_x),
        [like((2, cells, wide), f32), pulled],
        lows + (mix, wv, wo, wq, wk, cols, cots),
        flops=cube,
    )
    total = run(add_pull_kernel, [pulled], (total, swap(total, "gx", span_x, 1)))
    for level in range(1, span_x.bit_length() - 1):
        total = run(add_pull_kernel, [pulled], (total, swap(total, "gx", span_x, 1 << level)))
    layer_output = run(
        output_kernel, [like(field.shape, bf16)], (top, wo, both, cols), flops=cube
    )
    plane = run(
        functools.partial(gram_kernel, cells, lengths, factor_z),
        [like((rows, LANES), f32)],
        lows + (feat, full, same, qk_weight),
        flops=2 * cube,
    )
    total, plane = lax.optimization_barrier((total, plane))
    base = run(base_kernel, [like((rows, depth), f32)], (top, wv, both, cots, plane), flops=cube)
    field_grad = run(
        functools.partial(final_kernel, grid_x * grid_y),
        [like(field.shape, bf16)],
        swaps(total, "gy", span_y, False) + (feat_z, base),
        target=pltpu.HBM,
        scratch=chunked,
    )
    return (layer_output, field_grad)


def solution(mesh):
    placed = P(None, ("groups", "gx"), "gy", None)
    count = mesh.shape["gx"] * mesh.shape["gy"]

    def program(*arrays):
        _, grid_x, grid_y, depth = arrays[0].shape
        places = grid_x // mesh.shape["groups"] * grid_y
        small = places == LANES and places == 8 * count
        small = small and depth == LANES * mesh.shape["gx"] and count & (count - 1) == 0
        small = small and mesh.shape["gx"] > 3
        return jax.shard_map(
            per_device_kernels if small else per_device,
            mesh=mesh,
            in_specs=(placed, placed, P(), P(), P()),
            out_specs=(placed, placed),
            check_vma=False,
        )(*arrays)

    return program
```

```python
import functools
import math

import jax
import jax.numpy as jnp
import numpy as np
from jax import lax
from jax.experimental import pallas as pl
from jax.experimental.pallas import tpu as pltpu
from jax.sharding import PartitionSpec as P

WIDTH = 64
HEADS = 8
HEAD_DIM = 8
LANES = 128

EPSILON = 1e-06
PRECISE = lax.Precision.HIGHEST
AXES = ("gx", "gy")


def exchange(parts):
    return lax.all_to_all(parts, AXES, split_axis=0, concat_axis=0, tiled=True)


def swap(part, axis, size, step):
    return lax.ppermute(part, axis, [(i, i ^ step) for i in range(size)])


def gather(part, count):
    return exchange(jnp.broadcast_to(part[None], (count,) + part.shape))


def reduce_blocks(total, count):
    width, depth = total.shape
    blocks = total.reshape(width, depth // LANES, LANES).transpose(1, 0, 2)
    blocks = blocks.reshape(count, width * depth // LANES // count, LANES)
    mine = jnp.sum(exchange(blocks), axis=0)
    whole = gather(mine, count).reshape(depth // LANES, width, LANES)
    return whole.transpose(1, 0, 2).reshape(width, depth)


def axis_features(pooled, weights):
    inverse = lax.rsqrt(jnp.mean(pooled * pooled, axis=0, keepdims=True) + EPSILON)
    normed = pooled * inverse
    length = pooled.shape[1]
    factor = 1.0 / math.sqrt(HEAD_DIM * length)
    queries = jnp.dot(weights[0].T, normed, precision=PRECISE).reshape(HEADS, HEAD_DIM, length)
    keyset = jnp.dot(weights[1].T, normed, precision=PRECISE).reshape(HEADS, HEAD_DIM, length)
    return (normed, inverse, queries, keyset, factor)


def axis_kernel(queries, keyset, factor):
    scores = jnp.einsum("hdm,hdn->hmn", queries, keyset, precision=PRECISE)
    return (scores * factor).astype(jnp.bfloat16)


def kernel_backward(gram, queries, keyset, factor):
    grad_query = factor * jnp.einsum("hmn,hdn->hdm", gram, keyset, precision=PRECISE)
    grad_keyset = factor * jnp.einsum("hmn,hdm->hdn", gram, queries, precision=PRECISE)
    return (grad_query, grad_keyset)


def grad_of_normed(weights, grad_query, grad_keyset):
    length = grad_query.shape[-1]
    grad_normed = jnp.dot(weights[0], grad_query.reshape(WIDTH, length), precision=PRECISE)
    return grad_normed + jnp.dot(
        weights[1], grad_keyset.reshape(WIDTH, length), precision=PRECISE
    )


def pooled_grad(normed, inverse, grad_normed):
    return inverse * (grad_normed - normed * jnp.mean(grad_normed * normed, axis=0, keepdims=True))


def f32_einsum(pattern, left, right):
    return jnp.einsum(pattern, left, right, preferred_element_type=jnp.float32)


def per_device(field, cotangent, qk_weight, w_value, w_out):
    span_x = lax.axis_size("gx")
    span_y = lax.axis_size("gy")
    count = span_x * span_y
    rows_x, rows_y, depth = field.shape[1:]
    cells = rows_x * rows_y
    grid_x = rows_x * span_x
    grid_y = rows_y * span_y
    start_x = lax.axis_index("gx") * rows_x
    start_y = lax.axis_index("gy") * rows_y
    bf16 = jnp.bfloat16

    cols = field.reshape(WIDTH, cells, depth)
    cots = cotangent.reshape(WIDTH, cells, depth)

    sum_z = jnp.sum(cols, axis=1, dtype=jnp.float32)
    sum_rows = jnp.sum(cols, axis=2, dtype=jnp.float32)
    rows_all = gather(sum_rows.T, count).reshape(span_x, span_y, rows_x, rows_y, WIDTH)
    total_x = jnp.sum(rows_all, axis=(1, 3)).reshape(grid_x, WIDTH).T
    total_y = jnp.sum(rows_all, axis=(0, 2)).reshape(grid_y, WIDTH).T
    total_z = reduce_blocks(sum_z, count)

    normed_x, inverse_x, query_x, keyset_x, factor_x = axis_features(
        total_x / (grid_y * depth), qk_weight[0]
    )
    normed_y, inverse_y, query_y, keyset_y, factor_y = axis_features(
        total_y / (grid_x * depth), qk_weight[1]
    )
    normed_z, inverse_z, query_z, keyset_z, factor_z = axis_features(
        total_z / (grid_x * grid_y), qk_weight[2]
    )
    kernel_x = axis_kernel(query_x, keyset_x, factor_x)
    kernel_y = axis_kernel(query_y, keyset_y, factor_y)
    query_b = query_z.astype(bf16)
    keyset_b = keyset_z.astype(bf16)

    wv = w_value.reshape(WIDTH, HEADS, HEAD_DIM)
    wo = w_out.reshape(HEADS, HEAD_DIM, WIDTH)
    coef_f = f32_einsum("cpk,hgk->cphg", cols, keyset_b)
    coef_c = f32_einsum("cpz,hgz->cphg", cots, query_b)
    low_f = jnp.einsum("chd,cphg->phdg", wv.astype(jnp.float32), coef_f, precision=PRECISE)
    low_c = jnp.einsum("hdc,cphg->phdg", wo.astype(jnp.float32), coef_c, precision=PRECISE)
    squares = HEAD_DIM * HEAD_DIM
    both = jnp.stack([low_f, low_c]).astype(bf16).reshape(2, cells, HEADS * squares)
    both = gather(both, count).reshape(span_x, span_y, 2, rows_x, rows_y, HEADS * squares)
    both = both.transpose(2, 0, 3, 1, 4, 5).reshape(2, grid_x, grid_y, HEADS, squares)
    low_f, low_c = both[0], both[1]

    mid_f = f32_einsum("hyj,xjhq->xyhq", kernel_y, low_f).astype(bf16)
    top_f = f32_einsum("hxi,iyhq->xyhq", kernel_x, mid_f)
    mid_c = f32_einsum("hxi,xyhq->iyhq", kernel_x, low_c).astype(bf16)
    top_c = f32_einsum("hyj,xyhq->xjhq", kernel_y, mid_c)
    gram_x = factor_z * f32_einsum("myhq,nyhq->hmn", low_c, mid_f)
    gram_y = factor_z * f32_einsum("xmhq,xnhq->hmn", mid_c, low_f)

    def here(top):
        top = lax.dynamic_slice_in_dim(top, start_x, rows_x, 0)
        top = lax.dynamic_slice_in_dim(top, start_y, rows_y, 1)
        return top.reshape(cells, HEADS, HEAD_DIM, HEAD_DIM)

    left_f = factor_z * jnp.einsum(
        "hdc,phdg->cphg", wo.astype(jnp.float32), here(top_f), precision=PRECISE
    )
    left_c = factor_z * jnp.einsum(
        "chd,phdg->cphg", wv.astype(jnp.float32), here(top_c), precision=PRECISE
    )
    left_f = left_f.astype(bf16)
    left_c = left_c.astype(bf16)

    grad_query_z = f32_einsum("cphg,cpz->hgz", left_f, cots)
    grad_keyset_z = f32_einsum("cphg,cpz->hgz", left_c, cols)
    gn_z = reduce_blocks(grad_of_normed(qk_weight[2], grad_query_z, grad_keyset_z), count)

    layer_output = (cols.astype(jnp.float32) + f32_einsum("cphg,hgz->cpz", left_f, query_b)).astype(bf16)
    through = f32_einsum("cphg,hgz->cpz", left_c, keyset_b)

    gn_x = grad_of_normed(qk_weight[0], *kernel_backward(gram_x, query_x, keyset_x, factor_x))
    gn_y = grad_of_normed(qk_weight[1], *kernel_backward(gram_y, query_y, keyset_y, factor_y))
    pull_x = pooled_grad(normed_x, inverse_x, gn_x)
    pull_y = pooled_grad(normed_y, inverse_y, gn_y)
    pull_z = pooled_grad(normed_z, inverse_z, gn_z)
    local_x = lax.dynamic_slice_in_dim(pull_x, start_x, rows_x, 1) / (grid_y * depth)
    local_y = lax.dynamic_slice_in_dim(pull_y, start_y, rows_y, 1) / (grid_x * depth)
    local_xy = (local_x[:, :, None] + local_y[:, None, :]).reshape(WIDTH, cells)
    local_z = pull_z / (grid_x * grid_y)
    field_grad = (
        cots.astype(jnp.float32) + through + local_xy[:, :, None] + local_z[:, None, :]
    ).astype(bf16)
    return (layer_output.reshape(field.shape), field_grad.reshape(field.shape))


def split(x):
    high = x.astype(jnp.bfloat16)
    return high, (x - high.astype(jnp.float32)).astype(jnp.bfloat16)


NN = (((1,), (0,)), ((), ()))
NT = (((1,), (1,)), ((), ()))
TN = (((0,), (0,)), ((), ()))


def mul(left, right, dims=NN):
    return lax.dot_general(left, right, dims, preferred_element_type=jnp.float32)


def mul_near(left, right, dims=NN):
    left_high, left_low = split(left)
    right_high, right_low = split(right)
    return (
        mul(left_high, right_high, dims)
        + mul(left_low, right_high, dims)
        + mul(left_high, right_low, dims)
    )


def mul_left(left, right, dims=NN):
    rows = left.shape[0]
    both = mul(jnp.concatenate(split(left), axis=0), right, dims)
    return both[:rows] + both[rows:]


def number(shape, dim):
    return lax.broadcasted_iota(jnp.int32, shape, dim)


def join_halves(half_ref, mine_ref, other_ref):
    core = lax.axis_index("gx") & 1
    half_ref[core] = mine_ref[...]
    half_ref[core ^ 1] = other_ref[...]
    return jnp.concatenate([half_ref[0], half_ref[1]], axis=1)


def expand(part):
    depth = part.shape[1]
    part = part.reshape(HEADS, 1, HEAD_DIM, depth)
    part = jnp.broadcast_to(part, (HEADS, HEAD_DIM, HEAD_DIM, depth))
    return part.reshape(WIDTH * HEAD_DIM, depth).astype(jnp.bfloat16)


def spread(weights, top):
    left = weights[:, None, :] * top[None]
    return left.reshape(-1, left.shape[2]).astype(jnp.bfloat16)


def prepare_kernel(wv_ref, wo_ref, qk_ref, wv_out, wo_out, wq_out, wk_out, wz_out):
    wide = HEADS * HEAD_DIM * HEAD_DIM
    row = number((WIDTH, wide), 0)
    lane = number((WIDTH, wide), 1)
    by_channel = ((lane >> 3) == row).astype(jnp.bfloat16)
    by_factor = (((lane >> 6) * HEAD_DIM + (lane & 7)) == row).astype(jnp.bfloat16)
    wv_out[...] = mul(wv_ref[...], by_channel)
    wo_out[...] = mul(wo_ref[...], by_channel, TN)
    for index, out in ((0, wq_out), (1, wk_out)):
        high, low = split(qk_ref[2, index])
        out[0:WIDTH, :] = mul(high, by_factor).astype(jnp.bfloat16)
        out[WIDTH : 2 * WIDTH, :] = mul(low, by_factor).astype(jnp.bfloat16)
        wz_out[index * WIDTH : (index + 1) * WIDTH, :] = qk_ref[2, index].T


def sums_kernel(field_ref, *refs):
    outs, (cols_ref, data_ref, half_ref, semaphores) = refs[:-4], refs[-4:]
    _, rows_x, rows_y, depth = data_ref.shape
    cells = rows_x * rows_y
    chunks = semaphores.shape[0]
    size = WIDTH // chunks
    copies = [
        pltpu.make_async_copy(
            field_ref.at[pl.ds(index * size, size)],
            data_ref.at[pl.ds(index * size, size)],
            semaphores.at[index],
        )
        for index in range(chunks)
    ]
    for copy in copies:
        copy.start()
    own = jnp.zeros((cells, LANES), jnp.float32)
    pick = number((size, size * cells), 1) // cells == number((size, size * cells), 0)
    pick = pick.astype(jnp.bfloat16)
    for index, copy in enumerate(copies):
        copy.wait()
        rows = slice(index * size, (index + 1) * size)
        data = data_ref[rows].astype(jnp.float32)
        data = jnp.concatenate([data[:, at_x] for at_x in range(rows_x)], axis=1)
        lanes = data[..., :LANES]
        for start in range(LANES, depth, LANES):
            lanes = lanes + data[..., start : start + LANES]
        row_sums = jnp.sum(lanes, axis=2, keepdims=True)
        shape = lanes.shape
        mine = number(shape, 0) + index * size == number(shape, 2)
        own = own + jnp.sum(jnp.where(mine, row_sums, 0.0), axis=0)
        data = data.reshape(size * cells, depth).astype(jnp.bfloat16)
        cols_ref[index * size * cells : (index + 1) * size * cells, :] = data
        part = mul(pick, data)
        half_ref[0, rows, :] = part[:, : depth // 2]
        half_ref[1, rows, :] = part[:, depth // 2 :]
    for step, out in enumerate(outs):
        out[0:WIDTH, :] = half_ref[(lax.axis_index("gx") & 1) ^ step]
        out[WIDTH:, :] = jnp.concatenate([own] * (depth // 2 // LANES), axis=1)


def add_beside_kernel(known, mine_ref, other_ref, out_ref):
    out_ref[0:WIDTH, :] = mine_ref[0:WIDTH, :] + other_ref[0:WIDTH, :]
    lanes = known * WIDTH
    rest = out_ref.shape[1] - 2 * lanes
    rows = [mine_ref[WIDTH:, 0:lanes], other_ref[WIDTH:, 0:lanes]]
    if rest > 0:
        rows.append(jnp.zeros((rows[0].shape[0], rest), jnp.float32))
    out_ref[WIDTH:, :] = jnp.concatenate(rows, axis=1)


def narrow_kernel(total_ref, out_ref):
    out_ref[0:WIDTH, :] = total_ref[0:WIDTH, :].astype(jnp.bfloat16)
    high, low = split(total_ref[WIDTH:, :])
    out_ref[WIDTH:, :] = jnp.concatenate([high, low], axis=0)


def add_narrow_kernel(found_ref, part_ref, out_ref):
    known = found_ref.shape[0]
    part = part_ref[...].astype(jnp.float32)
    cells = (part.shape[0] - WIDTH) // 2
    out_ref[0:WIDTH, :] = found_ref[0:WIDTH, :] + part[0:WIDTH]
    out_ref[WIDTH:known, :] = found_ref[WIDTH:, :]
    out_ref[known:, :] = part[WIDTH : WIDTH + cells] + part[WIDTH + cells :]


def stack_kernel(*refs):
    refs[-1][...] = jnp.concatenate([ref[...] for ref in refs[:-1]], axis=0)


def factor_kernel(places, *refs):
    parts, feat_ref = refs[:-1], refs[-1]
    total = parts[0][0:WIDTH, :]
    for part in parts[1:]:
        total = total + part[0:WIDTH, :]
    pooled = total * (1.0 / places)
    inverse = lax.rsqrt(jnp.mean(pooled * pooled, axis=0, keepdims=True) + EPSILON)
    normed = pooled * inverse
    feat_ref[0:WIDTH, :] = normed
    feat_ref[WIDTH:, :] = jnp.broadcast_to(inverse, (HEAD_DIM, inverse.shape[1]))


def add_pull_kernel(*refs):
    total = refs[0][...].astype(jnp.float32)
    for part in refs[1:-1]:
        total = total + part[...].astype(jnp.float32)
    refs[-1][...] = total.astype(refs[-1].dtype)


def by_head(part):
    shape = (HEADS, part.shape[0], WIDTH)
    mine = number(shape, 0) == (number(shape, 2) >> 3)
    return jnp.where(mine, part[None], 0.0).reshape(-1, WIDTH)


def plane_kernel(cells, span_x, lengths, *refs):
    parts, (same_ref, qk_ref, mix_ref, feat_ref, full_ref) = refs[:-5], refs[-5:]
    totals = jnp.concatenate(
        [
            part[start : start + cells, step * WIDTH : (step + 1) * WIDTH]
            for step in range(span_x)
            for part in parts
            for start in range(WIDTH, part.shape[0], cells)
        ],
        axis=0,
    )
    places = totals.shape[0]
    high, low = split(totals)
    forward = backward = None
    for axis in range(2):
        same = same_ref[axis]
        pooled = (mul(same, high) + mul(same, low)) * (1.0 / lengths[axis][1])
        inverse = lax.rsqrt(jnp.mean(pooled * pooled, axis=1, keepdims=True) + EPSILON)
        normed = pooled * inverse
        query = mul_near(normed, qk_ref[axis, 0])
        keyset = mul_near(normed, qk_ref[axis, 1])
        feat_ref[4 * axis] = normed
        feat_ref[4 * axis + 1] = query
        feat_ref[4 * axis + 2] = keyset
        feat_ref[4 * axis + 3] = jnp.broadcast_to(inverse, (places, WIDTH))
        factor = 1.0 / math.sqrt(HEAD_DIM * lengths[axis][0])

        def scores(rows, other):
            found = mul_near(by_head(rows), other, NT) * factor
            return found.astype(jnp.bfloat16).astype(jnp.float32)

        full = scores(query, keyset)
        full_ref[axis] = full
        one = full.reshape(HEADS, places, places)[:, :cells].reshape(-1, places)
        two = scores(keyset[:cells], query)
        forward = one if forward is None else forward * one
        backward = two if backward is None else backward * two
    mix_ref[0] = forward
    mix_ref[1] = backward


def coef_kernel(mine_ref, other_ref, wz_ref, field_ref, cot_ref, wv_ref, wo_ref,
                send_ref, both_ref, feat_ref, half_ref):
    rows, depth = field_ref.shape
    cells = rows // WIDTH
    wide = HEADS * HEAD_DIM * HEAD_DIM
    feat = join_halves(half_ref, mine_ref, other_ref)
    feat_ref[...] = feat
    high, low = split(feat[:WIDTH])
    both = mul_left(wz_ref[...], high) + mul(wz_ref[...].astype(jnp.bfloat16), low)
    both_ref[...] = both.astype(jnp.bfloat16)
    query = expand(both[:WIDTH])
    keyset = expand(both[WIDTH:])
    low_f = mul(field_ref[...], keyset, NT).reshape(WIDTH, cells, wide)
    low_f = jnp.sum(wv_ref[...][:, None, :] * low_f, axis=0)
    low_c = mul(cot_ref[...], query, NT).reshape(WIDTH, cells, wide)
    low_c = jnp.sum(wo_ref[...][:, None, :] * low_c, axis=0)
    low = jnp.concatenate([low_f, low_c], axis=0).astype(jnp.bfloat16)
    send_ref[...] = low


def join_low(refs, cells):
    low = jnp.concatenate([ref[...].astype(jnp.float32) for ref in refs], axis=0)
    wide = low.shape[1]
    low = low.reshape(-1, 2 * cells, wide)
    return [
        low[:, start : start + cells].reshape(-1, wide).astype(jnp.bfloat16)
        for start in (0, cells)
    ]


def mix_kernel(factor, spans, *refs):
    lows, refs = refs[:spans], refs[spans:]
    mix_ref, wv_ref, wo_ref, wq_ref, wk_ref, field_ref, cot_ref, top_ref, out_ref = refs
    cells = field_ref.shape[0] // WIDTH
    low_f, low_c = join_low(lows, cells)
    wide = low_f.shape[1]
    shape = (HEADS, cells, wide)
    head = number(shape, 0) == (number(shape, 2) >> 6)

    def top(mix, low):
        found = mul_left(mix, low).reshape(shape)
        return jnp.sum(jnp.where(head, found, 0.0), axis=0) * factor

    top_f = top(mix_ref[0], low_f)
    top_c = top(mix_ref[1], low_c)
    top_ref[0] = top_f
    top_ref[1] = top_c
    left_f = spread(wo_ref[...], top_f)
    left_c = spread(wv_ref[...], top_c)

    def pull(weights, left, right):
        found = mul(weights, left, NT)
        return mul_left(found[:WIDTH] + found[WIDTH:], right)

    found = pull(wq_ref[...], left_f, cot_ref[...]) + pull(wk_ref[...], left_c, field_ref[...])
    out_ref[...] = found.astype(jnp.bfloat16)


def put_cells(ref, total):
    _, rows_x, rows_y, depth = ref.shape
    total = total.reshape(WIDTH, rows_x * rows_y, depth)
    for index in range(rows_x):
        rows = total[:, index * rows_y : (index + 1) * rows_y, :]
        ref[:, index, :, :] = rows.astype(jnp.bfloat16)


def output_kernel(top_ref, wo_ref, both_ref, field_ref, out_ref):
    query = expand(both_ref[...].astype(jnp.float32)[:WIDTH])
    left = spread(wo_ref[...], top_ref[0])
    put_cells(out_ref, mul(left, query) + field_ref[...].astype(jnp.float32))


def gram_kernel(cells, lengths, factor_z, *refs):
    lows, (feat_ref, full_ref, same_ref, qk_ref, out_ref) = refs[:-5], refs[-5:]
    low_f, low_c = join_low(lows, cells)
    places, wide = low_f.shape
    squares = HEAD_DIM * HEAD_DIM
    lane = number((places, LANES), 1)
    products = []
    for pair in range(wide // LANES):
        part_f = low_f[:, pair * LANES : (pair + 1) * LANES]
        part_c = low_c[:, pair * LANES : (pair + 1) * LANES]
        for half in range(LANES // squares):
            mine = (lane >> 6) == half
            products.append(mul(jnp.where(mine, part_c, jnp.zeros_like(part_c)), part_f, NT))
    product = jnp.concatenate(products, axis=0)
    factors = [1.0 / math.sqrt(HEAD_DIM * lengths[axis][0]) for axis in range(2)]
    queries = [by_head(feat_ref[4 * axis + 1]).astype(jnp.bfloat16) for axis in range(2)]
    keysets = [by_head(feat_ref[4 * axis + 2]).astype(jnp.bfloat16) for axis in range(2)]
    total = jnp.zeros((cells, WIDTH), jnp.float32)
    for axis in range(2):
        gram = (product * full_ref[1 - axis]).astype(jnp.bfloat16)
        across = jnp.concatenate(
            [gram[h * places : (h + 1) * places] for h in range(HEADS)], axis=1
        )
        scale = factors[axis] * factor_z
        grad_query = mul(across, keysets[axis]) * scale
        grad_keyset = mul(gram, queries[axis], TN) * scale
        found = mul_near(grad_query, qk_ref[axis, 0], NT) + mul_near(grad_keyset, qk_ref[axis, 1], NT)
        high, low = split(found)
        own = same_ref[axis, 0 : 2 * cells, :]
        found = (mul(own, high) + mul(own, low))[:cells]
        normed = feat_ref[4 * axis, 0:cells, :]
        inverse = feat_ref[4 * axis + 3, 0:cells, :]
        found = found - normed * jnp.mean(found * normed, axis=1, keepdims=True)
        total = total + inverse * found * (1.0 / lengths[axis][1])
    shape = (WIDTH, cells, WIDTH)
    own = jnp.where(number(shape, 0) == number(shape, 2), total[None], 0.0)
    out_ref[...] = mul_left(own.reshape(-1, WIDTH), jnp.ones((WIDTH, LANES), jnp.bfloat16))


def base_kernel(top_ref, wv_ref, both_ref, cot_ref, plane_ref, out_ref):
    keyset = expand(both_ref[...].astype(jnp.float32)[WIDTH:])
    left = spread(wv_ref[...], top_ref[1])
    found = mul(left, keyset) + cot_ref[...].astype(jnp.float32)
    columns = found.shape[1] // LANES
    out_ref[...] = found + jnp.concatenate([plane_ref[...]] * columns, axis=1)


def final_kernel(places, *refs):
    parts, refs = refs[:-5], refs[-5:]
    feat_ref, base_ref, out_ref, data_ref, semaphores = refs
    depth = base_ref.shape[1]
    _, rows_x, rows_y, _ = data_ref.shape
    found = parts[0][...].astype(jnp.float32)
    for part in parts[1:]:
        found = found + part[...].astype(jnp.float32)
    normed = feat_ref[0:WIDTH, :]
    inverse = feat_ref[WIDTH : WIDTH + 1, :]
    found = inverse * (found - normed * jnp.mean(found * normed, axis=0, keepdims=True))
    found = found * (1.0 / places)
    cells = rows_x * rows_y
    chunks = semaphores.shape[0]
    size = WIDTH // chunks
    copies = []
    for index in range(chunks):
        rows = slice(index * size, (index + 1) * size)
        base = base_ref[index * size * cells : (index + 1) * size * cells, :]
        total = base.reshape(size, cells, depth) + found[rows][:, None, :]
        for at_x in range(rows_x):
            part = total[:, at_x * rows_y : (at_x + 1) * rows_y, :]
            data_ref[rows, at_x, :, :] = part.astype(jnp.bfloat16)
        copy = pltpu.make_async_copy(
            data_ref.at[pl.ds(index * size, size)],
            out_ref.at[pl.ds(index * size, size)],
            semaphores.at[index],
        )
        copy.start()
        copies.append(copy)
    for copy in copies:
        copy.wait()


def rows_kernel(cot_ref, rows_ref, data_ref, semaphores):
    _, rows_x, rows_y, depth = data_ref.shape
    cells = rows_x * rows_y
    chunks = semaphores.shape[0]
    size = WIDTH // chunks
    copies = [
        pltpu.make_async_copy(
            cot_ref.at[pl.ds(index * size, size)],
            data_ref.at[pl.ds(index * size, size)],
            semaphores.at[index],
        )
        for index in range(chunks)
    ]
    for copy in copies:
        copy.start()
    for index, copy in enumerate(copies):
        copy.wait()
        data = data_ref[index * size : (index + 1) * size].astype(jnp.float32)
        data = jnp.concatenate([data[:, at_x] for at_x in range(rows_x)], axis=1)
        data = data.reshape(size * cells, depth).astype(jnp.bfloat16)
        rows_ref[index * size * cells : (index + 1) * size * cells, :] = data


def run(kernel, outs, operands, places=pltpu.VMEM, target=pltpu.VMEM, flops=0, scratch=(),
        mebibytes=16):
    moved = sum(x.size * x.dtype.itemsize for x in tuple(operands) + tuple(outs))
    found = pl.pallas_call(
        kernel,
        out_shape=tuple(outs),
        in_specs=[pl.BlockSpec(memory_space=places)] * len(operands),
        out_specs=tuple(pl.BlockSpec(memory_space=target) for _ in outs),
        scratch_shapes=list(scratch),
        compiler_params=pltpu.CompilerParams(vmem_limit_bytes=mebibytes * 1024 * 1024),
        cost_estimate=pl.CostEstimate(flops=flops, bytes_accessed=moved, transcendentals=0),
    )(*operands)
    return found[0] if len(outs) == 1 else found


def per_device_kernels(field, cotangent, qk_weight, w_value, w_out):
    span_x = lax.axis_size("gx")
    span_y = lax.axis_size("gy")
    count = span_x * span_y
    rows_x, rows_y, depth = field.shape[1:]
    cells = rows_x * rows_y
    places = count * cells
    grid_x = rows_x * span_x
    grid_y = rows_y * span_y
    rows = WIDTH * cells
    wide = WIDTH * HEAD_DIM
    f32, bf16 = jnp.float32, jnp.bfloat16
    like = jax.ShapeDtypeStruct
    lengths = ((grid_x, grid_y * depth), (grid_y, grid_x * depth))

    cell = np.arange(places)
    at_x = cell // cells // span_y * rows_x + cell % cells // rows_y
    at_y = cell // cells % span_y * rows_y + cell % rows_y
    same = jnp.asarray(
        np.stack([at_x[:, None] == at_x[None], at_y[:, None] == at_y[None]]), dtype=bf16
    )

    half = depth // 2
    halves = pltpu.VMEM((2, WIDTH, half), f32)
    chunked = [pltpu.VMEM(field.shape, bf16), pltpu.SemaphoreType.DMA((4,))]
    factor_z = 1.0 / math.sqrt(HEAD_DIM * depth)
    cube = rows * wide * depth * 2

    cots = run(
        rows_kernel,
        [like((rows, depth), bf16)],
        (pltpu.with_memory_space_constraint(cotangent, pltpu.HBM),),
        places=pltpu.HBM,
        flops=cube,
        scratch=chunked,
    )

    def swaps(sent, axis, size, farthest=True):
        if not isinstance(sent, (tuple, list)):
            sent = [sent] * size
        steps = range(size - 1, 0, -1)
        found = {}
        for step in steps if farthest else reversed(steps):
            found[step] = swap(sent[step], axis, size, step)
        return tuple(sent[:1]) + tuple(found[step] for step in steps)

    def taken(kernel, sent, dtype=None, last=False):
        found, *others = sent
        for part in others if last else others[:-1]:
            more = part.shape[0] if kernel is stack_kernel else part.shape[0] - WIDTH
            shape = (found.shape[0] + more,) + part.shape[1:]
            found = run(kernel, [like(shape, dtype or found.dtype)], (found, part))
        return (found,) if last else (found, others[-1])

    *sums, cols = run(
        sums_kernel,
        [like((WIDTH + cells, half), f32)] * 2 + [like((rows, depth), bf16)],
        (pltpu.with_memory_space_constraint(field, pltpu.HBM),),
        places=pltpu.HBM,
        flops=cube // 4,
        scratch=[chunked[0], halves, chunked[1]],
    )
    wv, wo, wq, wk, wz = run(
        prepare_kernel,
        [like((WIDTH, wide), f32)] * 2 + [like((2 * WIDTH, wide), bf16)] * 2
        + [like((2 * WIDTH, WIDTH), f32)],
        (w_value, w_out, qk_weight),
        flops=cube // 8,
    )
    total, other = sums
    for level in range(span_x.bit_length() - 1):
        step = 1 << level
        total = run(
            functools.partial(add_beside_kernel, step),
            [like((WIDTH + cells, half), f32)],
            (total, swap(total if level else other, "gx", span_x, step)),
        )
    sent = run(narrow_kernel, [like((WIDTH + 2 * cells, half), bf16)], (total,))
    for part in swaps(sent, "gy", span_y)[1:]:
        shape = (total.shape[0] + cells, half)
        total = run(add_narrow_kernel, [like(shape, f32)], (total, part))
    totals = (total,)
    totals, cots, wz = lax.optimization_barrier((totals, cots, wz))
    mine = run(
        functools.partial(factor_kernel, grid_x * grid_y),
        [like((WIDTH + HEAD_DIM, half), f32)],
        totals,
    )
    mix, feat, full = run(
        functools.partial(plane_kernel, cells, span_x, lengths),
        [like((2, HEADS * cells, places), f32), like((8, places, WIDTH), f32),
         like((2, HEADS * places, places), f32)],
        totals + (same, qk_weight),
        flops=cube // 2,
    )
    send, both, feat_z = run(
        coef_kernel,
        [like((2 * cells, wide), bf16), like((2 * WIDTH, depth), bf16),
         like((WIDTH + HEAD_DIM, depth), f32)],
        (mine, swap(mine, "gx", span_x, 1), wz, cols, cots, wv, wo),
        flops=2 * cube,
        scratch=[pltpu.VMEM((2, WIDTH + HEAD_DIM, half), f32)],
    )
    (low,) = taken(stack_kernel, swaps(send, "gy", span_y), last=True)
    first, *others = swaps(low, "gx", span_x, False)
    lows = (first,) + tuple(reversed(others))
    pulled = like((WIDTH, depth), bf16)
    top, total = run(
        functools.partial(mix_kernel, factor_z, span_x),
        [like((2, cells, wide), f32), pulled],
        lows + (mix, wv, wo, wq, wk, cols, cots),
        flops=cube,
    )
    total = run(add_pull_kernel, [pulled], (total, swap(total, "gx", span_x, 1)))
    for level in range(1, span_x.bit_length() - 1):
        total = run(add_pull_kernel, [pulled], (total, swap(total, "gx", span_x, 1 << level)))
    layer_output = run(
        output_kernel, [like(field.shape, bf16)], (top, wo, both, cols), flops=cube
    )
    plane = run(
        functools.partial(gram_kernel, cells, lengths, factor_z),
        [like((rows, LANES), f32)],
        lows + (feat, full, same, qk_weight),
        flops=2 * cube,
    )
    total, plane = lax.optimization_barrier((total, plane))
    base = run(base_kernel, [like((rows, depth), f32)], (top, wv, both, cots, plane), flops=cube)
    field_grad = run(
        functools.partial(final_kernel, grid_x * grid_y),
        [like(field.shape, bf16)],
        swaps(total, "gy", span_y, False) + (feat_z, base),
        target=pltpu.HBM,
        scratch=chunked,
    )
    return (layer_output, field_grad)


def solution(mesh):
    placed = P(None, ("groups", "gx"), "gy", None)
    count = mesh.shape["gx"] * mesh.shape["gy"]

    def program(*arrays):
        _, grid_x, grid_y, depth = arrays[0].shape
        places = grid_x // mesh.shape["groups"] * grid_y
        small = places == LANES and places == 8 * count
        small = small and depth == LANES * mesh.shape["gx"] and count & (count - 1) == 0
        small = small and mesh.shape["gx"] > 3
        return jax.shard_map(
            per_device_kernels if small else per_device,
            mesh=mesh,
            in_specs=(placed, placed, P(), P(), P()),
            out_specs=(placed, placed),
            check_vma=False,
        )(*arrays)

    return program
```
